32 devices in a mesh: seq: 8 (over y, x, core), head: 4 (over z).
Axes of the slice: x: 2, y: 2, z: 4, core: 2. Of those that a mesh axis runs over, the one named last changes fastest.
Arguments:
- tokens: bfloat16 [2, 4096, 2048], P(None, 'seq'), may hold values from -6 to 6
- gain_attn: float32 [2048], replicated, may hold values from 0.5 to 1.5
- w_query: bfloat16 [2048, 2048], P(None, 'head'), may hold values from -0.125 to 0.125
- w_key: bfloat16 [2048, 2048], P(None, 'head'), may hold values from -0.125 to 0.125
- w_value: bfloat16 [2048, 2048], P(None, 'head'), may hold values from -0.125 to 0.125
- w_forget: bfloat16 [2048, 256], P(None, 'head'), may hold values from -0.0625 to 0.0625
- forget_bias: float32 [256], P('head')
- w_out: bfloat16 [2048, 2048], P('head'), may hold values from -8 to 8
- gain_ffn: float32 [2048], replicated, may hold values from 0.5 to 1.5
- w_gate: bfloat16 [2048, 5632], P('seq', 'head'), may hold values from -0.125 to 0.125
- w_up: bfloat16 [2048, 5632], P('seq', 'head'), may hold values from -0.125 to 0.125
- w_down: bfloat16 [5632, 2048], P('head', 'seq'), may hold values from -0.078125 to 0.078125
- cotangent: bfloat16 [2, 4096, 2048], P(None, 'seq'), may hold values from -6 to 6
Outputs:
- out: bfloat16 [2, 4096, 2048], P(None, 'seq')
- in_grad: float32 [2, 4096, 2048], P(None, 'seq')
- grad_gain_attn: float32 [2048], P('seq')
- grad_w_query: float32 [2048, 2048], P('seq', 'head')
- grad_w_key: float32 [2048, 2048], P('seq', 'head')
- grad_w_value: float32 [2048, 2048], P('seq', 'head')
- grad_w_forget: float32 [2048, 256], P('seq', 'head')
- grad_forget_bias: float32 [256], P('head')
- grad_w_out: float32 [2048, 2048], P('head', 'seq')
- grad_gain_ffn: float32 [2048], P('seq')
- grad_w_gate: float32 [2048, 5632], P('seq', 'head')
- grad_w_up: float32 [2048, 5632], P('seq', 'head')
- grad_w_down: float32 [5632, 2048], P('head', 'seq')
The draws below stay inside these ranges and needn't reach their ends.
All inputs are finite; a program needn't handle non-finite values.
Results may differ from the reference program's by a relative error of at most 0.025.
Values may be sent and summed in bfloat16 or wider, within the bound.
No kernel may reach another device: no remote copies, remote signals or barrier semaphores. Data moves between devices by JAX's collectives and lax.ppermute only.
A program may use at most 320 MiB of HBM per device.

```python
import jax
import jax.numpy as jnp
from jax import lax

D = 2048
HEADS = 4
DH = 512
SLOTS = 64
FF = 5632
MB = 2
BLK = 128
SEQ_ROWS = 4096
LENGTH = 8192


rate_bound = 0.5


def draw_forget_bias(key, part):
    key = jax.random.fold_in(key, 7)
    first_key, second_key = jax.random.split(key)
    slot_total = HEADS * SLOTS
    slow_share = 0.5
    slow_slots = jax.random.uniform(first_key, (slot_total,)) < slow_share
    low_end = jnp.where(slow_slots, 0.2 / LENGTH, 0.005)
    high_end = jnp.where(slow_slots, 1.5 / LENGTH, 0.04)
    mixing = jax.random.uniform(second_key, (slot_total,))
    rate_start = low_end * jnp.exp(mixing * jnp.log(high_end / low_end))
    return jnp.log(rate_bound / rate_start - 1.0)


def block_levels(key, dims, shards, smallest, largest):
    loudness = 1.0
    for position, shards_of in shards:
        draws = jax.random.uniform(jax.random.fold_in(jax.random.fold_in(key, 6), position), (shards_of,), jnp.float32, smallest / len(shards), largest / len(shards))
        loudness = loudness * jnp.repeat(jnp.exp(draws), dims[position] // shards_of).reshape((-1,) + (1,) * (len(dims) - 1 - position))
    return loudness


def scatter_about(key, shape, deviation, limit, cuts=(), held_as=jnp.bfloat16):
    entries = deviation * jax.random.normal(key, shape, jnp.float32)
    if cuts:
        entries = entries * block_levels(key, shape, cuts, -0.22, 0.18)
    return jnp.clip(entries, -limit, limit).astype(held_as)


def setup_inputs(seed: int = 0) -> dict:
    streams_of = jax.random.split(jax.random.key(seed), 14)
    tokens = scatter_about(streams_of[0], (MB, SEQ_ROWS, D), 1.0, 6.0, ((1, 8),))
    gain_attn = jnp.clip(1.0 + 0.1 * jax.random.normal(streams_of[1], (D,), jnp.float32), 0.5, 1.5)
    w_query = scatter_about(streams_of[2], (D, HEADS * DH), D ** -0.5, 0.125, ((1, 4),))
    w_key = scatter_about(streams_of[3], (D, HEADS * DH), D ** -0.5, 0.125, ((1, 4),))
    w_value = scatter_about(streams_of[4], (D, HEADS * DH), D ** -0.5, 0.125, ((1, 4),))
    w_forget = scatter_about(streams_of[5], (D, HEADS * SLOTS), (4 * D) ** -0.5, 0.0625, ((1, 4),))
    forget_bias = draw_forget_bias(jax.random.fold_in(streams_of[13], 71), 0)
    w_out = scatter_about(streams_of[7], (HEADS * DH, D), 1.5, 8.0, ((0, 4),))
    gain_ffn = jnp.clip(1.0 + 0.1 * jax.random.normal(streams_of[8], (D,), jnp.float32), 0.5, 1.5)
    w_gate = scatter_about(streams_of[9], (D, FF), D ** -0.5, 0.125, ((0, 8), (1, 4)))
    w_up = scatter_about(streams_of[10], (D, FF), D ** -0.5, 0.125, ((0, 8), (1, 4)))
    w_down = scatter_about(streams_of[11], (FF, D), FF ** -0.5, 0.078125, ((0, 4), (1, 8)))
    cotangent = scatter_about(streams_of[12], (MB, SEQ_ROWS, D), 1.0, 6.0, ((1, 8),))
    return {"tokens": tokens, "gain_attn": gain_attn, "w_query": w_query, "w_key": w_key, "w_value": w_value, "w_forget": w_forget, "forget_bias": forget_bias, "w_out": w_out, "gain_ffn": gain_ffn, "w_gate": w_gate, "w_up": w_up, "w_down": w_down, "cotangent": cotangent}


norm_eps = 1e-06
rate_bound = 0.5
highest = lax.Precision.HIGHEST

@jax.custom_vjp
def low(v):
    return lax.optimization_barrier(v.astype(jnp.bfloat16)).astype(jnp.float32)

@jax.custom_vjp
def low_back(v):
    return v

def low_keep(v):
    return (low(v), None)

def low_pass(kept, grad):
    return (grad,)

def back_keep(v):
    return (v, None)

def back_low(kept, grad):
    return (low(grad),)
low.defvjp(low_keep, low_pass)
low_back.defvjp(back_keep, back_low)

def precise(left, right):
    return jnp.dot(left, right, precision=highest)

def rms_norm(values, gain):
    factor = lax.rsqrt(lax.optimization_barrier(jnp.mean(values * values, axis=-1, keepdims=True)) + norm_eps)
    return values * factor * gain

def block_core(query_rows, key_rows, value_rows, log_keep, slot_state):
    block_rows = query_rows.shape[0]
    head_width = query_rows.shape[1]
    causal = jnp.arange(block_rows)[:, None] >= jnp.arange(block_rows)[None, :]
    cumulative = jnp.cumsum(log_keep, axis=0)
    growth = jnp.exp(cumulative)
    inflow = jnp.exp(-cumulative) * -jnp.expm1(log_keep)
    pair_scores = jnp.where(causal, precise(query_rows, key_rows.T), 0.0)
    scores = growth * (precise(query_rows, slot_state[:, :head_width].T) + precise(pair_scores, inflow))
    slot_probs = jax.nn.softmax(scores, axis=-1)
    weights = slot_probs * growth
    mixing = jnp.where(causal, precise(weights, inflow.T), 0.0)
    output = precise(weights, slot_state[:, head_width:]) + precise(mixing, value_rows)
    joined = jnp.concatenate([key_rows, value_rows], 1)
    new_state = jnp.exp(cumulative[-1])[:, None] * (slot_state + precise(inflow.T, joined))
    return (output, new_state)

def head_scan(query_rows, key_rows, value_rows, log_keep):

    def advance(slot_state, pieces):
        output, new_state = block_core(pieces[0], pieces[1], pieces[2], pieces[3], slot_state)
        return (new_state, output)
    blocks = query_rows.shape[0] // BLK
    pieces_all = tuple((member.reshape(blocks, BLK, member.shape[1]) for member in (query_rows, key_rows, value_rows, log_keep)))
    start_state = jnp.zeros((SLOTS, 2 * DH), jnp.float32)
    unused, outputs = lax.scan(jax.checkpoint(advance), start_state, pieces_all)
    return outputs.reshape(query_rows.shape[0], DH)

def block_layer(tokens, gain_attn, w_query, w_key, w_value, w_forget, forget_bias, w_out, gain_ffn, w_gate, w_up, w_down):
    normed = low(rms_norm(tokens, gain_attn))
    query_rows = low(low_back(precise(normed, w_query)))
    key_rows = low(low_back(precise(normed, w_key)))
    value_rows = low(low_back(precise(normed, w_value)))
    forget_logit = low_back(precise(normed, w_forget) + forget_bias)
    log_keep = -rate_bound * jax.nn.sigmoid(-forget_logit)
    heads_out = []
    for head_pos in range(HEADS):
        columns = slice(head_pos * DH, (head_pos + 1) * DH)
        slot_cols = slice(head_pos * SLOTS, (head_pos + 1) * SLOTS)
        heads_out.append(head_scan(query_rows[:, columns], key_rows[:, columns], value_rows[:, columns], log_keep[:, slot_cols]))
    mixed_heads = low(jnp.concatenate(heads_out, 1))
    attended = low_back(precise(mixed_heads, w_out))
    hidden = tokens + attended
    normed_ffn = low(rms_norm(hidden, gain_ffn))
    gate_rows = low_back(precise(normed_ffn, w_gate))
    up_rows = low_back(precise(normed_ffn, w_up))
    act_rows = low(jax.nn.silu(gate_rows) * up_rows)
    ffn_rows = low_back(precise(act_rows, w_down))
    return hidden + ffn_rows

def reference(tokens, gain_attn, w_query, w_key, w_value, w_forget, forget_bias, w_out, gain_ffn, w_gate, w_up, w_down, cotangent):
    inputs = (tokens.reshape(LENGTH, D), gain_attn, w_query, w_key, w_value, w_forget, forget_bias, w_out, gain_ffn, w_gate, w_up, w_down)
    floats = tuple((member.astype(jnp.float32) for member in inputs))
    primal, pullback = jax.vjp(block_layer, *floats)
    gradients = pullback(cotangent.reshape(LENGTH, D).astype(jnp.float32))
    result_rows = primal.astype(jnp.bfloat16).reshape(MB, SEQ_ROWS, D)
    return (result_rows, gradients[0].reshape(MB, SEQ_ROWS, D), gradients[1], gradients[2], gradients[3], gradients[4], gradients[5], gradients[6], gradients[7], gradients[8], gradients[9], gradients[10], gradients[11])
```

```python
import functools

import jax
import jax.numpy as jnp
from jax import lax
from jax.experimental import pallas as pl
from jax.experimental.pallas import tpu as pltpu
from jax.sharding import PartitionSpec as P

CHUNK = 128
TILE = 256
EPS = 1e-06
RATE = 0.5
MIB = 2**20
f32 = jnp.float32
bf16 = jnp.bfloat16
highest = lax.Precision.HIGHEST


def nn(a, b):
    return lax.dot_general(a, b, (((1,), (0,)), ((), ())), preferred_element_type=f32)


def nt(a, b):
    return lax.dot_general(a, b, (((1,), (1,)), ((), ())), preferred_element_type=f32)


def tn(a, b):
    return lax.dot_general(a, b, (((0,), (0,)), ((), ())), preferred_element_type=f32)


def exact(a, b, dims):
    return lax.dot_general(a, b, (dims, ((), ())), precision=highest, preferred_element_type=f32)


def halves(a):
    high = a.astype(bf16)
    return high, (a - high.astype(f32)).astype(bf16)


def call(name, kernel, grid, in_specs, out_specs, out_shape, scratch=(), vmem=48, cost=None):
    return pl.pallas_call(
        kernel,
        name=name,
        grid=grid,
        in_specs=in_specs,
        out_specs=out_specs,
        out_shape=out_shape,
        scratch_shapes=scratch,
        compiler_params=pltpu.CompilerParams(
            dimension_semantics=("arbitrary",) * len(grid), vmem_limit_bytes=vmem * MIB
        ),
        cost_estimate=cost,
    )


def cost(flops, data):
    return pl.CostEstimate(flops=int(flops), bytes_accessed=int(data), transcendentals=0)


def fixed(shape):
    zeros = (0,) * len(shape)
    return pl.BlockSpec(shape, lambda *_: zeros, pipeline_mode=pl.Buffered(1))


def shaped(shape, dtype):
    return jax.ShapeDtypeStruct(shape, dtype)


def triangle(lower):
    r = lax.broadcasted_iota(jnp.int32, (CHUNK, CHUNK), 0)
    c = lax.broadcasted_iota(jnp.int32, (CHUNK, CHUNK), 1)
    return r >= c if lower else r <= c


def gates(z):
    la = -RATE * lax.logistic(-z)
    y = -la
    taken = jnp.ones_like(y)
    for n in range(9, 1, -1):
        taken = 1.0 - y * (1.0 / n) * taken
    taken = y * taken
    cum = exact(triangle(True).astype(f32), la, ((1,), (0,)))
    total = exact(la, jnp.ones((CHUNK, 128), f32), ((0,), (0,)))
    return la, cum, jnp.exp(-cum) * taken, total


def project_kernel(per_part, x_ref, gain_ref, wq_ref, wk_ref, wv_ref, wf_ref, bias_ref,
                   xn_ref, q_ref, k_ref, v_ref, z_ref, s_ref, d_ref, state, decay):
    @pl.when(lax.rem(pl.program_id(0), per_part) == 0)
    def _():
        state[...] = jnp.zeros_like(state)
        decay[...] = jnp.zeros_like(decay)

    x = x_ref[...].astype(f32)
    r1 = lax.rsqrt(jnp.mean(x * x, axis=-1, keepdims=True) + EPS)
    xn = (x * r1 * gain_ref[...]).astype(bf16)
    xn_ref[...] = xn
    q_ref[...] = nn(xn, wq_ref[...]).astype(bf16)
    k_ref[...] = nn(xn, wk_ref[...]).astype(bf16)
    v_ref[...] = nn(xn, wv_ref[...]).astype(bf16)
    z_ref[...] = nn(xn, wf_ref[...]) + bias_ref[...]
    width = k_ref.shape[1]
    for c in range(x_ref.shape[0] // CHUNK):
        rows = pl.ds(c * CHUNK, CHUNK)
        _, _, inflow, total = gates(z_ref[rows, :])
        spread = inflow.astype(bf16)
        keep = jnp.exp(total[:, :1])
        state[:, :width] = keep * (state[:, :width] + tn(spread, k_ref[rows, :]))
        state[:, width:] = keep * (state[:, width:] + tn(spread, v_ref[rows, :]))
        decay[...] += total
    s_ref[0] = state[...]
    d_ref[0] = decay[...]


def read_kernel(per_part, q_ref, k_ref, v_ref, z_ref, e0_ref, o_ref, p_ref, sc_ref, e_ref, state):
    @pl.when(lax.rem(pl.program_id(0), per_part) == 0)
    def _():
        state[...] = e0_ref[0]

    width = q_ref.shape[1]
    lower = triangle(True)
    for c in range(q_ref.shape[0] // CHUNK):
        rows = pl.ds(c * CHUNK, CHUNK)
        q, k, v = q_ref[rows, :], k_ref[rows, :], v_ref[rows, :]
        _, cum, inflow, total = gates(z_ref[rows, :])
        growth = jnp.exp(cum)
        e_ref[c] = state[...]
        i_hi, i_lo = halves(inflow)
        a_hi, a_lo = halves(jnp.where(lower, nt(q, k), 0.0))
        e_hi, e_lo = halves(state[:, :width])
        scores = growth * (
            nt(q, e_hi) + nt(q, e_lo) + nn(a_hi, i_hi) + (nn(a_hi, i_lo) + nn(a_lo, i_hi))
        )
        top = jnp.exp(scores - jnp.max(scores, axis=-1, keepdims=True))
        p = top / jnp.sum(top, axis=-1, keepdims=True)
        w = (p * growth).astype(bf16)
        mixing = jnp.where(lower, nt(w, i_hi), 0.0).astype(bf16)
        o_ref[rows, :] = (nn(w, state[:, width:].astype(bf16)) + nn(mixing, v)).astype(bf16)
        p_ref[rows, :] = p
        sc_ref[rows, :] = scores
        keep = jnp.exp(total[:, :1])
        state[:, :width] = keep * (state[:, :width] + tn(i_hi, k))
        state[:, width:] = keep * (state[:, width:] + tn(i_hi, v))


def back_kernel(per_part, dhn_ref, hid_ref, cot_ref, gain_ref, wo_ref, q_ref, k_ref, v_ref, z_ref, p_ref, sc_ref, e_ref,
                dhid_ref, datt_ref, dq_ref, dkl_ref, dvl_ref, h_ref, x1_ref, g_ref, s_ref, gg_ref, state):
    step = pl.program_id(0)

    @pl.when(lax.rem(step, per_part) == 0)
    def _():
        state[...] = jnp.zeros_like(state)

    @pl.when(step == 0)
    def _():
        gg_ref[...] = jnp.zeros_like(gg_ref)

    hidden = hid_ref[...]
    dhn = dhn_ref[...].astype(f32)
    r2 = lax.rsqrt(jnp.mean(hidden * hidden, axis=-1, keepdims=True) + EPS)
    gg_ref[...] += jnp.sum((dhn * hidden * r2).reshape(-1, 8, hidden.shape[1]), axis=0)
    u2 = gain_ref[...] * dhn
    dhid = (
        cot_ref[...].astype(f32)
        + r2 * u2
        - hidden * (r2 * r2 * r2) * jnp.mean(u2 * hidden, axis=-1, keepdims=True)
    )
    dhid_ref[...] = dhid
    datt_ref[...] = dhid.astype(bf16)
    width = q_ref.shape[1]
    do_all = nt(datt_ref[...], wo_ref[...]).astype(bf16)
    lower, upper = triangle(True), triangle(False)
    for c in reversed(range(q_ref.shape[0] // CHUNK)):
        rows = pl.ds(c * CHUNK, CHUNK)
        q, k, v = q_ref[rows, :], k_ref[rows, :], v_ref[rows, :]
        do = do_all[c * CHUNK : (c + 1) * CHUNK]
        _, cum, inflow, total = gates(z_ref[rows, :])
        growth = jnp.exp(cum)
        p = p_ref[rows, :]
        i_hi, i_lo = halves(inflow)
        b_hi, b_lo = halves(jnp.where(lower, nt(do, v), 0.0))
        ev_hi, ev_lo = halves(e_ref[c, :, width:])
        dp = growth * (
            nt(do, ev_hi) + nt(do, ev_lo) + nn(b_hi, i_hi) + (nn(b_hi, i_lo) + nn(b_lo, i_hi))
        )
        ds = p * (dp - jnp.sum(p * dp, axis=-1, keepdims=True))
        w = (p * growth).astype(bf16)
        gds = (growth * ds).astype(bf16)
        n = jnp.where(lower, nt(gds, i_hi), 0.0).astype(bf16)
        dq_ref[rows, :] = (nn(gds, e_ref[c, :, :width].astype(bf16)) + nn(n, k)).astype(bf16)
        n_t = jnp.where(upper, nt(i_hi, gds), 0.0).astype(bf16)
        m_t = jnp.where(upper, nt(i_hi, w), 0.0).astype(bf16)
        dkl_ref[rows, :] = nn(n_t, q)
        dvl_ref[rows, :] = nn(m_t, do)
        h_ref[rows, :] = ds * sc_ref[rows, :] + p * dp
        a_t = jnp.where(upper, nt(k, q), 0.0).astype(bf16)
        b_t = jnp.where(upper, nt(v, do), 0.0).astype(bf16)
        x1_ref[rows, :] = nn(a_t, gds) + nn(b_t, w)
        keep = jnp.exp(total[:, :1])
        g_k, g_v = tn(gds, q), tn(w, do)
        g_ref[c, :, :width] = g_k
        g_ref[c, :, width:] = g_v
        state[:, :width] = g_k + keep * state[:, :width]
        state[:, width:] = g_v + keep * state[:, width:]
    s_ref[0] = state[...]


def last_kernel(per_part, l0_ref, k_ref, v_ref, z_ref, e_ref, g_ref, dkl_ref, dvl_ref, h_ref, x1_ref, dq_ref, x_ref,
                wq_ref, wk_ref, wv_ref, wf_ref, dk_ref, dv_ref, dz_ref, dxn_ref, bias_ref, gg_ref, state):
    step = pl.program_id(0)

    @pl.when(lax.rem(step, per_part) == 0)
    def _():
        state[...] = l0_ref[0]

    @pl.when(step == 0)
    def _():
        gg_ref[...] = jnp.zeros_like(gg_ref)
        bias_ref[...] = jnp.zeros_like(bias_ref)

    width = k_ref.shape[1]
    low, up = triangle(True).astype(f32), triangle(False).astype(f32)
    for c in reversed(range(k_ref.shape[0] // CHUNK)):
        rows = pl.ds(c * CHUNK, CHUNK)
        k, v = k_ref[rows, :], v_ref[rows, :]
        z = z_ref[rows, :]
        _, cum, inflow, total = gates(z)
        i_hi = inflow.astype(bf16)
        keep = jnp.exp(total[:, :1])
        lg = keep * state[...]
        lg_k, lg_v = lg[:, :width].astype(bf16), lg[:, width:].astype(bf16)
        dk_ref[rows, :] = (dkl_ref[rows, :] + nn(i_hi, lg_k)).astype(bf16)
        dv_ref[rows, :] = (dvl_ref[rows, :] + nn(i_hi, lg_v)).astype(bf16)
        x1 = x1_ref[rows, :]
        x2 = nt(k, lg_k) + nt(v, lg_v)
        met = exact(jnp.ones((8, 2 * width), f32), lg * e_ref[c], ((1,), (1,)))
        h, r1 = h_ref[rows, :], inflow * x1
        dla = (
            exact(up, h - r1, ((1,), (0,)))
            + r1
            + exact(low, inflow * x2, ((1,), (0,)))
            + met[:1]
            - jnp.exp(-cum) * (x1 + x2)
        )
        rate = lax.logistic(-z)
        dz = (dla * RATE * rate * (1.0 - rate)).astype(bf16)
        dz_ref[rows, :] = dz
        bias_ref[...] += jnp.sum(dz.astype(f32).reshape(-1, 8, dz.shape[1]), axis=0)
        state[...] = g_ref[c] + lg
    dxn = (
        nt(dq_ref[...], wq_ref[...])
        + nt(dk_ref[...], wk_ref[...])
        + nt(dv_ref[...], wv_ref[...])
        + nt(dz_ref[...], wf_ref[...])
    )
    dxn_ref[...] = dxn.astype(bf16)
    x = x_ref[...].astype(f32)
    r1 = lax.rsqrt(jnp.mean(x * x, axis=-1, keepdims=True) + EPS)
    gg_ref[...] += jnp.sum((dxn * x * r1).reshape(-1, 8, x.shape[1]), axis=0)


def hidden_kernel(n_head, place_ref, *refs):
    o_refs, (x_ref, gain_ref), w_refs = refs[:n_head], refs[n_head : n_head + 2], refs[n_head + 2 : n_head + 7]
    hid_ref, hn_ref, blocks, weights, sems = refs[n_head + 7 :]
    quarter = w_refs[1].shape[1]
    copies = [pltpu.make_async_copy(w_refs[0], weights.at[0], sems.at[0])]
    for d in range(1, n_head):
        for i in range(4):
            rows = pl.ds(pl.multiple_of(place_ref[1 + i] * quarter, quarter), quarter)
            copies.append(
                pltpu.make_async_copy(w_refs[1 + i].at[d - 1], weights.at[d, rows, :], sems.at[len(copies)])
            )

    @pl.when(pl.program_id(0) == 0)
    def _():
        for copy in copies:
            copy.start()
        for copy in copies:
            copy.wait()

    for d in range(n_head):
        blocks[d] = o_refs[d][...]
    me = place_ref[0]
    attended = None
    for h in range(n_head):
        away = lax.rem(me - h + n_head, n_head)
        term = nn(blocks[away], weights[away])
        attended = term if attended is None else attended + term
    hidden = x_ref[...].astype(f32) + attended
    hid_ref[...] = hidden
    r2 = lax.rsqrt(jnp.mean(hidden * hidden, axis=-1, keepdims=True) + EPS)
    hn_ref[...] = (hidden * r2 * gain_ref[...]).astype(bf16)


def flat(ref):
    block = ref[...]
    return block.reshape(block.shape[0] * block.shape[1], block.shape[2])


def units_kernel(hn_ref, cot_ref, wg_ref, wu_ref, wd_ref, act_ref, dg_ref, du_ref):
    gate = nn(hn_ref[...], flat(wg_ref))
    up = nn(hn_ref[...], flat(wu_ref))
    dact = nn(cot_ref[...], flat(wd_ref))
    s = lax.logistic(gate)
    silu = gate * s
    act_ref[...] = (silu * up).astype(bf16)
    dg_ref[...] = (dact * up * s * (1.0 + gate * (1.0 - s))).astype(bf16)
    du_ref[...] = (dact * silu).astype(bf16)


def wide_kernel(pairs, *refs):
    outs = refs[2 * pairs :]
    total = nt(refs[0][...], flat(refs[pairs]))
    for i in range(1, pairs):
        total = total + nt(refs[i][...], flat(refs[pairs + i]))
    total = total.astype(bf16)
    for t, out in enumerate(outs):
        out[...] = total[t * TILE : (t + 1) * TILE]


def summed(pairs):
    total = tn(*pairs[0])
    for pair in pairs[1:]:
        total = total + tn(*pair)
    return total.astype(bf16)


def ffn_grad_kernel(*refs):
    cot_ref, out_ref = refs[(len(refs) - 2) // 4], refs[-1]
    parts = cot_ref.shape[0]
    hn, dg, du, act = refs[:parts], *(refs[i * parts + 1 : (i + 1) * parts + 1] for i in (1, 2, 3))
    blocks, _, width, units = out_ref.shape
    for i, grads in enumerate((dg, du)):
        block = summed([(hn[m][...], grads[m][...]) for m in range(parts)])
        out_ref[:, i] = block.reshape(blocks, width, units)
    block = summed([(cot_ref[m], act[m][...]) for m in range(parts)])
    out_ref[:, 2] = block.reshape(blocks, width, units)


def attn_grad_kernel(*refs):
    out_ref, dzw_ref = refs[-2:]
    xn_ref = refs[0]
    parts = (len(refs) - 3) // 6
    datt, dq, dk, dv, o, dz = (refs[1 + i * parts : 1 + (i + 1) * parts] for i in range(6))
    rows, width = dq[0].shape
    xn = [xn_ref[m * rows : (m + 1) * rows, :] for m in range(parts)]
    for i, grads in enumerate((dq, dk, dv)):
        out_ref[:, i * width : (i + 1) * width] = summed([(xn[m], grads[m][...]) for m in range(parts)])
    out_ref[:, 3 * width :] = summed([(datt[m][...], o[m][...]) for m in range(parts)])
    dzw_ref[...] = summed([(xn[m], dz[m][...]) for m in range(parts)])


def packed(decay, state):
    high = decay.astype(bf16)
    low = (decay - high.astype(f32)).astype(bf16)
    lane = lax.broadcasted_iota(jnp.int32, decay.shape[:-1] + (128,), decay.ndim - 1)
    return jnp.concatenate([state.astype(bf16), jnp.where(lane == 0, high, low)], -1)


def unpacked(arrived):
    tail = arrived[..., -128:].astype(f32)
    return tail[..., 0:1] + tail[..., 1:2], arrived[..., :-128].astype(f32)


def scan_states(decay, state, after, behind=()):
    n, me = lax.axis_size("seq"), lax.axis_index("seq")
    part = (jnp.ones_like(decay), jnp.zeros_like(state))
    whole = (decay, state)
    bit, arrivals = 1, []
    while bit < n:
        message = packed(*whole)
        if len(arrivals) < len(behind):
            message = behind_of(message, behind[len(arrivals)])
        arrivals.append(lax.ppermute(message, "seq", [(i, i ^ bit) for i in range(n)]))
        there = unpacked(arrivals[-1])
        first = (me & bit) == 0
        takes = first if after else jnp.logical_not(first)
        d, s = whole
        part = (
            jnp.where(takes, there[0] * part[0], part[0]),
            jnp.where(takes, part[1] + part[0] * there[1], part[1]),
        )
        whole = (
            d * there[0],
            jnp.where(takes, s + d * there[1], there[1] + there[0] * s),
        )
        bit *= 2
    return part, whole, arrivals


def chained(part, whole, parts):
    arriving = jnp.zeros_like(part[1][0])
    found = {}
    for m in parts:
        found[m] = part[1][m] + part[0][m] * arriving
        arriving = whole[1][m] + whole[0][m] * arriving
    return jnp.stack([found[m] for m in sorted(found)])


def turned(block, n):
    return [lax.ppermute(block, "head", [(i, (i + d) % n) for i in range(n)]) for d in range(1, n)]


def behind_of(value, *first):
    return lax.optimization_barrier((value,) + first)[0]


def added(a, b):
    return (a.astype(f32) + b.astype(f32)).astype(bf16)


class Line:
    INWARD, OUTWARD, MIDDLE = [(0, 1), (3, 2)], [(1, 0), (2, 3)], [(1, 2), (2, 1)]

    def __init__(self):
        me = lax.axis_index("head")
        self.end = (me == 0) | (me == 3)
        self.pair = self.total = None

    def step(self, piece=None, inputs=()):
        pair, total = self.pair, self.total
        sends = []
        if piece is not None and total is not None:
            sends.append((jnp.where(self.end, piece, total), self.INWARD + self.OUTWARD))
        elif piece is not None:
            sends.append((piece, self.INWARD))
        elif total is not None:
            sends.append((total, self.OUTWARD))
        if pair is not None:
            sends.append((pair, self.MIDDLE))
        values = [s[0] for s in sends] + list(inputs)
        gated = list(lax.optimization_barrier(tuple(values)))
        arrived = [lax.ppermute(g, "head", way) for g, (_, way) in zip(gated, sends)]
        outer = arrived[0] if piece is not None or total is not None else None
        self.pair = added(piece, outer) if piece is not None else None
        self.total = added(pair, arrived[-1]) if pair is not None else None
        done = jnp.where(self.end, outer, total) if total is not None else None
        return done, gated[len(sends) :]


def on_device(tokens, gain_attn, w_query, w_key, w_value, w_forget, forget_bias, w_out, gain_ffn, w_gate, w_up, w_down,
              cotangent):
    parts, part_rows, width = tokens.shape
    rows = parts * part_rows
    head = w_query.shape[1]
    slots = w_forget.shape[1]
    units = w_gate.shape[1]
    n_seq, n_head = lax.axis_size("seq"), lax.axis_size("head")
    span = w_gate.shape[0]
    steps = rows // TILE
    per_part = part_rows // TILE
    chunks = TILE // CHUNK

    gain1 = gain_attn.reshape(1, width)
    gain2 = gain_ffn.reshape(1, width)
    state_scratch = pltpu.VMEM((slots, 2 * head), f32)

    def tiled(columns, back=False):
        return pl.BlockSpec((TILE, columns), (lambda i: (per_part - 1 - i, 0)) if back else (lambda i: (i, 0)))

    def at(m, columns, back=False):
        return pl.BlockSpec(
            (TILE, columns),
            (lambda i: (m * per_part + per_part - 1 - i, 0)) if back else (lambda i: (m * per_part + i, 0)),
        )

    def part_at(m, columns, back=False):
        return pl.BlockSpec(
            (None, TILE, columns), (lambda i: (m, per_part - 1 - i, 0)) if back else (lambda i: (m, i, 0))
        )

    def chunked(back=False):
        return pl.BlockSpec(
            (chunks, slots, 2 * head), (lambda i: (per_part - 1 - i, 0, 0)) if back else (lambda i: (i, 0, 0))
        )

    def state_of(m, columns):
        return pl.BlockSpec((1, slots, columns), lambda i: (m, 0, 0))

    one_state = pl.BlockSpec((1, slots, 2 * head), lambda i: (0, 0, 0))
    per_chunk = shaped((part_rows // CHUNK, slots, 2 * head), f32)

    stacked = jnp.stack([w_gate, w_up, w_down.T])
    x = tokens.reshape(rows, width)
    place = lax.axis_index("seq")
    low_bit, high_bit = place & 1, (place & 2) // 2
    quarter = head // 4
    share = lax.dynamic_slice_in_dim(w_out, (2 * high_bit + low_bit) * quarter, quarter, 0)
    x, stacked, share = lax.optimization_barrier((x, stacked, share))
    full = lax.all_gather(stacked, "seq")
    shares = turned(share, n_head)
    all_rows = lambda c: pl.BlockSpec((TILE, c), lambda i: (i, 0))
    by_part = lambda c: pl.BlockSpec((1, slots, c), lambda i: (i // per_part, 0, 0))
    xn, q, k, v, z, local, decay_sum = call(
        "project",
        functools.partial(project_kernel, per_part),
        (steps,),
        [all_rows(width), fixed((1, width))] + [fixed((width, head))] * 3 + [fixed((width, slots)), fixed((1, slots))],
        [all_rows(width), all_rows(head), all_rows(head), all_rows(head), all_rows(slots), by_part(2 * head), by_part(128)],
        [shaped((rows, width), bf16)] + [shaped((rows, head), bf16)] * 3
        + [shaped((rows, slots), f32), shaped((parts, slots, 2 * head), f32), shaped((parts, slots, 128), f32)],
        [state_scratch, pltpu.VMEM((slots, 128), f32)],
        cost=cost(2 * rows * width * (3 * head + slots), 2 * rows * width * 3 + 2 * width * 3 * head),
    )(x, gain1, w_query, w_key, w_value, w_forget, forget_bias.reshape(1, slots))
    decay = jnp.exp(decay_sum[:, :, :1])
    before, everything, arrivals = scan_states(decay, local, False, shares[:2])
    entering = chained(before, everything, range(parts))

    held = jnp.stack(shares)
    held = behind_of(held, arrivals[1] if len(arrivals) > 1 else arrivals[0])
    across = lax.ppermute(held, "seq", [(i, i ^ 2) for i in range(n_seq)])
    beside = lax.ppermute(held, "seq", [(i, i ^ 1) for i in range(n_seq)])

    o, p, scores, e_chunks = [], [], [], []
    for m in range(parts):
        o_m, p_m, s_m, e_m = call(
            "read",
            functools.partial(read_kernel, per_part),
            (per_part,),
            [at(m, head)] * 3 + [at(m, slots), state_of(m, 2 * head)],
            [tiled(head), tiled(slots), tiled(slots), chunked()],
            [shaped((part_rows, head), bf16), shaped((part_rows, slots), f32), shaped((part_rows, slots), f32), per_chunk],
            [state_scratch],
            cost=cost(2 * part_rows * head * 600, 2 * part_rows * head * 4 + part_rows * slots * 64),
        )(q, k, v, z, entering)
        o.append(o_m)
        p.append(p_m)
        scores.append(s_m)
        e_chunks.append(e_m)

    turns = [turned(o_m, n_head) for o_m in o]
    beside_across = lax.ppermute(behind_of(across, turns[0][0]), "seq", [(i, i ^ 1) for i in range(n_seq)])
    low_place, high_place = 2 * high_bit, 2 * (1 - high_bit)
    places = jnp.stack(
        [lax.axis_index("head"), low_place + low_bit, high_place + low_bit, low_place + 1 - low_bit,
         high_place + 1 - low_bit]
    ).astype(jnp.int32)

    def project_out(m, own):
        return call(
            "hidden",
            functools.partial(hidden_kernel, n_head),
            (per_part,),
            [pl.BlockSpec(memory_space=pltpu.SMEM)] + [tiled(head)] * n_head + [at(m, width), fixed((1, width))]
            + [pl.BlockSpec(memory_space=pl.ANY)] * 5,
            [tiled(width), tiled(width)],
            [shaped((part_rows, width), f32), shaped((part_rows, width), bf16)],
            [pltpu.VMEM((n_head, TILE, head), bf16), pltpu.VMEM((n_head, head, width), bf16),
             pltpu.SemaphoreType.DMA((4 * n_head - 3,))],
            cost=cost(2 * part_rows * width * width, part_rows * width * 10 + 2 * width * width),
        )(places, own, *turns[m], x, gain2, w_out, held, across, beside, beside_across)

    unit_tile = 256
    unit_steps = pl.cdiv(units, unit_tile)

    def weight_tile(which):
        return pl.BlockSpec((n_seq, None, span, unit_tile), lambda j: (0, which, 0, j))

    def feed(m, hn):
        unit_out = pl.BlockSpec((part_rows, unit_tile), lambda j: (0, j))
        return call(
            "units",
            units_kernel,
            (unit_steps,),
            [fixed((part_rows, width)),
             pl.BlockSpec((None, part_rows, width), lambda j: (m, 0, 0), pipeline_mode=pl.Buffered(1)),
             weight_tile(0), weight_tile(1), weight_tile(2)],
            [unit_out] * 3,
            [shaped((part_rows, units), bf16)] * 3,
            cost=cost(6 * part_rows * width * units, 4 * part_rows * width + 6 * part_rows * units + 6 * width * units),
        )(hn, cotangent, full, full, full)

    group = max(1, TILE // span)
    wide = group * span
    pieces = part_rows // TILE

    def weight_rows(which):
        return pl.BlockSpec((group, None, span, units), lambda j: (j, which, 0, 0))

    def widened(name, sources, which):
        count = len(sources)
        return call(
            name,
            functools.partial(wide_kernel, count),
            (width // wide,),
            [fixed((part_rows, units))] * count + [weight_rows(i) for i in which],
            [pl.BlockSpec((TILE, wide), lambda j: (0, j))] * pieces,
            [shaped((TILE, width), bf16)] * pieces,
            cost=cost(2 * count * part_rows * width * units,
                      2 * count * (part_rows + width) * units + 2 * part_rows * width),
        )(*sources, *([full] * count))

    def back(m, dhn, hidden):
        return call(
            "back",
            functools.partial(back_kernel, per_part),
            (per_part,),
            [tiled(width, True), tiled(width, True), part_at(m, width, True), fixed((1, width)), fixed((head, width))]
            + [at(m, head, True)] * 3 + [at(m, slots, True)] + [tiled(slots, True)] * 2 + [chunked(True)],
            [tiled(width, True), tiled(width, True), tiled(head, True), tiled(head, True), tiled(head, True),
             tiled(slots, True), tiled(slots, True), chunked(True), one_state,
             pl.BlockSpec((8, width), lambda i: (0, 0))],
            [shaped((part_rows, width), f32), shaped((part_rows, width), bf16), shaped((part_rows, head), bf16),
             shaped((part_rows, head), f32), shaped((part_rows, head), f32), shaped((part_rows, slots), f32),
             shaped((part_rows, slots), f32), per_chunk, shaped((1, slots, 2 * head), f32), shaped((8, width), f32)],
            [state_scratch],
            cost=cost(2 * part_rows * width * head + 2 * part_rows * head * 1500,
                      part_rows * width * 14 + part_rows * head * 20),
        )(dhn, hidden, cotangent, gain2, w_out, q, k, v, z, p[m], scores[m], e_chunks[m])

    def last(m, leaving, saved):
        dq, dk_local, dv_local, h_sum, x_local, g_chunks = saved
        return call(
            "last",
            functools.partial(last_kernel, per_part),
            (per_part,),
            [state_of(m, 2 * head), at(m, head, True), at(m, head, True), at(m, slots, True), chunked(True), chunked(True),
             tiled(head, True), tiled(head, True), tiled(slots, True), tiled(slots, True), tiled(head, True),
             at(m, width, True)] + [fixed((width, head))] * 3 + [fixed((width, slots))],
            [tiled(head, True), tiled(head, True), tiled(slots, True), tiled(width, True),
             pl.BlockSpec((8, slots), lambda i: (0, 0)), pl.BlockSpec((8, width), lambda i: (0, 0))],
            [shaped((part_rows, head), bf16), shaped((part_rows, head), bf16), shaped((part_rows, slots), bf16),
             shaped((part_rows, width), bf16), shaped((8, slots), f32), shaped((8, width), f32)],
            [state_scratch],
            cost=cost(2 * part_rows * width * (3 * head + slots),
                      part_rows * width * 8 + part_rows * head * 20 + width * head * 6),
        )(leaving, k, v, z, e_chunks[m], g_chunks, dk_local, dv_local, h_sum, x_local, dq, x,
          w_query, w_key, w_value, w_forget)

    def ffn_grads(normed, gates, ups, acts):
        return call(
            "ffn_grads",
            ffn_grad_kernel,
            (width // wide,),
            [pl.BlockSpec((part_rows, wide), lambda j: (0, j))] * parts
            + [pl.BlockSpec((parts, part_rows, wide), lambda j: (0, 0, j))]
            + [fixed((part_rows, units))] * (3 * parts),
            pl.BlockSpec((group, 3, span, units), lambda j: (j, 0, 0, 0)),
            shaped((n_seq, 3, span, units), bf16),
            cost=cost(6 * rows * width * units, 4 * rows * width + 6 * rows * units + 6 * width * units),
            vmem=56,
        )(*normed, cotangent, *gates, *ups, *acts)

    line = Line()
    sums, order, live = {}, [], {}

    def advance(key=None, piece=None):
        names = list(live)
        done, gated = line.step(piece, [live[n] for n in names])
        live.update(zip(names, gated))
        order.append(key)
        if done is not None:
            sums[order[-3]] = done

    def joined(kind, m):
        return jnp.concatenate([sums[kind, m, t] for t in range(pieces)], 0)

    hidden, hn, act, dgate, dup, backs, lasts = ([None] * parts for _ in range(7))

    def forward(m, own):
        live["hidden", m], live["hn", m] = project_out(m, own)
        live["act", m], live["dgate", m], live["dup", m] = feed(m, live["hn", m])

    forward(0, o[0])
    dhn_parts = widened("dhn", (live["dgate", 0], live["dup", 0]), (0, 1))
    live["o", 1] = o[1]
    advance(("dhn", 0, 0), dhn_parts[0])

    forward(1, live["o", 1])
    live["later"] = dhn_parts[1]
    advance(("dhn", 0, 1), live.pop("later"))

    dhn_parts = widened("dhn", (live["dgate", 1], live["dup", 1]), (0, 1))
    ffn_a = widened("ffn", (live["act", 0],), (2,))
    live["later"], live["ffn", 0], live["ffn", 1] = dhn_parts[1], *ffn_a
    advance(("dhn", 1, 0), dhn_parts[0])

    live["ffn", 2], live["ffn", 3] = widened("ffn", (live["act", 1],), (2,))
    advance(("dhn", 1, 1), live.pop("later"))

    grads = ffn_grads(*([live[n, m] for m in range(parts)] for n in ("hn", "dgate", "dup", "act")))
    for n in ("hn", "dgate", "dup", "act"):
        for m in range(parts):
            del live[n, m]
    live["ffn_grads"] = grads
    advance(("ffn", 0, 0), live.pop(("ffn", 0)))

    ffn_shares = lax.psum_scatter(live.pop("ffn_grads"), "seq", scatter_dimension=0)
    backs[0] = back(0, joined("dhn", 0), live["hidden", 0])
    live["back", 0] = backs[0][8]
    advance(("ffn", 0, 1), live.pop(("ffn", 1)))

    advance(("ffn", 1, 0), live.pop(("ffn", 2)))

    backs[1] = back(1, joined("dhn", 1), live["hidden", 1])
    live["back", 1] = backs[1][8]
    advance(("ffn", 1, 1), live.pop(("ffn", 3)))

    local_back = jnp.concatenate([live.pop(("back", m)) for m in range(parts)], 0)
    behind, everything, _ = scan_states(decay, local_back, True)
    live["leaving"] = chained(behind, everything, reversed(range(parts)))
    live["ffn_shares"] = ffn_shares
    advance()

    lasts[0] = last(0, live["leaving"], backs[0][2:8])
    live["dxn", 0], live["dxn", 1] = lasts[0][3][:TILE], lasts[0][3][TILE:]
    ffn_shares = live.pop("ffn_shares")
    advance(("dxn", 0, 0), live.pop(("dxn", 0)))

    lasts[1] = last(1, live.pop("leaving"), backs[1][2:8])
    live["dxn", 2], live["dxn", 3], live["xn"] = lasts[1][3][:TILE], lasts[1][3][TILE:], xn
    advance(("dxn", 0, 1), live.pop(("dxn", 1)))
    xn = live.pop("xn")

    attn_grads, forget_grads = call(
        "attn_grads",
        attn_grad_kernel,
        (width // TILE,),
        [pl.BlockSpec((rows, TILE), lambda j: (0, j))] + [pl.BlockSpec((part_rows, TILE), lambda j: (0, j))] * parts
        + [fixed((part_rows, head))] * (4 * parts) + [fixed((part_rows, slots))] * parts,
        [pl.BlockSpec((TILE, 4 * head), lambda j: (j, 0)), pl.BlockSpec((TILE, slots), lambda j: (j, 0))],
        [shaped((width, 4 * head), bf16), shaped((width, slots), bf16)],
        cost=cost(2 * rows * width * (4 * head + slots), 4 * rows * width + 8 * rows * head + 8 * width * head),
    )(xn, *[b[1] for b in backs], *[b[2] for b in backs], *[n[0] for n in lasts], *[n[1] for n in lasts], *o,
      *[n[2] for n in lasts])
    live["attn_grads"] = attn_grads
    bias_sum = sum(jnp.sum(n[4], 0) for n in lasts)
    gain1_sum = sum(jnp.sum(n[5], 0) for n in lasts)
    gain2_sum = sum(jnp.sum(b[9], 0) for b in backs)
    small = jnp.concatenate(
        [
            forget_grads,
            gain2_sum.astype(bf16)[:, None],
            gain1_sum.astype(bf16)[:, None],
            jnp.zeros((width, 128 - 2 - slots % 128), bf16),
        ],
        1,
    ).reshape(n_seq, span, -1)
    bias_row = jnp.pad(jnp.stack(halves(bias_sum)), ((0, 14), (0, small.shape[2] - slots)))
    small = jnp.concatenate([small, jnp.broadcast_to(bias_row, (n_seq,) + bias_row.shape)], 1)
    live["small"] = small
    outs, in_grads = [], []

    def finish_out(m):
        outs.append((live.pop(("hidden", m)) + joined("ffn", m).astype(f32)).astype(bf16))

    def finish_grad(m):
        dxn = joined("dxn", m)
        xf = tokens[m].astype(f32)
        r1 = lax.rsqrt(jnp.mean(xf * xf, axis=-1, keepdims=True) + EPS)
        u1 = gain1 * dxn.astype(f32)
        in_grads.append(backs[m][0] + r1 * u1 - xf * (r1 * r1 * r1) * jnp.mean(u1 * xf, axis=-1, keepdims=True))

    advance(("dxn", 1, 0), live.pop(("dxn", 2)))
    small_shares = lax.psum_scatter(live.pop("small"), "seq", scatter_dimension=0).astype(f32)
    attn_shares = lax.psum_scatter(live.pop("attn_grads"), "seq", scatter_dimension=0, tiled=True).astype(f32)
    bias_total = small_shares[span, :slots] + small_shares[span + 1, :slots]
    gain1_total = small_shares[:span, slots + 1]
    bit = 1
    while bit < n_head:
        gain1_total = gain1_total + lax.ppermute(gain1_total, "head", [(i, i ^ bit) for i in range(n_head)])
        bit *= 2

    finish_out(0)
    live["out", 0] = outs[0]
    advance(("dxn", 1, 1), live.pop(("dxn", 3)))
    finish_out(1)
    live["out", 1] = outs[1]
    advance()
    finish_grad(0)
    live["in_grad"] = in_grads[0]
    advance()
    finish_grad(1)
    outs, in_grads[0] = [live["out", m] for m in range(parts)], live["in_grad"]

    return (
        jnp.stack(outs),
        jnp.stack(in_grads),
        gain1_total,
        attn_shares[:, :head],
        attn_shares[:, head : 2 * head],
        attn_shares[:, 2 * head : 3 * head],
        small_shares[:span, :slots],
        bias_total,
        attn_shares[:, 3 * head :].T,
        small_shares[:span, slots],
        ffn_shares[0].astype(f32),
        ffn_shares[1].astype(f32),
        ffn_shares[2].astype(f32).T,
    )


def solution(mesh):
    rows, both = P(None, "seq", None), P("seq", "head")
    by_head, down = P(None, "head"), P("head", "seq")
    return jax.shard_map(
        on_device,
        mesh=mesh,
        in_specs=(rows, P(), by_head, by_head, by_head, by_head, P("head"), P("head", None), P(), both, both, down, rows),
        out_specs=(rows, rows, P("seq"), both, both, both, both, P("head"), down, P("seq"), both, both, down),
        check_vma=False,
    )
```

```python
import functools

import jax
import jax.numpy as jnp
from jax import lax
from jax.experimental import pallas as pl
from jax.experimental.pallas import tpu as pltpu
from jax.sharding import PartitionSpec as P

CHUNK = 128
TILE = 256
EPS = 1e-06
RATE = 0.5
MIB = 2**20
f32 = jnp.float32
bf16 = jnp.bfloat16
highest = lax.Precision.HIGHEST


def nn(a, b):
    return lax.dot_general(a, b, (((1,), (0,)), ((), ())), preferred_element_type=f32)


def nt(a, b):
    return lax.dot_general(a, b, (((1,), (1,)), ((), ())), preferred_element_type=f32)


def tn(a, b):
    return lax.dot_general(a, b, (((0,), (0,)), ((), ())), preferred_element_type=f32)


def exact(a, b, dims):
    return lax.dot_general(a, b, (dims, ((), ())), precision=highest, preferred_element_type=f32)


def halves(a):
    high = a.astype(bf16)
    return high, (a - high.astype(f32)).astype(bf16)


def call(name, kernel, grid, in_specs, out_specs, out_shape, scratch=(), vmem=48, cost=None):
    return pl.pallas_call(
        kernel,
        name=name,
        grid=grid,
        in_specs=in_specs,
        out_specs=out_specs,
        out_shape=out_shape,
        scratch_shapes=scratch,
        compiler_params=pltpu.CompilerParams(
            dimension_semantics=("arbitrary",) * len(grid), vmem_limit_bytes=vmem * MIB
        ),
        cost_estimate=cost,
    )


def cost(flops, data):
    return pl.CostEstimate(flops=int(flops), bytes_accessed=int(data), transcendentals=0)


def fixed(shape):
    zeros = (0,) * len(shape)
    return pl.BlockSpec(shape, lambda *_: zeros, pipeline_mode=pl.Buffered(1))


def shaped(shape, dtype):
    return jax.ShapeDtypeStruct(shape, dtype)


def triangle(lower):
    r = lax.broadcasted_iota(jnp.int32, (CHUNK, CHUNK), 0)
    c = lax.broadcasted_iota(jnp.int32, (CHUNK, CHUNK), 1)
    return r >= c if lower else r <= c


def gates(z):
    la = -RATE * lax.logistic(-z)
    y = -la
    taken = jnp.ones_like(y)
    for n in range(9, 1, -1):
        taken = 1.0 - y * (1.0 / n) * taken
    taken = y * taken
    cum = exact(triangle(True).astype(f32), la, ((1,), (0,)))
    total = exact(la, jnp.ones((CHUNK, 128), f32), ((0,), (0,)))
    return la, cum, jnp.exp(-cum) * taken, total


def project_kernel(per_part, x_ref, gain_ref, wq_ref, wk_ref, wv_ref, wf_ref, bias_ref,
                   xn_ref, q_ref, k_ref, v_ref, z_ref, s_ref, d_ref, sent_ref, state, decay):
    @pl.when(lax.rem(pl.program_id(0), per_part) == 0)
    def _():
        state[...] = jnp.zeros_like(state)
        decay[...] = jnp.zeros_like(decay)

    x = x_ref[...].astype(f32)
    r1 = lax.rsqrt(jnp.mean(x * x, axis=-1, keepdims=True) + EPS)
    xn = (x * r1 * gain_ref[...]).astype(bf16)
    xn_ref[...] = xn
    q_ref[...] = nn(xn, wq_ref[...]).astype(bf16)
    k_ref[...] = nn(xn, wk_ref[...]).astype(bf16)
    v_ref[...] = nn(xn, wv_ref[...]).astype(bf16)
    z_ref[...] = nn(xn, wf_ref[...]) + bias_ref[...]
    width = k_ref.shape[1]
    for c in range(x_ref.shape[0] // CHUNK):
        rows = pl.ds(c * CHUNK, CHUNK)
        _, _, inflow, total = gates(z_ref[rows, :])
        spread = inflow.astype(bf16)
        keep = jnp.exp(total[:, :1])
        state[:, :width] = keep * (state[:, :width] + tn(spread, k_ref[rows, :]))
        state[:, width:] = keep * (state[:, width:] + tn(spread, v_ref[rows, :]))
        decay[...] += total
    s_ref[0] = state[...]
    d_ref[0] = jnp.exp(decay[...])
    pack(sent_ref, 0, jnp.exp(decay[...]), state[...])


def read_kernel(per_part, q_ref, k_ref, v_ref, z_ref, e0_ref, o_ref, p_ref, sc_ref, e_ref, state):
    @pl.when(lax.rem(pl.program_id(0), per_part) == 0)
    def _():
        state[...] = e0_ref[0]

    width = q_ref.shape[1]
    lower = triangle(True)
    for c in range(q_ref.shape[0] // CHUNK):
        rows = pl.ds(c * CHUNK, CHUNK)
        q, k, v = q_ref[rows, :], k_ref[rows, :], v_ref[rows, :]
        _, cum, inflow, total = gates(z_ref[rows, :])
        growth = jnp.exp(cum)
        e_ref[c] = state[...]
        i_hi, i_lo = halves(inflow)
        a_hi, a_lo = halves(jnp.where(lower, nt(q, k), 0.0))
        e_hi, e_lo = halves(state[:, :width])
        scores = growth * (
            nt(q, e_hi) + nt(q, e_lo) + nn(a_hi, i_hi) + (nn(a_hi, i_lo) + nn(a_lo, i_hi))
        )
        top = jnp.exp(scores - jnp.max(scores, axis=-1, keepdims=True))
        p = top / jnp.sum(top, axis=-1, keepdims=True)
        w = (p * growth).astype(bf16)
        mixing = jnp.where(lower, nt(w, i_hi), 0.0).astype(bf16)
        o_ref[rows, :] = (nn(w, state[:, width:].astype(bf16)) + nn(mixing, v)).astype(bf16)
        p_ref[rows, :] = p
        sc_ref[rows, :] = scores
        keep = jnp.exp(total[:, :1])
        state[:, :width] = keep * (state[:, :width] + tn(i_hi, k))
        state[:, width:] = keep * (state[:, width:] + tn(i_hi, v))


def back_kernel(dhn_ref, hid_ref, cot_ref, gain_ref, wo_ref, q_ref, k_ref, v_ref, z_ref, p_ref, sc_ref, e_ref,
                dhid_ref, datt_ref, dq_ref, dkl_ref, dvl_ref, h_ref, x1_ref, g_ref, s_ref, d_ref, gg_ref, state, decay):
    step = pl.program_id(0)

    @pl.when(step == 0)
    def _():
        state[...] = jnp.zeros_like(state)
        decay[...] = jnp.zeros_like(decay)
        gg_ref[...] = jnp.zeros_like(gg_ref)

    hidden = hid_ref[...]
    dhn = dhn_ref[...].astype(f32)
    r2 = lax.rsqrt(jnp.mean(hidden * hidden, axis=-1, keepdims=True) + EPS)
    gg_ref[...] += jnp.sum((dhn * hidden * r2).reshape(-1, 8, hidden.shape[1]), axis=0)
    u2 = gain_ref[...] * dhn
    dhid = (
        cot_ref[...].astype(f32)
        + r2 * u2
        - hidden * (r2 * r2 * r2) * jnp.mean(u2 * hidden, axis=-1, keepdims=True)
    )
    dhid_ref[...] = dhid
    datt = dhid.astype(bf16)
    datt_ref[...] = datt
    width = q_ref.shape[1]
    do = nt(datt, wo_ref[...]).astype(bf16)
    lower, upper = triangle(True), triangle(False)
    q, k, v = q_ref[...], k_ref[...], v_ref[...]
    _, cum, inflow, total = gates(z_ref[...])
    growth = jnp.exp(cum)
    p = p_ref[...]
    i_hi, i_lo = halves(inflow)
    b_hi, b_lo = halves(jnp.where(lower, nt(do, v), 0.0))
    ev_hi, ev_lo = halves(e_ref[0, :, width:])
    dp = growth * (nt(do, ev_hi) + nt(do, ev_lo) + nn(b_hi, i_hi) + (nn(b_hi, i_lo) + nn(b_lo, i_hi)))
    ds = p * (dp - jnp.sum(p * dp, axis=-1, keepdims=True))
    w = (p * growth).astype(bf16)
    gds = (growth * ds).astype(bf16)
    n = jnp.where(lower, nt(gds, i_hi), 0.0).astype(bf16)
    dq_ref[...] = (nn(gds, e_ref[0, :, :width].astype(bf16)) + nn(n, k)).astype(bf16)
    n_t = jnp.where(upper, nt(i_hi, gds), 0.0).astype(bf16)
    m_t = jnp.where(upper, nt(i_hi, w), 0.0).astype(bf16)
    dkl_ref[...] = nn(n_t, q)
    dvl_ref[...] = nn(m_t, do)
    h_ref[...] = ds * sc_ref[...] + p * dp
    a_t = jnp.where(upper, nt(k, q), 0.0).astype(bf16)
    b_t = jnp.where(upper, nt(v, do), 0.0).astype(bf16)
    x1_ref[...] = nn(a_t, gds) + nn(b_t, w)
    keep = jnp.exp(total[:, :1])
    g_k, g_v = tn(gds, q), tn(w, do)
    g_ref[0, :, :width] = g_k
    g_ref[0, :, width:] = g_v
    state[:, :width] = g_k + keep * state[:, :width]
    state[:, width:] = g_v + keep * state[:, width:]
    decay[...] += total
    s_ref[...] = state[...]
    d_ref[...] = jnp.exp(decay[...])


def last_kernel(l0_ref, k_ref, v_ref, z_ref, e_ref, g_ref, dkl_ref, dvl_ref, h_ref, x1_ref, dq_ref, x_ref,
                wq_ref, wk_ref, wv_ref, wf_ref, dk_ref, dv_ref, dz_ref, dxn_ref, bias_ref, gg_ref, state):
    step = pl.program_id(0)

    @pl.when(step == 0)
    def _():
        state[...] = l0_ref[...]
        gg_ref[...] = jnp.zeros_like(gg_ref)
        bias_ref[...] = jnp.zeros_like(bias_ref)

    width = k_ref.shape[1]
    low, up = triangle(True).astype(f32), triangle(False).astype(f32)
    k, v, z = k_ref[...], v_ref[...], z_ref[...]
    _, cum, inflow, total = gates(z)
    i_hi = inflow.astype(bf16)
    keep = jnp.exp(total[:, :1])
    lg = keep * state[...]
    lg_k, lg_v = lg[:, :width].astype(bf16), lg[:, width:].astype(bf16)
    dk = (dkl_ref[...] + nn(i_hi, lg_k)).astype(bf16)
    dv = (dvl_ref[...] + nn(i_hi, lg_v)).astype(bf16)
    dk_ref[...] = dk
    dv_ref[...] = dv
    x1 = x1_ref[...]
    x2 = nt(k, lg_k) + nt(v, lg_v)
    met = exact(jnp.ones((8, 2 * width), f32), lg * e_ref[0], ((1,), (1,)))
    h, r1 = h_ref[...], inflow * x1
    dla = (
        exact(up, h - r1, ((1,), (0,)))
        + r1
        + exact(low, inflow * x2, ((1,), (0,)))
        + met[:1]
        - jnp.exp(-cum) * (x1 + x2)
    )
    rate = lax.logistic(-z)
    dz = (dla * RATE * rate * (1.0 - rate)).astype(bf16)
    dz_ref[...] = dz
    bias_ref[...] += jnp.sum(dz.astype(f32).reshape(-1, 8, dz.shape[1]), axis=0)
    state[...] = g_ref[0] + lg
    dxn = nt(dq_ref[...], wq_ref[...]) + nt(dk, wk_ref[...]) + nt(dv, wv_ref[...]) + nt(dz, wf_ref[...])
    dxn_ref[...] = dxn.astype(bf16)
    x = x_ref[...].astype(f32)
    r1 = lax.rsqrt(jnp.mean(x * x, axis=-1, keepdims=True) + EPS)
    gg_ref[...] += jnp.sum((dxn * x * r1).reshape(-1, 8, x.shape[1]), axis=0)


def hidden_kernel(n_head, place_ref, *refs):
    o_refs, (x_ref, gain_ref), w_refs = refs[:n_head], refs[n_head : n_head + 2], refs[n_head + 2 : n_head + 7]
    hid_ref, hn_ref, blocks, weights, sems = refs[n_head + 7 :]
    quarter = w_refs[1].shape[1]
    copies = [pltpu.make_async_copy(w_refs[0], weights.at[0], sems.at[0])]
    for d in range(1, n_head):
        for i in range(4):
            rows = pl.ds(pl.multiple_of(place_ref[1 + i] * quarter, quarter), quarter)
            copies.append(
                pltpu.make_async_copy(w_refs[1 + i].at[d - 1], weights.at[d, rows, :], sems.at[len(copies)])
            )

    @pl.when(pl.program_id(0) == 0)
    def _():
        for copy in copies:
            copy.start()
        for copy in copies:
            copy.wait()

    for d in range(n_head):
        blocks[d] = o_refs[d][...]
    me = place_ref[0]
    attended = None
    for h in range(n_head):
        away = lax.rem(me - h + n_head, n_head)
        term = nn(blocks[away], weights[away])
        attended = term if attended is None else attended + term
    hidden = x_ref[...].astype(f32) + attended
    hid_ref[...] = hidden
    r2 = lax.rsqrt(jnp.mean(hidden * hidden, axis=-1, keepdims=True) + EPS)
    hn_ref[...] = (hidden * r2 * gain_ref[...]).astype(bf16)


def out_kernel(hid_ref, ffn_ref, *refs):
    refs[-1][0] = (hid_ref[...] + ffn_ref[...].astype(f32)).astype(bf16)


def in_grad_kernel(dhid_ref, dxn_ref, x_ref, gain_ref, *refs):
    x = x_ref[...].astype(f32)
    r1 = lax.rsqrt(jnp.mean(x * x, axis=-1, keepdims=True) + EPS)
    u1 = gain_ref[...] * dxn_ref[...].astype(f32)
    refs[-1][0] = dhid_ref[...] + r1 * u1 - x * (r1 * r1 * r1) * jnp.mean(u1 * x, axis=-1, keepdims=True)


def flat(ref):
    block = ref[...]
    return block.reshape(block.shape[0] * block.shape[1], block.shape[2])


def units_kernel(hn_ref, cot_ref, wg_ref, wu_ref, wd_ref, act_ref, dg_ref, du_ref):
    gate = nn(hn_ref[...], flat(wg_ref))
    up = nn(hn_ref[...], flat(wu_ref))
    dact = nn(cot_ref[...], flat(wd_ref))
    s = lax.logistic(gate)
    silu = gate * s
    act_ref[...] = (silu * up).astype(bf16)
    dg_ref[...] = (dact * up * s * (1.0 + gate * (1.0 - s))).astype(bf16)
    du_ref[...] = (dact * silu).astype(bf16)


def wide_kernel(pairs, *refs):
    outs = refs[2 * pairs :]
    total = nt(refs[0][...], flat(refs[pairs]))
    for i in range(1, pairs):
        total = total + nt(refs[i][...], flat(refs[pairs + i]))
    total = total.astype(bf16)
    for t, out in enumerate(outs):
        out[...] = total[t * TILE : (t + 1) * TILE]


def summed(pairs):
    total = tn(*pairs[0])
    for pair in pairs[1:]:
        total = total + tn(*pair)
    return total.astype(bf16)


def down_grad_kernel(*refs):
    cot_ref, act, out_ref = refs[0], refs[1:-1], refs[-1]
    block = summed([(cot_ref[m], a[...]) for m, a in enumerate(act)])
    out_ref[...] = block.reshape(out_ref.shape)


def wide_grad_kernel(*refs):
    out_ref = refs[-1]
    parts = (len(refs) - 2) // 3
    hn, dg, du = refs[:parts], refs[parts : 2 * parts], refs[2 * parts : 3 * parts]
    blocks, _, width, units = out_ref.shape
    for i, grads in enumerate((dg, du)):
        block = summed([(hn[m][...], grads[m][...]) for m in range(parts)])
        out_ref[:, i] = block.reshape(blocks, width, units)


def attn_grad_kernel(count, parts, *refs):
    out_ref, dzw_ref = refs[-2:]
    xn_ref = refs[0]
    datt, dq, dk, dv, dz = (refs[1 + i * count : 1 + (i + 1) * count] for i in range(5))
    o = refs[1 + 5 * count : 1 + 5 * count + parts]
    rows, width = dq[0].shape
    xn = [xn_ref[i * rows : (i + 1) * rows, :] for i in range(count)]
    for i, grads in enumerate((dq, dk, dv)):
        out_ref[:, i * width : (i + 1) * width] = summed([(x, g[...]) for x, g in zip(xn, grads)])
    each = count // parts
    o_rows = [o[i // each][(i % each) * rows : (i % each + 1) * rows, :] for i in range(count)]
    out_ref[:, 3 * width :] = summed([(d[...], r) for d, r in zip(datt, o_rows)])
    dzw_ref[...] = summed([(x, g[...]) for x, g in zip(xn, dz)])


def pack(ref, m, decay, state):
    high, low = halves(decay)
    lane = lax.broadcasted_iota(jnp.int32, decay.shape, 1)
    width = state.shape[1]
    ref[m, :, :width] = state.astype(bf16)
    ref[m, :, width:] = jnp.where(lane == 0, high.astype(f32), low.astype(f32)).astype(bf16)


def fold_kernel(parts, pieces, *refs):
    s_refs, d_refs, (s_out, d_out, sent) = refs[: parts * pieces], refs[parts * pieces : -3], refs[-3:]
    for m in range(parts):
        s, d = s_refs[m * pieces + pieces - 1][...], d_refs[m * pieces + pieces - 1][...]
        for t in reversed(range(pieces - 1)):
            here = d_refs[m * pieces + t][...]
            s, d = s_refs[m * pieces + t][...] + here[:, :1] * s, here * d
        s_out[m], d_out[m] = s, d
        pack(sent, m, d, s)


def hop_kernel(bit, after, first, final, parts, pieces, *refs):
    refs = list(refs)
    s_ref, d_ref, got_ref = refs[:3]
    refs = refs[3:]
    if not first:
        part_s_ref, part_d_ref = refs[:2]
        refs = refs[2:]
    early = (lax.axis_index("seq") & bit) == 0
    takes = early if after else jnp.logical_not(early)
    width = s_ref.shape[2]
    found = []
    for m in range(parts):
        tail = got_ref[m, :, width:].astype(f32)
        there_d, there_s = tail[:, :1] + tail[:, 1:2], got_ref[m, :, :width].astype(f32)
        s, d = s_ref[m], d_ref[m]
        there_wide = jnp.broadcast_to(there_d, d.shape)
        new_s = jnp.where(takes, s + d[:, :1] * there_s, there_s + there_d * s)
        if first:
            part_s, part_d = jnp.where(takes, there_s, 0.0), jnp.where(takes, there_wide, 1.0)
        else:
            part_s, part_d = part_s_ref[m], part_d_ref[m]
            part_s = jnp.where(takes, part_s + part_d[:, :1] * there_s, part_s)
            part_d = jnp.where(takes, part_d * there_wide, part_d)
        found.append((new_s, d * there_wide, part_s, part_d))
    if not final:
        s_out, d_out, part_s_out, part_d_out, sent = refs
        for m, (s, d, part_s, part_d) in enumerate(found):
            s_out[m], d_out[m], part_s_out[m], part_d_out[m] = s, d, part_s, part_d
            pack(sent, m, d, s)
        return
    *own, out = refs
    arriving = jnp.zeros_like(found[0][0])
    for m in reversed(range(parts)) if after else range(parts):
        s, d, part_s, part_d = found[m]
        enters = part_s + part_d[:, :1] * arriving
        arriving = s + d[:, :1] * arriving
        for t in reversed(range(pieces)) if after else range(1):
            out[m * pieces + t if after else m] = enters
            if after and t:
                here = m * pieces + t
                enters = own[here][...] + own[parts * pieces + here][:, :1] * enters


def in_vmem(name, kernel, operands, shapes):
    return pl.pallas_call(
        kernel,
        name=name,
        in_specs=[pl.BlockSpec(memory_space=pltpu.VMEM)] * len(operands),
        out_specs=[pl.BlockSpec(memory_space=pltpu.VMEM)] * len(shapes),
        out_shape=shapes,
        compiler_params=pltpu.CompilerParams(vmem_limit_bytes=48 * MIB),
        cost_estimate=cost(0, 6 * MIB),
    )(*operands)


def scan_states(n, state, decay, sent, after, own=(), pieces=1, behind=()):
    parts, slots, width = state.shape
    part, bit, hops = [], 1, 0
    while bit < n:
        if hops < len(behind):
            sent = behind_of(sent, *behind[hops])
        got = lax.ppermute(sent, "seq", [(i, i ^ bit) for i in range(n)])
        final = 2 * bit == n
        shapes = [shaped(state.shape, f32), shaped(decay.shape, f32)] * 2 + [shaped(sent.shape, bf16)]
        if final:
            shapes = [shaped((parts * pieces, slots, width), f32)]
        results = in_vmem(
            "hop",
            functools.partial(hop_kernel, bit, after, not part, final, parts, pieces),
            [state, decay, got, *part, *(own if final else ())],
            shapes,
        )
        if final:
            return results[0]
        state, decay, *part, sent = results
        bit, hops = 2 * bit, hops + 1


def turned(block, n):
    return [lax.ppermute(block, "head", [(i, (i + d) % n) for i in range(n)]) for d in range(1, n)]


def behind_of(value, *first):
    return lax.optimization_barrier((value,) + first)[0]


def join_kernel(has, *refs):
    refs = iter(refs)
    piece, outer, pair, middle, total, coming = (next(refs) if h else None for h in has)
    makes = (piece is not None, pair is not None or coming is not None, total is not None)
    new_pair, new_total, done = (next(refs) if m else None for m in makes)
    me = lax.axis_index("head")
    end = (me == 0) | (me == 3)

    def each(work):
        @pl.loop(0, TILE // 32)
        def _(i):
            work(pl.ds(pl.multiple_of(i * 32, 32), 32))

    def both(a, b, rows):
        return (a[rows, :].astype(f32) + b[rows, :].astype(f32)).astype(bf16)

    @pl.when(end)
    def _():
        def work(rows):
            if coming is not None:
                new_total[rows, :] = coming[rows, :]
            if done is not None:
                done[rows, :] = outer[rows, :]

        each(work)

    @pl.when(jnp.logical_not(end))
    def _():
        def work(rows):
            if piece is not None:
                new_pair[rows, :] = both(piece, outer, rows)
            if pair is not None:
                new_total[rows, :] = both(pair, middle, rows)
            if done is not None:
                done[rows, :] = total[rows, :]

        each(work)


class Line:
    INWARD, OUTWARD, MIDDLE = [(0, 1), (3, 2)], [(1, 0), (2, 3)], [(1, 2), (2, 1)]

    def __init__(self):
        self.piece = self.pair = self.payload = None
        self.returns = False

    def load(self, piece):
        self.piece = self.payload = piece

    def step(self, inputs):
        piece, pair, payload, returns = self.piece, self.pair, self.payload, self.returns
        values = [v for v in (payload, pair) if v is not None] + inputs
        values = list(lax.optimization_barrier(tuple(values)))
        outer = middle = None
        if payload is not None:
            payload = values.pop(0)
            way = (self.INWARD if piece is not None else []) + (self.OUTWARD if returns else [])
            outer = lax.ppermute(payload, "head", way)
        if pair is not None:
            pair = values.pop(0)
            middle = lax.ppermute(pair, "head", self.MIDDLE)
        self.waiting = (piece, outer, pair, middle, payload if returns else None)
        return values

    def join(self, coming=None):
        piece, outer, pair, middle, total = self.waiting
        if piece is None and total is None:
            outer = None
        operands = [piece, outer, pair, middle, total, coming]
        makes = [piece is not None, pair is not None or coming is not None, total is not None]
        arrays = [o for o in operands if o is not None]
        results = in_vmem(
            "join",
            functools.partial(join_kernel, [o is not None for o in operands]),
            arrays,
            [shaped(arrays[0].shape, bf16)] * sum(makes),
        )
        results = iter(results)
        self.pair, self.payload, done = (next(results) if m else None for m in makes)
        self.returns = pair is not None
        self.piece = coming
        return done


def on_device(tokens, gain_attn, w_query, w_key, w_value, w_forget, forget_bias, w_out, gain_ffn, w_gate, w_up, w_down,
              cotangent):
    parts, part_rows, width = tokens.shape
    rows = parts * part_rows
    head = w_query.shape[1]
    slots = w_forget.shape[1]
    units = w_gate.shape[1]
    n_seq, n_head = lax.axis_size("seq"), lax.axis_size("head")
    span = w_gate.shape[0]
    steps = rows // TILE
    per_part = part_rows // TILE
    chunks = TILE // CHUNK

    gain1 = gain_attn.reshape(1, width)
    gain2 = gain_ffn.reshape(1, width)
    state_scratch = pltpu.VMEM((slots, 2 * head), f32)

    def tiled(columns, back=False):
        return pl.BlockSpec((TILE, columns), (lambda i: (per_part - 1 - i, 0)) if back else (lambda i: (i, 0)))

    def at(m, columns, back=False):
        return pl.BlockSpec(
            (TILE, columns),
            (lambda i: (m * per_part + per_part - 1 - i, 0)) if back else (lambda i: (m * per_part + i, 0)),
        )

    def part_at(m, columns, back=False):
        return pl.BlockSpec(
            (None, TILE, columns), (lambda i: (m, per_part - 1 - i, 0)) if back else (lambda i: (m, i, 0))
        )

    def chunked(back=False):
        return pl.BlockSpec(
            (chunks, slots, 2 * head), (lambda i: (per_part - 1 - i, 0, 0)) if back else (lambda i: (i, 0, 0))
        )

    def state_of(m, columns):
        return pl.BlockSpec((1, slots, columns), lambda i: (m, 0, 0))

    one_state = pl.BlockSpec((1, slots, 2 * head), lambda i: (0, 0, 0))
    per_chunk = shaped((part_rows // CHUNK, slots, 2 * head), f32)

    stacked = jnp.stack([w_gate, w_up, w_down.T])
    x = tokens.reshape(rows, width)
    place = lax.axis_index("seq")
    low_bit, high_bit = place & 1, (place & 2) // 2
    quarter = head // 4
    share = lax.dynamic_slice_in_dim(w_out, (2 * high_bit + low_bit) * quarter, quarter, 0)
    x, stacked, share = lax.optimization_barrier((x, stacked, share))
    full = lax.all_gather(stacked, "seq")
    shares = turned(share, n_head)
    all_rows = lambda c: pl.BlockSpec((TILE, c), lambda i: (i, 0))
    by_part = lambda c: pl.BlockSpec((1, slots, c), lambda i: (i // per_part, 0, 0))
    xn, q, k, v, z, local, decay, sent = call(
        "project",
        functools.partial(project_kernel, per_part),
        (steps,),
        [all_rows(width), fixed((1, width))] + [fixed((width, head))] * 3 + [fixed((width, slots)), fixed((1, slots))],
        [all_rows(width), all_rows(head), all_rows(head), all_rows(head), all_rows(slots), by_part(2 * head), by_part(128),
         by_part(2 * head + 128)],
        [shaped((rows, width), bf16)] + [shaped((rows, head), bf16)] * 3
        + [shaped((rows, slots), f32), shaped((parts, slots, 2 * head), f32), shaped((parts, slots, 128), f32),
           shaped((parts, slots, 2 * head + 128), bf16)],
        [state_scratch, pltpu.VMEM((slots, 128), f32)],
        cost=cost(2 * rows * width * (3 * head + slots), 2 * rows * width * 3 + 2 * width * 3 * head),
    )(x, gain1, w_query, w_key, w_value, w_forget, forget_bias.reshape(1, slots))
    entering = scan_states(n_seq, local, decay, sent, False, behind=[(shares[0], shares[-1])])

    o, p, scores, e_chunks = [], [], [], []
    for m in range(parts):
        o_m, p_m, s_m, e_m = call(
            "read",
            functools.partial(read_kernel, per_part),
            (per_part,),
            [at(m, head)] * 3 + [at(m, slots), state_of(m, 2 * head)],
            [tiled(head), tiled(slots), tiled(slots), chunked()],
            [shaped((part_rows, head), bf16), shaped((part_rows, slots), f32), shaped((part_rows, slots), f32), per_chunk],
            [state_scratch],
            cost=cost(2 * part_rows * head * 600, 2 * part_rows * head * 4 + part_rows * slots * 64),
        )(q, k, v, z, entering)
        o.append(o_m)
        p.append(p_m)
        scores.append(s_m)
        e_chunks.append(e_m)

    turns = [turned(o_m, n_head) for o_m in o]
    held = jnp.stack(list(lax.optimization_barrier((*shares, o[0]))[: n_head - 1]))
    across = lax.ppermute(held, "seq", [(i, i ^ 2) for i in range(n_seq)])
    beside = lax.ppermute(held, "seq", [(i, i ^ 1) for i in range(n_seq)])
    beside_across = lax.ppermute(behind_of(across, *turns[0], o[1]), "seq", [(i, i ^ 1) for i in range(n_seq)])
    low_place, high_place = 2 * high_bit, 2 * (1 - high_bit)
    places = jnp.stack(
        [lax.axis_index("head"), low_place + low_bit, high_place + low_bit, low_place + 1 - low_bit,
         high_place + 1 - low_bit]
    ).astype(jnp.int32)

    def project_out(m, own):
        return call(
            "hidden",
            functools.partial(hidden_kernel, n_head),
            (per_part,),
            [pl.BlockSpec(memory_space=pltpu.SMEM)] + [tiled(head)] * n_head + [at(m, width), fixed((1, width))]
            + [pl.BlockSpec(memory_space=pl.ANY)] * 5,
            [tiled(width), tiled(width)],
            [shaped((part_rows, width), f32), shaped((part_rows, width), bf16)],
            [pltpu.VMEM((n_head, TILE, head), bf16), pltpu.VMEM((n_head, head, width), bf16),
             pltpu.SemaphoreType.DMA((4 * n_head - 3,))],
            cost=cost(2 * part_rows * width * width, part_rows * width * 10 + 2 * width * width),
        )(places, own, *turns[m], x, gain2, w_out, held, across, beside, beside_across)

    unit_tile = 256
    unit_steps = pl.cdiv(units, unit_tile)

    def weight_tile(which):
        return pl.BlockSpec((n_seq, None, span, unit_tile), lambda j: (0, which, 0, j))

    def feed(m, hn):
        unit_out = pl.BlockSpec((part_rows, unit_tile), lambda j: (0, j))
        return call(
            "units",
            units_kernel,
            (unit_steps,),
            [fixed((part_rows, width)),
             pl.BlockSpec((None, part_rows, width), lambda j: (m, 0, 0), pipeline_mode=pl.Buffered(1)),
             weight_tile(0), weight_tile(1), weight_tile(2)],
            [unit_out] * 3,
            [shaped((part_rows, units), bf16)] * 3,
            cost=cost(6 * part_rows * width * units, 4 * part_rows * width + 6 * part_rows * units + 6 * width * units),
        )(hn, cotangent, full, full, full)

    group = max(1, TILE // span)
    wide = group * span
    pieces = part_rows // TILE

    def weight_rows(which):
        return pl.BlockSpec((group, None, span, units), lambda j: (j, which, 0, 0))

    def widened(name, sources, which):
        count = len(sources)
        return call(
            name,
            functools.partial(wide_kernel, count),
            (width // wide,),
            [fixed((part_rows, units))] * count + [weight_rows(i) for i in which],
            [pl.BlockSpec((TILE, wide), lambda j: (0, j))] * pieces,
            [shaped((TILE, width), bf16)] * pieces,
            cost=cost(2 * count * part_rows * width * units,
                      2 * count * (part_rows + width) * units + 2 * part_rows * width),
        )(*sources, *([full] * count))

    def chunk_rows(m, t, columns, within=False):
        start = (0 if within else m * part_rows // CHUNK) + t * chunks
        return pl.BlockSpec((CHUNK, columns), lambda i: (start + chunks - 1 - i, 0))

    def chunk_state(t):
        return pl.BlockSpec((1, slots, 2 * head), lambda i: (t * chunks + chunks - 1 - i, 0, 0))

    def own_rows(columns):
        return pl.BlockSpec((CHUNK, columns), lambda i: (chunks - 1 - i, 0))

    def whole(shape):
        return pl.BlockSpec(shape, lambda i: (0,) * len(shape))

    def back(m, t, dhn, hidden):
        return call(
            "back",
            back_kernel,
            (chunks,),
            [own_rows(width), chunk_rows(m, t, width, True),
             pl.BlockSpec((None, CHUNK, width), lambda i: (m, t * chunks + chunks - 1 - i, 0)),
             fixed((1, width)), fixed((head, width))]
            + [chunk_rows(m, t, head)] * 3 + [chunk_rows(m, t, slots)] + [chunk_rows(m, t, slots, True)] * 2
            + [chunk_state(t)],
            [own_rows(width), own_rows(width), own_rows(head), own_rows(head), own_rows(head), own_rows(slots),
             own_rows(slots), chunk_state(0), whole((slots, 2 * head)), whole((slots, 128)), whole((8, width))],
            [shaped((TILE, width), f32), shaped((TILE, width), bf16), shaped((TILE, head), bf16),
             shaped((TILE, head), f32), shaped((TILE, head), f32), shaped((TILE, slots), f32),
             shaped((TILE, slots), f32), shaped((chunks, slots, 2 * head), f32), shaped((slots, 2 * head), f32),
             shaped((slots, 128), f32), shaped((8, width), f32)],
            [state_scratch, pltpu.VMEM((slots, 128), f32)],
            cost=cost(2 * TILE * width * head + 2 * TILE * head * 1500, TILE * width * 14 + TILE * head * 20),
        )(dhn, hidden, cotangent, gain2, w_out, q, k, v, z, p[m], scores[m], e_chunks[m])

    def last(m, t, leaving, saved):
        dq, dk_local, dv_local, h_sum, x_local, g_chunks = saved
        here = m * pieces + t
        return call(
            "last",
            last_kernel,
            (chunks,),
            [pl.BlockSpec((None, slots, 2 * head), lambda i: (here, 0, 0)), chunk_rows(m, t, head),
             chunk_rows(m, t, head), chunk_rows(m, t, slots), chunk_state(t), chunk_state(0), own_rows(head),
             own_rows(head), own_rows(slots), own_rows(slots), own_rows(head), chunk_rows(m, t, width)]
            + [fixed((width, head))] * 3 + [fixed((width, slots))],
            [own_rows(head), own_rows(head), own_rows(slots), own_rows(width), whole((8, slots)), whole((8, width))],
            [shaped((TILE, head), bf16), shaped((TILE, head), bf16), shaped((TILE, slots), bf16),
             shaped((TILE, width), bf16), shaped((8, slots), f32), shaped((8, width), f32)],
            [state_scratch],
            cost=cost(2 * TILE * width * (3 * head + slots), TILE * width * 8 + TILE * head * 20 + width * head * 6),
        )(leaving, k, v, z, e_chunks[m], g_chunks, dk_local, dv_local, h_sum, x_local, dq, x,
          w_query, w_key, w_value, w_forget)

    grads_shape = shaped((n_seq, 3, span, units), bf16)

    def down_grads(acts):
        return call(
            "down_grads",
            down_grad_kernel,
            (width // wide,),
            [pl.BlockSpec((parts, part_rows, wide), lambda j: (0, 0, j))] + [fixed((part_rows, units))] * parts,
            pl.BlockSpec((group, 1, span, units), lambda j: (j, 2, 0, 0)),
            grads_shape,
            cost=cost(2 * rows * width * units, 2 * (rows * width + rows * units + width * units)),
        )(cotangent, *acts)

    def wide_grads(normed, gates, ups, held_grads):
        return pl.pallas_call(
            wide_grad_kernel,
            name="wide_grads",
            grid=(width // wide,),
            in_specs=[pl.BlockSpec((part_rows, wide), lambda j: (0, j))] * parts
            + [fixed((part_rows, units))] * (2 * parts) + [pl.BlockSpec(memory_space=pl.ANY)],
            out_specs=pl.BlockSpec((group, 2, span, units), lambda j: (j, 0, 0, 0)),
            out_shape=grads_shape,
            input_output_aliases={3 * parts: 0},
            compiler_params=pltpu.CompilerParams(dimension_semantics=("arbitrary",), vmem_limit_bytes=48 * MIB),
            cost_estimate=cost(4 * rows * width * units, 2 * (rows * width + 2 * rows * units + 2 * width * units)),
        )(*normed, *gates, *ups, held_grads)

    line = Line()
    live = {}

    def start():
        names = list(live)
        live.update(zip(names, line.step([live[n] for n in names])))

    def end(coming=None, done=None):
        total = line.join(coming)
        if done is not None:
            live[done] = total

    backs, lasts = {}, {}
    outs, in_grads = [None], [None]
    quarter_rows = TILE // 2

    def piece_rows(m, t):
        first = m * 2 * per_part + 2 * t
        return lambda i: ((first + i) // (2 * per_part), (first + i) % (2 * per_part), 0)

    def into(name, kernel, m, t, kept, dtype, inputs, specs):
        spec = pl.BlockSpec((1, quarter_rows, width), piece_rows(m, t))
        old = [] if kept[0] is None else [kept[0]]
        kept[0] = pl.pallas_call(
            kernel,
            name=name,
            grid=(2,),
            in_specs=specs + [pl.BlockSpec(memory_space=pl.ANY)] * len(old),
            out_specs=spec,
            out_shape=shaped(tokens.shape, dtype),
            input_output_aliases={len(specs): 0} if old else {},
            compiler_params=pltpu.CompilerParams(dimension_semantics=("arbitrary",), vmem_limit_bytes=32 * MIB),
            cost_estimate=cost(0, TILE * width * 10),
        )(*inputs, *old)

    piece_spec = pl.BlockSpec((quarter_rows, width), lambda i: (i, 0))

    def finish_out(m, t):
        held_rows = pl.BlockSpec((quarter_rows, width), lambda i: (2 * t + i, 0))
        into("out", out_kernel, m, t, outs, bf16, [live["hidden", m], live.pop(("ffn", m, t))], [held_rows, piece_spec])

    def finish_grad(m, t):
        x_rows = pl.BlockSpec((quarter_rows, width), lambda i: (m * 2 * per_part + 2 * t + i, 0))
        into("in_grad", in_grad_kernel, m, t, in_grads, f32, [backs[m, t][0], live.pop(("dxn", m, t)), x, gain1],
             [piece_spec, piece_spec, x_rows, pl.BlockSpec((1, width), lambda i: (0, 0))])

    def go_back(m, t):
        backs[m, t] = back(m, t, live.pop(("dhn", m, t)), live["hidden", m])
        live["back", m, t] = backs[m, t][8]

    def go_last(m, t):
        lasts[m, t] = last(m, t, live["leaving"], backs[m, t][2:8])
        live["dxn_part", m, t] = lasts[m, t][3]

    def forward(m, own):
        live["hidden", m], live["hn", m] = project_out(m, own)
        live["act", m], live["dgate", m], live["dup", m] = feed(m, live["hn", m])

    forward(0, o[0])
    dhn_a = widened("dhn", (live["dgate", 0], live["dup", 0]), (0, 1))
    live["o", 1] = o[1]
    live["dhn_a"] = dhn_a[1]
    line.load(dhn_a[0])
    start()
    forward(1, live.pop(("o", 1)))
    end(live.pop("dhn_a"))
    start()
    live["dhn_b"], live["dhn_c"] = widened("dhn", (live["dgate", 1], live["dup", 1]), (0, 1))
    live["ffn_a"], live["ffn_b"] = widened("ffn", (live["act", 0],), (2,))
    end(live.pop("dhn_b"))
    start()
    live["ffn_c"], live["ffn_d"] = widened("ffn", (live["act", 1],), (2,))
    live["grads"] = down_grads([live["act", m] for m in range(parts)])
    end(live.pop("dhn_c"), ("dhn", 0, 0))
    start()
    live["grads"] = wide_grads(*([live[n, m] for m in range(parts)] for n in ("hn", "dgate", "dup")), live["grads"])
    for n in ("hn", "dgate", "dup", "act"):
        for m in range(parts):
            del live[n, m]
    end(live.pop("ffn_a"), ("dhn", 0, 1))
    start()
    ffn_shares = lax.psum_scatter(live.pop("grads"), "seq", scatter_dimension=0)
    go_back(0, 0)
    go_back(0, 1)
    end(live.pop("ffn_b"), ("dhn", 1, 0))
    start()
    go_back(1, 0)
    end(live.pop("ffn_c"), ("dhn", 1, 1))
    start()
    go_back(1, 1)
    every = [(m, t) for m in range(parts) for t in range(pieces)]
    for key in every:
        live.pop(("back", *key))
    own = [backs[key][8] for key in every] + [backs[key][9] for key in every]
    folded = in_vmem(
        "fold",
        functools.partial(fold_kernel, parts, pieces),
        own,
        [shaped(local.shape, f32), shaped(decay.shape, f32), shaped(sent.shape, bf16)],
    )
    live["folded"] = folded[2]
    end(live.pop("ffn_d"), ("ffn", 0, 0))
    start()
    live["leaving"] = scan_states(n_seq, folded[0], folded[1], live.pop("folded"), True, own, pieces)
    go_last(0, 0)
    end(live.pop(("dxn_part", 0, 0)), ("ffn", 0, 1))
    start()
    go_last(0, 1)
    go_last(1, 0)
    live["ffn_shares"] = ffn_shares
    end(live.pop(("dxn_part", 0, 1)), ("ffn", 1, 0))
    start()
    ffn_shares = live.pop("ffn_shares")
    go_last(1, 1)
    live.pop("leaving")
    attn_grads, forget_grads = call(
        "attn_grads",
        functools.partial(attn_grad_kernel, len(every), parts),
        (width // TILE,),
        [pl.BlockSpec((rows, TILE), lambda j: (0, j))] + [pl.BlockSpec((TILE, TILE), lambda j: (0, j))] * len(every)
        + [fixed((TILE, head))] * (3 * len(every)) + [fixed((TILE, slots))] * len(every)
        + [fixed((part_rows, head))] * parts,
        [pl.BlockSpec((TILE, 4 * head), lambda j: (j, 0)), pl.BlockSpec((TILE, slots), lambda j: (j, 0))],
        [shaped((width, 4 * head), bf16), shaped((width, slots), bf16)],
        cost=cost(2 * rows * width * (4 * head + slots), 4 * rows * width + 8 * rows * head + 8 * width * head),
    )(xn, *[backs[key][1] for key in every], *[backs[key][2] for key in every],
      *[lasts[key][i] for i in range(3) for key in every], *o)
    live["attn_grads"] = attn_grads
    bias_sum = sum(jnp.sum(n[4], 0) for n in lasts.values())
    gain1_sum = sum(jnp.sum(n[5], 0) for n in lasts.values())
    gain2_sum = sum(jnp.sum(n[10], 0) for n in backs.values())
    small = jnp.concatenate(
        [
            forget_grads,
            gain2_sum.astype(bf16)[:, None],
            gain1_sum.astype(bf16)[:, None],
            jnp.zeros((width, 128 - 2 - slots % 128), bf16),
        ],
        1,
    ).reshape(n_seq, span, -1)
    bias_row = jnp.pad(jnp.stack(halves(bias_sum)), ((0, 14), (0, small.shape[2] - slots)))
    live["small"] = jnp.concatenate([small, jnp.broadcast_to(bias_row, (n_seq,) + bias_row.shape)], 1)
    end(live.pop(("dxn_part", 1, 0)), ("ffn", 1, 1))
    start()
    small_shares = lax.psum_scatter(live.pop("small"), "seq", scatter_dimension=0).astype(f32)
    attn_shares = lax.psum_scatter(live.pop("attn_grads"), "seq", scatter_dimension=0, tiled=True).astype(f32)
    bias_total = small_shares[span, :slots] + small_shares[span + 1, :slots]
    gain1_total = small_shares[:span, slots + 1]
    bit = 1
    while bit < n_head:
        gain1_total = gain1_total + lax.ppermute(gain1_total, "head", [(i, i ^ bit) for i in range(n_head)])
        bit *= 2
    for t in range(pieces):
        finish_out(0, t)
    live["out"] = outs[0]
    end(live.pop(("dxn_part", 1, 1)), ("dxn", 0, 0))
    start()
    outs[0] = live.pop("out")
    for t in range(pieces):
        finish_out(1, t)
    finish_grad(0, 0)
    live["out"], live["in_grad"] = outs[0], in_grads[0]
    end(None, ("dxn", 0, 1))
    start()
    in_grads[0] = live.pop("in_grad")
    finish_grad(0, 1)
    live["in_grad"] = in_grads[0]
    end(None, ("dxn", 1, 0))
    start()
    in_grads[0] = live.pop("in_grad")
    finish_grad(1, 0)
    live["in_grad"] = in_grads[0]
    end(None, ("dxn", 1, 1))
    finish_grad(1, 1)

    return (
        live["out"],
        in_grads[0],
        gain1_total,
        attn_shares[:, :head],
        attn_shares[:, head : 2 * head],
        attn_shares[:, 2 * head : 3 * head],
        small_shares[:span, :slots],
        bias_total,
        attn_shares[:, 3 * head :].T,
        small_shares[:span, slots],
        ffn_shares[0].astype(f32),
        ffn_shares[1].astype(f32),
        ffn_shares[2].astype(f32).T,
    )


def solution(mesh):
    rows, both = P(None, "seq", None), P("seq", "head")
    by_head, down = P(None, "head"), P("head", "seq")
    return jax.shard_map(
        on_device,
        mesh=mesh,
        in_specs=(rows, P(), by_head, by_head, by_head, by_head, P("head"), P("head", None), P(), both, both, down, rows),
        out_specs=(rows, rows, P("seq"), both, both, both, both, P("head"), down, P("seq"), both, both, down),
        check_vma=False,
    )
```

```python
import functools

import jax
import jax.numpy as jnp
from jax import lax
from jax.experimental import pallas as pl
from jax.experimental.pallas import tpu as pltpu
from jax.sharding import PartitionSpec as P

CHUNK = 128
TILE = 256
EPS = 1e-06
RATE = 0.5
MIB = 2**20
f32 = jnp.float32
bf16 = jnp.bfloat16
highest = lax.Precision.HIGHEST


def nn(a, b):
    return lax.dot_general(a, b, (((1,), (0,)), ((), ())), preferred_element_type=f32)


def nt(a, b):
    return lax.dot_general(a, b, (((1,), (1,)), ((), ())), preferred_element_type=f32)


def tn(a, b):
    return lax.dot_general(a, b, (((0,), (0,)), ((), ())), preferred_element_type=f32)


def exact(a, b, dims):
    return lax.dot_general(a, b, (dims, ((), ())), precision=highest, preferred_element_type=f32)


def halves(a):
    high = a.astype(bf16)
    return high, (a - high.astype(f32)).astype(bf16)


def call(name, kernel, grid, in_specs, out_specs, out_shape, scratch=(), vmem=48, cost=None, loose=(), loose_out=(),
         aliases=None):
    single = not isinstance(out_shape, list)
    shapes = [out_shape] if single else out_shape
    shapes = [s if i in loose_out else pltpu.HBM(s.shape, s.dtype) for i, s in enumerate(shapes)]
    function = pl.pallas_call(
        kernel,
        name=name,
        grid=grid,
        in_specs=in_specs,
        out_specs=out_specs,
        out_shape=shapes[0] if single else shapes,
        scratch_shapes=scratch,
        input_output_aliases=aliases or {},
        compiler_params=pltpu.CompilerParams(
            dimension_semantics=("arbitrary",) * len(grid), vmem_limit_bytes=vmem * MIB
        ),
        cost_estimate=cost,
    )

    def run(*operands):
        return function(*[
            o if i in loose or spec.memory_space == pltpu.SMEM else pltpu.with_memory_space_constraint(o, pltpu.HBM)
            for i, (o, spec) in enumerate(zip(operands, in_specs))
        ])

    return run


def cost(flops, data):
    return pl.CostEstimate(flops=int(flops), bytes_accessed=int(data), transcendentals=0)


def fixed(shape):
    zeros = (0,) * len(shape)
    return pl.BlockSpec(shape, lambda *_: zeros, pipeline_mode=pl.Buffered(1))


def shaped(shape, dtype):
    return jax.ShapeDtypeStruct(shape, dtype)


def triangle(lower):
    r = lax.broadcasted_iota(jnp.int32, (CHUNK, CHUNK), 0)
    c = lax.broadcasted_iota(jnp.int32, (CHUNK, CHUNK), 1)
    return r >= c if lower else r <= c


def gates(z):
    la = -RATE * lax.logistic(-z)
    y = -la
    taken = jnp.ones_like(y)
    for n in range(9, 1, -1):
        taken = 1.0 - y * (1.0 / n) * taken
    taken = y * taken
    cum = exact(triangle(True).astype(f32), la, ((1,), (0,)))
    total = exact(la, jnp.ones((CHUNK, 128), f32), ((0,), (0,)))
    return la, cum, jnp.exp(-cum) * taken, total


def project_kernel(per_part, x_ref, gain_ref, wq_ref, wk_ref, wv_ref, wf_ref, bias_ref,
                   xn_ref, q_ref, k_ref, v_ref, z_ref, s_ref, d_ref, sent_ref, state, decay):
    @pl.when(lax.rem(pl.program_id(0), per_part) == 0)
    def _():
        state[...] = jnp.zeros_like(state)
        decay[...] = jnp.zeros_like(decay)

    x = x_ref[...].astype(f32)
    r1 = lax.rsqrt(jnp.mean(x * x, axis=-1, keepdims=True) + EPS)
    xn = (x * r1 * gain_ref[...]).astype(bf16)
    xn_ref[...] = xn
    q_ref[...] = nn(xn, wq_ref[...]).astype(bf16)
    k_ref[...] = nn(xn, wk_ref[...]).astype(bf16)
    v_ref[...] = nn(xn, wv_ref[...]).astype(bf16)
    z_ref[...] = nn(xn, wf_ref[...]) + bias_ref[...]
    width = k_ref.shape[1]
    for c in range(x_ref.shape[0] // CHUNK):
        rows = pl.ds(c * CHUNK, CHUNK)
        _, _, inflow, total = gates(z_ref[rows, :])
        spread = inflow.astype(bf16)
        keep = jnp.exp(total[:, :1])
        state[:, :width] = keep * (state[:, :width] + tn(spread, k_ref[rows, :]))
        state[:, width:] = keep * (state[:, width:] + tn(spread, v_ref[rows, :]))
        decay[...] += total
    s_ref[0] = state[...]
    d_ref[0] = jnp.exp(decay[...])
    pack(sent_ref, 0, jnp.exp(decay[...]), state[...])


def read_kernel(q_ref, k_ref, v_ref, z_ref, e0_ref, wo_ref, o_ref, p_ref, sc_ref, e_ref, left_ref, att_ref, state):
    @pl.when(pl.program_id(0) == 0)
    def _():
        state[...] = e0_ref[...]

    width = q_ref.shape[1]
    lower = triangle(True)
    q, k, v = q_ref[...], k_ref[...], v_ref[...]
    _, cum, inflow, total = gates(z_ref[...])
    growth = jnp.exp(cum)
    e_ref[0] = state[...]
    i_hi, i_lo = halves(inflow)
    a_hi, a_lo = halves(jnp.where(lower, nt(q, k), 0.0))
    e_hi, e_lo = halves(state[:, :width])
    scores = growth * (nt(q, e_hi) + nt(q, e_lo) + nn(a_hi, i_hi) + (nn(a_hi, i_lo) + nn(a_lo, i_hi)))
    top = jnp.exp(scores - jnp.max(scores, axis=-1, keepdims=True))
    p = top / jnp.sum(top, axis=-1, keepdims=True)
    w = (p * growth).astype(bf16)
    mixing = jnp.where(lower, nt(w, i_hi), 0.0).astype(bf16)
    o = (nn(w, state[:, width:].astype(bf16)) + nn(mixing, v)).astype(bf16)
    o_ref[...] = o
    att_ref[...] = nn(o, wo_ref[...]).astype(bf16)
    p_ref[...] = p
    sc_ref[...] = scores
    keep = jnp.exp(total[:, :1])
    state[:, :width] = keep * (state[:, :width] + tn(i_hi, k))
    state[:, width:] = keep * (state[:, width:] + tn(i_hi, v))
    left_ref[...] = state[...]


def back_kernel(dhn_ref, hid_ref, cot_ref, gain_ref, wo_ref, q_ref, k_ref, v_ref, z_ref, p_ref, sc_ref, e_ref,
                dhid_ref, datt_ref, dq_ref, dkl_ref, dvl_ref, h_ref, x1_ref, g_ref, s_ref, d_ref, gg_ref, state, decay):
    step = pl.program_id(0)

    @pl.when(step == 0)
    def _():
        state[...] = jnp.zeros_like(state)
        decay[...] = jnp.zeros_like(decay)
        gg_ref[...] = jnp.zeros_like(gg_ref)

    hidden = hid_ref[...]
    dhn = dhn_ref[...].astype(f32)
    r2 = lax.rsqrt(jnp.mean(hidden * hidden, axis=-1, keepdims=True) + EPS)
    gg_ref[...] += jnp.sum((dhn * hidden * r2).reshape(-1, 8, hidden.shape[1]), axis=0)
    u2 = gain_ref[...] * dhn
    dhid = (
        cot_ref[...].astype(f32)
        + r2 * u2
        - hidden * (r2 * r2 * r2) * jnp.mean(u2 * hidden, axis=-1, keepdims=True)
    )
    dhid_ref[...] = dhid
    datt = dhid.astype(bf16)
    datt_ref[...] = datt
    width = q_ref.shape[1]
    do = nt(datt, wo_ref[...]).astype(bf16)
    lower, upper = triangle(True), triangle(False)
    q, k, v = q_ref[...], k_ref[...], v_ref[...]
    _, cum, inflow, total = gates(z_ref[...])
    growth = jnp.exp(cum)
    p = p_ref[...]
    i_hi, i_lo = halves(inflow)
    b_hi, b_lo = halves(jnp.where(lower, nt(do, v), 0.0))
    ev_hi, ev_lo = halves(e_ref[0, :, width:])
    dp = growth * (nt(do, ev_hi) + nt(do, ev_lo) + nn(b_hi, i_hi) + (nn(b_hi, i_lo) + nn(b_lo, i_hi)))
    ds = p * (dp - jnp.sum(p * dp, axis=-1, keepdims=True))
    w = (p * growth).astype(bf16)
    gds = (growth * ds).astype(bf16)
    n = jnp.where(lower, nt(gds, i_hi), 0.0).astype(bf16)
    dq_ref[...] = (nn(gds, e_ref[0, :, :width].astype(bf16)) + nn(n, k)).astype(bf16)
    n_t = jnp.where(upper, nt(i_hi, gds), 0.0).astype(bf16)
    m_t = jnp.where(upper, nt(i_hi, w), 0.0).astype(bf16)
    dkl_ref[...] = nn(n_t, q)
    dvl_ref[...] = nn(m_t, do)
    h_ref[...] = ds * sc_ref[...] + p * dp
    a_t = jnp.where(upper, nt(k, q), 0.0).astype(bf16)
    b_t = jnp.where(upper, nt(v, do), 0.0).astype(bf16)
    x1_ref[...] = nn(a_t, gds) + nn(b_t, w)
    keep = jnp.exp(total[:, :1])
    g_k, g_v = tn(gds, q), tn(w, do)
    g_ref[0, :, :width] = g_k
    g_ref[0, :, width:] = g_v
    state[:, :width] = g_k + keep * state[:, :width]
    state[:, width:] = g_v + keep * state[:, width:]
    decay[...] += total
    s_ref[...] = state[...]
    d_ref[...] = jnp.exp(decay[...])


def last_kernel(l0_ref, k_ref, v_ref, z_ref, e_ref, g_ref, dkl_ref, dvl_ref, h_ref, x1_ref, dq_ref, x_ref,
                wq_ref, wk_ref, wv_ref, wf_ref, dk_ref, dv_ref, dz_ref, dxn_ref, bias_ref, gg_ref, state):
    step = pl.program_id(0)

    @pl.when(step == 0)
    def _():
        state[...] = l0_ref[...]
        gg_ref[...] = jnp.zeros_like(gg_ref)
        bias_ref[...] = jnp.zeros_like(bias_ref)

    width = k_ref.shape[1]
    low, up = triangle(True).astype(f32), triangle(False).astype(f32)
    k, v, z = k_ref[...], v_ref[...], z_ref[...]
    _, cum, inflow, total = gates(z)
    i_hi = inflow.astype(bf16)
    keep = jnp.exp(total[:, :1])
    lg = keep * state[...]
    lg_k, lg_v = lg[:, :width].astype(bf16), lg[:, width:].astype(bf16)
    dk = (dkl_ref[...] + nn(i_hi, lg_k)).astype(bf16)
    dv = (dvl_ref[...] + nn(i_hi, lg_v)).astype(bf16)
    dk_ref[...] = dk
    dv_ref[...] = dv
    x1 = x1_ref[...]
    x2 = nt(k, lg_k) + nt(v, lg_v)
    met = exact(jnp.ones((8, 2 * width), f32), lg * e_ref[0], ((1,), (1,)))
    h, r1 = h_ref[...], inflow * x1
    dla = (
        exact(up, h - r1, ((1,), (0,)))
        + r1
        + exact(low, inflow * x2, ((1,), (0,)))
        + met[:1]
        - jnp.exp(-cum) * (x1 + x2)
    )
    rate = lax.logistic(-z)
    dz = (dla * RATE * rate * (1.0 - rate)).astype(bf16)
    dz_ref[...] = dz
    bias_ref[...] += jnp.sum(dz.astype(f32).reshape(-1, 8, dz.shape[1]), axis=0)
    state[...] = g_ref[0] + lg
    dxn = nt(dq_ref[...], wq_ref[...]) + nt(dk, wk_ref[...]) + nt(dv, wv_ref[...]) + nt(dz, wf_ref[...])
    dxn_ref[...] = dxn.astype(bf16)
    x = x_ref[...].astype(f32)
    r1 = lax.rsqrt(jnp.mean(x * x, axis=-1, keepdims=True) + EPS)
    gg_ref[...] += jnp.sum((dxn * x * r1).reshape(-1, 8, x.shape[1]), axis=0)


def out_kernel(hid_ref, ffn_ref, *refs):
    refs[-1][0] = (hid_ref[...] + ffn_ref[...].astype(f32)).astype(bf16)


def in_grad_kernel(dhid_ref, dxn_ref, x_ref, gain_ref, *refs):
    x = x_ref[...].astype(f32)
    r1 = lax.rsqrt(jnp.mean(x * x, axis=-1, keepdims=True) + EPS)
    u1 = gain_ref[...] * dxn_ref[...].astype(f32)
    refs[-1][0] = dhid_ref[...] + r1 * u1 - x * (r1 * r1 * r1) * jnp.mean(u1 * x, axis=-1, keepdims=True)


def feed_kernel(first_row, x_ref, att_ref, gain_ref, cot_ref, full_ref, hid_ref, hn_ref, act_ref, dg_ref, du_ref,
                ffn_ref, dhn_ref, weights, x, cot, hid, hn, act, dg, du, ffn, in_sems, out_sems, weight_sems):
    rows, width = x.shape
    units = act.shape[1]
    blocks, _, span, _ = weights.shape
    tiles = [(u, min(TILE, units - u)) for u in range(0, units, TILE)]
    here = pl.ds(first_row, rows)
    reads = [pltpu.make_async_copy(source.at[here, :], target, in_sems.at[i])
             for i, (source, target) in enumerate(((x_ref, x), (cot_ref, cot)))]
    loads = [pltpu.make_async_copy(full_ref.at[:, :, :, pl.ds(u, size)], weights.at[:, :, :, pl.ds(u, size)],
                                   weight_sems.at[i]) for i, (u, size) in enumerate(tiles)]
    writes = [pltpu.make_async_copy(source, target, out_sems.at[i])
              for i, (source, target) in enumerate(
                  ((hid, hid_ref), (hn, hn_ref), (act, act_ref), (dg, dg_ref), (du, du_ref), (ffn, ffn_ref)))]
    for copy in reads + loads:
        copy.start()
    for copy in reads:
        copy.wait()
    hidden = x[...].astype(f32) + att_ref[...].astype(f32)
    hid[...] = hidden
    r2 = lax.rsqrt(jnp.mean(hidden * hidden, axis=-1, keepdims=True) + EPS)
    hn[...] = (hidden * r2 * gain_ref[...]).astype(bf16)
    writes[0].start()
    writes[1].start()
    for (u, size), load in zip(tiles, loads):
        load.wait()
        gate, up, dact = (
            nn(left[...], weights[:, i, :, u : u + size].reshape(width, size))
            for i, left in enumerate((hn, hn, cot))
        )
        s = lax.logistic(gate)
        silu = gate * s
        act[:, u : u + size] = (silu * up).astype(bf16)
        dg[:, u : u + size] = (dact * up * s * (1.0 + gate * (1.0 - s))).astype(bf16)
        du[:, u : u + size] = (dact * silu).astype(bf16)
    for write in writes[2:5]:
        write.start()
    group = max(1, TILE // span)
    for b in range(0, blocks, group):
        columns = slice(b * span, (b + group) * span)
        w_gate, w_up, w_down = (weights[b : b + group, i].reshape(group * span, units) for i in range(3))
        ffn[:, columns] = nt(act[...], w_down).astype(bf16)
        dhn_ref[:, columns] = (nt(dg[...], w_gate) + nt(du[...], w_up)).astype(bf16)
    writes[5].start()
    for write in writes:
        write.wait()


def summed(pairs):
    total = tn(*pairs[0])
    for pair in pairs[1:]:
        total = total + tn(*pair)
    return total.astype(bf16)


def down_grad_kernel(*refs):
    cot_ref, act, out_ref = refs[0], refs[1:-1], refs[-1]
    rows = act[0].shape[0]
    block = summed([(cot_ref[i * rows : (i + 1) * rows, :], a[...]) for i, a in enumerate(act)])
    out_ref[...] = block.reshape(out_ref.shape)


def wide_grad_kernel(*refs):
    out_ref = refs[-1]
    count = (len(refs) - 2) // 3
    hn, dg, du = refs[:count], refs[count : 2 * count], refs[2 * count : 3 * count]
    blocks, _, width, units = out_ref.shape
    for i, grads in enumerate((dg, du)):
        block = summed([(h[...], g[...]) for h, g in zip(hn, grads)])
        out_ref[:, i] = block.reshape(blocks, width, units)


def attn_grad_kernel(count, *refs):
    out_ref, dzw_ref = refs[-2:]
    xn_ref = refs[0]
    datt, dq, dk, dv, dz, o = (refs[1 + i * count : 1 + (i + 1) * count] for i in range(6))
    rows, width = dq[0].shape
    xn = [xn_ref[i * rows : (i + 1) * rows, :] for i in range(count)]
    for i, grads in enumerate((dq, dk, dv)):
        out_ref[:, i * width : (i + 1) * width] = summed([(x, g[...]) for x, g in zip(xn, grads)])
    out_ref[:, 3 * width :] = summed([(d[...], r[...]) for d, r in zip(datt, o)])
    dzw_ref[...] = summed([(x, g[...]) for x, g in zip(xn, dz)])


def pack(ref, m, decay, state):
    high, low = halves(decay)
    lane = lax.broadcasted_iota(jnp.int32, decay.shape, 1)
    width = state.shape[1]
    ref[m, :, :width] = state.astype(bf16)
    ref[m, :, width:] = jnp.where(lane == 0, high.astype(f32), low.astype(f32)).astype(bf16)


def fold_kernel(parts, pieces, *refs):
    s_refs, d_refs, (s_out, d_out, sent) = refs[: parts * pieces], refs[parts * pieces : -3], refs[-3:]
    for m in range(parts):
        s, d = s_refs[m * pieces + pieces - 1][...], d_refs[m * pieces + pieces - 1][...]
        for t in reversed(range(pieces - 1)):
            here = d_refs[m * pieces + t][...]
            s, d = s_refs[m * pieces + t][...] + here[:, :1] * s, here * d
        s_out[m], d_out[m] = s, d
        pack(sent, m, d, s)


def hop_kernel(bit, after, first, final, parts, pieces, *refs):
    refs = list(refs)
    s_ref, d_ref, got_ref = refs[:3]
    refs = refs[3:]
    if not first:
        part_s_ref, part_d_ref = refs[:2]
        refs = refs[2:]
    early = (lax.axis_index("seq") & bit) == 0
    takes = early if after else jnp.logical_not(early)
    width = s_ref.shape[2]
    found = []
    for m in range(parts):
        tail = got_ref[m, :, width:].astype(f32)
        there_d, there_s = tail[:, :1] + tail[:, 1:2], got_ref[m, :, :width].astype(f32)
        s, d = s_ref[m], d_ref[m]
        there_wide = jnp.broadcast_to(there_d, d.shape)
        new_s = jnp.where(takes, s + d[:, :1] * there_s, there_s + there_d * s)
        if first:
            part_s, part_d = jnp.where(takes, there_s, 0.0), jnp.where(takes, there_wide, 1.0)
        else:
            part_s, part_d = part_s_ref[m], part_d_ref[m]
            part_s = jnp.where(takes, part_s + part_d[:, :1] * there_s, part_s)
            part_d = jnp.where(takes, part_d * there_wide, part_d)
        found.append((new_s, d * there_wide, part_s, part_d))
    if not final:
        s_out, d_out, part_s_out, part_d_out, sent = refs
        for m, (s, d, part_s, part_d) in enumerate(found):
            s_out[m], d_out[m], part_s_out[m], part_d_out[m] = s, d, part_s, part_d
            pack(sent, m, d, s)
        return
    *own, out = refs
    arriving = jnp.zeros_like(found[0][0])
    for m in reversed(range(parts)) if after else range(parts):
        s, d, part_s, part_d = found[m]
        enters = part_s + part_d[:, :1] * arriving
        arriving = s + d[:, :1] * arriving
        for t in reversed(range(pieces)) if after else range(1):
            out[m * pieces + t if after else m] = enters
            if after and t:
                here = m * pieces + t
                enters = own[here][...] + own[parts * pieces + here][:, :1] * enters


def in_vmem(name, kernel, operands, shapes):
    return pl.pallas_call(
        kernel,
        name=name,
        in_specs=[pl.BlockSpec(memory_space=pltpu.VMEM)] * len(operands),
        out_specs=[pl.BlockSpec(memory_space=pltpu.VMEM)] * len(shapes),
        out_shape=shapes,
        compiler_params=pltpu.CompilerParams(vmem_limit_bytes=48 * MIB),
        cost_estimate=cost(0, 6 * MIB),
    )(*operands)


def scan_states(n, state, decay, sent, after, own=(), pieces=1, tie=None):
    parts, slots, width = state.shape
    part, bit, hops = [], 1, 0
    while bit < n:
        got = lax.ppermute(sent, "seq", [(i, i ^ bit) for i in range(n)])
        final = 2 * bit == n
        shapes = [shaped(state.shape, f32), shaped(decay.shape, f32)] * 2 + [shaped(sent.shape, bf16)]
        if final:
            shapes = [shaped((parts * pieces, slots, width), f32)]
        results = in_vmem(
            "hop",
            functools.partial(hop_kernel, bit, after, not part, final, parts, pieces),
            [state, decay, got, *part, *(own if final else ())],
            shapes,
        )
        if final:
            return results[0]
        state, decay, *part, sent = results
        if tie is not None and not hops:
            sent = tie(sent)
        bit, hops = 2 * bit, hops + 1


def behind_of(value, *first):
    return lax.optimization_barrier((value,) + first)[0]


def join_kernel(has, *refs):
    refs = iter(refs)
    piece, outer, pair, middle, total, coming = (next(refs) if h else None for h in has)
    makes = (piece is not None, pair is not None or coming is not None, total is not None)
    new_pair, new_total, done = (next(refs) if m else None for m in makes)
    me = lax.axis_index("head")
    end = (me == 0) | (me == 3)

    def each(work):
        @pl.loop(0, TILE // 32)
        def _(i):
            work(pl.ds(pl.multiple_of(i * 32, 32), 32))

    def both(a, b, rows):
        return (a[rows, :].astype(f32) + b[rows, :].astype(f32)).astype(bf16)

    @pl.when(end)
    def _():
        def work(rows):
            if coming is not None:
                new_total[rows, :] = coming[rows, :]
            if done is not None:
                done[rows, :] = outer[rows, :]

        each(work)

    @pl.when(jnp.logical_not(end))
    def _():
        def work(rows):
            if piece is not None:
                new_pair[rows, :] = both(piece, outer, rows)
            if pair is not None:
                new_total[rows, :] = both(pair, middle, rows)
            if done is not None:
                done[rows, :] = total[rows, :]

        each(work)


class Line:
    INWARD, OUTWARD, MIDDLE = [(0, 1), (3, 2)], [(1, 0), (2, 3)], [(1, 2), (2, 1)]

    def __init__(self):
        self.piece = self.pair = self.payload = None
        self.returns = False

    def load(self, piece):
        self.piece = self.payload = piece

    def step(self, inputs):
        piece, pair, payload, returns = self.piece, self.pair, self.payload, self.returns
        values = [v for v in (payload, pair) if v is not None] + inputs
        values = list(lax.optimization_barrier(tuple(values)))
        outer = middle = None
        if payload is not None:
            payload = values.pop(0)
            way = (self.INWARD if piece is not None else []) + (self.OUTWARD if returns else [])
            outer = lax.ppermute(payload, "head", way)
        if pair is not None:
            pair = values.pop(0)
            middle = lax.ppermute(pair, "head", self.MIDDLE)
        self.waiting = (piece, outer, pair, middle, payload if returns else None)
        return values

    def join(self, coming=None):
        piece, outer, pair, middle, total = self.waiting
        if piece is None and total is None:
            outer = None
        operands = [piece, outer, pair, middle, total, coming]
        makes = [piece is not None, pair is not None or coming is not None, total is not None]
        arrays = [o for o in operands if o is not None]
        results = in_vmem(
            "join",
            functools.partial(join_kernel, [o is not None for o in operands]),
            arrays,
            [shaped(arrays[0].shape, bf16)] * sum(makes),
        )
        results = iter(results)
        self.pair, self.payload, done = (next(results) if m else None for m in makes)
        self.returns = pair is not None
        self.piece = coming
        return done


def on_device(tokens, gain_attn, w_query, w_key, w_value, w_forget, forget_bias, w_out, gain_ffn, w_gate, w_up, w_down,
              cotangent):
    parts, part_rows, width = tokens.shape
    rows = parts * part_rows
    head = w_query.shape[1]
    slots = w_forget.shape[1]
    units = w_gate.shape[1]
    n_seq, n_head = lax.axis_size("seq"), lax.axis_size("head")
    span = w_gate.shape[0]
    per_part = pieces = part_rows // TILE
    chunks = TILE // CHUNK
    every = [(m, t) for m in range(parts) for t in range(pieces)]

    x = tokens.reshape(rows, width)
    cot = cotangent.reshape(rows, width)
    gain1 = gain_attn.reshape(1, width)
    gain2 = gain_ffn.reshape(1, width)
    state_scratch = pltpu.VMEM((slots, 2 * head), f32)
    decay_scratch = pltpu.VMEM((slots, 128), f32)
    anywhere = pl.BlockSpec(memory_space=pl.ANY)
    in_place = pl.BlockSpec(memory_space=pltpu.VMEM)

    stacked = jnp.stack([w_gate, w_up, w_down.T])
    x, stacked = lax.optimization_barrier((x, stacked))
    full = lax.all_gather(stacked, "seq")

    all_rows = lambda c: pl.BlockSpec((TILE, c), lambda i: (i, 0))
    by_part = lambda c: pl.BlockSpec((1, slots, c), lambda i: (i // per_part, 0, 0))
    xn, q, k, v, z, local, decay, sent = call(
        "project",
        functools.partial(project_kernel, per_part),
        (rows // TILE,),
        [all_rows(width), fixed((1, width))] + [fixed((width, head))] * 3 + [fixed((width, slots)), fixed((1, slots))],
        [all_rows(width), all_rows(head), all_rows(head), all_rows(head), all_rows(slots), by_part(2 * head), by_part(128),
         by_part(2 * head + 128)],
        [shaped((rows, width), bf16)] + [shaped((rows, head), bf16)] * 3
        + [shaped((rows, slots), f32), shaped((parts, slots, 2 * head), f32), shaped((parts, slots, 128), f32),
           shaped((parts, slots, 2 * head + 128), bf16)],
        [state_scratch, decay_scratch],
        cost=cost(2 * rows * width * (3 * head + slots), 2 * rows * width * 3 + 2 * width * 3 * head),
        loose_out=(5, 6, 7),
    )(x, gain1, w_query, w_key, w_value, w_forget, forget_bias.reshape(1, slots))
    entering = scan_states(n_seq, local, decay, sent, False)

    def chunk_rows(m, t, columns, back):
        start = (m * pieces + t) * chunks
        return pl.BlockSpec((CHUNK, columns), lambda i: (start + (chunks - 1 - i if back else i), 0))

    def own_rows(columns, back):
        return pl.BlockSpec((CHUNK, columns), lambda i: (chunks - 1 - i if back else i, 0))

    def chunk_state(back):
        return pl.BlockSpec((1, slots, 2 * head), lambda i: (chunks - 1 - i if back else i, 0, 0))

    def whole(shape):
        return pl.BlockSpec(shape, lambda i: (0,) * len(shape))

    def state_of(m):
        return pl.BlockSpec((None, slots, 2 * head), lambda i: (m, 0, 0))

    states_shape = shaped((chunks, slots, 2 * head), f32)

    def read(m, t, entering, which):
        return call(
            "read",
            read_kernel,
            (chunks,),
            [chunk_rows(m, t, head, False)] * 3 + [chunk_rows(m, t, slots, False), state_of(which), fixed((head, width))],
            [own_rows(head, False), own_rows(slots, False), own_rows(slots, False), chunk_state(False),
             pl.BlockSpec((None, slots, 2 * head), lambda i: (0, 0, 0)), own_rows(width, False)],
            [shaped((TILE, head), bf16), shaped((TILE, slots), f32), shaped((TILE, slots), f32), states_shape,
             shaped((1, slots, 2 * head), f32), shaped((TILE, width), bf16)],
            [state_scratch],
            cost=cost(2 * TILE * head * (600 + width), 2 * TILE * (head * 4 + width) + 2 * head * width),
            loose=(4,),
            loose_out=(4, 5),
        )(q, k, v, z, entering, w_out)

    def feed(m, t, attended):
        tile_count = pl.cdiv(units, TILE)
        vmem = pltpu.VMEM
        return call(
            "feed",
            functools.partial(feed_kernel, (m * pieces + t) * TILE),
            (),
            [anywhere, in_place, in_place, anywhere, anywhere],
            [anywhere] * 6 + [in_place],
            [shaped((TILE, width), f32), shaped((TILE, width), bf16)] + [shaped((TILE, units), bf16)] * 3
            + [shaped((TILE, width), bf16)] * 2,
            [vmem((n_seq, 3, span, units), bf16), vmem((TILE, width), bf16), vmem((TILE, width), bf16),
             vmem((TILE, width), f32), vmem((TILE, width), bf16)] + [vmem((TILE, units), bf16)] * 3
            + [vmem((TILE, width), bf16), pltpu.SemaphoreType.DMA((2,)), pltpu.SemaphoreType.DMA((6,)),
               pltpu.SemaphoreType.DMA((tile_count,))],
            cost=cost(12 * TILE * width * units, 6 * width * units + TILE * width * 14),
            loose=(1, 2),
            loose_out=(6,),
        )(x, attended, gain2, cot, full)

    group = max(1, TILE // span)
    wide = group * span
    grads_shape = shaped((n_seq, 3, span, units), bf16)

    def down_grads(acts):
        return call(
            "down_grads",
            down_grad_kernel,
            (width // wide,),
            [pl.BlockSpec((rows, wide), lambda j: (0, j))] + [fixed((TILE, units))] * len(acts),
            pl.BlockSpec((group, 1, span, units), lambda j: (j, 2, 0, 0)),
            grads_shape,
            cost=cost(2 * rows * width * units, 2 * (rows * width + rows * units + width * units)),
        )(cot, *acts)

    def wide_grads(normed, gates, ups, held_grads):
        count = len(normed)
        return call(
            "wide_grads",
            wide_grad_kernel,
            (width // wide,),
            [pl.BlockSpec((TILE, wide), lambda j: (0, j))] * count
            + [fixed((TILE, units))] * (2 * count) + [anywhere],
            pl.BlockSpec((group, 2, span, units), lambda j: (j, 0, 0, 0)),
            grads_shape,
            cost=cost(4 * rows * width * units, 2 * (rows * width + 2 * rows * units + 2 * width * units)),
            aliases={3 * count: 0},
        )(*normed, *gates, *ups, held_grads)

    def back(m, t, dhn, hidden):
        o, p, scores, e_chunks = reads[m, t][:4]
        return call(
            "back",
            back_kernel,
            (chunks,),
            [own_rows(width, True), own_rows(width, True), chunk_rows(m, t, width, True), fixed((1, width)),
             fixed((head, width))]
            + [chunk_rows(m, t, head, True)] * 3 + [chunk_rows(m, t, slots, True)] + [own_rows(slots, True)] * 2
            + [chunk_state(True)],
            [own_rows(width, True)] * 2 + [own_rows(head, True)] * 3 + [own_rows(slots, True)] * 2
            + [chunk_state(True), whole((slots, 2 * head)), whole((slots, 128)), whole((8, width))],
            [shaped((TILE, width), f32), shaped((TILE, width), bf16), shaped((TILE, head), bf16),
             shaped((TILE, head), f32), shaped((TILE, head), f32), shaped((TILE, slots), f32),
             shaped((TILE, slots), f32), states_shape, shaped((slots, 2 * head), f32), shaped((slots, 128), f32),
             shaped((8, width), f32)],
            [state_scratch, decay_scratch],
            cost=cost(2 * TILE * width * head + 2 * TILE * head * 1500, TILE * width * 14 + TILE * head * 20),
            loose=(0,),
            loose_out=(8, 9),
        )(dhn, hidden, cot, gain2, w_out, q, k, v, z, p, scores, e_chunks)

    def last(m, t, leaving, saved):
        dq, dk_local, dv_local, h_sum, x_local, g_chunks = saved
        return call(
            "last",
            last_kernel,
            (chunks,),
            [state_of(m * pieces + t), chunk_rows(m, t, head, True), chunk_rows(m, t, head, True),
             chunk_rows(m, t, slots, True), chunk_state(True), chunk_state(True), own_rows(head, True),
             own_rows(head, True), own_rows(slots, True), own_rows(slots, True), own_rows(head, True),
             chunk_rows(m, t, width, True)] + [fixed((width, head))] * 3 + [fixed((width, slots))],
            [own_rows(head, True), own_rows(head, True), own_rows(slots, True), own_rows(width, True), whole((8, slots)),
             whole((8, width))],
            [shaped((TILE, head), bf16), shaped((TILE, head), bf16), shaped((TILE, slots), bf16),
             shaped((TILE, width), bf16), shaped((8, slots), f32), shaped((8, width), f32)],
            [state_scratch],
            cost=cost(2 * TILE * width * (3 * head + slots), TILE * width * 8 + TILE * head * 20 + width * head * 6),
            loose=(0,),
            loose_out=(3,),
        )(leaving, k, v, z, reads[m, t][3], g_chunks, dk_local, dv_local, h_sum, x_local, dq, x,
          w_query, w_key, w_value, w_forget)

    line = Line()
    live = {}

    def start():
        names = list(live)
        live.update(zip(names, line.step([live[n] for n in names])))

    def end(coming=None, done=None):
        total = line.join(coming)
        if done is not None:
            live[done] = total

    reads, backs, lasts = {}, {}, {}
    outs, in_grads = [None], [None]
    eighth = TILE // 2

    def into(name, kernel, m, t, kept, dtype, inputs, specs):
        spec = pl.BlockSpec((1, eighth, width), lambda i: (m, 2 * t + i, 0))
        old = [] if kept[0] is None else [kept[0]]
        kept[0] = call(
            name,
            kernel,
            (2,),
            specs + [anywhere] * len(old),
            spec,
            shaped(tokens.shape, dtype),
            cost=cost(0, TILE * width * 10),
            loose=(1,),
            aliases={len(specs): 0} if old else None,
        )(*inputs, *old)

    piece_spec = pl.BlockSpec((eighth, width), lambda i: (i, 0))

    def finish_out(m, t):
        into("out", out_kernel, m, t, outs, bf16, [live.pop(("hidden", m, t)), live.pop(("ffn", m, t))],
             [piece_spec, piece_spec])

    def finish_grad(m, t):
        x_rows = pl.BlockSpec((eighth, width), lambda i: (2 * (m * pieces + t) + i, 0))
        into("in_grad", in_grad_kernel, m, t, in_grads, f32, [backs[m, t][0], live.pop(("dxn", m, t)), x, gain1],
             [piece_spec, piece_spec, x_rows, pl.BlockSpec((1, width), lambda i: (0, 0))])

    def go_read(m, t):
        before = live["entering"] if t == 0 else live.pop("left")
        reads[m, t] = read(m, t, before, m if t == 0 else 0)
        if t + 1 < pieces:
            live["left"] = reads[m, t][4]
        return reads[m, t][5]

    def go_feed(m, t):
        made = feed(m, t, live.pop(("att", m, t)))
        for name, value in zip(("hidden", "hn", "act", "dgate", "dup", "ffn_part"), made):
            live[name, m, t] = value
        return made[6]

    def go_back(m, t):
        backs[m, t] = back(m, t, live.pop(("dhn", m, t)), live["hidden", m, t])
        live["back", m, t] = backs[m, t][8]

    def go_last(m, t):
        lasts[m, t] = last(m, t, live["leaving"], backs[m, t][2:8])
        live["dxn_part", m, t] = lasts[m, t][3]

    def taken(name):
        return [live.pop((name, *key)) for key in every]

    live["entering"] = entering
    line.load(go_read(0, 0))
    start()
    end(go_read(0, 1))
    start()
    end(go_read(1, 0))
    start()
    end(go_read(1, 1), ("att", 0, 0))
    live.pop("entering")
    start()
    end(go_feed(0, 0), ("att", 0, 1))
    start()
    end(go_feed(0, 1), ("att", 1, 0))
    start()
    end(go_feed(1, 0), ("att", 1, 1))
    start()
    end(go_feed(1, 1), ("dhn", 0, 0))
    start()
    live["grads"] = down_grads(taken("act"))
    go_back(0, 0)
    end(live.pop(("ffn_part", 0, 0)), ("dhn", 0, 1))
    start()
    live["grads"] = wide_grads(taken("hn"), taken("dgate"), taken("dup"), live["grads"])
    end(live.pop(("ffn_part", 0, 1)), ("dhn", 1, 0))
    start()
    ffn_shares = lax.psum_scatter(live.pop("grads"), "seq", scatter_dimension=0)
    go_back(0, 1)
    go_back(1, 0)
    end(live.pop(("ffn_part", 1, 0)), ("dhn", 1, 1))
    start()
    go_back(1, 1)
    taken("back")
    own = [backs[key][8] for key in every] + [backs[key][9] for key in every]
    folded = in_vmem(
        "fold",
        functools.partial(fold_kernel, parts, pieces),
        own,
        [shaped(local.shape, f32), shaped(decay.shape, f32), shaped(sent.shape, bf16)],
    )

    def next_step(sent):
        live["sent"] = sent
        end(live.pop(("ffn_part", 1, 1)), ("ffn", 0, 0))
        start()
        return live.pop("sent")

    live["leaving"] = scan_states(n_seq, *folded, True, own, pieces, next_step)
    go_last(0, 0)
    end(live.pop(("dxn_part", 0, 0)), ("ffn", 0, 1))
    start()
    go_last(0, 1)
    go_last(1, 0)
    end(live.pop(("dxn_part", 0, 1)), ("ffn", 1, 0))
    start()
    go_last(1, 1)
    live.pop("leaving")
    attn_grads, forget_grads = call(
        "attn_grads",
        functools.partial(attn_grad_kernel, len(every)),
        (width // TILE,),
        [pl.BlockSpec((rows, TILE), lambda j: (0, j))] + [pl.BlockSpec((TILE, TILE), lambda j: (0, j))] * len(every)
        + [fixed((TILE, head))] * (3 * len(every)) + [fixed((TILE, slots))] * len(every)
        + [fixed((TILE, head))] * len(every),
        [pl.BlockSpec((TILE, 4 * head), lambda j: (j, 0)), pl.BlockSpec((TILE, slots), lambda j: (j, 0))],
        [shaped((width, 4 * head), bf16), shaped((width, slots), bf16)],
        cost=cost(2 * rows * width * (4 * head + slots), 4 * rows * width + 8 * rows * head + 8 * width * head),
    )(xn, *[backs[key][1] for key in every], *[backs[key][2] for key in every],
      *[lasts[key][i] for i in range(3) for key in every], *[reads[key][0] for key in every])
    live["attn_grads"] = attn_grads
    bias_sum = jnp.sum(sum(n[4] for n in lasts.values()), 0)
    gain1_sum = jnp.sum(sum(n[5] for n in lasts.values()), 0)
    gain2_sum = jnp.sum(sum(n[10] for n in backs.values()), 0)
    small = jnp.concatenate(
        [
            forget_grads,
            gain2_sum.astype(bf16)[:, None],
            gain1_sum.astype(bf16)[:, None],
            jnp.zeros((width, 128 - 2 - slots % 128), bf16),
        ],
        1,
    ).reshape(n_seq, span, -1)
    bias_row = jnp.pad(jnp.stack(halves(bias_sum)), ((0, 14), (0, small.shape[2] - slots)))
    live["small"] = jnp.concatenate([small, jnp.broadcast_to(bias_row, (n_seq,) + bias_row.shape)], 1)
    end(live.pop(("dxn_part", 1, 0)), ("ffn", 1, 1))
    start()
    small_shares = lax.psum_scatter(live.pop("small"), "seq", scatter_dimension=0)
    attn_shares = lax.psum_scatter(live.pop("attn_grads"), "seq", scatter_dimension=0, tiled=True)
    finish_out(0, 0)
    finish_out(0, 1)
    live["out"], live["ffn_shares"] = outs[0], ffn_shares
    end(live.pop(("dxn_part", 1, 1)), ("dxn", 0, 0))
    start()
    outs[0], ffn_shares = live.pop("out"), live.pop("ffn_shares")
    finish_out(1, 0)
    finish_out(1, 1)
    finish_grad(0, 0)
    live["out"], live["in_grad"] = outs[0], in_grads[0]
    end(None, ("dxn", 0, 1))
    start()
    in_grads[0] = live.pop("in_grad")
    finish_grad(0, 1)
    live["in_grad"], live["small"] = in_grads[0], small_shares
    end(None, ("dxn", 1, 0))
    start()
    in_grads[0], small_shares = live.pop("in_grad"), live.pop("small").astype(f32)
    gain1_total = small_shares[:span, slots + 1]
    bit = 1
    while bit < n_head:
        gain1_total = gain1_total + lax.ppermute(gain1_total, "head", [(i, i ^ bit) for i in range(n_head)])
        bit *= 2
    finish_grad(1, 0)
    end(None, ("dxn", 1, 1))
    live["dxn", 1, 1], attn_shares = lax.optimization_barrier((live["dxn", 1, 1], attn_shares))
    attn_shares = attn_shares.astype(f32)
    finish_grad(1, 1)

    return (
        live["out"],
        in_grads[0],
        gain1_total,
        attn_shares[:, :head],
        attn_shares[:, head : 2 * head],
        attn_shares[:, 2 * head : 3 * head],
        small_shares[:span, :slots],
        small_shares[span, :slots] + small_shares[span + 1, :slots],
        attn_shares[:, 3 * head :].T,
        small_shares[:span, slots],
        ffn_shares[0].astype(f32),
        ffn_shares[1].astype(f32),
        ffn_shares[2].astype(f32).T,
    )


def solution(mesh):
    rows, both = P(None, "seq", None), P("seq", "head")
    by_head, down = P(None, "head"), P("head", "seq")
    return jax.shard_map(
        on_device,
        mesh=mesh,
        in_specs=(rows, P(), by_head, by_head, by_head, by_head, P("head"), P("head", None), P(), both, both, down, rows),
        out_specs=(rows, rows, P("seq"), both, both, both, both, P("head"), down, P("seq"), both, both, down),
        check_vma=False,
    )
```

```python
import functools

import jax
import jax.numpy as jnp
from jax import lax
from jax.experimental import pallas as pl
from jax.experimental.pallas import tpu as pltpu
from jax.sharding import PartitionSpec as P

CHUNK = 128
TILE = 256
EPS = 1e-06
RATE = 0.5
MIB = 2**20
f32 = jnp.float32
bf16 = jnp.bfloat16
highest = lax.Precision.HIGHEST


def nn(a, b):
    return lax.dot_general(a, b, (((1,), (0,)), ((), ())), preferred_element_type=f32)


def nt(a, b):
    return lax.dot_general(a, b, (((1,), (1,)), ((), ())), preferred_element_type=f32)


def tn(a, b):
    return lax.dot_general(a, b, (((0,), (0,)), ((), ())), preferred_element_type=f32)


def exact(a, b, dims):
    return lax.dot_general(a, b, (dims, ((), ())), precision=highest, preferred_element_type=f32)


def halves(a):
    high = a.astype(bf16)
    return high, (a - high.astype(f32)).astype(bf16)


def call(name, kernel, grid, in_specs, out_specs, out_shape, scratch=(), vmem=48, cost=None, loose=(), loose_out=(),
         aliases=None):
    single = not isinstance(out_shape, list)
    shapes = [out_shape] if single else out_shape
    shapes = [s if i in loose_out else pltpu.HBM(s.shape, s.dtype) for i, s in enumerate(shapes)]
    function = pl.pallas_call(
        kernel,
        name=name,
        grid=grid,
        in_specs=in_specs,
        out_specs=out_specs,
        out_shape=shapes[0] if single else shapes,
        scratch_shapes=scratch,
        input_output_aliases=aliases or {},
        compiler_params=pltpu.CompilerParams(
            dimension_semantics=("arbitrary",) * len(grid), vmem_limit_bytes=vmem * MIB
        ),
        cost_estimate=cost,
    )

    def run(*operands):
        return function(*[
            o if i in loose or spec.memory_space == pltpu.SMEM else pltpu.with_memory_space_constraint(o, pltpu.HBM)
            for i, (o, spec) in enumerate(zip(operands, in_specs))
        ])

    return run


def cost(flops, data):
    return pl.CostEstimate(flops=int(flops), bytes_accessed=int(data), transcendentals=0)


def fixed(shape):
    zeros = (0,) * len(shape)
    return pl.BlockSpec(shape, lambda *_: zeros, pipeline_mode=pl.Buffered(1))


def shaped(shape, dtype):
    return jax.ShapeDtypeStruct(shape, dtype)


def triangle(lower):
    r = lax.broadcasted_iota(jnp.int32, (CHUNK, CHUNK), 0)
    c = lax.broadcasted_iota(jnp.int32, (CHUNK, CHUNK), 1)
    return r >= c if lower else r <= c


def gates(z):
    la = -RATE * lax.logistic(-z)
    y = -la
    taken = jnp.ones_like(y)
    for n in range(9, 1, -1):
        taken = 1.0 - y * (1.0 / n) * taken
    taken = y * taken
    cum = exact(triangle(True).astype(f32), la, ((1,), (0,)))
    return cum, jnp.exp(-cum) * taken


def turned_last(cum):
    return jnp.broadcast_to(cum[CHUNK - 1 :, :], cum.shape).T


def halves_sum(ones, values):
    high, low = halves(values)
    both = nn(ones.astype(bf16), jnp.concatenate([high, low], 1))
    width = values.shape[1]
    return both[:, :width] + both[:, width:]


def project_kernel(per_part, x_ref, gain_ref, wq_ref, wk_ref, wv_ref, wf_ref, bias_ref,
                   xn_ref, q_ref, k_ref, v_ref, z_ref, cum_ref, in_ref, s_ref, d_ref, sent_ref, state, decay):
    @pl.when(lax.rem(pl.program_id(0), per_part) == 0)
    def _():
        state[...] = jnp.zeros_like(state)
        decay[...] = jnp.zeros_like(decay)

    x = x_ref[...].astype(f32)
    r1 = lax.rsqrt(jnp.mean(x * x, axis=-1, keepdims=True) + EPS)
    xn = (x * r1 * gain_ref[...]).astype(bf16)
    xn_ref[...] = xn
    q_ref[...] = nn(xn, wq_ref[...]).astype(bf16)
    k_ref[...] = nn(xn, wk_ref[...]).astype(bf16)
    v_ref[...] = nn(xn, wv_ref[...]).astype(bf16)
    z_ref[...] = nn(xn, wf_ref[...]) + bias_ref[...]
    width = k_ref.shape[1]
    for c in range(x_ref.shape[0] // CHUNK):
        rows = pl.ds(c * CHUNK, CHUNK)
        cum, inflow = gates(z_ref[rows, :])
        cum_ref[rows, :] = cum
        in_ref[rows, :] = inflow
        total = turned_last(cum)
        spread = inflow.astype(bf16)
        keep = jnp.exp(total[:, :1])
        state[:, :width] = keep * (state[:, :width] + tn(spread, k_ref[rows, :]))
        state[:, width:] = keep * (state[:, width:] + tn(spread, v_ref[rows, :]))
        decay[...] += total
    s_ref[0] = state[...]
    d_ref[0] = jnp.exp(decay[...])
    pack(sent_ref, 0, jnp.exp(decay[...]), state[...])


def read_kernel(q_ref, k_ref, v_ref, cum_ref, in_ref, e0_ref, wo_ref, o_ref, p_ref, sc_ref, e_ref, left_ref, att_ref, state):
    @pl.when(pl.program_id(0) == 0)
    def _():
        state[...] = e0_ref[...]

    width = q_ref.shape[1]
    lower = triangle(True)
    q, k, v = q_ref[...], k_ref[...], v_ref[...]
    cum, inflow = cum_ref[...], in_ref[...]
    total = turned_last(cum)
    growth = jnp.exp(cum)
    e_ref[0] = state[...]
    i_hi, i_lo = halves(inflow)
    a_hi, a_lo = halves(jnp.where(lower, nt(q, k), 0.0))
    e_hi, e_lo = halves(state[:, :width])
    scores = growth * (nt(q, e_hi) + nt(q, e_lo) + nn(a_hi, i_hi) + (nn(a_hi, i_lo) + nn(a_lo, i_hi)))
    top = jnp.exp(scores - jnp.max(scores, axis=-1, keepdims=True))
    p = top / jnp.sum(top, axis=-1, keepdims=True)
    w = (p * growth).astype(bf16)
    mixing = jnp.where(lower, nt(w, i_hi), 0.0).astype(bf16)
    o = (nn(w, state[:, width:].astype(bf16)) + nn(mixing, v)).astype(bf16)
    o_ref[...] = o
    att_ref[...] = nn(o, wo_ref[...]).astype(bf16)
    p_ref[...] = p
    sc_ref[...] = scores
    keep = jnp.exp(total[:, :1])
    state[:, :width] = keep * (state[:, :width] + tn(i_hi, k))
    state[:, width:] = keep * (state[:, width:] + tn(i_hi, v))
    left_ref[...] = state[...]


def back_kernel(dhn_ref, hid_ref, cot_ref, gain_ref, wo_ref, q_ref, k_ref, v_ref, cum_ref, in_ref, p_ref, sc_ref,
                e_ref, dhid_ref, datt_ref, dq_ref, dkl_ref, dvl_ref, h_ref, x1_ref, g_ref, s_ref, d_ref, gg_ref, state, decay):
    step = pl.program_id(0)

    @pl.when(step == 0)
    def _():
        state[...] = jnp.zeros_like(state)
        decay[...] = jnp.zeros_like(decay)
        gg_ref[...] = jnp.zeros_like(gg_ref)

    hidden = hid_ref[...]
    dhn = dhn_ref[...].astype(f32)
    r2 = lax.rsqrt(jnp.mean(hidden * hidden, axis=-1, keepdims=True) + EPS)
    gg_ref[...] += jnp.sum((dhn * hidden * r2).reshape(-1, 8, hidden.shape[1]), axis=0)
    u2 = gain_ref[...] * dhn
    dhid = (
        cot_ref[...].astype(f32)
        + r2 * u2
        - hidden * (r2 * r2 * r2) * jnp.mean(u2 * hidden, axis=-1, keepdims=True)
    )
    dhid_ref[...] = dhid
    datt = dhid.astype(bf16)
    datt_ref[...] = datt
    width = q_ref.shape[1]
    do = nt(datt, wo_ref[...]).astype(bf16)
    lower, upper = triangle(True), triangle(False)
    q, k, v = q_ref[...], k_ref[...], v_ref[...]
    cum, inflow = cum_ref[...], in_ref[...]
    total = turned_last(cum)
    growth = jnp.exp(cum)
    p = p_ref[...]
    i_hi, i_lo = halves(inflow)
    b_hi, b_lo = halves(jnp.where(lower, nt(do, v), 0.0))
    ev_hi, ev_lo = halves(e_ref[0, :, width:])
    dp = growth * (nt(do, ev_hi) + nt(do, ev_lo) + nn(b_hi, i_hi) + (nn(b_hi, i_lo) + nn(b_lo, i_hi)))
    ds = p * (dp - jnp.sum(p * dp, axis=-1, keepdims=True))
    w = (p * growth).astype(bf16)
    gds = (growth * ds).astype(bf16)
    n = jnp.where(lower, nt(gds, i_hi), 0.0).astype(bf16)
    dq_ref[...] = (nn(gds, e_ref[0, :, :width].astype(bf16)) + nn(n, k)).astype(bf16)
    n_t = jnp.where(upper, nt(i_hi, gds), 0.0).astype(bf16)
    m_t = jnp.where(upper, nt(i_hi, w), 0.0).astype(bf16)
    dkl_ref[...] = nn(n_t, q)
    dvl_ref[...] = nn(m_t, do)
    h_ref[...] = ds * sc_ref[...] + p * dp
    a_t = jnp.where(upper, nt(k, q), 0.0).astype(bf16)
    b_t = jnp.where(upper, nt(v, do), 0.0).astype(bf16)
    x1_ref[...] = nn(a_t, gds) + nn(b_t, w)
    keep = jnp.exp(total[:, :1])
    g_k, g_v = tn(gds, q), tn(w, do)
    g_ref[0, :, :width] = g_k
    g_ref[0, :, width:] = g_v
    state[:, :width] = g_k + keep * state[:, :width]
    state[:, width:] = g_v + keep * state[:, width:]
    decay[...] += total
    s_ref[...] = state[...]
    d_ref[...] = jnp.exp(decay[...])


def last_kernel(l0_ref, k_ref, v_ref, z_ref, cum_ref, in_ref, e_ref, g_ref, dkl_ref, dvl_ref, h_ref, x1_ref, dq_ref, x_ref,
                wq_ref, wk_ref, wv_ref, wf_ref, dk_ref, dv_ref, dz_ref, dxn_ref, bias_ref, gg_ref, state):
    step = pl.program_id(0)

    @pl.when(step == 0)
    def _():
        state[...] = l0_ref[...]
        gg_ref[...] = jnp.zeros_like(gg_ref)
        bias_ref[...] = jnp.zeros_like(bias_ref)

    width = k_ref.shape[1]
    k, v, z = k_ref[...], v_ref[...], z_ref[...]
    cum, inflow = cum_ref[...], in_ref[...]
    total = turned_last(cum)
    i_hi = inflow.astype(bf16)
    keep = jnp.exp(total[:, :1])
    lg = keep * state[...]
    lg_k, lg_v = lg[:, :width].astype(bf16), lg[:, width:].astype(bf16)
    dk = (dkl_ref[...] + nn(i_hi, lg_k)).astype(bf16)
    dv = (dvl_ref[...] + nn(i_hi, lg_v)).astype(bf16)
    dk_ref[...] = dk
    dv_ref[...] = dv
    x1 = x1_ref[...]
    x2 = nt(k, lg_k) + nt(v, lg_v)
    met = jnp.broadcast_to(jnp.sum(lg * e_ref[0], axis=1, keepdims=True), (lg.shape[0], CHUNK)).T
    h, r1 = h_ref[...], inflow * x1
    dla = (
        halves_sum(triangle(False), h - r1)
        + r1
        + halves_sum(triangle(True), inflow * x2)
        + met
        - jnp.exp(-cum) * (x1 + x2)
    )
    rate = lax.logistic(-z)
    dz = (dla * RATE * rate * (1.0 - rate)).astype(bf16)
    dz_ref[...] = dz
    bias_ref[...] += jnp.sum(dz.astype(f32).reshape(-1, 8, dz.shape[1]), axis=0)
    state[...] = g_ref[0] + lg
    dxn = nt(dq_ref[...], wq_ref[...]) + nt(dk, wk_ref[...]) + nt(dv, wv_ref[...]) + nt(dz, wf_ref[...])
    dxn_ref[...] = dxn.astype(bf16)
    x = x_ref[...].astype(f32)
    r1 = lax.rsqrt(jnp.mean(x * x, axis=-1, keepdims=True) + EPS)
    gg_ref[...] += jnp.sum((dxn * x * r1).reshape(-1, 8, x.shape[1]), axis=0)


def out_kernel(hid_ref, ffn_ref, *refs):
    refs[-1][0] = (hid_ref[...] + ffn_ref[...].astype(f32)).astype(bf16)


def in_grad_kernel(dhid_ref, dxn_ref, x_ref, gain_ref, *refs):
    x = x_ref[...].astype(f32)
    r1 = lax.rsqrt(jnp.mean(x * x, axis=-1, keepdims=True) + EPS)
    u1 = gain_ref[...] * dxn_ref[...].astype(f32)
    refs[-1][0] = dhid_ref[...] + r1 * u1 - x * (r1 * r1 * r1) * jnp.mean(u1 * x, axis=-1, keepdims=True)


def feed_kernel(first_row, x_ref, att_ref, gain_ref, cot_ref, full_ref, hid_ref, hn_ref, act_ref, dg_ref, du_ref,
                ffn_ref, dhn_ref, weights, x, cot, hid, hn, act, dg, du, ffn, in_sems, out_sems, weight_sems):
    rows, width = x.shape
    units = act.shape[1]
    blocks, _, span, _ = weights.shape
    tiles = [(u, min(TILE, units - u)) for u in range(0, units, TILE)]
    here = pl.ds(first_row, rows)
    reads = [pltpu.make_async_copy(source.at[here, :], target, in_sems.at[i])
             for i, (source, target) in enumerate(((x_ref, x), (cot_ref, cot)))]
    loads = [pltpu.make_async_copy(full_ref.at[:, :, :, pl.ds(u, size)], weights.at[:, :, :, pl.ds(u, size)],
                                   weight_sems.at[i]) for i, (u, size) in enumerate(tiles)]
    writes = [pltpu.make_async_copy(source, target, out_sems.at[i])
              for i, (source, target) in enumerate(
                  ((hid, hid_ref), (hn, hn_ref), (act, act_ref), (dg, dg_ref), (du, du_ref), (ffn, ffn_ref)))]
    for copy in reads + loads:
        copy.start()
    for copy in reads:
        copy.wait()
    hidden = x[...].astype(f32) + att_ref[...].astype(f32)
    hid[...] = hidden
    r2 = lax.rsqrt(jnp.mean(hidden * hidden, axis=-1, keepdims=True) + EPS)
    hn[...] = (hidden * r2 * gain_ref[...]).astype(bf16)
    writes[0].start()
    writes[1].start()
    for (u, size), load in zip(tiles, loads):
        load.wait()
        gate, up, dact = (
            nn(left[...], weights[:, i, :, u : u + size].reshape(width, size))
            for i, left in enumerate((hn, hn, cot))
        )
        s = lax.logistic(gate)
        silu = gate * s
        act[:, u : u + size] = (silu * up).astype(bf16)
        dg[:, u : u + size] = (dact * up * s * (1.0 + gate * (1.0 - s))).astype(bf16)
        du[:, u : u + size] = (dact * silu).astype(bf16)
    for write in writes[2:5]:
        write.start()
    group = max(1, TILE // span)
    for b in range(0, blocks, group):
        columns = slice(b * span, (b + group) * span)
        w_gate, w_up, w_down = (weights[b : b + group, i].reshape(group * span, units) for i in range(3))
        ffn[:, columns] = nt(act[...], w_down).astype(bf16)
        dhn_ref[:, columns] = (nt(dg[...], w_gate) + nt(du[...], w_up)).astype(bf16)
    writes[5].start()
    for write in writes:
        write.wait()


def summed(pairs):
    total = tn(*pairs[0])
    for pair in pairs[1:]:
        total = total + tn(*pair)
    return total.astype(bf16)


def down_grad_kernel(*refs):
    cot_ref, act, out_ref = refs[0], refs[1:-1], refs[-1]
    rows = act[0].shape[0]
    block = summed([(cot_ref[i * rows : (i + 1) * rows, :], a[...]) for i, a in enumerate(act)])
    out_ref[...] = block.reshape(out_ref.shape)


def wide_grad_kernel(*refs):
    out_ref = refs[-1]
    count = (len(refs) - 2) // 3
    hn, dg, du = refs[:count], refs[count : 2 * count], refs[2 * count : 3 * count]
    blocks, _, width, units = out_ref.shape
    for i, grads in enumerate((dg, du)):
        block = summed([(h[...], g[...]) for h, g in zip(hn, grads)])
        out_ref[:, i] = block.reshape(blocks, width, units)


def query_grad_kernel(count, *refs):
    xn_ref, out_ref = refs[0], refs[-1]
    datt, dq, o = (refs[1 + i * count : 1 + (i + 1) * count] for i in range(3))
    rows, width = dq[0].shape
    xn = [xn_ref[i * rows : (i + 1) * rows, :] for i in range(count)]
    out_ref[:, :width] = summed([(x, g[...]) for x, g in zip(xn, dq)])
    out_ref[:, width:] = summed([(d[...], r[...]) for d, r in zip(datt, o)])


def state_grad_kernel(count, *refs):
    xn_ref, out_ref = refs[0], refs[-1]
    dk, dv, dz, bias, gain1, gain2 = (refs[1 + i * count : 1 + (i + 1) * count] for i in range(6))
    rows, width = dk[0].shape
    slots = dz[0].shape[1]
    groups, high, _ = out_ref.shape
    span = high - 16
    xn = [xn_ref[i * rows : (i + 1) * rows, :] for i in range(count)]
    for i, grads in enumerate((dk, dv)):
        block = summed([(x, g[...]) for x, g in zip(xn, grads)])
        out_ref[:, :span, i * width : (i + 1) * width] = block.reshape(groups, span, width)
    forget = tn(xn[0], dz[0][...])
    for x, g in zip(xn[1:], dz[1:]):
        forget = forget + tn(x, g[...])
    pad = 128 - slots % 128

    def padded(values):
        return jnp.concatenate([values, jnp.zeros((values.shape[0], pad), f32)], 1)

    def column(parts):
        total = parts[0][...]
        for part in parts[1:]:
            total = total + part[...]
        return jnp.sum(total.T, axis=1, keepdims=True)

    small = padded(forget)
    lane = lax.broadcasted_iota(jnp.int32, small.shape, 1)
    small = jnp.where(lane == slots, column(gain2), jnp.where(lane == slots + 1, column(gain1), small))
    out_ref[:, :span, 2 * width :] = small.astype(bf16).reshape(groups, span, slots + pad)
    total = bias[0][...]
    for part in bias[1:]:
        total = total + part[...]
    total = padded(jnp.broadcast_to(jnp.sum(total, axis=0, keepdims=True), (16, slots)))
    upper = total.astype(bf16).astype(f32)
    row = lax.broadcasted_iota(jnp.int32, total.shape, 0)
    tail = jnp.where(row == 0, upper, jnp.where(row == 1, total - upper, 0.0)).astype(bf16)
    for g in range(groups):
        out_ref[g, span:, : 2 * width] = jnp.zeros((16, 2 * width), bf16)
        out_ref[g, span:, 2 * width :] = tail


def pack(ref, m, decay, state):
    high, low = halves(decay)
    lane = lax.broadcasted_iota(jnp.int32, decay.shape, 1)
    width = state.shape[1]
    ref[m, :, :width] = state.astype(bf16)
    ref[m, :, width:] = jnp.where(lane == 0, high.astype(f32), low.astype(f32)).astype(bf16)


def fold_kernel(parts, pieces, *refs):
    s_refs, d_refs, (s_out, d_out, sent) = refs[: parts * pieces], refs[parts * pieces : -3], refs[-3:]
    for m in range(parts):
        s, d = s_refs[m * pieces + pieces - 1][...], d_refs[m * pieces + pieces - 1][...]
        for t in reversed(range(pieces - 1)):
            here = d_refs[m * pieces + t][...]
            s, d = s_refs[m * pieces + t][...] + here[:, :1] * s, here * d
        s_out[m], d_out[m] = s, d
        pack(sent, m, d, s)


def hop_kernel(bit, after, first, final, parts, pieces, *refs):
    refs = list(refs)
    s_ref, d_ref, got_ref = refs[:3]
    refs = refs[3:]
    if not first:
        part_s_ref, part_d_ref = refs[:2]
        refs = refs[2:]
    early = (lax.axis_index("seq") & bit) == 0
    takes = early if after else jnp.logical_not(early)
    width = s_ref.shape[2]
    found = []
    for m in range(parts):
        tail = got_ref[m, :, width:].astype(f32)
        there_d, there_s = tail[:, :1] + tail[:, 1:2], got_ref[m, :, :width].astype(f32)
        s, d = s_ref[m], d_ref[m]
        there_wide = jnp.broadcast_to(there_d, d.shape)
        new_s = jnp.where(takes, s + d[:, :1] * there_s, there_s + there_d * s)
        if first:
            part_s, part_d = jnp.where(takes, there_s, 0.0), jnp.where(takes, there_wide, 1.0)
        else:
            part_s, part_d = part_s_ref[m], part_d_ref[m]
            part_s = jnp.where(takes, part_s + part_d[:, :1] * there_s, part_s)
            part_d = jnp.where(takes, part_d * there_wide, part_d)
        found.append((new_s, d * there_wide, part_s, part_d))
    if not final:
        s_out, d_out, part_s_out, part_d_out, sent = refs
        for m, (s, d, part_s, part_d) in enumerate(found):
            s_out[m], d_out[m], part_s_out[m], part_d_out[m] = s, d, part_s, part_d
            pack(sent, m, d, s)
        return
    *own, out = refs
    arriving = jnp.zeros_like(found[0][0])
    for m in reversed(range(parts)) if after else range(parts):
        s, d, part_s, part_d = found[m]
        enters = part_s + part_d[:, :1] * arriving
        arriving = s + d[:, :1] * arriving
        for t in reversed(range(pieces)) if after else range(1):
            out[m * pieces + t if after else m] = enters
            if after and t:
                here = m * pieces + t
                enters = own[here][...] + own[parts * pieces + here][:, :1] * enters


def in_vmem(name, kernel, operands, shapes):
    return pl.pallas_call(
        kernel,
        name=name,
        in_specs=[pl.BlockSpec(memory_space=pltpu.VMEM)] * len(operands),
        out_specs=[pl.BlockSpec(memory_space=pltpu.VMEM)] * len(shapes),
        out_shape=shapes,
        compiler_params=pltpu.CompilerParams(vmem_limit_bytes=48 * MIB),
        cost_estimate=cost(0, 6 * MIB),
    )(*operands)


def scan_states(n, state, decay, sent, after, own=(), pieces=1, tie=None):
    parts, slots, width = state.shape
    part, bit, hops = [], 1, 0
    while bit < n:
        got = lax.ppermute(sent, "seq", [(i, i ^ bit) for i in range(n)])
        final = 2 * bit == n
        shapes = [shaped(state.shape, f32), shaped(decay.shape, f32)] * 2 + [shaped(sent.shape, bf16)]
        if final:
            shapes = [shaped((parts * pieces, slots, width), f32)]
        results = in_vmem(
            "hop",
            functools.partial(hop_kernel, bit, after, not part, final, parts, pieces),
            [state, decay, got, *part, *(own if final else ())],
            shapes,
        )
        if final:
            return results[0]
        state, decay, *part, sent = results
        if tie is not None and not hops:
            sent = tie(sent)
        bit, hops = 2 * bit, hops + 1


def behind_of(value, *first):
    return lax.optimization_barrier((value,) + first)[0]


def join_kernel(has, *refs):
    refs = iter(refs)
    piece, outer, pair, middle, total, coming = (next(refs) if h else None for h in has)
    makes = (piece is not None, pair is not None or coming is not None, total is not None)
    new_pair, new_total, done = (next(refs) if m else None for m in makes)
    me = lax.axis_index("head")
    end = (me == 0) | (me == 3)

    def each(work):
        @pl.loop(0, TILE // 32)
        def _(i):
            work(pl.ds(pl.multiple_of(i * 32, 32), 32))

    def both(a, b, rows):
        return a[rows, :] + b[rows, :]

    @pl.when(end)
    def _():
        def work(rows):
            if coming is not None:
                new_total[rows, :] = coming[rows, :]
            if done is not None:
                done[rows, :] = outer[rows, :]

        each(work)

    @pl.when(jnp.logical_not(end))
    def _():
        def work(rows):
            if piece is not None:
                new_pair[rows, :] = both(piece, outer, rows)
            if pair is not None:
                new_total[rows, :] = both(pair, middle, rows)
            if done is not None:
                done[rows, :] = total[rows, :]

        each(work)


class Line:
    INWARD, OUTWARD, MIDDLE = [(0, 1), (3, 2)], [(1, 0), (2, 3)], [(1, 2), (2, 1)]

    def __init__(self):
        self.piece = self.pair = self.payload = None
        self.returns = False

    def load(self, piece):
        self.piece = self.payload = piece

    def step(self, inputs):
        piece, pair, payload, returns = self.piece, self.pair, self.payload, self.returns
        values = [v for v in (payload, pair) if v is not None] + inputs
        values = list(lax.optimization_barrier(tuple(values)))
        outer = middle = None
        if payload is not None:
            payload = values.pop(0)
            way = (self.INWARD if piece is not None else []) + (self.OUTWARD if returns else [])
            outer = lax.ppermute(payload, "head", way)
        if pair is not None:
            pair = values.pop(0)
            middle = lax.ppermute(pair, "head", self.MIDDLE)
        self.waiting = (piece, outer, pair, middle, payload if returns else None)
        return values

    def join(self, coming=None):
        piece, outer, pair, middle, total = self.waiting
        if piece is None and total is None:
            outer = None
        operands = [piece, outer, pair, middle, total, coming]
        makes = [piece is not None, pair is not None or coming is not None, total is not None]
        arrays = [o for o in operands if o is not None]
        results = in_vmem(
            "join",
            functools.partial(join_kernel, [o is not None for o in operands]),
            arrays,
            [shaped(arrays[0].shape, bf16)] * sum(makes),
        )
        results = iter(results)
        self.pair, self.payload, done = (next(results) if m else None for m in makes)
        self.returns = pair is not None
        self.piece = coming
        return done


def on_device(tokens, gain_attn, w_query, w_key, w_value, w_forget, forget_bias, w_out, gain_ffn, w_gate, w_up, w_down,
              cotangent):
    parts, part_rows, width = tokens.shape
    rows = parts * part_rows
    head = w_query.shape[1]
    slots = w_forget.shape[1]
    units = w_gate.shape[1]
    n_seq, n_head = lax.axis_size("seq"), lax.axis_size("head")
    span = w_gate.shape[0]
    per_part = pieces = part_rows // TILE
    chunks = TILE // CHUNK
    every = [(m, t) for m in range(parts) for t in range(pieces)]

    x = tokens.reshape(rows, width)
    cot = cotangent.reshape(rows, width)
    gain1 = gain_attn.reshape(1, width)
    gain2 = gain_ffn.reshape(1, width)
    state_scratch = pltpu.VMEM((slots, 2 * head), f32)
    decay_scratch = pltpu.VMEM((slots, 128), f32)
    anywhere = pl.BlockSpec(memory_space=pl.ANY)
    in_place = pl.BlockSpec(memory_space=pltpu.VMEM)

    all_rows = lambda c: pl.BlockSpec((TILE, c), lambda i: (i, 0))
    by_part = lambda c: pl.BlockSpec((1, slots, c), lambda i: (i // per_part, 0, 0))
    xn, q, k, v, z, cum, inflow, local, decay, sent = call(
        "project",
        functools.partial(project_kernel, per_part),
        (rows // TILE,),
        [all_rows(width), fixed((1, width))] + [fixed((width, head))] * 3 + [fixed((width, slots)), fixed((1, slots))],
        [all_rows(width), all_rows(head), all_rows(head), all_rows(head)] + [all_rows(slots)] * 3
        + [by_part(2 * head), by_part(128), by_part(2 * head + 128)],
        [shaped((rows, width), bf16)] + [shaped((rows, head), bf16)] * 3
        + [shaped((rows, slots), f32)] * 3 + [shaped((parts, slots, 2 * head), f32), shaped((parts, slots, 128), f32),
                                             shaped((parts, slots, 2 * head + 128), bf16)],
        [state_scratch, decay_scratch],
        cost=cost(2 * rows * width * (3 * head + slots), 2 * rows * width * 3 + 2 * width * 3 * head),
        loose_out=(7, 8, 9),
    )(x, gain1, w_query, w_key, w_value, w_forget, forget_bias.reshape(1, slots))
    stacked = []

    def stack_weights(sent):
        gate, down, sent = lax.optimization_barrier((w_gate, w_down, sent))
        stacked.append(jnp.stack([gate, w_up, down.T]))
        return sent

    entering = scan_states(n_seq, local, decay, sent, False, tie=stack_weights)
    full = lax.all_gather(stacked[0], "seq")

    def chunk_rows(m, t, columns, back):
        start = (m * pieces + t) * chunks
        return pl.BlockSpec((CHUNK, columns), lambda i: (start + (chunks - 1 - i if back else i), 0))

    def own_rows(columns, back):
        return pl.BlockSpec((CHUNK, columns), lambda i: (chunks - 1 - i if back else i, 0))

    def chunk_state(back):
        return pl.BlockSpec((1, slots, 2 * head), lambda i: (chunks - 1 - i if back else i, 0, 0))

    def whole(shape):
        return pl.BlockSpec(shape, lambda i: (0,) * len(shape))

    def state_of(m):
        return pl.BlockSpec((None, slots, 2 * head), lambda i: (m, 0, 0))

    states_shape = shaped((chunks, slots, 2 * head), f32)

    def read(m, t, entering, which):
        return call(
            "read",
            read_kernel,
            (chunks,),
            [chunk_rows(m, t, head, False)] * 3 + [chunk_rows(m, t, slots, False)] * 2
            + [state_of(which), fixed((head, width))],
            [own_rows(head, False), own_rows(slots, False), own_rows(slots, False), chunk_state(False),
             pl.BlockSpec((None, slots, 2 * head), lambda i: (0, 0, 0)), own_rows(width, False)],
            [shaped((TILE, head), bf16), shaped((TILE, slots), f32), shaped((TILE, slots), f32), states_shape,
             shaped((1, slots, 2 * head), f32), shaped((TILE, width), bf16)],
            [state_scratch],
            cost=cost(2 * TILE * head * (600 + width), 2 * TILE * (head * 4 + width) + 2 * head * width),
            loose=(5,),
            loose_out=(4, 5),
        )(q, k, v, cum, inflow, entering, w_out)

    def feed(m, t, attended):
        tile_count = pl.cdiv(units, TILE)
        vmem = pltpu.VMEM
        return call(
            "feed",
            functools.partial(feed_kernel, (m * pieces + t) * TILE),
            (),
            [anywhere, in_place, in_place, anywhere, anywhere],
            [anywhere] * 6 + [in_place],
            [shaped((TILE, width), f32), shaped((TILE, width), bf16)] + [shaped((TILE, units), bf16)] * 3
            + [shaped((TILE, width), bf16)] * 2,
            [vmem((n_seq, 3, span, units), bf16), vmem((TILE, width), bf16), vmem((TILE, width), bf16),
             vmem((TILE, width), f32), vmem((TILE, width), bf16)] + [vmem((TILE, units), bf16)] * 3
            + [vmem((TILE, width), bf16), pltpu.SemaphoreType.DMA((2,)), pltpu.SemaphoreType.DMA((6,)),
               pltpu.SemaphoreType.DMA((tile_count,))],
            cost=cost(12 * TILE * width * units, 6 * width * units + TILE * width * 14),
            loose=(1, 2),
            loose_out=(6,),
        )(x, attended, gain2, cot, full)

    group = max(1, TILE // span)
    wide = group * span
    grads_shape = shaped((n_seq, 3, span, units), bf16)

    def down_grads(acts):
        return call(
            "down_grads",
            down_grad_kernel,
            (width // wide,),
            [pl.BlockSpec((rows, wide), lambda j: (0, j))] + [fixed((TILE, units))] * len(acts),
            pl.BlockSpec((group, 1, span, units), lambda j: (j, 2, 0, 0)),
            grads_shape,
            cost=cost(2 * rows * width * units, 2 * (rows * width + rows * units + width * units)),
        )(cot, *acts)

    def wide_grads(normed, gates, ups, held_grads):
        count = len(normed)
        return call(
            "wide_grads",
            wide_grad_kernel,
            (width // wide,),
            [pl.BlockSpec((TILE, wide), lambda j: (0, j))] * count
            + [fixed((TILE, units))] * (2 * count) + [anywhere],
            pl.BlockSpec((group, 2, span, units), lambda j: (j, 0, 0, 0)),
            grads_shape,
            cost=cost(4 * rows * width * units, 2 * (rows * width + 2 * rows * units + 2 * width * units)),
            aliases={3 * count: 0},
        )(*normed, *gates, *ups, held_grads)

    def back(m, t, dhn, hidden):
        o, p, scores, e_chunks = reads[m, t][:4]
        return call(
            "back",
            back_kernel,
            (chunks,),
            [own_rows(width, True), own_rows(width, True), chunk_rows(m, t, width, True), fixed((1, width)),
             fixed((head, width))]
            + [chunk_rows(m, t, head, True)] * 3 + [chunk_rows(m, t, slots, True)] * 2 + [own_rows(slots, True)] * 2
            + [chunk_state(True)],
            [own_rows(width, True)] * 2 + [own_rows(head, True)] * 3 + [own_rows(slots, True)] * 2
            + [chunk_state(True), whole((slots, 2 * head)), whole((slots, 128)), whole((8, width))],
            [shaped((TILE, width), f32), shaped((TILE, width), bf16), shaped((TILE, head), bf16),
             shaped((TILE, head), f32), shaped((TILE, head), f32), shaped((TILE, slots), f32),
             shaped((TILE, slots), f32), states_shape, shaped((slots, 2 * head), f32), shaped((slots, 128), f32),
             shaped((8, width), f32)],
            [state_scratch, decay_scratch],
            cost=cost(2 * TILE * width * head + 2 * TILE * head * 1500, TILE * width * 14 + TILE * head * 20),
            loose=(0,),
            loose_out=(8, 9),
        )(dhn, hidden, cot, gain2, w_out, q, k, v, cum, inflow, p, scores, e_chunks)

    def last(m, t, leaving, saved):
        dq, dk_local, dv_local, h_sum, x_local, g_chunks = saved
        return call(
            "last",
            last_kernel,
            (chunks,),
            [state_of(m * pieces + t), chunk_rows(m, t, head, True), chunk_rows(m, t, head, True),
             *[chunk_rows(m, t, slots, True)] * 3, chunk_state(True), chunk_state(True), own_rows(head, True),
             own_rows(head, True), own_rows(slots, True), own_rows(slots, True), own_rows(head, True),
             chunk_rows(m, t, width, True)] + [fixed((width, head))] * 3 + [fixed((width, slots))],
            [own_rows(head, True), own_rows(head, True), own_rows(slots, True), own_rows(width, True), whole((8, slots)),
             whole((8, width))],
            [shaped((TILE, head), bf16), shaped((TILE, head), bf16), shaped((TILE, slots), bf16),
             shaped((TILE, width), bf16), shaped((8, slots), f32), shaped((8, width), f32)],
            [state_scratch],
            cost=cost(2 * TILE * width * (3 * head + slots), TILE * width * 8 + TILE * head * 20 + width * head * 6),
            loose=(0,),
            loose_out=(3,),
        )(leaving, k, v, z, cum, inflow, reads[m, t][3], g_chunks, dk_local, dv_local, h_sum, x_local, dq, x,
          w_query, w_key, w_value, w_forget)

    line = Line()
    live = {}

    def start():
        names = list(live)
        live.update(zip(names, line.step([live[n] for n in names])))

    def end(coming=None, done=None):
        total = line.join(coming)
        if done is not None:
            live[done] = total

    reads, backs, lasts = {}, {}, {}
    outs, in_grads = [None], [None]
    eighth = TILE // 2

    def into(name, kernel, m, t, kept, dtype, inputs, specs):
        spec = pl.BlockSpec((1, eighth, width), lambda i: (m, 2 * t + i, 0))
        old = [] if kept[0] is None else [kept[0]]
        kept[0] = call(
            name,
            kernel,
            (2,),
            specs + [anywhere] * len(old),
            spec,
            shaped(tokens.shape, dtype),
            cost=cost(0, TILE * width * 10),
            loose=(1,),
            aliases={len(specs): 0} if old else None,
        )(*inputs, *old)

    piece_spec = pl.BlockSpec((eighth, width), lambda i: (i, 0))

    def finish_out(m, t):
        into("out", out_kernel, m, t, outs, bf16, [live.pop(("hidden", m, t)), live.pop(("ffn", m, t))],
             [piece_spec, piece_spec])

    def finish_grad(m, t):
        x_rows = pl.BlockSpec((eighth, width), lambda i: (2 * (m * pieces + t) + i, 0))
        into("in_grad", in_grad_kernel, m, t, in_grads, f32, [backs[m, t][0], live.pop(("dxn", m, t)), x, gain1],
             [piece_spec, piece_spec, x_rows, pl.BlockSpec((1, width), lambda i: (0, 0))])

    def go_read(m, t):
        before = live["entering"] if t == 0 else live.pop("left")
        reads[m, t] = read(m, t, before, m if t == 0 else 0)
        if t + 1 < pieces:
            live["left"] = reads[m, t][4]
        return reads[m, t][5]

    def go_feed(m, t):
        made = feed(m, t, live.pop(("att", m, t)))
        for name, value in zip(("hidden", "hn", "act", "dgate", "dup", "ffn_part"), made):
            live[name, m, t] = value
        return made[6]

    def go_back(m, t):
        backs[m, t] = back(m, t, live.pop(("dhn", m, t)), live["hidden", m, t])
        live["back", m, t] = backs[m, t][8]

    def go_last(m, t):
        lasts[m, t] = last(m, t, live["leaving"], backs[m, t][2:8])
        live["dxn_part", m, t] = lasts[m, t][3]

    def taken(name):
        return [live.pop((name, *key)) for key in every]

    live["entering"] = entering
    line.load(go_read(0, 0))
    start()
    end(go_read(0, 1))
    start()
    end(go_read(1, 0))
    start()
    end(go_read(1, 1), ("att", 0, 0))
    live.pop("entering")
    start()
    end(go_feed(0, 0), ("att", 0, 1))
    start()
    end(go_feed(0, 1), ("att", 1, 0))
    start()
    end(go_feed(1, 0), ("att", 1, 1))
    start()
    end(go_feed(1, 1), ("dhn", 0, 0))
    start()
    live["grads"] = down_grads(taken("act"))
    go_back(0, 0)
    end(live.pop(("ffn_part", 0, 0)), ("dhn", 0, 1))
    start()
    live["grads"] = wide_grads(taken("hn"), taken("dgate"), taken("dup"), live["grads"])
    end(live.pop(("ffn_part", 0, 1)), ("dhn", 1, 0))
    start()
    ffn_shares = lax.psum_scatter(live.pop("grads"), "seq", scatter_dimension=0)
    go_back(0, 1)
    go_back(1, 0)
    end(live.pop(("ffn_part", 1, 0)), ("dhn", 1, 1))
    start()
    go_back(1, 1)
    taken("back")
    own = [backs[key][8] for key in every] + [backs[key][9] for key in every]
    folded = in_vmem(
        "fold",
        functools.partial(fold_kernel, parts, pieces),
        own,
        [shaped(local.shape, f32), shaped(decay.shape, f32), shaped(sent.shape, bf16)],
    )

    def next_step(sent):
        live["sent"], live["xn"] = sent, xn
        end(live.pop(("ffn_part", 1, 1)), ("ffn", 0, 0))
        start()
        return live.pop("sent")

    live["leaving"] = scan_states(n_seq, *folded, True, own, pieces, next_step)
    xn_started = live.pop("xn")
    grad_columns = [pl.BlockSpec((rows, TILE), lambda j: (0, j))]
    piece_columns = [pl.BlockSpec((TILE, TILE), lambda j: (0, j))] * len(every)
    piece_whole = [fixed((TILE, head))] * len(every)
    live["query_grads"] = call(
        "query_grads",
        functools.partial(query_grad_kernel, len(every)),
        (width // TILE,),
        grad_columns + piece_columns + piece_whole * 2,
        pl.BlockSpec((TILE, 2 * head), lambda j: (j, 0)),
        shaped((width, 2 * head), bf16),
        cost=cost(4 * rows * width * head, 4 * rows * width + 4 * rows * head + 4 * width * head),
    )(xn_started, *[backs[key][1] for key in every], *[backs[key][2] for key in every], *[reads[key][0] for key in every])
    go_last(0, 0)
    end(live.pop(("dxn_part", 0, 0)), ("ffn", 0, 1))
    start()
    query_shares = lax.psum_scatter(live.pop("query_grads"), "seq", scatter_dimension=0, tiled=True)
    go_last(0, 1)
    go_last(1, 0)
    go_last(1, 1)
    live["xn"] = xn
    end(live.pop(("dxn_part", 0, 1)), ("ffn", 1, 0))
    start()
    live.pop("leaving")
    few = [pl.BlockSpec((8, TILE), lambda j: (0, j))] * len(every)
    live["state_grads"] = call(
        "state_grads",
        functools.partial(state_grad_kernel, len(every)),
        (width // TILE,),
        grad_columns + piece_whole * 2 + [fixed((TILE, slots))] * len(every) + [fixed((8, slots))] * len(every) + few * 2,
        pl.BlockSpec((group, span + 16, 2 * head + 128), lambda j: (j, 0, 0)),
        shaped((n_seq, span + 16, 2 * head + 128), bf16),
        cost=cost(4 * rows * width * head, 2 * rows * width + 4 * rows * head + 4 * width * head),
    )(live.pop("xn"), *[lasts[key][i] for i in (0, 1, 2, 4, 5) for key in every], *[backs[key][10] for key in every])
    end(live.pop(("dxn_part", 1, 0)), ("ffn", 1, 1))
    start()
    state_shares = lax.psum_scatter(live.pop("state_grads"), "seq", scatter_dimension=0)
    finish_out(0, 0)
    finish_out(0, 1)
    live["out"], live["ffn_shares"] = outs[0], ffn_shares
    end(live.pop(("dxn_part", 1, 1)), ("dxn", 0, 0))
    start()
    outs[0], ffn_shares = live.pop("out"), live.pop("ffn_shares")
    finish_out(1, 0)
    finish_out(1, 1)
    finish_grad(0, 0)
    live["out"], live["in_grad"] = outs[0], in_grads[0]
    end(None, ("dxn", 0, 1))
    start()
    in_grads[0] = live.pop("in_grad")
    finish_grad(0, 1)
    live["in_grad"] = in_grads[0]
    end(None, ("dxn", 1, 0))
    start()
    in_grads[0] = live.pop("in_grad")
    gain1_total = state_shares[:span, 2 * head + slots + 1].astype(f32)
    bit = 1
    while bit < n_head:
        gain1_total = gain1_total + lax.ppermute(gain1_total, "head", [(i, i ^ bit) for i in range(n_head)])
        bit *= 2
    finish_grad(1, 0)
    end(None, ("dxn", 1, 1))
    finish_grad(1, 1)
    query_shares = query_shares.astype(f32)
    state_shares = state_shares.astype(f32)
    small_shares = state_shares[:, 2 * head :]

    return (
        live["out"],
        in_grads[0],
        gain1_total,
        query_shares[:, :head],
        state_shares[:span, :head],
        state_shares[:span, head : 2 * head],
        small_shares[:span, :slots],
        small_shares[span, :slots] + small_shares[span + 1, :slots],
        query_shares[:, head:].T,
        small_shares[:span, slots],
        ffn_shares[0].astype(f32),
        ffn_shares[1].astype(f32),
        ffn_shares[2].astype(f32).T,
    )


def solution(mesh):
    rows, both = P(None, "seq", None), P("seq", "head")
    by_head, down = P(None, "head"), P("head", "seq")
    return jax.shard_map(
        on_device,
        mesh=mesh,
        in_specs=(rows, P(), by_head, by_head, by_head, by_head, P("head"), P("head", None), P(), both, both, down, rows),
        out_specs=(rows, rows, P("seq"), both, both, both, both, P("head"), down, P("seq"), both, both, down),
        check_vma=False,
    )
```

```python
import functools

import jax
import jax.numpy as jnp
from jax import lax
from jax.experimental import pallas as pl
from jax.experimental.pallas import tpu as pltpu
from jax.sharding import PartitionSpec as P

CHUNK = 128
TILE = 256
EPS = 1e-06
RATE = 0.5
MIB = 2**20
f32 = jnp.float32
bf16 = jnp.bfloat16
highest = lax.Precision.HIGHEST


def nn(a, b):
    return lax.dot_general(a, b, (((1,), (0,)), ((), ())), preferred_element_type=f32)


def nt(a, b):
    return lax.dot_general(a, b, (((1,), (1,)), ((), ())), preferred_element_type=f32)


def tn(a, b):
    return lax.dot_general(a, b, (((0,), (0,)), ((), ())), preferred_element_type=f32)


def exact(a, b, dims):
    return lax.dot_general(a, b, (dims, ((), ())), precision=highest, preferred_element_type=f32)


def halves(a):
    high = a.astype(bf16)
    return high, (a - high.astype(f32)).astype(bf16)


def call(name, kernel, grid, in_specs, out_specs, out_shape, scratch=(), vmem=24, cost=None, loose=(), loose_out=(),
         aliases=None):
    single = not isinstance(out_shape, list)
    shapes = [out_shape] if single else out_shape
    shapes = [s if i in loose_out else pltpu.HBM(s.shape, s.dtype) for i, s in enumerate(shapes)]
    function = pl.pallas_call(
        kernel,
        name=name,
        grid=grid,
        in_specs=in_specs,
        out_specs=out_specs,
        out_shape=shapes[0] if single else shapes,
        scratch_shapes=scratch,
        input_output_aliases=aliases or {},
        compiler_params=pltpu.CompilerParams(
            dimension_semantics=("arbitrary",) * len(grid), vmem_limit_bytes=vmem * MIB
        ),
        cost_estimate=cost,
    )

    def run(*operands):
        return function(*[
            o if i in loose or spec.memory_space == pltpu.SMEM else pltpu.with_memory_space_constraint(o, pltpu.HBM)
            for i, (o, spec) in enumerate(zip(operands, in_specs))
        ])

    return run


def cost(flops, data):
    return pl.CostEstimate(flops=int(flops), bytes_accessed=int(data), transcendentals=0)


def fixed(shape):
    zeros = (0,) * len(shape)
    return pl.BlockSpec(shape, lambda *_: zeros, pipeline_mode=pl.Buffered(1))


def shaped(shape, dtype):
    return jax.ShapeDtypeStruct(shape, dtype)


def triangle(lower):
    r = lax.broadcasted_iota(jnp.int32, (CHUNK, CHUNK), 0)
    c = lax.broadcasted_iota(jnp.int32, (CHUNK, CHUNK), 1)
    return r >= c if lower else r <= c


def gates(z):
    la = -RATE * lax.logistic(-z)
    y = -la
    taken = jnp.ones_like(y)
    for n in range(9, 1, -1):
        taken = 1.0 - y * (1.0 / n) * taken
    taken = y * taken
    cum = exact(triangle(True).astype(f32), la, ((1,), (0,)))
    return cum, jnp.exp(-cum) * taken


def turned_last(cum):
    return jnp.broadcast_to(cum[CHUNK - 1 :, :], cum.shape).T


def halves_sum(ones, values):
    high, low = halves(values)
    both = nn(ones.astype(bf16), jnp.concatenate([high, low], 1))
    width = values.shape[1]
    return both[:, :width] + both[:, width:]


def project_kernel(per_part, x_ref, gain_ref, wq_ref, wk_ref, wv_ref, wf_ref, bias_ref,
                   xn_ref, q_ref, k_ref, v_ref, z_ref, cum_ref, in_ref, s_ref, d_ref, sent_ref, state, decay):
    @pl.when(lax.rem(pl.program_id(0), per_part) == 0)
    def _():
        state[...] = jnp.zeros_like(state)
        decay[...] = jnp.zeros_like(decay)

    x = x_ref[...].astype(f32)
    r1 = lax.rsqrt(jnp.mean(x * x, axis=-1, keepdims=True) + EPS)
    xn = (x * r1 * gain_ref[...]).astype(bf16)
    xn_ref[...] = xn
    q_ref[...] = nn(xn, wq_ref[...]).astype(bf16)
    k_ref[...] = nn(xn, wk_ref[...]).astype(bf16)
    v_ref[...] = nn(xn, wv_ref[...]).astype(bf16)
    z_ref[...] = nn(xn, wf_ref[...]) + bias_ref[...]
    width = k_ref.shape[1]
    for c in range(x_ref.shape[0] // CHUNK):
        rows = pl.ds(c * CHUNK, CHUNK)
        cum, inflow = gates(z_ref[rows, :])
        cum_ref[rows, :] = cum
        in_ref[rows, :] = inflow
        total = turned_last(cum)
        spread = inflow.astype(bf16)
        keep = jnp.exp(total[:, :1])
        state[:, :width] = keep * (state[:, :width] + tn(spread, k_ref[rows, :]))
        state[:, width:] = keep * (state[:, width:] + tn(spread, v_ref[rows, :]))
        decay[...] += total
    s_ref[0] = state[...]
    d_ref[0] = jnp.exp(decay[...])
    pack(sent_ref, 0, jnp.exp(decay[...]), state[...])


def read_kernel(q_ref, k_ref, v_ref, cum_ref, in_ref, e0_ref, wo_ref, o_ref, p_ref, sc_ref, e_ref, left_ref, att_ref, state):
    @pl.when(pl.program_id(0) == 0)
    def _():
        state[...] = e0_ref[...]

    width = q_ref.shape[1]
    lower = triangle(True)
    q, k, v = q_ref[...], k_ref[...], v_ref[...]
    cum, inflow = cum_ref[...], in_ref[...]
    total = turned_last(cum)
    growth = jnp.exp(cum)
    e_ref[0] = state[...]
    i_hi, i_lo = halves(inflow)
    a_hi, a_lo = halves(jnp.where(lower, nt(q, k), 0.0))
    e_hi, e_lo = halves(state[:, :width])
    scores = growth * (nt(q, e_hi) + nt(q, e_lo) + nn(a_hi, i_hi) + (nn(a_hi, i_lo) + nn(a_lo, i_hi)))
    top = jnp.exp(scores - jnp.max(scores, axis=-1, keepdims=True))
    p = top / jnp.sum(top, axis=-1, keepdims=True)
    w = (p * growth).astype(bf16)
    mixing = jnp.where(lower, nt(w, i_hi), 0.0).astype(bf16)
    o = (nn(w, state[:, width:].astype(bf16)) + nn(mixing, v)).astype(bf16)
    o_ref[...] = o
    att_ref[...] = nn(o, wo_ref[...]).astype(bf16)
    p_ref[...] = p
    sc_ref[...] = scores
    keep = jnp.exp(total[:, :1])
    state[:, :width] = keep * (state[:, :width] + tn(i_hi, k))
    state[:, width:] = keep * (state[:, width:] + tn(i_hi, v))
    left_ref[...] = state[...]


def back_kernel(dhn_ref, hid_ref, cot_ref, gain_ref, wo_ref, q_ref, k_ref, v_ref, cum_ref, in_ref, p_ref, sc_ref,
                e_ref, dhid_ref, datt_ref, dq_ref, dkl_ref, dvl_ref, h_ref, x1_ref, g_ref, s_ref, d_ref, gg_ref, state, decay):
    step = pl.program_id(0)

    @pl.when(step == 0)
    def _():
        state[...] = jnp.zeros_like(state)
        decay[...] = jnp.zeros_like(decay)
        gg_ref[...] = jnp.zeros_like(gg_ref)

    hidden = hid_ref[...]
    dhn = dhn_ref[...].astype(f32)
    r2 = lax.rsqrt(jnp.mean(hidden * hidden, axis=-1, keepdims=True) + EPS)
    gg_ref[...] += jnp.sum((dhn * hidden * r2).reshape(-1, 8, hidden.shape[1]), axis=0)
    u2 = gain_ref[...] * dhn
    dhid = (
        cot_ref[...].astype(f32)
        + r2 * u2
        - hidden * (r2 * r2 * r2) * jnp.mean(u2 * hidden, axis=-1, keepdims=True)
    )
    dhid_ref[...] = dhid
    datt = dhid.astype(bf16)
    datt_ref[...] = datt
    width = q_ref.shape[1]
    do = nt(datt, wo_ref[...]).astype(bf16)
    lower, upper = triangle(True), triangle(False)
    q, k, v = q_ref[...], k_ref[...], v_ref[...]
    cum, inflow = cum_ref[...], in_ref[...]
    total = turned_last(cum)
    growth = jnp.exp(cum)
    p = p_ref[...]
    i_hi, i_lo = halves(inflow)
    b_hi, b_lo = halves(jnp.where(lower, nt(do, v), 0.0))
    ev_hi, ev_lo = halves(e_ref[0, :, width:])
    dp = growth * (nt(do, ev_hi) + nt(do, ev_lo) + nn(b_hi, i_hi) + (nn(b_hi, i_lo) + nn(b_lo, i_hi)))
    ds = p * (dp - jnp.sum(p * dp, axis=-1, keepdims=True))
    w = (p * growth).astype(bf16)
    gds = (growth * ds).astype(bf16)
    n = jnp.where(lower, nt(gds, i_hi), 0.0).astype(bf16)
    dq_ref[...] = (nn(gds, e_ref[0, :, :width].astype(bf16)) + nn(n, k)).astype(bf16)
    n_t = jnp.where(upper, nt(i_hi, gds), 0.0).astype(bf16)
    m_t = jnp.where(upper, nt(i_hi, w), 0.0).astype(bf16)
    dkl_ref[...] = nn(n_t, q)
    dvl_ref[...] = nn(m_t, do)
    h_ref[...] = ds * sc_ref[...] + p * dp
    a_t = jnp.where(upper, nt(k, q), 0.0).astype(bf16)
    b_t = jnp.where(upper, nt(v, do), 0.0).astype(bf16)
    x1_ref[...] = nn(a_t, gds) + nn(b_t, w)
    keep = jnp.exp(total[:, :1])
    g_k, g_v = tn(gds, q), tn(w, do)
    g_ref[0, :, :width] = g_k
    g_ref[0, :, width:] = g_v
    state[:, :width] = g_k + keep * state[:, :width]
    state[:, width:] = g_v + keep * state[:, width:]
    decay[...] += total
    s_ref[...] = state[...]
    d_ref[...] = jnp.exp(decay[...])


def last_kernel(l0_ref, k_ref, v_ref, z_ref, cum_ref, in_ref, e_ref, g_ref, dkl_ref, dvl_ref, h_ref, x1_ref, dq_ref, x_ref,
                wq_ref, wk_ref, wv_ref, wf_ref, dk_ref, dv_ref, dz_ref, dxn_ref, bias_ref, gg_ref,
                state, wq, wk, wv, wf, sems):
    step, steps = pl.program_id(0), pl.num_programs(0)
    loads = [pltpu.make_async_copy(source, target, sems.at[i])
             for i, (source, target) in enumerate(((wq_ref, wq), (wk_ref, wk), (wv_ref, wv), (wf_ref, wf)))]

    @pl.when(step == 0)
    def _():
        for load in loads:
            load.start()
        state[...] = l0_ref[...]
        bias_ref[...] = jnp.zeros_like(bias_ref)

    width = k_ref.shape[1]
    k, v, z = k_ref[...], v_ref[...], z_ref[...]
    cum, inflow = cum_ref[...], in_ref[...]
    total = turned_last(cum)
    i_hi = inflow.astype(bf16)
    keep = jnp.exp(total[:, :1])
    lg = keep * state[...]
    lg_k, lg_v = lg[:, :width].astype(bf16), lg[:, width:].astype(bf16)
    rows = pl.ds(pl.multiple_of((steps - 1 - step) * CHUNK, CHUNK), CHUNK)
    dk_ref[rows, :] = (dkl_ref[...] + nn(i_hi, lg_k)).astype(bf16)
    dv_ref[rows, :] = (dvl_ref[...] + nn(i_hi, lg_v)).astype(bf16)
    x1 = x1_ref[...]
    x2 = nt(k, lg_k) + nt(v, lg_v)
    met = jnp.broadcast_to(jnp.sum(lg * e_ref[0], axis=1, keepdims=True), (lg.shape[0], CHUNK)).T
    h, r1 = h_ref[...], inflow * x1
    dla = (
        halves_sum(triangle(False), h - r1)
        + r1
        + halves_sum(triangle(True), inflow * x2)
        + met
        - jnp.exp(-cum) * (x1 + x2)
    )
    rate = lax.logistic(-z)
    dz = (dla * RATE * rate * (1.0 - rate)).astype(bf16)
    dz_ref[rows, :] = dz
    bias_ref[...] += jnp.sum(dz.astype(f32).reshape(-1, 8, dz.shape[1]), axis=0)
    state[...] = g_ref[0] + lg

    @pl.when(step == steps - 1)
    def _():
        for load in loads:
            load.wait()
        dxn = nt(dq_ref[...], wq[...]) + nt(dk_ref[...], wk[...]) + nt(dv_ref[...], wv[...]) + nt(dz_ref[...], wf[...])
        dxn_ref[...] = dxn.astype(bf16)
        x = x_ref[...].astype(f32)
        r1 = lax.rsqrt(jnp.mean(x * x, axis=-1, keepdims=True) + EPS)
        gg_ref[...] = jnp.sum((dxn * x * r1).reshape(-1, 8, x.shape[1]), axis=0)


def out_kernel(hid_ref, ffn_ref, *refs):
    refs[-1][0] = (hid_ref[...] + ffn_ref[...].astype(f32)).astype(bf16)


def in_grad_kernel(dhid_ref, dxn_ref, x_ref, gain_ref, *refs):
    x = x_ref[...].astype(f32)
    r1 = lax.rsqrt(jnp.mean(x * x, axis=-1, keepdims=True) + EPS)
    u1 = gain_ref[...] * dxn_ref[...].astype(f32)
    refs[-1][0] = dhid_ref[...] + r1 * u1 - x * (r1 * r1 * r1) * jnp.mean(u1 * x, axis=-1, keepdims=True)


def feed_kernel(first_row, x_ref, att_ref, gain_ref, cot_ref, full_ref, hid_ref, hn_ref, act_ref, dg_ref, du_ref,
                ffn_ref, dhn_ref, weights, x, cot, hid, hn, act, dg, du, ffn, in_sems, out_sems, weight_sems):
    rows, width = x.shape
    units = act.shape[1]
    blocks, _, span, _ = weights.shape
    tiles = [(u, min(TILE, units - u)) for u in range(0, units, TILE)]
    here = pl.ds(first_row, rows)
    reads = [pltpu.make_async_copy(source.at[here, :], target, in_sems.at[i])
             for i, (source, target) in enumerate(((x_ref, x), (cot_ref, cot)))]
    loads = [pltpu.make_async_copy(full_ref.at[:, :, :, pl.ds(u, size)], weights.at[:, :, :, pl.ds(u, size)],
                                   weight_sems.at[i]) for i, (u, size) in enumerate(tiles)]
    writes = [pltpu.make_async_copy(source, target, out_sems.at[i])
              for i, (source, target) in enumerate(
                  ((hid, hid_ref), (hn, hn_ref), (act, act_ref), (dg, dg_ref), (du, du_ref), (ffn, ffn_ref)))]
    for copy in reads + loads:
        copy.start()
    for copy in reads:
        copy.wait()
    hidden = x[...].astype(f32) + att_ref[...].astype(f32)
    hid[...] = hidden
    r2 = lax.rsqrt(jnp.mean(hidden * hidden, axis=-1, keepdims=True) + EPS)
    hn[...] = (hidden * r2 * gain_ref[...]).astype(bf16)
    writes[0].start()
    writes[1].start()
    for (u, size), load in zip(tiles, loads):
        load.wait()
        gate, up, dact = (
            nn(left[...], weights[:, i, :, u : u + size].reshape(width, size))
            for i, left in enumerate((hn, hn, cot))
        )
        s = lax.logistic(gate)
        silu = gate * s
        act[:, u : u + size] = (silu * up).astype(bf16)
        dg[:, u : u + size] = (dact * up * s * (1.0 + gate * (1.0 - s))).astype(bf16)
        du[:, u : u + size] = (dact * silu).astype(bf16)
    for write in writes[2:5]:
        write.start()
    group = max(1, TILE // span)
    for b in range(0, blocks, group):
        columns = slice(b * span, (b + group) * span)
        w_gate, w_up, w_down = (weights[b : b + group, i].reshape(group * span, units) for i in range(3))
        ffn[:, columns] = nt(act[...], w_down).astype(bf16)
        dhn_ref[:, columns] = (nt(dg[...], w_gate) + nt(du[...], w_up)).astype(bf16)
    writes[5].start()
    for write in writes:
        write.wait()


def summed(pairs):
    total = tn(*pairs[0])
    for pair in pairs[1:]:
        total = total + tn(*pair)
    return total.astype(bf16)


def down_grad_kernel(*refs):
    cot_ref, act, out_ref = refs[0], refs[1:-1], refs[-1]
    rows = act[0].shape[0]
    block = summed([(cot_ref[i * rows : (i + 1) * rows, :], a[...]) for i, a in enumerate(act)])
    out_ref[...] = block.reshape(out_ref.shape)


def wide_grad_kernel(*refs):
    out_ref = refs[-1]
    count = (len(refs) - 1) // 3
    hn, dg, du = refs[:count], refs[count : 2 * count], refs[2 * count : 3 * count]
    blocks, _, width, units = out_ref.shape
    for i, grads in enumerate((dg, du)):
        block = summed([(h[...], g[...]) for h, g in zip(hn, grads)])
        out_ref[:, i] = block.reshape(blocks, width, units)


def query_grad_kernel(count, *refs):
    xn_ref, out_ref = refs[0], refs[-1]
    datt, dq, o = (refs[1 + i * count : 1 + (i + 1) * count] for i in range(3))
    rows, width = dq[0].shape
    xn = [xn_ref[i * rows : (i + 1) * rows, :] for i in range(count)]
    out_ref[:, :width] = summed([(x, g[...]) for x, g in zip(xn, dq)])
    out_ref[:, width:] = summed([(d[...], r[...]) for d, r in zip(datt, o)])


def state_grad_kernel(count, *refs):
    xn_ref, query_ref, out_ref = refs[0], refs[-2], refs[-1]
    dk, dv, dz, bias, gain1, gain2 = (refs[1 + i * count : 1 + (i + 1) * count] for i in range(6))
    rows, width = dk[0].shape
    slots = dz[0].shape[1]
    groups, high, _ = out_ref.shape
    span = high - 16
    xn = [xn_ref[i * rows : (i + 1) * rows, :] for i in range(count)]
    for i, grads in enumerate((dk, dv)):
        block = summed([(x, g[...]) for x, g in zip(xn, grads)])
        out_ref[:, :span, (2 + i) * width : (3 + i) * width] = block.reshape(groups, span, width)
    out_ref[:, :span, : 2 * width] = query_ref[...].reshape(groups, span, 2 * width)
    forget = tn(xn[0], dz[0][...])
    for x, g in zip(xn[1:], dz[1:]):
        forget = forget + tn(x, g[...])
    pad = 128 - slots % 128

    def padded(values):
        return jnp.concatenate([values, jnp.zeros((values.shape[0], pad), f32)], 1)

    def column(parts):
        total = parts[0][...]
        for part in parts[1:]:
            total = total + part[...]
        return jnp.sum(total.T, axis=1, keepdims=True)

    small = padded(forget)
    lane = lax.broadcasted_iota(jnp.int32, small.shape, 1)
    small = jnp.where(lane == slots, column(gain2), jnp.where(lane == slots + 1, column(gain1), small))
    out_ref[:, :span, 4 * width :] = small.astype(bf16).reshape(groups, span, slots + pad)
    total = bias[0][...]
    for part in bias[1:]:
        total = total + part[...]
    total = padded(jnp.broadcast_to(jnp.sum(total, axis=0, keepdims=True), (16, slots)))
    upper = total.astype(bf16).astype(f32)
    row = lax.broadcasted_iota(jnp.int32, total.shape, 0)
    tail = jnp.where(row == 0, upper, jnp.where(row == 1, total - upper, 0.0)).astype(bf16)
    for g in range(groups):
        out_ref[g, span:, : 4 * width] = jnp.zeros((16, 4 * width), bf16)
        out_ref[g, span:, 4 * width :] = tail


def pack(ref, m, decay, state):
    high, low = halves(decay)
    lane = lax.broadcasted_iota(jnp.int32, decay.shape, 1)
    width = state.shape[1]
    ref[m, :, :width] = state.astype(bf16)
    ref[m, :, width:] = jnp.where(lane == 0, high.astype(f32), low.astype(f32)).astype(bf16)


def fold_kernel(parts, pieces, *refs):
    s_refs, d_refs, (s_out, d_out, sent) = refs[: parts * pieces], refs[parts * pieces : -3], refs[-3:]
    for m in range(parts):
        s, d = s_refs[m * pieces + pieces - 1][...], d_refs[m * pieces + pieces - 1][...]
        for t in reversed(range(pieces - 1)):
            here = d_refs[m * pieces + t][...]
            s, d = s_refs[m * pieces + t][...] + here[:, :1] * s, here * d
        s_out[m], d_out[m] = s, d
        pack(sent, m, d, s)


def hop_kernel(bit, after, first, final, parts, pieces, *refs):
    refs = list(refs)
    s_ref, d_ref, got_ref = refs[:3]
    refs = refs[3:]
    if not first:
        part_s_ref, part_d_ref = refs[:2]
        refs = refs[2:]
    early = (lax.axis_index("seq") & bit) == 0
    takes = early if after else jnp.logical_not(early)
    width = s_ref.shape[2]
    found = []
    for m in range(parts):
        tail = got_ref[m, :, width:].astype(f32)
        there_d, there_s = tail[:, :1] + tail[:, 1:2], got_ref[m, :, :width].astype(f32)
        s, d = s_ref[m], d_ref[m]
        there_wide = jnp.broadcast_to(there_d, d.shape)
        new_s = jnp.where(takes, s + d[:, :1] * there_s, there_s + there_d * s)
        if first:
            part_s, part_d = jnp.where(takes, there_s, 0.0), jnp.where(takes, there_wide, 1.0)
        else:
            part_s, part_d = part_s_ref[m], part_d_ref[m]
            part_s = jnp.where(takes, part_s + part_d[:, :1] * there_s, part_s)
            part_d = jnp.where(takes, part_d * there_wide, part_d)
        found.append((new_s, d * there_wide, part_s, part_d))
    if not final:
        s_out, d_out, part_s_out, part_d_out, sent = refs
        for m, (s, d, part_s, part_d) in enumerate(found):
            s_out[m], d_out[m], part_s_out[m], part_d_out[m] = s, d, part_s, part_d
            pack(sent, m, d, s)
        return
    *own, out = refs
    arriving = jnp.zeros_like(found[0][0])
    for m in reversed(range(parts)) if after else range(parts):
        s, d, part_s, part_d = found[m]
        enters = part_s + part_d[:, :1] * arriving
        arriving = s + d[:, :1] * arriving
        for t in reversed(range(pieces)) if after else range(1):
            out[m * pieces + t if after else m] = enters
            if after and t:
                here = m * pieces + t
                enters = own[here][...] + own[parts * pieces + here][:, :1] * enters


def in_vmem(name, kernel, operands, shapes):
    return pl.pallas_call(
        kernel,
        name=name,
        in_specs=[pl.BlockSpec(memory_space=pltpu.VMEM)] * len(operands),
        out_specs=[pl.BlockSpec(memory_space=pltpu.VMEM)] * len(shapes),
        out_shape=shapes,
        compiler_params=pltpu.CompilerParams(vmem_limit_bytes=12 * MIB),
        cost_estimate=cost(0, 6 * MIB),
    )(*operands)


def scan_states(n, state, decay, sent, after, own=(), pieces=1, tie=None, last_tie=None):
    parts, slots, width = state.shape
    part, bit, hops = [], 1, 0
    while bit < n:
        got = lax.ppermute(sent, "seq", [(i, i ^ bit) for i in range(n)])
        final = 2 * bit == n
        shapes = [shaped(state.shape, f32), shaped(decay.shape, f32)] * 2 + [shaped(sent.shape, bf16)]
        if final:
            shapes = [shaped((parts * pieces, slots, width), f32)]
        if final and last_tie is not None:
            state = behind_of(state, last_tie)
        results = in_vmem(
            "hop",
            functools.partial(hop_kernel, bit, after, not part, final, parts, pieces),
            [state, decay, got, *part, *(own if final else ())],
            shapes,
        )
        if final:
            return results[0]
        state, decay, *part, sent = results
        if tie is not None and not hops:
            sent = tie(sent)
        bit, hops = 2 * bit, hops + 1


def behind_of(value, *first):
    return lax.optimization_barrier((value,) + first)[0]


def join_kernel(has, *refs):
    refs = iter(refs)
    piece, outer, pair, middle, total, coming = (next(refs) if h else None for h in has)
    makes = (piece is not None, pair is not None or coming is not None, total is not None)
    new_pair, new_total, done = (next(refs) if m else None for m in makes)
    me = lax.axis_index("head")
    end = (me == 0) | (me == 3)

    def each(work):
        @pl.loop(0, TILE // 32)
        def _(i):
            work(pl.ds(pl.multiple_of(i * 32, 32), 32))

    def both(a, b, rows):
        return a[rows, :] + b[rows, :]

    @pl.when(end)
    def _():
        def work(rows):
            if coming is not None:
                new_total[rows, :] = coming[rows, :]
            if done is not None:
                done[rows, :] = outer[rows, :]

        each(work)

    @pl.when(jnp.logical_not(end))
    def _():
        def work(rows):
            if piece is not None:
                new_pair[rows, :] = both(piece, outer, rows)
            if pair is not None:
                new_total[rows, :] = both(pair, middle, rows)
            if done is not None:
                done[rows, :] = total[rows, :]

        each(work)


class Line:
    INWARD, OUTWARD, MIDDLE = [(0, 1), (3, 2)], [(1, 0), (2, 3)], [(1, 2), (2, 1)]

    def __init__(self):
        self.piece = self.pair = self.payload = None
        self.returns = False

    def load(self, piece):
        self.piece = self.payload = piece

    def step(self, inputs):
        piece, pair, payload, returns = self.piece, self.pair, self.payload, self.returns
        values = [v for v in (payload, pair) if v is not None] + inputs
        values = list(lax.optimization_barrier(tuple(values)))
        outer = middle = None
        if payload is not None:
            payload = values.pop(0)
            way = (self.INWARD if piece is not None else []) + (self.OUTWARD if returns else [])
            outer = lax.ppermute(payload, "head", way)
        if pair is not None:
            pair = values.pop(0)
            middle = lax.ppermute(pair, "head", self.MIDDLE)
        self.waiting = (piece, outer, pair, middle, payload if returns else None)
        return values

    def join(self, coming=None):
        piece, outer, pair, middle, total = self.waiting
        if piece is None and total is None:
            outer = None
        operands = [piece, outer, pair, middle, total, coming]
        makes = [piece is not None, pair is not None or coming is not None, total is not None]
        arrays = [o for o in operands if o is not None]
        results = in_vmem(
            "join",
            functools.partial(join_kernel, [o is not None for o in operands]),
            arrays,
            [shaped(arrays[0].shape, bf16)] * sum(makes),
        )
        results = iter(results)
        self.pair, self.payload, done = (next(results) if m else None for m in makes)
        self.returns = pair is not None
        self.piece = coming
        return done


def on_device(tokens, gain_attn, w_query, w_key, w_value, w_forget, forget_bias, w_out, gain_ffn, w_gate, w_up, w_down,
              cotangent):
    parts, part_rows, width = tokens.shape
    rows = parts * part_rows
    head = w_query.shape[1]
    slots = w_forget.shape[1]
    units = w_gate.shape[1]
    n_seq, n_head = lax.axis_size("seq"), lax.axis_size("head")
    span = w_gate.shape[0]
    per_part = pieces = part_rows // TILE
    chunks = TILE // CHUNK
    every = [(m, t) for m in range(parts) for t in range(pieces)]

    x = tokens.reshape(rows, width)
    cot = cotangent.reshape(rows, width)
    gain1 = gain_attn.reshape(1, width)
    gain2 = gain_ffn.reshape(1, width)
    state_scratch = pltpu.VMEM((slots, 2 * head), f32)
    decay_scratch = pltpu.VMEM((slots, 128), f32)
    anywhere = pl.BlockSpec(memory_space=pl.ANY)
    in_place = pl.BlockSpec(memory_space=pltpu.VMEM)

    all_rows = lambda c: pl.BlockSpec((TILE, c), lambda i: (i, 0))
    by_part = lambda c: pl.BlockSpec((1, slots, c), lambda i: (i // per_part, 0, 0))
    xn, q, k, v, z, cum, inflow, local, decay, sent = call(
        "project",
        functools.partial(project_kernel, per_part),
        (rows // TILE,),
        [all_rows(width), fixed((1, width))] + [fixed((width, head))] * 3 + [fixed((width, slots)), fixed((1, slots))],
        [all_rows(width), all_rows(head), all_rows(head), all_rows(head)] + [all_rows(slots)] * 3
        + [by_part(2 * head), by_part(128), by_part(2 * head + 128)],
        [shaped((rows, width), bf16)] + [shaped((rows, head), bf16)] * 3
        + [shaped((rows, slots), f32)] * 3 + [shaped((parts, slots, 2 * head), f32), shaped((parts, slots, 128), f32),
                                             shaped((parts, slots, 2 * head + 128), bf16)],
        [state_scratch, decay_scratch],
        cost=cost(2 * rows * width * (3 * head + slots), 2 * rows * width * 3 + 2 * width * 3 * head),
        loose_out=(7, 8, 9),
    )(x, gain1, w_query, w_key, w_value, w_forget, forget_bias.reshape(1, slots))
    stacked = []

    def stack_weights(sent):
        gate, down, sent = lax.optimization_barrier((w_gate, w_down, sent))
        stacked.append(jnp.stack([gate, w_up, down.T]))
        return sent

    entering = scan_states(n_seq, local, decay, sent, False, tie=stack_weights)
    full = lax.all_gather(stacked[0], "seq")

    def chunk_rows(m, t, columns, back):
        start = (m * pieces + t) * chunks
        return pl.BlockSpec((CHUNK, columns), lambda i: (start + (chunks - 1 - i if back else i), 0))

    def own_rows(columns, back):
        return pl.BlockSpec((CHUNK, columns), lambda i: (chunks - 1 - i if back else i, 0))

    def chunk_state(back):
        return pl.BlockSpec((1, slots, 2 * head), lambda i: (chunks - 1 - i if back else i, 0, 0))

    def whole(shape):
        return pl.BlockSpec(shape, lambda i: (0,) * len(shape))

    def state_of(m):
        return pl.BlockSpec((None, slots, 2 * head), lambda i: (m, 0, 0))

    states_shape = shaped((chunks, slots, 2 * head), f32)

    def read(m, t, entering, which):
        return call(
            "read",
            read_kernel,
            (chunks,),
            [chunk_rows(m, t, head, False)] * 3 + [chunk_rows(m, t, slots, False)] * 2
            + [state_of(which), fixed((head, width))],
            [own_rows(head, False), own_rows(slots, False), own_rows(slots, False), chunk_state(False),
             pl.BlockSpec((None, slots, 2 * head), lambda i: (0, 0, 0)), own_rows(width, False)],
            [shaped((TILE, head), bf16), shaped((TILE, slots), f32), shaped((TILE, slots), f32), states_shape,
             shaped((1, slots, 2 * head), f32), shaped((TILE, width), bf16)],
            [state_scratch],
            cost=cost(2 * TILE * head * (600 + width), 2 * TILE * (head * 4 + width) + 2 * head * width),
            loose=(5,),
            loose_out=(4, 5),
        )(q, k, v, cum, inflow, entering, w_out)

    def feed(m, t, attended):
        tile_count = pl.cdiv(units, TILE)
        vmem = pltpu.VMEM
        return call(
            "feed",
            functools.partial(feed_kernel, (m * pieces + t) * TILE),
            (),
            [anywhere, in_place, in_place, anywhere, anywhere],
            [anywhere] * 6 + [in_place],
            [shaped((TILE, width), f32), shaped((TILE, width), bf16)] + [shaped((TILE, units), bf16)] * 3
            + [shaped((TILE, width), bf16)] * 2,
            [vmem((n_seq, 3, span, units), bf16), vmem((TILE, width), bf16), vmem((TILE, width), bf16),
             vmem((TILE, width), f32), vmem((TILE, width), bf16)] + [vmem((TILE, units), bf16)] * 3
            + [vmem((TILE, width), bf16), pltpu.SemaphoreType.DMA((2,)), pltpu.SemaphoreType.DMA((6,)),
               pltpu.SemaphoreType.DMA((tile_count,))],
            cost=cost(12 * TILE * width * units, 6 * width * units + TILE * width * 14),
            vmem=44,
            loose=(1, 2),
            loose_out=(6,),
        )(x, attended, gain2, cot, full)

    group = max(1, TILE // span)
    columns = group * span
    def down_grads(acts):
        return call(
            "down_grads",
            down_grad_kernel,
            (width // columns,),
            [pl.BlockSpec((rows, columns), lambda j: (0, j))] + [fixed((TILE, units))] * len(acts),
            pl.BlockSpec((group, span, units), lambda j: (j, 0, 0)),
            shaped((n_seq, span, units), bf16),
            cost=cost(2 * rows * width * units, 2 * (rows * width + rows * units + width * units)),
        )(cot, *acts)

    def wide_grads(normed, gates, ups):
        count = len(normed)
        return call(
            "wide_grads",
            wide_grad_kernel,
            (width // columns,),
            [pl.BlockSpec((TILE, columns), lambda j: (0, j))] * count
            + [fixed((TILE, units))] * (2 * count),
            pl.BlockSpec((group, 2, span, units), lambda j: (j, 0, 0, 0)),
            shaped((n_seq, 2, span, units), bf16),
            cost=cost(4 * rows * width * units, 2 * (rows * width + 2 * rows * units + 2 * width * units)),
        )(*normed, *gates, *ups)

    def back(m, t, dhn, hidden):
        o, p, scores, e_chunks = reads[m, t][:4]
        return call(
            "back",
            back_kernel,
            (chunks,),
            [own_rows(width, True), own_rows(width, True), chunk_rows(m, t, width, True), fixed((1, width)),
             fixed((head, width))]
            + [chunk_rows(m, t, head, True)] * 3 + [chunk_rows(m, t, slots, True)] * 2 + [own_rows(slots, True)] * 2
            + [chunk_state(True)],
            [own_rows(width, True)] * 2 + [own_rows(head, True)] * 3 + [own_rows(slots, True)] * 2
            + [chunk_state(True), whole((slots, 2 * head)), whole((slots, 128)), whole((8, width))],
            [shaped((TILE, width), f32), shaped((TILE, width), bf16), shaped((TILE, head), bf16),
             shaped((TILE, head), f32), shaped((TILE, head), f32), shaped((TILE, slots), f32),
             shaped((TILE, slots), f32), states_shape, shaped((slots, 2 * head), f32), shaped((slots, 128), f32),
             shaped((8, width), f32)],
            [state_scratch, decay_scratch],
            cost=cost(2 * TILE * width * head + 2 * TILE * head * 1500, TILE * width * 14 + TILE * head * 20),
            loose=(0,),
            loose_out=(8, 9),
        )(dhn, hidden, cot, gain2, w_out, q, k, v, cum, inflow, p, scores, e_chunks)

    def last(m, t, leaving, saved):
        dq, dk_local, dv_local, h_sum, x_local, g_chunks = saved
        here = m * pieces + t
        return call(
            "last",
            last_kernel,
            (chunks,),
            [state_of(here), chunk_rows(m, t, head, True), chunk_rows(m, t, head, True),
             *[chunk_rows(m, t, slots, True)] * 3, chunk_state(True), chunk_state(True), own_rows(head, True),
             own_rows(head, True), own_rows(slots, True), own_rows(slots, True), whole((TILE, head)),
             pl.BlockSpec((TILE, width), lambda i: (here, 0))] + [anywhere] * 4,
            [whole((TILE, head)), whole((TILE, head)), whole((TILE, slots)), whole((TILE, width)), whole((8, slots)),
             whole((8, width))],
            [shaped((TILE, head), bf16), shaped((TILE, head), bf16), shaped((TILE, slots), bf16),
             shaped((TILE, width), bf16), shaped((8, slots), f32), shaped((8, width), f32)],
            [state_scratch] + [pltpu.VMEM((width, head), bf16)] * 3
            + [pltpu.VMEM((width, slots), bf16), pltpu.SemaphoreType.DMA((4,))],
            cost=cost(2 * TILE * width * (3 * head + slots), TILE * width * 8 + TILE * head * 20 + width * head * 6),
            loose=(0,),
            loose_out=(3,),
        )(leaving, k, v, z, cum, inflow, reads[m, t][3], g_chunks, dk_local, dv_local, h_sum, x_local, dq, x,
          w_query, w_key, w_value, w_forget)

    line = Line()
    live = {}

    def start():
        names = list(live)
        live.update(zip(names, line.step([live[n] for n in names])))

    def end(coming=None, done=None):
        total = line.join(coming)
        if done is not None:
            live[done] = total

    reads, backs, lasts = {}, {}, {}
    outs, in_grads = [None], [None]
    eighth = TILE // 2

    def into(name, kernel, m, t, kept, dtype, inputs, specs):
        spec = pl.BlockSpec((1, eighth, width), lambda i: (m, 2 * t + i, 0))
        old = [] if kept[0] is None else [kept[0]]
        kept[0] = call(
            name,
            kernel,
            (2,),
            specs + [anywhere] * len(old),
            spec,
            shaped(tokens.shape, dtype),
            cost=cost(0, TILE * width * 10),
            loose=(1,),
            aliases={len(specs): 0} if old else None,
        )(*inputs, *old)

    piece_spec = pl.BlockSpec((eighth, width), lambda i: (i, 0))

    def finish_out(m, t):
        into("out", out_kernel, m, t, outs, bf16, [live.pop(("hidden", m, t)), live.pop(("ffn", m, t))],
             [piece_spec, piece_spec])

    def finish_grad(m, t):
        x_rows = pl.BlockSpec((eighth, width), lambda i: (2 * (m * pieces + t) + i, 0))
        into("in_grad", in_grad_kernel, m, t, in_grads, f32, [backs[m, t][0], live.pop(("dxn", m, t)), x, gain1],
             [piece_spec, piece_spec, x_rows, pl.BlockSpec((1, width), lambda i: (0, 0))])

    def go_read(m, t):
        before = live["entering"] if t == 0 else live.pop("left")
        reads[m, t] = read(m, t, before, m if t == 0 else 0)
        if t + 1 < pieces:
            live["left"] = reads[m, t][4]
        return reads[m, t][5]

    def go_feed(m, t):
        made = feed(m, t, live.pop(("att", m, t)))
        for name, value in zip(("hidden", "hn", "act", "dgate", "dup", "ffn_part"), made):
            live[name, m, t] = value
        return made[6]

    def go_back(m, t):
        backs[m, t] = back(m, t, live.pop(("dhn", m, t)), live["hidden", m, t])
        live["back", m, t] = backs[m, t][8]

    def go_last(m, t):
        lasts[m, t] = last(m, t, live["leaving"], backs[m, t][2:8])
        live["dxn_part", m, t] = lasts[m, t][3]

    def taken(name):
        return [live.pop((name, *key)) for key in every]

    live["entering"] = entering
    line.load(go_read(0, 0))
    start()
    end(go_read(0, 1))
    start()
    end(go_read(1, 0))
    start()
    end(go_read(1, 1), ("att", 0, 0))
    live.pop("entering")
    start()
    end(go_feed(0, 0), ("att", 0, 1))
    start()
    end(go_feed(0, 1), ("att", 1, 0))
    start()
    end(go_feed(1, 0), ("att", 1, 1))
    start()
    end(go_feed(1, 1), ("dhn", 0, 0))
    start()
    live["down_grads"] = down_grads(taken("act"))
    go_back(0, 0)
    end(live.pop(("ffn_part", 0, 0)), ("dhn", 0, 1))
    start()
    down_shares = lax.psum_scatter(live.pop("down_grads"), "seq", scatter_dimension=0)
    live["wide_grads"] = wide_grads(taken("hn"), taken("dgate"), taken("dup"))
    end(live.pop(("ffn_part", 0, 1)), ("dhn", 1, 0))
    start()
    wide = live.pop("wide_grads")
    go_back(0, 1)
    go_back(1, 0)
    end(live.pop(("ffn_part", 1, 0)), ("dhn", 1, 1))
    start()
    go_back(1, 1)
    taken("back")
    own = [backs[key][8] for key in every] + [backs[key][9] for key in every]
    folded = in_vmem(
        "fold",
        functools.partial(fold_kernel, parts, pieces),
        own,
        [shaped(local.shape, f32), shaped(decay.shape, f32), shaped(sent.shape, bf16)],
    )

    live["xn"] = xn
    end(live.pop(("ffn_part", 1, 1)), ("ffn", 0, 0))
    start()
    xn_columns = [pl.BlockSpec((rows, TILE), lambda j: (0, j))]
    piece_columns = [pl.BlockSpec((TILE, TILE), lambda j: (0, j))] * len(every)
    piece_whole = [fixed((TILE, head))] * len(every)
    query_grads = call(
        "query_grads",
        functools.partial(query_grad_kernel, len(every)),
        (width // TILE,),
        xn_columns + piece_columns + piece_whole * 2,
        pl.BlockSpec((TILE, 2 * head), lambda j: (j, 0)),
        shaped((width, 2 * head), bf16),
        cost=cost(4 * rows * width * head, 4 * rows * width + 4 * rows * head + 4 * width * head),
    )(live.pop("xn"), *[backs[key][1] for key in every], *[backs[key][2] for key in every],
      *[reads[key][0] for key in every])
    live["leaving"] = scan_states(n_seq, *folded, True, own, pieces, last_tie=query_grads)
    live["query_grads"], live["wide"] = query_grads, wide
    go_last(0, 0)
    end(live.pop(("dxn_part", 0, 0)), ("ffn", 0, 1))
    start()
    wide_shares = lax.psum_scatter(live.pop("wide"), "seq", scatter_dimension=0)
    go_last(0, 1)
    go_last(1, 0)
    go_last(1, 1)
    live["xn"] = xn
    end(live.pop(("dxn_part", 0, 1)), ("ffn", 1, 0))
    start()
    live.pop("leaving")
    few = [pl.BlockSpec((8, TILE), lambda j: (0, j))] * len(every)
    live["state_grads"] = call(
        "state_grads",
        functools.partial(state_grad_kernel, len(every)),
        (width // TILE,),
        xn_columns + piece_whole * 2 + [fixed((TILE, slots))] * len(every) + [fixed((8, slots))] * len(every) + few * 2
        + [pl.BlockSpec((TILE, 2 * head), lambda j: (j, 0))],
        pl.BlockSpec((group, span + 16, 4 * head + 128), lambda j: (j, 0, 0)),
        shaped((n_seq, span + 16, 4 * head + 128), bf16),
        cost=cost(4 * rows * width * head, 2 * rows * width + 4 * rows * head + 4 * width * head),
    )(live.pop("xn"), *[lasts[key][i] for i in (0, 1, 2, 4, 5) for key in every], *[backs[key][10] for key in every],
      live.pop("query_grads"))
    end(live.pop(("dxn_part", 1, 0)), ("ffn", 1, 1))
    start()
    attn_shares = lax.psum_scatter(live.pop("state_grads"), "seq", scatter_dimension=0)
    finish_out(0, 0)
    finish_out(0, 1)
    live["out"], live["down"], live["wide"] = outs[0], down_shares, wide_shares
    end(live.pop(("dxn_part", 1, 1)), ("dxn", 0, 0))
    start()
    outs[0], down_shares, wide_shares = live.pop("out"), live.pop("down"), live.pop("wide")
    finish_out(1, 0)
    finish_out(1, 1)
    finish_grad(0, 0)
    live["out"], live["in_grad"] = outs[0], in_grads[0]
    end(None, ("dxn", 0, 1))
    start()
    in_grads[0] = live.pop("in_grad")
    finish_grad(0, 1)
    live["in_grad"], live["attn"] = in_grads[0], attn_shares
    end(None, ("dxn", 1, 0))
    start()
    in_grads[0], late = live.pop("in_grad"), live.pop("attn").astype(f32)
    gain1_total = late[:span, 4 * head + slots + 1]
    bit = 1
    while bit < n_head:
        gain1_total = gain1_total + lax.ppermute(gain1_total, "head", [(i, i ^ bit) for i in range(n_head)])
        bit *= 2
    finish_grad(1, 0)
    end(None, ("dxn", 1, 1))
    finish_grad(1, 1)
    small_shares = late[:, 4 * head :]

    return (
        live["out"],
        in_grads[0],
        gain1_total,
        late[:span, :head],
        late[:span, 2 * head : 3 * head],
        late[:span, 3 * head : 4 * head],
        small_shares[:span, :slots],
        small_shares[span, :slots] + small_shares[span + 1, :slots],
        late[:span, head : 2 * head].T,
        small_shares[:span, slots],
        wide_shares[0].astype(f32),
        wide_shares[1].astype(f32),
        down_shares.astype(f32).T,
    )


def solution(mesh):
    rows, both = P(None, "seq", None), P("seq", "head")
    by_head, down = P(None, "head"), P("head", "seq")
    return jax.shard_map(
        on_device,
        mesh=mesh,
        in_specs=(rows, P(), by_head, by_head, by_head, by_head, P("head"), P("head", None), P(), both, both, down, rows),
        out_specs=(rows, rows, P("seq"), both, both, both, both, P("head"), down, P("seq"), both, both, down),
        check_vma=False,
    )
```

```python
import functools

import jax
import jax.numpy as jnp
from jax import lax
from jax.experimental import pallas as pl
from jax.experimental.pallas import tpu as pltpu
from jax.sharding import PartitionSpec as P

CHUNK = 128
TILE = 256
EPS = 1e-06
RATE = 0.5
MIB = 2**20
f32 = jnp.float32
bf16 = jnp.bfloat16
highest = lax.Precision.HIGHEST


def nn(a, b):
    return lax.dot_general(a, b, (((1,), (0,)), ((), ())), preferred_element_type=f32)


def nt(a, b):
    return lax.dot_general(a, b, (((1,), (1,)), ((), ())), preferred_element_type=f32)


def tn(a, b):
    return lax.dot_general(a, b, (((0,), (0,)), ((), ())), preferred_element_type=f32)


def exact(a, b, dims):
    return lax.dot_general(a, b, (dims, ((), ())), precision=highest, preferred_element_type=f32)


def halves(a):
    high = a.astype(bf16)
    return high, (a - high.astype(f32)).astype(bf16)


def call(name, kernel, grid, in_specs, out_specs, out_shape, scratch=(), vmem=24, cost=None, loose=(), loose_out=(),
         aliases=None):
    single = not isinstance(out_shape, list)
    shapes = [out_shape] if single else out_shape
    shapes = [s if i in loose_out else pltpu.HBM(s.shape, s.dtype) for i, s in enumerate(shapes)]
    function = pl.pallas_call(
        kernel,
        name=name,
        grid=grid,
        in_specs=in_specs,
        out_specs=out_specs,
        out_shape=shapes[0] if single else shapes,
        scratch_shapes=scratch,
        input_output_aliases=aliases or {},
        compiler_params=pltpu.CompilerParams(
            dimension_semantics=("arbitrary",) * len(grid), vmem_limit_bytes=vmem * MIB
        ),
        cost_estimate=cost,
    )

    def run(*operands):
        return function(*[
            o if i in loose or spec.memory_space == pltpu.SMEM else pltpu.with_memory_space_constraint(o, pltpu.HBM)
            for i, (o, spec) in enumerate(zip(operands, in_specs))
        ])

    return run


def cost(flops, data):
    return pl.CostEstimate(flops=int(flops), bytes_accessed=int(data), transcendentals=0)


def fixed(shape):
    zeros = (0,) * len(shape)
    return pl.BlockSpec(shape, lambda *_: zeros, pipeline_mode=pl.Buffered(1))


def shaped(shape, dtype):
    return jax.ShapeDtypeStruct(shape, dtype)


def triangle(lower):
    r = lax.broadcasted_iota(jnp.int32, (CHUNK, CHUNK), 0)
    c = lax.broadcasted_iota(jnp.int32, (CHUNK, CHUNK), 1)
    return r >= c if lower else r <= c


def gates(z):
    la = -RATE * lax.logistic(-z)
    y = -la
    taken = jnp.ones_like(y)
    for n in range(9, 1, -1):
        taken = 1.0 - y * (1.0 / n) * taken
    taken = y * taken
    cum = exact(triangle(True).astype(f32), la, ((1,), (0,)))
    return cum, jnp.exp(-cum) * taken


def turned_last(cum):
    return jnp.broadcast_to(cum[CHUNK - 1 :, :], cum.shape).T


def halves_sum(ones, values):
    high, low = halves(values)
    both = nn(ones.astype(bf16), jnp.concatenate([high, low], 1))
    width = values.shape[1]
    return both[:, :width] + both[:, width:]


def project_kernel(per_part, x_ref, gain_ref, wk_ref, wv_ref, wf_ref, bias_ref,
                   xn_ref, k_ref, v_ref, z_ref, cum_ref, in_ref, s_ref, d_ref, sent_ref, state, decay):
    @pl.when(lax.rem(pl.program_id(0), per_part) == 0)
    def _():
        state[...] = jnp.zeros_like(state)
        decay[...] = jnp.zeros_like(decay)

    x = x_ref[...].astype(f32)
    r1 = lax.rsqrt(jnp.mean(x * x, axis=-1, keepdims=True) + EPS)
    xn = (x * r1 * gain_ref[...]).astype(bf16)
    xn_ref[...] = xn
    k_ref[...] = nn(xn, wk_ref[...]).astype(bf16)
    v_ref[...] = nn(xn, wv_ref[...]).astype(bf16)
    z_ref[...] = nt(xn, wf_ref[...]) + bias_ref[...]
    width = k_ref.shape[1]
    for c in range(x_ref.shape[0] // CHUNK):
        rows = pl.ds(c * CHUNK, CHUNK)
        cum, inflow = gates(z_ref[rows, :])
        cum_ref[rows, :] = cum
        in_ref[rows, :] = inflow
        total = turned_last(cum)
        spread = inflow.astype(bf16)
        keep = jnp.exp(total[:, :1])
        state[:, :width] = keep * (state[:, :width] + tn(spread, k_ref[rows, :]))
        state[:, width:] = keep * (state[:, width:] + tn(spread, v_ref[rows, :]))
        decay[...] += total
    s_ref[0] = state[...]
    d_ref[0] = jnp.exp(decay[...])
    pack(sent_ref, 0, jnp.exp(decay[...]), state[...])


def query_kernel(xn_ref, wq_ref, q_ref):
    q_ref[...] = nn(xn_ref[...], wq_ref[...]).astype(bf16)


def read_kernel(q_ref, k_ref, v_ref, cum_ref, in_ref, e0_ref, wo_ref, o_ref, p_ref, sc_ref, e_ref, left_ref, att_ref, state):
    @pl.when(pl.program_id(0) == 0)
    def _():
        state[...] = e0_ref[...]

    width = q_ref.shape[1]
    lower = triangle(True)
    q, k, v = q_ref[...], k_ref[...], v_ref[...]
    cum, inflow = cum_ref[...], in_ref[...]
    total = turned_last(cum)
    growth = jnp.exp(cum)
    e_ref[0] = state[...]
    i_hi, i_lo = halves(inflow)
    a_hi, a_lo = halves(jnp.where(lower, nt(q, k), 0.0))
    e_hi, e_lo = halves(state[:, :width])
    scores = growth * (nt(q, e_hi) + nt(q, e_lo) + nn(a_hi, i_hi) + (nn(a_hi, i_lo) + nn(a_lo, i_hi)))
    top = jnp.exp(scores - jnp.max(scores, axis=-1, keepdims=True))
    p = top / jnp.sum(top, axis=-1, keepdims=True)
    w = (p * growth).astype(bf16)
    mixing = jnp.where(lower, nt(w, i_hi), 0.0).astype(bf16)
    o = (nn(w, state[:, width:].astype(bf16)) + nn(mixing, v)).astype(bf16)
    o_ref[...] = o
    att_ref[...] = nn(o, wo_ref[...]).astype(bf16)
    p_ref[...] = p
    sc_ref[...] = scores
    keep = jnp.exp(total[:, :1])
    state[:, :width] = keep * (state[:, :width] + tn(i_hi, k))
    state[:, width:] = keep * (state[:, width:] + tn(i_hi, v))
    left_ref[...] = state[...]


def back_kernel(dhn_ref, hid_ref, cot_ref, gain_ref, wo_ref, q_ref, k_ref, v_ref, cum_ref, in_ref, p_ref, sc_ref,
                e_ref, datt_ref, dq_ref, dkl_ref, dvl_ref, h_ref, x1_ref, g_ref, s_ref, d_ref, gg_ref, state, decay):
    step = pl.program_id(0)

    @pl.when(step == 0)
    def _():
        state[...] = jnp.zeros_like(state)
        decay[...] = jnp.zeros_like(decay)
        gg_ref[...] = jnp.zeros_like(gg_ref)

    hidden = hid_ref[...].astype(f32)
    dhn = dhn_ref[...].astype(f32)
    r2 = lax.rsqrt(jnp.mean(hidden * hidden, axis=-1, keepdims=True) + EPS)
    gg_ref[...] += jnp.sum((dhn * hidden * r2).reshape(-1, 8, hidden.shape[1]), axis=0)
    u2 = gain_ref[...] * dhn
    dhid = (
        cot_ref[...].astype(f32)
        + r2 * u2
        - hidden * (r2 * r2 * r2) * jnp.mean(u2 * hidden, axis=-1, keepdims=True)
    )
    datt = dhid.astype(bf16)
    datt_ref[...] = datt
    width = q_ref.shape[1]
    do = nt(datt, wo_ref[...]).astype(bf16)
    lower, upper = triangle(True), triangle(False)
    q, k, v = q_ref[...], k_ref[...], v_ref[...]
    cum, inflow = cum_ref[...], in_ref[...]
    total = turned_last(cum)
    growth = jnp.exp(cum)
    p = p_ref[...]
    i_hi, i_lo = halves(inflow)
    b_hi, b_lo = halves(jnp.where(lower, nt(do, v), 0.0))
    ev_hi, ev_lo = halves(e_ref[0, :, width:])
    dp = growth * (nt(do, ev_hi) + nt(do, ev_lo) + nn(b_hi, i_hi) + (nn(b_hi, i_lo) + nn(b_lo, i_hi)))
    ds = p * (dp - jnp.sum(p * dp, axis=-1, keepdims=True))
    w = (p * growth).astype(bf16)
    gds = (growth * ds).astype(bf16)
    n = jnp.where(lower, nt(gds, i_hi), 0.0).astype(bf16)
    dq_ref[...] = (nn(gds, e_ref[0, :, :width].astype(bf16)) + nn(n, k)).astype(bf16)
    n_t = jnp.where(upper, nt(i_hi, gds), 0.0).astype(bf16)
    m_t = jnp.where(upper, nt(i_hi, w), 0.0).astype(bf16)
    dkl_ref[...] = nn(n_t, q)
    dvl_ref[...] = nn(m_t, do)
    h_ref[...] = ds * sc_ref[...] + p * dp
    a_t = jnp.where(upper, nt(k, q), 0.0).astype(bf16)
    b_t = jnp.where(upper, nt(v, do), 0.0).astype(bf16)
    x1_ref[...] = nn(a_t, gds) + nn(b_t, w)
    keep = jnp.exp(total[:, :1])
    g_k, g_v = tn(gds, q), tn(w, do)
    g_ref[0, :, :width] = g_k
    g_ref[0, :, width:] = g_v
    state[:, :width] = g_k + keep * state[:, :width]
    state[:, width:] = g_v + keep * state[:, width:]
    decay[...] += total
    s_ref[...] = state[...]
    d_ref[...] = jnp.exp(decay[...])


def last_kernel(l0_ref, k_ref, v_ref, z_ref, cum_ref, in_ref, e_ref, g_ref, dkl_ref, dvl_ref, h_ref, x1_ref, dq_ref, x_ref,
                wq_ref, wk_ref, wv_ref, wf_ref, dk_ref, dv_ref, dz_ref, dxn_ref, bias_ref, gg_ref,
                state, wq, wk, wv, wf, sems):
    step, steps = pl.program_id(0), pl.num_programs(0)
    loads = [pltpu.make_async_copy(source, target, sems.at[i])
             for i, (source, target) in enumerate(((wq_ref, wq), (wk_ref, wk), (wv_ref, wv), (wf_ref, wf)))]

    @pl.when(step == 0)
    def _():
        for load in loads:
            load.start()
        state[...] = l0_ref[...]
        bias_ref[...] = jnp.zeros_like(bias_ref)

    width = k_ref.shape[1]
    k, v, z = k_ref[...], v_ref[...], z_ref[...]
    cum, inflow = cum_ref[...], in_ref[...]
    total = turned_last(cum)
    i_hi = inflow.astype(bf16)
    keep = jnp.exp(total[:, :1])
    lg = keep * state[...]
    lg_k, lg_v = lg[:, :width].astype(bf16), lg[:, width:].astype(bf16)
    rows = pl.ds(pl.multiple_of((steps - 1 - step) * CHUNK, CHUNK), CHUNK)
    dk_ref[rows, :] = (dkl_ref[...] + nn(i_hi, lg_k)).astype(bf16)
    dv_ref[rows, :] = (dvl_ref[...] + nn(i_hi, lg_v)).astype(bf16)
    x1 = x1_ref[...]
    x2 = nt(k, lg_k) + nt(v, lg_v)
    met = jnp.broadcast_to(jnp.sum(lg * e_ref[0], axis=1, keepdims=True), (lg.shape[0], CHUNK)).T
    h, r1 = h_ref[...], inflow * x1
    dla = (
        halves_sum(triangle(False), h - r1)
        + r1
        + halves_sum(triangle(True), inflow * x2)
        + met
        - jnp.exp(-cum) * (x1 + x2)
    )
    rate = lax.logistic(-z)
    dz = (dla * RATE * rate * (1.0 - rate)).astype(bf16)
    dz_ref[rows, :] = dz
    bias_ref[...] += jnp.sum(dz.astype(f32).reshape(-1, 8, dz.shape[1]), axis=0)
    state[...] = g_ref[0] + lg

    @pl.when(step == steps - 1)
    def _():
        for load in loads:
            load.wait()
        dxn = nt(dq_ref[...], wq[...]) + nt(dk_ref[...], wk[...]) + nt(dv_ref[...], wv[...]) + nn(dz_ref[...], wf[...])
        dxn_ref[...] = dxn.astype(bf16)
        x = x_ref[...].astype(f32)
        r1 = lax.rsqrt(jnp.mean(x * x, axis=-1, keepdims=True) + EPS)
        gg_ref[...] = jnp.sum((dxn * x * r1).reshape(-1, 8, x.shape[1]), axis=0)


def out_kernel(hid_ref, ffn_ref, *refs):
    refs[-1][0] = (hid_ref[...].astype(f32) + ffn_ref[...].astype(f32)).astype(bf16)


def in_grad_kernel(dhid_ref, dxn_ref, x_ref, gain_ref, *refs):
    x = x_ref[...].astype(f32)
    r1 = lax.rsqrt(jnp.mean(x * x, axis=-1, keepdims=True) + EPS)
    u1 = gain_ref[...] * dxn_ref[...].astype(f32)
    refs[-1][0] = dhid_ref[...].astype(f32) + r1 * u1 - x * (r1 * r1 * r1) * jnp.mean(u1 * x, axis=-1, keepdims=True)


def feed_kernel(first_row, x_ref, att_ref, gain_ref, cot_ref, full_ref, hid_ref, hn_ref, act_ref, dg_ref, du_ref,
                ffn_ref, dhn_ref, weights, x, cot, hid, hn, act, dg, du, ffn, in_sems, out_sems, weight_sems):
    rows, width = x.shape
    units = act.shape[1]
    blocks, _, span, _ = weights.shape
    tiles = [(u, min(TILE, units - u)) for u in range(0, units, TILE)]
    here = pl.ds(first_row, rows)
    reads = [pltpu.make_async_copy(source.at[here, :], target, in_sems.at[i])
             for i, (source, target) in enumerate(((x_ref, x), (cot_ref, cot)))]
    loads = [pltpu.make_async_copy(full_ref.at[:, :, :, pl.ds(u, size)], weights.at[:, :, :, pl.ds(u, size)],
                                   weight_sems.at[i]) for i, (u, size) in enumerate(tiles)]
    writes = [pltpu.make_async_copy(source, target, out_sems.at[i])
              for i, (source, target) in enumerate(
                  ((hid, hid_ref), (hn, hn_ref), (act, act_ref), (dg, dg_ref), (du, du_ref), (ffn, ffn_ref)))]
    for copy in reads + loads:
        copy.start()
    for copy in reads:
        copy.wait()
    hidden = x[...].astype(f32) + att_ref[...].astype(f32)
    hid[...] = hidden.astype(bf16)
    r2 = lax.rsqrt(jnp.mean(hidden * hidden, axis=-1, keepdims=True) + EPS)
    hn[...] = (hidden * r2 * gain_ref[...]).astype(bf16)
    writes[0].start()
    writes[1].start()
    for (u, size), load in zip(tiles, loads):
        load.wait()
        gate, up, dact = (
            nn(left[...], weights[:, i, :, u : u + size].reshape(width, size))
            for i, left in enumerate((hn, hn, cot))
        )
        s = lax.logistic(gate)
        silu = gate * s
        act[:, u : u + size] = (silu * up).astype(bf16)
        dg[:, u : u + size] = (dact * up * s * (1.0 + gate * (1.0 - s))).astype(bf16)
        du[:, u : u + size] = (dact * silu).astype(bf16)
    for write in writes[2:5]:
        write.start()
    group = max(1, TILE // span)
    for b in range(0, blocks, group):
        columns = slice(b * span, (b + group) * span)
        w_gate, w_up, w_down = (weights[b : b + group, i].reshape(group * span, units) for i in range(3))
        ffn[:, columns] = nt(act[...], w_down).astype(bf16)
        dhn_ref[:, columns] = (nt(dg[...], w_gate) + nt(du[...], w_up)).astype(bf16)
    writes[5].start()
    for write in writes:
        write.wait()


def summed(pairs):
    total = tn(*pairs[0])
    for pair in pairs[1:]:
        total = total + tn(*pair)
    return total.astype(bf16)


def down_grad_kernel(*refs):
    cot_ref, act, out_ref = refs[0], refs[1:-1], refs[-1]
    rows = act[0].shape[0]
    block = summed([(cot_ref[i * rows : (i + 1) * rows, :], a[...]) for i, a in enumerate(act)])
    out_ref[...] = block.reshape(out_ref.shape)


def wide_grad_kernel(*refs):
    out_ref = refs[-1]
    count = (len(refs) - 1) // 3
    hn, dg, du = refs[:count], refs[count : 2 * count], refs[2 * count : 3 * count]
    blocks, _, width, units = out_ref.shape
    for i, grads in enumerate((dg, du)):
        block = summed([(h[...], g[...]) for h, g in zip(hn, grads)])
        out_ref[:, i] = block.reshape(blocks, width, units)


def query_grad_kernel(count, *refs):
    xn_ref, out_ref = refs[0], refs[-1]
    datt, dq, o = (refs[1 + i * count : 1 + (i + 1) * count] for i in range(3))
    rows, width = dq[0].shape
    xn = [xn_ref[i * rows : (i + 1) * rows, :] for i in range(count)]
    out_ref[:, :width] = summed([(x, g[...]) for x, g in zip(xn, dq)])
    out_ref[:, width:] = summed([(d[...], r[...]) for d, r in zip(datt, o)])


def state_grad_kernel(count, *refs):
    xn_ref, query_ref, out_ref = refs[0], refs[-2], refs[-1]
    dk, dv, dz, bias, gain1, gain2 = (refs[1 + i * count : 1 + (i + 1) * count] for i in range(6))
    rows, width = dk[0].shape
    slots = dz[0].shape[1]
    groups, high, _ = out_ref.shape
    span = high - 16
    xn = [xn_ref[i * rows : (i + 1) * rows, :] for i in range(count)]
    for i, grads in enumerate((dk, dv)):
        block = summed([(x, g[...]) for x, g in zip(xn, grads)])
        out_ref[:, :span, (2 + i) * width : (3 + i) * width] = block.reshape(groups, span, width)
    out_ref[:, :span, : 2 * width] = query_ref[...].reshape(groups, span, 2 * width)
    forget = tn(xn[0], dz[0][...])
    for x, g in zip(xn[1:], dz[1:]):
        forget = forget + tn(x, g[...])
    pad = 128 - slots % 128

    def padded(values):
        return jnp.concatenate([values, jnp.zeros((values.shape[0], pad), f32)], 1)

    def column(parts):
        total = parts[0][...]
        for part in parts[1:]:
            total = total + part[...]
        return jnp.sum(total.T, axis=1, keepdims=True)

    small = padded(forget)
    lane = lax.broadcasted_iota(jnp.int32, small.shape, 1)
    small = jnp.where(lane == slots, column(gain2), jnp.where(lane == slots + 1, column(gain1), small))
    out_ref[:, :span, 4 * width :] = small.astype(bf16).reshape(groups, span, slots + pad)
    total = bias[0][...]
    for part in bias[1:]:
        total = total + part[...]
    total = padded(jnp.broadcast_to(jnp.sum(total, axis=0, keepdims=True), (16, slots)))
    upper = total.astype(bf16).astype(f32)
    row = lax.broadcasted_iota(jnp.int32, total.shape, 0)
    tail = jnp.where(row == 0, upper, jnp.where(row == 1, total - upper, 0.0)).astype(bf16)
    for g in range(groups):
        out_ref[g, span:, : 4 * width] = jnp.zeros((16, 4 * width), bf16)
        out_ref[g, span:, 4 * width :] = tail


def pack(ref, m, decay, state):
    high, low = halves(decay)
    lane = lax.broadcasted_iota(jnp.int32, decay.shape, 1)
    width = state.shape[1]
    ref[m, :, :width] = state.astype(bf16)
    ref[m, :, width:] = jnp.where(lane == 0, high.astype(f32), low.astype(f32)).astype(bf16)


def fold_kernel(parts, pieces, *refs):
    s_refs, d_refs, (s_out, d_out, sent) = refs[: parts * pieces], refs[parts * pieces : -3], refs[-3:]
    for m in range(parts):
        s, d = s_refs[m * pieces + pieces - 1][...], d_refs[m * pieces + pieces - 1][...]
        for t in reversed(range(pieces - 1)):
            here = d_refs[m * pieces + t][...]
            s, d = s_refs[m * pieces + t][...] + here[:, :1] * s, here * d
        s_out[m], d_out[m] = s, d
        pack(sent, m, d, s)


def hop_kernel(bit, after, first, final, parts, pieces, *refs):
    refs = list(refs)
    s_ref, d_ref, got_ref = refs[:3]
    refs = refs[3:]
    if not first:
        part_s_ref, part_d_ref = refs[:2]
        refs = refs[2:]
    early = (lax.axis_index("seq") & bit) == 0
    takes = early if after else jnp.logical_not(early)
    width = s_ref.shape[2]
    found = []
    for m in range(parts):
        tail = got_ref[m, :, width:].astype(f32)
        there_d, there_s = tail[:, :1] + tail[:, 1:2], got_ref[m, :, :width].astype(f32)
        s, d = s_ref[m], d_ref[m]
        there_wide = jnp.broadcast_to(there_d, d.shape)
        new_s = jnp.where(takes, s + d[:, :1] * there_s, there_s + there_d * s)
        if first:
            part_s, part_d = jnp.where(takes, there_s, 0.0), jnp.where(takes, there_wide, 1.0)
        else:
            part_s, part_d = part_s_ref[m], part_d_ref[m]
            part_s = jnp.where(takes, part_s + part_d[:, :1] * there_s, part_s)
            part_d = jnp.where(takes, part_d * there_wide, part_d)
        found.append((new_s, d * there_wide, part_s, part_d))
    if not final:
        s_out, d_out, part_s_out, part_d_out, sent = refs
        for m, (s, d, part_s, part_d) in enumerate(found):
            s_out[m], d_out[m], part_s_out[m], part_d_out[m] = s, d, part_s, part_d
            pack(sent, m, d, s)
        return
    *own, out = refs
    arriving = jnp.zeros_like(found[0][0])
    for m in reversed(range(parts)) if after else range(parts):
        s, d, part_s, part_d = found[m]
        enters = part_s + part_d[:, :1] * arriving
        arriving = s + d[:, :1] * arriving
        for t in reversed(range(pieces)) if after else range(1):
            out[m * pieces + t if after else m] = enters
            if after and t:
                here = m * pieces + t
                enters = own[here][...] + own[parts * pieces + here][:, :1] * enters


def in_vmem(name, kernel, operands, shapes):
    return pl.pallas_call(
        kernel,
        name=name,
        in_specs=[pl.BlockSpec(memory_space=pltpu.VMEM)] * len(operands),
        out_specs=[pl.BlockSpec(memory_space=pltpu.VMEM)] * len(shapes),
        out_shape=shapes,
        compiler_params=pltpu.CompilerParams(vmem_limit_bytes=12 * MIB),
        cost_estimate=cost(0, 6 * MIB),
    )(*operands)


def scan_states(n, state, decay, sent, after, own=(), pieces=1, tie=None, last_tie=None):
    parts, slots, width = state.shape
    part, bit, hops = [], 1, 0
    while bit < n:
        got = lax.ppermute(sent, "seq", [(i, i ^ bit) for i in range(n)])
        final = 2 * bit == n
        shapes = [shaped(state.shape, f32), shaped(decay.shape, f32)] * 2 + [shaped(sent.shape, bf16)]
        if final:
            shapes = [shaped((parts * pieces, slots, width), f32)]
        if final and last_tie is not None:
            state = behind_of(state, *last_tie)
        results = in_vmem(
            "hop",
            functools.partial(hop_kernel, bit, after, not part, final, parts, pieces),
            [state, decay, got, *part, *(own if final else ())],
            shapes,
        )
        if final:
            return results[0]
        state, decay, *part, sent = results
        if tie is not None and not hops:
            sent = tie(sent)
        bit, hops = 2 * bit, hops + 1


def behind_of(value, *first):
    return lax.optimization_barrier((value,) + first)[0]


def join_kernel(has, *refs):
    refs = iter(refs)
    piece, outer, pair, middle, total, coming = (next(refs) if h else None for h in has)
    makes = (piece is not None, pair is not None or coming is not None, total is not None)
    new_pair, new_total, done = (next(refs) if m else None for m in makes)
    me = lax.axis_index("head")
    end = (me == 0) | (me == 3)

    def each(work):
        @pl.loop(0, TILE // 32)
        def _(i):
            work(pl.ds(pl.multiple_of(i * 32, 32), 32))

    def both(a, b, rows):
        return a[rows, :] + b[rows, :]

    @pl.when(end)
    def _():
        def work(rows):
            if coming is not None:
                new_total[rows, :] = coming[rows, :]
            if done is not None:
                done[rows, :] = outer[rows, :]

        each(work)

    @pl.when(jnp.logical_not(end))
    def _():
        def work(rows):
            if piece is not None:
                new_pair[rows, :] = both(piece, outer, rows)
            if pair is not None:
                new_total[rows, :] = both(pair, middle, rows)
            if done is not None:
                done[rows, :] = total[rows, :]

        each(work)


class Line:
    INWARD, OUTWARD, MIDDLE = [(0, 1), (3, 2)], [(1, 0), (2, 3)], [(1, 2), (2, 1)]

    def __init__(self):
        self.piece = self.pair = self.payload = None
        self.returns = False

    def load(self, piece):
        self.piece = self.payload = piece

    def step(self, inputs):
        piece, pair, payload, returns = self.piece, self.pair, self.payload, self.returns
        values = [v for v in (payload, pair) if v is not None] + inputs
        values = list(lax.optimization_barrier(tuple(values)))
        outer = middle = None
        if payload is not None:
            payload = values.pop(0)
            way = (self.INWARD if piece is not None else []) + (self.OUTWARD if returns else [])
            outer = lax.ppermute(payload, "head", way)
        if pair is not None:
            pair = values.pop(0)
            middle = lax.ppermute(pair, "head", self.MIDDLE)
        self.waiting = (piece, outer, pair, middle, payload if returns else None)
        return values

    def join(self, coming=None):
        piece, outer, pair, middle, total = self.waiting
        if piece is None and total is None:
            outer = None
        operands = [piece, outer, pair, middle, total, coming]
        makes = [piece is not None, pair is not None or coming is not None, total is not None]
        arrays = [o for o in operands if o is not None]
        results = in_vmem(
            "join",
            functools.partial(join_kernel, [o is not None for o in operands]),
            arrays,
            [shaped(arrays[0].shape, bf16)] * sum(makes),
        )
        results = iter(results)
        self.pair, self.payload, done = (next(results) if m else None for m in makes)
        self.returns = pair is not None
        self.piece = coming
        return done


def on_device(tokens, gain_attn, w_query, w_key, w_value, w_forget, forget_bias, w_out, gain_ffn, w_gate, w_up, w_down,
              cotangent):
    parts, part_rows, width = tokens.shape
    rows = parts * part_rows
    head = w_query.shape[1]
    slots = w_forget.shape[1]
    units = w_gate.shape[1]
    n_seq, n_head = lax.axis_size("seq"), lax.axis_size("head")
    span = w_gate.shape[0]
    per_part = pieces = part_rows // TILE
    chunks = TILE // CHUNK
    every = [(m, t) for m in range(parts) for t in range(pieces)]

    x = tokens.reshape(rows, width)
    cot = cotangent.reshape(rows, width)
    gain1 = gain_attn.reshape(1, width)
    gain2 = gain_ffn.reshape(1, width)
    state_scratch = pltpu.VMEM((slots, 2 * head), f32)
    decay_scratch = pltpu.VMEM((slots, 128), f32)
    anywhere = pl.BlockSpec(memory_space=pl.ANY)
    in_place = pl.BlockSpec(memory_space=pltpu.VMEM)

    all_rows = lambda c: pl.BlockSpec((TILE, c), lambda i: (i, 0))
    by_part = lambda c: pl.BlockSpec((1, slots, c), lambda i: (i // per_part, 0, 0))
    forget_rows = w_forget.T
    xn, k, v, z, cum, inflow, local, decay, sent = call(
        "project",
        functools.partial(project_kernel, per_part),
        (rows // TILE,),
        [all_rows(width), fixed((1, width))] + [fixed((width, head))] * 2 + [fixed((slots, width)), fixed((1, slots))],
        [all_rows(width), all_rows(head), all_rows(head)] + [all_rows(slots)] * 3
        + [by_part(2 * head), by_part(128), by_part(2 * head + 128)],
        [shaped((rows, width), bf16)] + [shaped((rows, head), bf16)] * 2
        + [shaped((rows, slots), f32)] * 3 + [shaped((parts, slots, 2 * head), f32), shaped((parts, slots, 128), f32),
                                             shaped((parts, slots, 2 * head + 128), bf16)],
        [state_scratch, decay_scratch],
        cost=cost(2 * rows * width * (2 * head + slots), 2 * rows * width * 3 + 2 * width * 2 * head),
        loose_out=(6, 7, 8),
    )(x, gain1, w_key, w_value, forget_rows, forget_bias.reshape(1, slots))
    q = call(
        "query",
        query_kernel,
        (rows // TILE,),
        [all_rows(width), fixed((width, head))],
        all_rows(head),
        shaped((rows, head), bf16),
        cost=cost(2 * rows * width * head, 2 * rows * (width + head) + 2 * width * head),
    )(xn, w_query)
    stacked = []

    def stack_weights(sent):
        gate, down, sent = lax.optimization_barrier((w_gate, w_down, sent))
        stacked.append(jnp.stack([gate, w_up, down.T]))
        return sent

    entering = scan_states(n_seq, local, decay, sent, False, tie=stack_weights)
    full = lax.all_gather(stacked[0], "seq")

    def chunk_rows(m, t, columns, back):
        start = (m * pieces + t) * chunks
        return pl.BlockSpec((CHUNK, columns), lambda i: (start + (chunks - 1 - i if back else i), 0))

    def own_rows(columns, back):
        return pl.BlockSpec((CHUNK, columns), lambda i: (chunks - 1 - i if back else i, 0))

    def chunk_state(back):
        return pl.BlockSpec((1, slots, 2 * head), lambda i: (chunks - 1 - i if back else i, 0, 0))

    def whole(shape):
        return pl.BlockSpec(shape, lambda i: (0,) * len(shape))

    def state_of(m):
        return pl.BlockSpec((None, slots, 2 * head), lambda i: (m, 0, 0))

    states_shape = shaped((chunks, slots, 2 * head), f32)

    def read(m, t, entering, which):
        return call(
            "read",
            read_kernel,
            (chunks,),
            [chunk_rows(m, t, head, False)] * 3 + [chunk_rows(m, t, slots, False)] * 2
            + [state_of(which), fixed((head, width))],
            [own_rows(head, False), own_rows(slots, False), own_rows(slots, False), chunk_state(False),
             pl.BlockSpec((None, slots, 2 * head), lambda i: (0, 0, 0)), own_rows(width, False)],
            [shaped((TILE, head), bf16), shaped((TILE, slots), f32), shaped((TILE, slots), f32), states_shape,
             shaped((1, slots, 2 * head), f32), shaped((TILE, width), bf16)],
            [state_scratch],
            cost=cost(2 * TILE * head * (600 + width), 2 * TILE * (head * 4 + width) + 2 * head * width),
            loose=(5,),
            loose_out=(4, 5),
        )(q, k, v, cum, inflow, entering, w_out)

    def feed(m, t, attended):
        tile_count = pl.cdiv(units, TILE)
        vmem = pltpu.VMEM
        return call(
            "feed",
            functools.partial(feed_kernel, (m * pieces + t) * TILE),
            (),
            [anywhere, in_place, in_place, anywhere, anywhere],
            [anywhere] * 6 + [in_place],
            [shaped((TILE, width), bf16)] * 2 + [shaped((TILE, units), bf16)] * 3
            + [shaped((TILE, width), bf16)] * 2,
            [vmem((n_seq, 3, span, units), bf16), vmem((TILE, width), bf16), vmem((TILE, width), bf16),
             vmem((TILE, width), bf16), vmem((TILE, width), bf16)] + [vmem((TILE, units), bf16)] * 3
            + [vmem((TILE, width), bf16), pltpu.SemaphoreType.DMA((2,)), pltpu.SemaphoreType.DMA((6,)),
               pltpu.SemaphoreType.DMA((tile_count,))],
            cost=cost(12 * TILE * width * units, 6 * width * units + TILE * width * 14),
            vmem=44,
            loose=(1, 2),
            loose_out=(6,),
        )(x, attended, gain2, cot, full)

    group = max(1, TILE // span)
    columns = group * span
    def down_grads(acts):
        return call(
            "down_grads",
            down_grad_kernel,
            (width // columns // 2,),
            [pl.BlockSpec((rows, 2 * columns), lambda j: (0, j))] + [fixed((TILE, units))] * len(acts),
            pl.BlockSpec((2 * group, span, units), lambda j: (j, 0, 0)),
            shaped((n_seq, span, units), bf16),
            cost=cost(2 * rows * width * units, 2 * (rows * width + rows * units + width * units)),
        )(cot, *acts)

    def wide_grads(normed, gates, ups):
        count = len(normed)
        return call(
            "wide_grads",
            wide_grad_kernel,
            (width // columns,),
            [pl.BlockSpec((TILE, columns), lambda j: (0, j))] * count
            + [fixed((TILE, units))] * (2 * count),
            pl.BlockSpec((group, 2, span, units), lambda j: (j, 0, 0, 0)),
            shaped((n_seq, 2, span, units), bf16),
            cost=cost(4 * rows * width * units, 2 * (rows * width + 2 * rows * units + 2 * width * units)),
        )(*normed, *gates, *ups)

    def back(m, t, dhn, hidden):
        o, p, scores, e_chunks = reads[m, t][:4]
        return call(
            "back",
            back_kernel,
            (chunks,),
            [own_rows(width, True), own_rows(width, True), chunk_rows(m, t, width, True), fixed((1, width)),
             fixed((head, width))]
            + [chunk_rows(m, t, head, True)] * 3 + [chunk_rows(m, t, slots, True)] * 2 + [own_rows(slots, True)] * 2
            + [chunk_state(True)],
            [own_rows(width, True)] + [own_rows(head, True)] * 3 + [own_rows(slots, True)] * 2
            + [chunk_state(True), whole((slots, 2 * head)), whole((slots, 128)), whole((8, width))],
            [shaped((TILE, width), bf16), shaped((TILE, head), bf16),
             shaped((TILE, head), f32), shaped((TILE, head), f32), shaped((TILE, slots), f32),
             shaped((TILE, slots), f32), states_shape, shaped((slots, 2 * head), f32), shaped((slots, 128), f32),
             shaped((8, width), f32)],
            [state_scratch, decay_scratch],
            cost=cost(2 * TILE * width * head + 2 * TILE * head * 1500, TILE * width * 14 + TILE * head * 20),
            loose=(0,),
            loose_out=(7, 8),
        )(dhn, hidden, cot, gain2, w_out, q, k, v, cum, inflow, p, scores, e_chunks)

    def last(m, t, leaving, saved):
        dq, dk_local, dv_local, h_sum, x_local, g_chunks = saved
        here = m * pieces + t
        return call(
            "last",
            last_kernel,
            (chunks,),
            [state_of(here), chunk_rows(m, t, head, True), chunk_rows(m, t, head, True),
             *[chunk_rows(m, t, slots, True)] * 3, chunk_state(True), chunk_state(True), own_rows(head, True),
             own_rows(head, True), own_rows(slots, True), own_rows(slots, True), whole((TILE, head)),
             pl.BlockSpec((TILE, width), lambda i: (here, 0))] + [anywhere] * 4,
            [whole((TILE, head)), whole((TILE, head)), whole((TILE, slots)), whole((TILE, width)), whole((8, slots)),
             whole((8, width))],
            [shaped((TILE, head), bf16), shaped((TILE, head), bf16), shaped((TILE, slots), bf16),
             shaped((TILE, width), bf16), shaped((8, slots), f32), shaped((8, width), f32)],
            [state_scratch] + [pltpu.VMEM((width, head), bf16)] * 3
            + [pltpu.VMEM((slots, width), bf16), pltpu.SemaphoreType.DMA((4,))],
            cost=cost(2 * TILE * width * (3 * head + slots), TILE * width * 8 + TILE * head * 20 + width * head * 6),
            loose=(0,),
            loose_out=(3,),
        )(leaving, k, v, z, cum, inflow, reads[m, t][3], g_chunks, dk_local, dv_local, h_sum, x_local, dq, x,
          w_query, w_key, w_value, forget_rows)

    line = Line()
    live = {}

    def start():
        names = list(live)
        live.update(zip(names, line.step([live[n] for n in names])))

    def end(coming=None, done=None):
        total = line.join(coming)
        if done is not None:
            live[done] = total

    reads, backs, lasts = {}, {}, {}
    outs, in_grads = [None], [None]
    eighth = TILE // 2

    def into(name, kernel, m, t, kept, dtype, inputs, specs):
        spec = pl.BlockSpec((1, eighth, width), lambda i: (m, 2 * t + i, 0))
        old = [] if kept[0] is None else [kept[0]]
        kept[0] = call(
            name,
            kernel,
            (2,),
            specs + [anywhere] * len(old),
            spec,
            shaped(tokens.shape, dtype),
            cost=cost(0, TILE * width * 10),
            loose=(1,),
            aliases={len(specs): 0} if old else None,
        )(*inputs, *old)

    piece_spec = pl.BlockSpec((eighth, width), lambda i: (i, 0))

    def finish_out(m, t):
        into("out", out_kernel, m, t, outs, bf16, [live.pop(("hidden", m, t)), live.pop(("ffn", m, t))],
             [piece_spec, piece_spec])

    def finish_grad(m, t):
        x_rows = pl.BlockSpec((eighth, width), lambda i: (2 * (m * pieces + t) + i, 0))
        into("in_grad", in_grad_kernel, m, t, in_grads, f32, [backs[m, t][0], live.pop(("dxn", m, t)), x, gain1],
             [piece_spec, piece_spec, x_rows, pl.BlockSpec((1, width), lambda i: (0, 0))])

    def go_read(m, t):
        before = live["entering"] if t == 0 else live.pop("left")
        reads[m, t] = read(m, t, before, m if t == 0 else 0)
        if t + 1 < pieces:
            live["left"] = reads[m, t][4]
        return reads[m, t][5]

    def go_feed(m, t):
        made = feed(m, t, live.pop(("att", m, t)))
        for name, value in zip(("hidden", "hn", "act", "dgate", "dup", "ffn_part"), made):
            live[name, m, t] = value
        return made[6]

    def go_back(m, t):
        backs[m, t] = back(m, t, live.pop(("dhn", m, t)), live["hidden", m, t])
        live["back", m, t] = backs[m, t][7]

    def go_last(m, t):
        lasts[m, t] = last(m, t, live["leaving"], backs[m, t][1:7])
        live["dxn_part", m, t] = lasts[m, t][3]

    def taken(name):
        return [live.pop((name, *key)) for key in every]

    live["entering"] = entering
    line.load(go_read(0, 0))
    start()
    end(go_read(0, 1))
    start()
    end(go_read(1, 0))
    start()
    end(go_read(1, 1), ("att", 0, 0))
    live.pop("entering")
    start()
    end(go_feed(0, 0), ("att", 0, 1))
    start()
    end(go_feed(0, 1), ("att", 1, 0))
    start()
    end(go_feed(1, 0), ("att", 1, 1))
    start()
    end(go_feed(1, 1), ("dhn", 0, 0))
    start()
    live["wide_grads"] = wide_grads(taken("hn"), taken("dgate"), taken("dup"))
    end(live.pop(("ffn_part", 0, 0)), ("dhn", 0, 1))
    start()
    wide_shares = lax.psum_scatter(live.pop("wide_grads"), "seq", scatter_dimension=0)
    go_back(0, 0)
    live["down_grads"] = down_grads(taken("act"))
    end(live.pop(("ffn_part", 0, 1)), ("dhn", 1, 0))
    start()
    down_shares = lax.psum_scatter(live.pop("down_grads"), "seq", scatter_dimension=0)
    go_back(0, 1)
    go_back(1, 0)
    end(live.pop(("ffn_part", 1, 0)), ("dhn", 1, 1))
    start()
    go_back(1, 1)
    taken("back")
    own = [backs[key][7] for key in every] + [backs[key][8] for key in every]
    folded = in_vmem(
        "fold",
        functools.partial(fold_kernel, parts, pieces),
        own,
        [shaped(local.shape, f32), shaped(decay.shape, f32), shaped(sent.shape, bf16)],
    )

    xn_columns = [pl.BlockSpec((rows, TILE), lambda j: (0, j))]
    piece_columns = [pl.BlockSpec((TILE, TILE), lambda j: (0, j))] * len(every)
    piece_whole = [fixed((TILE, head))] * len(every)
    made = []

    def next_step(sent):
        live["xn"] = xn
        end(behind_of(live.pop(("ffn_part", 1, 1)), sent), ("ffn", 0, 0))
        start()
        made.append(query_gradients(live.pop("xn")))
        return sent

    query_gradients = lambda xn: call(
        "query_grads",
        functools.partial(query_grad_kernel, len(every)),
        (width // TILE,),
        xn_columns + piece_columns + piece_whole * 2,
        pl.BlockSpec((TILE, 2 * head), lambda j: (j, 0)),
        shaped((width, 2 * head), bf16),
        cost=cost(4 * rows * width * head, 4 * rows * width + 4 * rows * head + 4 * width * head),
    )(xn, *[backs[key][0] for key in every], *[backs[key][1] for key in every],
      *[reads[key][0] for key in every])
    live["leaving"] = scan_states(n_seq, *folded, True, own, pieces, next_step, made)
    live["query_grads"], live["wide"] = made[0], wide_shares
    go_last(0, 0)
    end(live.pop(("dxn_part", 0, 0)), ("ffn", 0, 1))
    start()
    wide_shares = live.pop("wide")
    go_last(0, 1)
    go_last(1, 0)
    go_last(1, 1)
    live["xn"] = xn
    end(live.pop(("dxn_part", 0, 1)), ("ffn", 1, 0))
    start()
    live.pop("leaving")
    few = [pl.BlockSpec((8, TILE), lambda j: (0, j))] * len(every)
    live["state_grads"] = call(
        "state_grads",
        functools.partial(state_grad_kernel, len(every)),
        (width // TILE,),
        xn_columns + piece_whole * 2 + [fixed((TILE, slots))] * len(every) + [fixed((8, slots))] * len(every) + few * 2
        + [pl.BlockSpec((TILE, 2 * head), lambda j: (j, 0))],
        pl.BlockSpec((group, span + 16, 4 * head + 128), lambda j: (j, 0, 0)),
        shaped((n_seq, span + 16, 4 * head + 128), bf16),
        cost=cost(4 * rows * width * head, 2 * rows * width + 4 * rows * head + 4 * width * head),
    )(live.pop("xn"), *[lasts[key][i] for i in (0, 1, 2, 4, 5) for key in every], *[backs[key][9] for key in every],
      live.pop("query_grads"))
    live["down"] = down_shares
    end(live.pop(("dxn_part", 1, 0)), ("ffn", 1, 1))
    start()
    down_shares = live.pop("down")
    attn_shares = lax.psum_scatter(live.pop("state_grads"), "seq", scatter_dimension=0)
    finish_out(0, 0)
    finish_out(0, 1)
    live["out"] = outs[0]
    end(live.pop(("dxn_part", 1, 1)), ("dxn", 0, 0))
    start()
    outs[0] = live.pop("out")
    finish_out(1, 0)
    finish_out(1, 1)
    finish_grad(0, 0)
    live["out"], live["in_grad"] = outs[0], in_grads[0]
    end(None, ("dxn", 0, 1))
    start()
    in_grads[0] = live.pop("in_grad")
    finish_grad(0, 1)
    live["in_grad"], live["attn"] = in_grads[0], attn_shares
    end(None, ("dxn", 1, 0))
    start()
    in_grads[0], late = live.pop("in_grad"), live.pop("attn").astype(f32)
    gain1_total = late[:span, 4 * head + slots + 1]
    others = [lax.ppermute(gain1_total, "head", [(i, i ^ d) for i in range(n_head)]) for d in (1, 2, 3)]
    gain1_total = (gain1_total + others[0]) + (others[1] + others[2])
    finish_grad(1, 0)
    end(None, ("dxn", 1, 1))
    finish_grad(1, 1)
    small_shares = late[:, 4 * head :]

    return (
        live["out"],
        in_grads[0],
        gain1_total,
        late[:span, :head],
        late[:span, 2 * head : 3 * head],
        late[:span, 3 * head : 4 * head],
        small_shares[:span, :slots],
        small_shares[span, :slots] + small_shares[span + 1, :slots],
        late[:span, head : 2 * head].T,
        small_shares[:span, slots],
        wide_shares[0].astype(f32),
        wide_shares[1].astype(f32),
        down_shares.astype(f32).T,
    )


def solution(mesh):
    rows, both = P(None, "seq", None), P("seq", "head")
    by_head, down = P(None, "head"), P("head", "seq")
    return jax.shard_map(
        on_device,
        mesh=mesh,
        in_specs=(rows, P(), by_head, by_head, by_head, by_head, P("head"), P("head", None), P(), both, both, down, rows),
        out_specs=(rows, rows, P("seq"), both, both, both, both, P("head"), down, P("seq"), both, both, down),
        check_vma=False,
    )
```

```python
import functools

import jax
import jax.numpy as jnp
from jax import lax
from jax.experimental import pallas as pl
from jax.experimental.pallas import tpu as pltpu
from jax.sharding import PartitionSpec as P

CHUNK = 128
TILE = 256
EPS = 1e-06
RATE = 0.5
MIB = 2**20
f32 = jnp.float32
bf16 = jnp.bfloat16
highest = lax.Precision.HIGHEST


def nn(a, b):
    return lax.dot_general(a, b, (((1,), (0,)), ((), ())), preferred_element_type=f32)


def nt(a, b):
    return lax.dot_general(a, b, (((1,), (1,)), ((), ())), preferred_element_type=f32)


def tn(a, b):
    return lax.dot_general(a, b, (((0,), (0,)), ((), ())), preferred_element_type=f32)


def exact(a, b, dims):
    return lax.dot_general(a, b, (dims, ((), ())), precision=highest, preferred_element_type=f32)


def halves(a):
    high = a.astype(bf16)
    return high, (a - high.astype(f32)).astype(bf16)


def call(name, kernel, grid, in_specs, out_specs, out_shape, scratch=(), vmem=24, cost=None, loose=(), loose_out=(),
         aliases=None):
    single = not isinstance(out_shape, list)
    shapes = [out_shape] if single else out_shape
    shapes = [s if i in loose_out else pltpu.HBM(s.shape, s.dtype) for i, s in enumerate(shapes)]
    function = pl.pallas_call(
        kernel,
        name=name,
        grid=grid,
        in_specs=in_specs,
        out_specs=out_specs,
        out_shape=shapes[0] if single else shapes,
        scratch_shapes=scratch,
        input_output_aliases=aliases or {},
        compiler_params=pltpu.CompilerParams(
            dimension_semantics=("arbitrary",) * len(grid), vmem_limit_bytes=vmem * MIB
        ),
        cost_estimate=cost,
    )

    def run(*operands):
        return function(*[
            o if i in loose or spec.memory_space == pltpu.SMEM else pltpu.with_memory_space_constraint(o, pltpu.HBM)
            for i, (o, spec) in enumerate(zip(operands, in_specs))
        ])

    return run


def cost(flops, data):
    return pl.CostEstimate(flops=int(flops), bytes_accessed=int(data), transcendentals=0)


def fixed(shape):
    zeros = (0,) * len(shape)
    return pl.BlockSpec(shape, lambda *_: zeros, pipeline_mode=pl.Buffered(1))


def shaped(shape, dtype):
    return jax.ShapeDtypeStruct(shape, dtype)


def triangle(lower):
    r = lax.broadcasted_iota(jnp.int32, (CHUNK, CHUNK), 0)
    c = lax.broadcasted_iota(jnp.int32, (CHUNK, CHUNK), 1)
    return r >= c if lower else r <= c


def gates(z):
    la = -RATE * lax.logistic(-z)
    y = -la
    taken = jnp.ones_like(y)
    for n in range(9, 1, -1):
        taken = 1.0 - y * (1.0 / n) * taken
    taken = y * taken
    cum = exact(triangle(True).astype(f32), la, ((1,), (0,)))
    return cum, jnp.exp(-cum) * taken


def turned_last(cum):
    return jnp.broadcast_to(cum[CHUNK - 1 :, :], cum.shape).T


def halves_sum(ones, values):
    high, low = halves(values)
    both = nn(ones.astype(bf16), jnp.concatenate([high, low], 1))
    width = values.shape[1]
    return both[:, :width] + both[:, width:]


def project_kernel(per_part, x_ref, gain_ref, wk_ref, wv_ref, wf_ref, bias_ref,
                   xn_ref, k_ref, v_ref, z_ref, cum_ref, in_ref, s_ref, d_ref, sent_ref, state, decay):
    @pl.when(lax.rem(pl.program_id(0), per_part) == 0)
    def _():
        state[...] = jnp.zeros_like(state)
        decay[...] = jnp.zeros_like(decay)

    x = x_ref[...].astype(f32)
    r1 = lax.rsqrt(jnp.mean(x * x, axis=-1, keepdims=True) + EPS)
    xn = (x * r1 * gain_ref[...]).astype(bf16)
    xn_ref[...] = xn
    k_ref[...] = nn(xn, wk_ref[...]).astype(bf16)
    v_ref[...] = nn(xn, wv_ref[...]).astype(bf16)
    z_ref[...] = nt(xn, wf_ref[...]) + bias_ref[...]
    width = k_ref.shape[1]
    for c in range(x_ref.shape[0] // CHUNK):
        rows = pl.ds(c * CHUNK, CHUNK)
        cum, inflow = gates(z_ref[rows, :])
        cum_ref[rows, :] = cum
        in_ref[rows, :] = inflow
        total = turned_last(cum)
        spread = inflow.astype(bf16)
        keep = jnp.exp(total[:, :1])
        state[:, :width] = keep * (state[:, :width] + tn(spread, k_ref[rows, :]))
        state[:, width:] = keep * (state[:, width:] + tn(spread, v_ref[rows, :]))
        decay[...] += total
    s_ref[0] = state[...]
    d_ref[0] = jnp.exp(decay[...])
    pack(sent_ref, 0, jnp.exp(decay[...]), state[...])


def query_kernel(xn_ref, wq_ref, q_ref):
    q_ref[...] = nn(xn_ref[...], wq_ref[...]).astype(bf16)


def read_kernel(q_ref, k_ref, v_ref, cum_ref, in_ref, e0_ref, wo_ref, o_ref, p_ref, sc_ref, e_ref, left_ref, att_ref, state):
    @pl.when(pl.program_id(0) == 0)
    def _():
        state[...] = e0_ref[...]

    width = q_ref.shape[1]
    lower = triangle(True)
    q, k, v = q_ref[...], k_ref[...], v_ref[...]
    cum, inflow = cum_ref[...], in_ref[...]
    total = turned_last(cum)
    growth = jnp.exp(cum)
    e_ref[0] = state[...]
    i_hi, i_lo = halves(inflow)
    a_hi, a_lo = halves(jnp.where(lower, nt(q, k), 0.0))
    e_hi, e_lo = halves(state[:, :width])
    scores = growth * (nt(q, e_hi) + nt(q, e_lo) + nn(a_hi, i_hi) + (nn(a_hi, i_lo) + nn(a_lo, i_hi)))
    top = jnp.exp(scores - jnp.max(scores, axis=-1, keepdims=True))
    p = top / jnp.sum(top, axis=-1, keepdims=True)
    w = (p * growth).astype(bf16)
    mixing = jnp.where(lower, nt(w, i_hi), 0.0).astype(bf16)
    o = (nn(w, state[:, width:].astype(bf16)) + nn(mixing, v)).astype(bf16)
    o_ref[...] = o
    att_ref[...] = nn(o, wo_ref[...]).astype(bf16)
    p_ref[...] = p
    sc_ref[...] = scores
    keep = jnp.exp(total[:, :1])
    state[:, :width] = keep * (state[:, :width] + tn(i_hi, k))
    state[:, width:] = keep * (state[:, width:] + tn(i_hi, v))
    left_ref[...] = state[...]


def back_kernel(dhn_ref, hid_ref, cot_ref, gain_ref, wo_ref, q_ref, k_ref, v_ref, cum_ref, in_ref, p_ref, sc_ref,
                e_ref, datt_ref, dq_ref, dkl_ref, dvl_ref, h_ref, x1_ref, g_ref, s_ref, d_ref, gg_ref, state, decay):
    step = pl.program_id(0)

    @pl.when(step == 0)
    def _():
        state[...] = jnp.zeros_like(state)
        decay[...] = jnp.zeros_like(decay)
        gg_ref[...] = jnp.zeros_like(gg_ref)

    hidden = hid_ref[...].astype(f32)
    dhn = dhn_ref[...].astype(f32)
    r2 = lax.rsqrt(jnp.mean(hidden * hidden, axis=-1, keepdims=True) + EPS)
    gg_ref[...] += jnp.sum((dhn * hidden * r2).reshape(-1, 8, hidden.shape[1]), axis=0)
    u2 = gain_ref[...] * dhn
    dhid = (
        cot_ref[...].astype(f32)
        + r2 * u2
        - hidden * (r2 * r2 * r2) * jnp.mean(u2 * hidden, axis=-1, keepdims=True)
    )
    datt = dhid.astype(bf16)
    datt_ref[...] = datt
    width = q_ref.shape[1]
    do = nt(datt, wo_ref[...]).astype(bf16)
    lower, upper = triangle(True), triangle(False)
    q, k, v = q_ref[...], k_ref[...], v_ref[...]
    cum, inflow = cum_ref[...], in_ref[...]
    total = turned_last(cum)
    growth = jnp.exp(cum)
    p = p_ref[...]
    i_hi, i_lo = halves(inflow)
    b_hi, b_lo = halves(jnp.where(lower, nt(do, v), 0.0))
    ev_hi, ev_lo = halves(e_ref[0, :, width:])
    dp = growth * (nt(do, ev_hi) + nt(do, ev_lo) + nn(b_hi, i_hi) + (nn(b_hi, i_lo) + nn(b_lo, i_hi)))
    ds = p * (dp - jnp.sum(p * dp, axis=-1, keepdims=True))
    w = (p * growth).astype(bf16)
    gds = (growth * ds).astype(bf16)
    n = jnp.where(lower, nt(gds, i_hi), 0.0).astype(bf16)
    dq_ref[...] = (nn(gds, e_ref[0, :, :width].astype(bf16)) + nn(n, k)).astype(bf16)
    n_t = jnp.where(upper, nt(i_hi, gds), 0.0).astype(bf16)
    m_t = jnp.where(upper, nt(i_hi, w), 0.0).astype(bf16)
    dkl_ref[...] = nn(n_t, q)
    dvl_ref[...] = nn(m_t, do)
    h_ref[...] = ds * sc_ref[...] + p * dp
    a_t = jnp.where(upper, nt(k, q), 0.0).astype(bf16)
    b_t = jnp.where(upper, nt(v, do), 0.0).astype(bf16)
    x1_ref[...] = nn(a_t, gds) + nn(b_t, w)
    keep = jnp.exp(total[:, :1])
    g_k, g_v = tn(gds, q), tn(w, do)
    g_ref[0, :, :width] = g_k
    g_ref[0, :, width:] = g_v
    state[:, :width] = g_k + keep * state[:, :width]
    state[:, width:] = g_v + keep * state[:, width:]
    decay[...] += total
    s_ref[...] = state[...]
    d_ref[...] = jnp.exp(decay[...])


def last_kernel(l0_ref, k_ref, v_ref, z_ref, cum_ref, in_ref, e_ref, g_ref, dkl_ref, dvl_ref, h_ref, x1_ref, dq_ref, x_ref,
                wq_ref, wk_ref, wv_ref, wf_ref, dk_ref, dv_ref, dz_ref, dxn_ref, bias_ref, gg_ref,
                state, wq, wk, wv, wf, sems):
    step, steps = pl.program_id(0), pl.num_programs(0)
    loads = [pltpu.make_async_copy(source, target, sems.at[i])
             for i, (source, target) in enumerate(((wq_ref, wq), (wk_ref, wk), (wv_ref, wv), (wf_ref, wf)))]

    @pl.when(step == 0)
    def _():
        for load in loads:
            load.start()
        state[...] = l0_ref[...]
        bias_ref[...] = jnp.zeros_like(bias_ref)

    width = k_ref.shape[1]
    k, v, z = k_ref[...], v_ref[...], z_ref[...]
    cum, inflow = cum_ref[...], in_ref[...]
    total = turned_last(cum)
    i_hi = inflow.astype(bf16)
    keep = jnp.exp(total[:, :1])
    lg = keep * state[...]
    lg_k, lg_v = lg[:, :width].astype(bf16), lg[:, width:].astype(bf16)
    rows = pl.ds(pl.multiple_of((steps - 1 - step) * CHUNK, CHUNK), CHUNK)
    dk_ref[rows, :] = (dkl_ref[...] + nn(i_hi, lg_k)).astype(bf16)
    dv_ref[rows, :] = (dvl_ref[...] + nn(i_hi, lg_v)).astype(bf16)
    x1 = x1_ref[...]
    x2 = nt(k, lg_k) + nt(v, lg_v)
    met = jnp.broadcast_to(jnp.sum(lg * e_ref[0], axis=1, keepdims=True), (lg.shape[0], CHUNK)).T
    h, r1 = h_ref[...], inflow * x1
    dla = (
        halves_sum(triangle(False), h - r1)
        + r1
        + halves_sum(triangle(True), inflow * x2)
        + met
        - jnp.exp(-cum) * (x1 + x2)
    )
    rate = lax.logistic(-z)
    dz = (dla * RATE * rate * (1.0 - rate)).astype(bf16)
    dz_ref[rows, :] = dz
    bias_ref[...] += jnp.sum(dz.astype(f32).reshape(-1, 8, dz.shape[1]), axis=0)
    state[...] = g_ref[0] + lg

    @pl.when(step == steps - 1)
    def _():
        for load in loads:
            load.wait()
        dxn = nt(dq_ref[...], wq[...]) + nt(dk_ref[...], wk[...]) + nt(dv_ref[...], wv[...]) + nn(dz_ref[...], wf[...])
        dxn_ref[...] = dxn.astype(bf16)
        x = x_ref[...].astype(f32)
        r1 = lax.rsqrt(jnp.mean(x * x, axis=-1, keepdims=True) + EPS)
        gg_ref[...] = jnp.sum((dxn * x * r1).reshape(-1, 8, x.shape[1]), axis=0)


def out_kernel(hid_ref, ffn_ref, *refs):
    refs[-1][0] = (hid_ref[...].astype(f32) + ffn_ref[...].astype(f32)).astype(bf16)


def in_grad_kernel(dhid_ref, dxn_ref, x_ref, gain_ref, *refs):
    x = x_ref[...].astype(f32)
    r1 = lax.rsqrt(jnp.mean(x * x, axis=-1, keepdims=True) + EPS)
    u1 = gain_ref[...] * dxn_ref[...].astype(f32)
    refs[-1][0] = dhid_ref[...].astype(f32) + r1 * u1 - x * (r1 * r1 * r1) * jnp.mean(u1 * x, axis=-1, keepdims=True)


def feed_kernel(first_row, x_ref, att_ref, gain_ref, cot_ref, full_ref, hid_ref, hn_ref, act_ref, dg_ref, du_ref,
                ffn_ref, dhn_ref, weights, x, cot, hid, hn, act, dg, du, ffn, in_sems, out_sems, weight_sems):
    rows, width = x.shape
    units = act.shape[1]
    blocks, _, span, _ = weights.shape
    tiles = [(u, min(TILE, units - u)) for u in range(0, units, TILE)]
    here = pl.ds(first_row, rows)
    reads = [pltpu.make_async_copy(source.at[here, :], target, in_sems.at[i])
             for i, (source, target) in enumerate(((x_ref, x), (cot_ref, cot)))]
    loads = [pltpu.make_async_copy(full_ref.at[:, :, :, pl.ds(u, size)], weights.at[:, :, :, pl.ds(u, size)],
                                   weight_sems.at[i]) for i, (u, size) in enumerate(tiles)]
    writes = [pltpu.make_async_copy(source, target, out_sems.at[i])
              for i, (source, target) in enumerate(
                  ((hid, hid_ref), (hn, hn_ref), (act, act_ref), (dg, dg_ref), (du, du_ref), (ffn, ffn_ref)))]
    for copy in reads + loads:
        copy.start()
    for copy in reads:
        copy.wait()
    hidden = x[...].astype(f32) + att_ref[...].astype(f32)
    hid[...] = hidden.astype(bf16)
    r2 = lax.rsqrt(jnp.mean(hidden * hidden, axis=-1, keepdims=True) + EPS)
    hn[...] = (hidden * r2 * gain_ref[...]).astype(bf16)
    writes[0].start()
    writes[1].start()
    for (u, size), load in zip(tiles, loads):
        load.wait()
        gate, up, dact = (
            nn(left[...], weights[:, i, :, u : u + size].reshape(width, size))
            for i, left in enumerate((hn, hn, cot))
        )
        s = lax.logistic(gate)
        silu = gate * s
        act[:, u : u + size] = (silu * up).astype(bf16)
        dg[:, u : u + size] = (dact * up * s * (1.0 + gate * (1.0 - s))).astype(bf16)
        du[:, u : u + size] = (dact * silu).astype(bf16)
    for write in writes[2:5]:
        write.start()
    group = max(1, TILE // span)
    for b in range(0, blocks, group):
        columns = slice(b * span, (b + group) * span)
        w_gate, w_up, w_down = (weights[b : b + group, i].reshape(group * span, units) for i in range(3))
        ffn[:, columns] = nt(act[...], w_down).astype(bf16)
        dhn_ref[:, columns] = (nt(dg[...], w_gate) + nt(du[...], w_up)).astype(bf16)
    writes[5].start()
    for write in writes:
        write.wait()


def summed(pairs):
    total = tn(*pairs[0])
    for pair in pairs[1:]:
        total = total + tn(*pair)
    return total.astype(bf16)


def down_grad_kernel(*refs):
    cot_ref, act, out_ref = refs[0], refs[1:-1], refs[-1]
    rows = act[0].shape[0]
    block = summed([(cot_ref[i * rows : (i + 1) * rows, :], a[...]) for i, a in enumerate(act)])
    out_ref[...] = block.reshape(out_ref.shape)


def wide_grad_kernel(*refs):
    out_ref = refs[-1]
    count = (len(refs) - 1) // 3
    hn, dg, du = refs[:count], refs[count : 2 * count], refs[2 * count : 3 * count]
    blocks, _, width, units = out_ref.shape
    for i, grads in enumerate((dg, du)):
        block = summed([(h[...], g[...]) for h, g in zip(hn, grads)])
        out_ref[:, i] = block.reshape(blocks, width, units)


def query_grad_kernel(count, first_column, *refs):
    xn_ref, out_ref, block, sems = refs[0], refs[-3], refs[-2], refs[-1]
    datt, dq, o = (refs[1 + i * count : 1 + (i + 1) * count] for i in range(3))
    rows, width = dq[0].shape
    _, groups, span, columns = block.shape
    step, steps = pl.program_id(0), pl.num_programs(0)

    def copy(at):
        slot = lax.rem(at, 2)
        return pltpu.make_async_copy(
            block.at[slot], out_ref.at[pl.ds(at * groups, groups), :, pl.ds(first_column, columns)], sems.at[slot]
        )

    @pl.when(step >= 2)
    def _():
        copy(step - 2).wait()

    xn = [xn_ref[i * rows : (i + 1) * rows, :] for i in range(count)]
    slot = lax.rem(step, 2)
    query = summed([(x, g[...]) for x, g in zip(xn, dq)])
    block[slot, :, :, :width] = query.reshape(groups, span, width)
    output = summed([(d[...], r[...]) for d, r in zip(datt, o)])
    block[slot, :, :, width:] = output.reshape(groups, span, width)
    copy(step).start()

    @pl.when(step == steps - 1)
    def _():
        copy(step - 1).wait()
        copy(step).wait()


def state_grad_kernel(count, *refs):
    xn_ref, out_ref = refs[0], refs[-1]
    dk, dv, dz, bias, gain1, gain2 = (refs[1 + i * count : 1 + (i + 1) * count] for i in range(6))
    rows, width = dk[0].shape
    slots = dz[0].shape[1]
    groups, high, _ = out_ref.shape
    span = high - 16
    xn = [xn_ref[i * rows : (i + 1) * rows, :] for i in range(count)]
    for i, grads in enumerate((dk, dv)):
        block = summed([(x, g[...]) for x, g in zip(xn, grads)])
        out_ref[:, :span, i * width : (i + 1) * width] = block.reshape(groups, span, width)
    forget = tn(xn[0], dz[0][...])
    for x, g in zip(xn[1:], dz[1:]):
        forget = forget + tn(x, g[...])
    pad = 128 - slots % 128

    def padded(values):
        return jnp.concatenate([values, jnp.zeros((values.shape[0], pad), f32)], 1)

    def column(parts):
        total = parts[0][...]
        for part in parts[1:]:
            total = total + part[...]
        return jnp.sum(total.T, axis=1, keepdims=True)

    small = padded(forget)
    lane = lax.broadcasted_iota(jnp.int32, small.shape, 1)
    small = jnp.where(lane == slots, column(gain2), jnp.where(lane == slots + 1, column(gain1), small))
    out_ref[:, :span, 2 * width :] = small.astype(bf16).reshape(groups, span, slots + pad)
    total = bias[0][...]
    for part in bias[1:]:
        total = total + part[...]
    total = padded(jnp.broadcast_to(jnp.sum(total, axis=0, keepdims=True), (16, slots)))
    upper = total.astype(bf16).astype(f32)
    row = lax.broadcasted_iota(jnp.int32, total.shape, 0)
    tail = jnp.where(row == 0, upper, jnp.where(row == 1, total - upper, 0.0)).astype(bf16)
    for g in range(groups):
        out_ref[g, span:, : 2 * width] = jnp.zeros((16, 2 * width), bf16)
        out_ref[g, span:, 2 * width :] = tail


def pack(ref, m, decay, state):
    high, low = halves(decay)
    lane = lax.broadcasted_iota(jnp.int32, decay.shape, 1)
    width = state.shape[1]
    ref[m, :, :width] = state.astype(bf16)
    ref[m, :, width:] = jnp.where(lane == 0, high.astype(f32), low.astype(f32)).astype(bf16)


def fold_kernel(parts, pieces, *refs):
    s_refs, d_refs, (s_out, d_out, sent) = refs[: parts * pieces], refs[parts * pieces : -3], refs[-3:]
    for m in range(parts):
        s, d = s_refs[m * pieces + pieces - 1][...], d_refs[m * pieces + pieces - 1][...]
        for t in reversed(range(pieces - 1)):
            here = d_refs[m * pieces + t][...]
            s, d = s_refs[m * pieces + t][...] + here[:, :1] * s, here * d
        s_out[m], d_out[m] = s, d
        pack(sent, m, d, s)


def hop_kernel(bit, after, first, final, parts, pieces, *refs):
    refs = list(refs)
    s_ref, d_ref, got_ref = refs[:3]
    refs = refs[3:]
    if not first:
        part_s_ref, part_d_ref = refs[:2]
        refs = refs[2:]
    early = (lax.axis_index("seq") & bit) == 0
    takes = early if after else jnp.logical_not(early)
    width = s_ref.shape[2]
    found = []
    for m in range(parts):
        tail = got_ref[m, :, width:].astype(f32)
        there_d, there_s = tail[:, :1] + tail[:, 1:2], got_ref[m, :, :width].astype(f32)
        s, d = s_ref[m], d_ref[m]
        there_wide = jnp.broadcast_to(there_d, d.shape)
        new_s = jnp.where(takes, s + d[:, :1] * there_s, there_s + there_d * s)
        if first:
            part_s, part_d = jnp.where(takes, there_s, 0.0), jnp.where(takes, there_wide, 1.0)
        else:
            part_s, part_d = part_s_ref[m], part_d_ref[m]
            part_s = jnp.where(takes, part_s + part_d[:, :1] * there_s, part_s)
            part_d = jnp.where(takes, part_d * there_wide, part_d)
        found.append((new_s, d * there_wide, part_s, part_d))
    if not final:
        s_out, d_out, part_s_out, part_d_out, sent = refs
        for m, (s, d, part_s, part_d) in enumerate(found):
            s_out[m], d_out[m], part_s_out[m], part_d_out[m] = s, d, part_s, part_d
            pack(sent, m, d, s)
        return
    *own, out = refs
    arriving = jnp.zeros_like(found[0][0])
    for m in reversed(range(parts)) if after else range(parts):
        s, d, part_s, part_d = found[m]
        enters = part_s + part_d[:, :1] * arriving
        arriving = s + d[:, :1] * arriving
        for t in reversed(range(pieces)) if after else range(1):
            out[m * pieces + t if after else m] = enters
            if after and t:
                here = m * pieces + t
                enters = own[here][...] + own[parts * pieces + here][:, :1] * enters


def in_vmem(name, kernel, operands, shapes):
    return pl.pallas_call(
        kernel,
        name=name,
        in_specs=[pl.BlockSpec(memory_space=pltpu.VMEM)] * len(operands),
        out_specs=[pl.BlockSpec(memory_space=pltpu.VMEM)] * len(shapes),
        out_shape=shapes,
        compiler_params=pltpu.CompilerParams(vmem_limit_bytes=12 * MIB),
        cost_estimate=cost(0, 6 * MIB),
    )(*operands)


def scan_states(n, state, decay, sent, after, own=(), pieces=1, ties=()):
    parts, slots, width = state.shape
    part, bit, hops = [], 1, 0
    while bit < n:
        got = lax.ppermute(sent, "seq", [(i, i ^ bit) for i in range(n)])
        final = 2 * bit == n
        shapes = [shaped(state.shape, f32), shaped(decay.shape, f32)] * 2 + [shaped(sent.shape, bf16)]
        if final:
            shapes = [shaped((parts * pieces, slots, width), f32)]
        if hops < len(ties) and ties[hops] is not None:
            state = ties[hops](state, got)
        results = in_vmem(
            "hop",
            functools.partial(hop_kernel, bit, after, not part, final, parts, pieces),
            [state, decay, got, *part, *(own if final else ())],
            shapes,
        )
        if final:
            return results[0]
        state, decay, *part, sent = results
        bit, hops = 2 * bit, hops + 1


def behind_of(value, *first):
    return lax.optimization_barrier((value,) + first)[0]


def join_kernel(has, *refs):
    refs = iter(refs)
    piece, outer, pair, middle, total, coming = (next(refs) if h else None for h in has)
    makes = (piece is not None, pair is not None or coming is not None, total is not None)
    new_pair, new_total, done = (next(refs) if m else None for m in makes)
    me = lax.axis_index("head")
    end = (me == 0) | (me == 3)

    def each(work):
        @pl.loop(0, TILE // 32)
        def _(i):
            work(pl.ds(pl.multiple_of(i * 32, 32), 32))

    def both(a, b, rows):
        return a[rows, :] + b[rows, :]

    @pl.when(end)
    def _():
        def work(rows):
            if coming is not None:
                new_total[rows, :] = coming[rows, :]
            if done is not None:
                done[rows, :] = outer[rows, :]

        each(work)

    @pl.when(jnp.logical_not(end))
    def _():
        def work(rows):
            if piece is not None:
                new_pair[rows, :] = both(piece, outer, rows)
            if pair is not None:
                new_total[rows, :] = both(pair, middle, rows)
            if done is not None:
                done[rows, :] = total[rows, :]

        each(work)


class Line:
    INWARD, OUTWARD, MIDDLE = [(0, 1), (3, 2)], [(1, 0), (2, 3)], [(1, 2), (2, 1)]

    def __init__(self):
        self.piece = self.pair = self.payload = None
        self.returns = False

    def load(self, piece):
        self.piece = self.payload = piece

    def step(self, inputs):
        piece, pair, payload, returns = self.piece, self.pair, self.payload, self.returns
        values = [v for v in (payload, pair) if v is not None] + inputs
        values = list(lax.optimization_barrier(tuple(values)))
        outer = middle = None
        if payload is not None:
            payload = values.pop(0)
            way = (self.INWARD if piece is not None else []) + (self.OUTWARD if returns else [])
            outer = lax.ppermute(payload, "head", way)
        if pair is not None:
            pair = values.pop(0)
            middle = lax.ppermute(pair, "head", self.MIDDLE)
        self.waiting = (piece, outer, pair, middle, payload if returns else None)
        return values

    def join(self, coming=None, after=()):
        piece, outer, pair, middle, total = self.waiting
        if after:
            outer = behind_of(outer, *after)
        if piece is None and total is None:
            outer = None
        operands = [piece, outer, pair, middle, total, coming]
        makes = [piece is not None, pair is not None or coming is not None, total is not None]
        arrays = [o for o in operands if o is not None]
        results = in_vmem(
            "join",
            functools.partial(join_kernel, [o is not None for o in operands]),
            arrays,
            [shaped(arrays[0].shape, bf16)] * sum(makes),
        )
        results = iter(results)
        self.pair, self.payload, done = (next(results) if m else None for m in makes)
        self.returns = pair is not None
        self.piece = coming
        return done


def on_device(tokens, gain_attn, w_query, w_key, w_value, w_forget, forget_bias, w_out, gain_ffn, w_gate, w_up, w_down,
              cotangent):
    parts, part_rows, width = tokens.shape
    rows = parts * part_rows
    head = w_query.shape[1]
    slots = w_forget.shape[1]
    units = w_gate.shape[1]
    n_seq, n_head = lax.axis_size("seq"), lax.axis_size("head")
    span = w_gate.shape[0]
    per_part = pieces = part_rows // TILE
    chunks = TILE // CHUNK
    every = [(m, t) for m in range(parts) for t in range(pieces)]

    x = tokens.reshape(rows, width)
    cot = cotangent.reshape(rows, width)
    gain1 = gain_attn.reshape(1, width)
    gain2 = gain_ffn.reshape(1, width)
    state_scratch = pltpu.VMEM((slots, 2 * head), f32)
    decay_scratch = pltpu.VMEM((slots, 128), f32)
    anywhere = pl.BlockSpec(memory_space=pl.ANY)
    in_place = pl.BlockSpec(memory_space=pltpu.VMEM)

    all_rows = lambda c: pl.BlockSpec((TILE, c), lambda i: (i, 0))
    by_part = lambda c: pl.BlockSpec((1, slots, c), lambda i: (i // per_part, 0, 0))
    forget_rows = w_forget.T
    xn, k, v, z, cum, inflow, local, decay, sent = call(
        "project",
        functools.partial(project_kernel, per_part),
        (rows // TILE,),
        [all_rows(width), fixed((1, width))] + [fixed((width, head))] * 2 + [fixed((slots, width)), fixed((1, slots))],
        [all_rows(width), all_rows(head), all_rows(head)] + [all_rows(slots)] * 3
        + [by_part(2 * head), by_part(128), by_part(2 * head + 128)],
        [shaped((rows, width), bf16)] + [shaped((rows, head), bf16)] * 2
        + [shaped((rows, slots), f32)] * 3 + [shaped((parts, slots, 2 * head), f32), shaped((parts, slots, 128), f32),
                                             shaped((parts, slots, 2 * head + 128), bf16)],
        [state_scratch, decay_scratch],
        cost=cost(2 * rows * width * (2 * head + slots), 2 * rows * width * 3 + 2 * width * 2 * head),
        loose_out=(6, 7, 8),
    )(x, gain1, w_key, w_value, forget_rows, forget_bias.reshape(1, slots))
    q = call(
        "query",
        query_kernel,
        (rows // TILE,),
        [all_rows(width), fixed((width, head))],
        all_rows(head),
        shaped((rows, head), bf16),
        cost=cost(2 * rows * width * head, 2 * rows * (width + head) + 2 * width * head),
    )(xn, w_query)
    stacked = []

    def stack_weights(state, got):
        gate, down, _ = lax.optimization_barrier((w_gate, w_down, got))
        stacked.append(jnp.stack([gate, w_up, down.T]))
        return state

    entering = scan_states(n_seq, local, decay, sent, False, ties=[stack_weights])
    full = lax.all_gather(stacked[0], "seq")

    def chunk_rows(m, t, columns, back):
        start = (m * pieces + t) * chunks
        return pl.BlockSpec((CHUNK, columns), lambda i: (start + (chunks - 1 - i if back else i), 0))

    def own_rows(columns, back):
        return pl.BlockSpec((CHUNK, columns), lambda i: (chunks - 1 - i if back else i, 0))

    def chunk_state(back):
        return pl.BlockSpec((1, slots, 2 * head), lambda i: (chunks - 1 - i if back else i, 0, 0))

    def whole(shape):
        return pl.BlockSpec(shape, lambda i: (0,) * len(shape))

    def state_of(m):
        return pl.BlockSpec((None, slots, 2 * head), lambda i: (m, 0, 0))

    states_shape = shaped((chunks, slots, 2 * head), f32)

    def read(m, t, entering, which):
        return call(
            "read",
            read_kernel,
            (chunks,),
            [chunk_rows(m, t, head, False)] * 3 + [chunk_rows(m, t, slots, False)] * 2
            + [state_of(which), fixed((head, width))],
            [own_rows(head, False), own_rows(slots, False), own_rows(slots, False), chunk_state(False),
             pl.BlockSpec((None, slots, 2 * head), lambda i: (0, 0, 0)), own_rows(width, False)],
            [shaped((TILE, head), bf16), shaped((TILE, slots), f32), shaped((TILE, slots), f32), states_shape,
             shaped((1, slots, 2 * head), f32), shaped((TILE, width), bf16)],
            [state_scratch],
            cost=cost(2 * TILE * head * (600 + width), 2 * TILE * (head * 4 + width) + 2 * head * width),
            loose=(5,),
            loose_out=(4, 5),
        )(q, k, v, cum, inflow, entering, w_out)

    def feed(m, t, attended):
        tile_count = pl.cdiv(units, TILE)
        vmem = pltpu.VMEM
        return call(
            "feed",
            functools.partial(feed_kernel, (m * pieces + t) * TILE),
            (),
            [anywhere, in_place, in_place, anywhere, anywhere],
            [anywhere] * 6 + [in_place],
            [shaped((TILE, width), bf16)] * 2 + [shaped((TILE, units), bf16)] * 3
            + [shaped((TILE, width), bf16)] * 2,
            [vmem((n_seq, 3, span, units), bf16), vmem((TILE, width), bf16), vmem((TILE, width), bf16),
             vmem((TILE, width), bf16), vmem((TILE, width), bf16)] + [vmem((TILE, units), bf16)] * 3
            + [vmem((TILE, width), bf16), pltpu.SemaphoreType.DMA((2,)), pltpu.SemaphoreType.DMA((6,)),
               pltpu.SemaphoreType.DMA((tile_count,))],
            cost=cost(12 * TILE * width * units, 6 * width * units + TILE * width * 14),
            vmem=44,
            loose=(1, 2),
            loose_out=(6,),
        )(x, attended, gain2, cot, full)

    group = max(1, TILE // span)
    columns = group * span
    def down_grads(acts):
        return call(
            "down_grads",
            down_grad_kernel,
            (width // columns // 2,),
            [pl.BlockSpec((rows, 2 * columns), lambda j: (0, j))] + [fixed((TILE, units))] * len(acts),
            pl.BlockSpec((2 * group, span, units), lambda j: (j, 0, 0)),
            shaped((n_seq, span, units + 2 * head), bf16),
            cost=cost(2 * rows * width * units, 2 * (rows * width + rows * units + width * units)),
        )(cot, *acts)

    def wide_grads(normed, gates, ups):
        count = len(normed)
        return call(
            "wide_grads",
            wide_grad_kernel,
            (width // columns,),
            [pl.BlockSpec((TILE, columns), lambda j: (0, j))] * count
            + [fixed((TILE, units))] * (2 * count),
            pl.BlockSpec((group, 2, span, units), lambda j: (j, 0, 0, 0)),
            shaped((n_seq, 2, span, units), bf16),
            cost=cost(4 * rows * width * units, 2 * (rows * width + 2 * rows * units + 2 * width * units)),
        )(*normed, *gates, *ups)

    def back(m, t, dhn, hidden):
        o, p, scores, e_chunks = reads[m, t][:4]
        return call(
            "back",
            back_kernel,
            (chunks,),
            [own_rows(width, True), own_rows(width, True), chunk_rows(m, t, width, True), fixed((1, width)),
             fixed((head, width))]
            + [chunk_rows(m, t, head, True)] * 3 + [chunk_rows(m, t, slots, True)] * 2 + [own_rows(slots, True)] * 2
            + [chunk_state(True)],
            [own_rows(width, True)] + [own_rows(head, True)] * 3 + [own_rows(slots, True)] * 2
            + [chunk_state(True), whole((slots, 2 * head)), whole((slots, 128)), whole((8, width))],
            [shaped((TILE, width), bf16), shaped((TILE, head), bf16),
             shaped((TILE, head), f32), shaped((TILE, head), f32), shaped((TILE, slots), f32),
             shaped((TILE, slots), f32), states_shape, shaped((slots, 2 * head), f32), shaped((slots, 128), f32),
             shaped((8, width), f32)],
            [state_scratch, decay_scratch],
            cost=cost(2 * TILE * width * head + 2 * TILE * head * 1500, TILE * width * 14 + TILE * head * 20),
            loose=(0,),
            loose_out=(7, 8),
        )(dhn, hidden, cot, gain2, w_out, q, k, v, cum, inflow, p, scores, e_chunks)

    def last(m, t, leaving, saved):
        dq, dk_local, dv_local, h_sum, x_local, g_chunks = saved
        here = m * pieces + t
        return call(
            "last",
            last_kernel,
            (chunks,),
            [state_of(here), chunk_rows(m, t, head, True), chunk_rows(m, t, head, True),
             *[chunk_rows(m, t, slots, True)] * 3, chunk_state(True), chunk_state(True), own_rows(head, True),
             own_rows(head, True), own_rows(slots, True), own_rows(slots, True), whole((TILE, head)),
             pl.BlockSpec((TILE, width), lambda i: (here, 0))] + [anywhere] * 4,
            [whole((TILE, head)), whole((TILE, head)), whole((TILE, slots)), whole((TILE, width)), whole((8, slots)),
             whole((8, width))],
            [shaped((TILE, head), bf16), shaped((TILE, head), bf16), shaped((TILE, slots), bf16),
             shaped((TILE, width), bf16), shaped((8, slots), f32), shaped((8, width), f32)],
            [state_scratch] + [pltpu.VMEM((width, head), bf16)] * 3
            + [pltpu.VMEM((slots, width), bf16), pltpu.SemaphoreType.DMA((4,))],
            cost=cost(2 * TILE * width * (3 * head + slots), TILE * width * 8 + TILE * head * 20 + width * head * 6),
            loose=(0,),
            loose_out=(3,),
        )(leaving, k, v, z, cum, inflow, reads[m, t][3], g_chunks, dk_local, dv_local, h_sum, x_local, dq, x,
          w_query, w_key, w_value, forget_rows)

    line = Line()
    live = {}

    def start():
        names = list(live)
        live.update(zip(names, line.step([live[n] for n in names])))

    def end(coming=None, done=None, after=()):
        total = line.join(coming, after)
        if done is not None:
            live[done] = total

    reads, backs, lasts = {}, {}, {}
    outs, in_grads = [None], [None]
    eighth = TILE // 2

    def into(name, kernel, m, t, kept, dtype, inputs, specs):
        spec = pl.BlockSpec((1, eighth, width), lambda i: (m, 2 * t + i, 0))
        old = [] if kept[0] is None else [kept[0]]
        kept[0] = call(
            name,
            kernel,
            (2,),
            specs + [anywhere] * len(old),
            spec,
            shaped(tokens.shape, dtype),
            cost=cost(0, TILE * width * 10),
            loose=(1,),
            aliases={len(specs): 0} if old else None,
        )(*inputs, *old)

    piece_spec = pl.BlockSpec((eighth, width), lambda i: (i, 0))

    def finish_out(m, t):
        into("out", out_kernel, m, t, outs, bf16, [live.pop(("hidden", m, t)), live.pop(("ffn", m, t))],
             [piece_spec, piece_spec])

    def finish_grad(m, t):
        x_rows = pl.BlockSpec((eighth, width), lambda i: (2 * (m * pieces + t) + i, 0))
        into("in_grad", in_grad_kernel, m, t, in_grads, f32, [backs[m, t][0], live.pop(("dxn", m, t)), x, gain1],
             [piece_spec, piece_spec, x_rows, pl.BlockSpec((1, width), lambda i: (0, 0))])

    def go_read(m, t):
        before = live["entering"] if t == 0 else live.pop("left")
        reads[m, t] = read(m, t, before, m if t == 0 else 0)
        if t + 1 < pieces:
            live["left"] = reads[m, t][4]
        return reads[m, t][5]

    def go_feed(m, t):
        made = feed(m, t, live.pop(("att", m, t)))
        for name, value in zip(("hidden", "hn", "act", "dgate", "dup", "ffn_part"), made):
            live[name, m, t] = value
        return made[6]

    def go_back(m, t):
        backs[m, t] = back(m, t, live.pop(("dhn", m, t)), live["hidden", m, t])
        live["back", m, t] = backs[m, t][7]

    def go_last(m, t):
        lasts[m, t] = last(m, t, live["leaving"], backs[m, t][1:7])
        live["dxn_part", m, t] = lasts[m, t][3]

    def taken(name):
        return [live.pop((name, *key)) for key in every]

    live["entering"] = entering
    line.load(go_read(0, 0))
    start()
    end(go_read(0, 1))
    start()
    end(go_read(1, 0))
    start()
    end(go_read(1, 1), ("att", 0, 0))
    live.pop("entering")
    start()
    end(go_feed(0, 0), ("att", 0, 1))
    start()
    end(go_feed(0, 1), ("att", 1, 0))
    start()
    end(go_feed(1, 0), ("att", 1, 1))
    start()
    end(go_feed(1, 1), ("dhn", 0, 0))
    start()
    live["wide_grads"] = wide_grads(taken("hn"), taken("dgate"), taken("dup"))
    end(live.pop(("ffn_part", 0, 0)), ("dhn", 0, 1))
    start()
    wide_shares = lax.psum_scatter(live.pop("wide_grads"), "seq", scatter_dimension=0)
    go_back(0, 0)
    go_back(0, 1)
    end(live.pop(("ffn_part", 0, 1)), ("dhn", 1, 0))
    start()
    go_back(1, 0)
    end(live.pop(("ffn_part", 1, 0)), ("dhn", 1, 1))
    start()
    go_back(1, 1)
    taken("back")
    own = [backs[key][7] for key in every] + [backs[key][8] for key in every]
    folded = in_vmem(
        "fold",
        functools.partial(fold_kernel, parts, pieces),
        own,
        [shaped(local.shape, f32), shaped(decay.shape, f32), shaped(sent.shape, bf16)],
    )

    xn_columns = [pl.BlockSpec((rows, TILE), lambda j: (0, j))]
    piece_columns = [pl.BlockSpec((TILE, TILE), lambda j: (0, j))] * len(every)
    piece_whole = [fixed((TILE, head))] * len(every)
    made = []

    def beside_first(state, got):
        live["xn"] = xn
        end(behind_of(live.pop(("ffn_part", 1, 1)), got), ("ffn", 0, 0))
        start()
        made.append(live.pop("xn"))
        return state

    def beside_second(state, got):
        acts = taken("act")
        acts[0] = behind_of(acts[0], state)
        made.append(down_grads(acts))
        return behind_of(state, made[1])

    def beside_third(state, got):
        grads = call(
            "query_grads",
            functools.partial(query_grad_kernel, len(every), units),
            (width // columns,),
            xn_columns + piece_columns + piece_whole * 2 + [anywhere],
            anywhere,
            shaped((n_seq, span, units + 2 * head), bf16),
            [pltpu.VMEM((2, group, span, 2 * head), bf16), pltpu.SemaphoreType.DMA((2,))],
            cost=cost(4 * rows * width * head, 4 * rows * width + 4 * rows * head + 4 * width * head),
            aliases={1 + 3 * len(every): 0},
        )(behind_of(made[0], state), *[backs[key][0] for key in every], *[backs[key][1] for key in every],
          *[reads[key][0] for key in every], made[1])
        made.append(grads)
        return behind_of(state, grads)

    ties = [beside_first, beside_second, beside_third]
    live["leaving"] = scan_states(n_seq, *folded, True, own, pieces, ties)
    live["query_grads"], live["wide"] = made[2], wide_shares
    go_last(0, 0)
    end(live.pop(("dxn_part", 0, 0)), ("ffn", 0, 1))
    start()
    wide_shares = live.pop("wide")
    down_shares = lax.psum_scatter(live.pop("query_grads"), "seq", scatter_dimension=0)
    go_last(0, 1)
    go_last(1, 0)
    go_last(1, 1)
    live["xn"] = xn
    end(live.pop(("dxn_part", 0, 1)), ("ffn", 1, 0))
    start()
    live.pop("leaving")
    few = [pl.BlockSpec((8, TILE), lambda j: (0, j))] * len(every)
    live["state_grads"] = call(
        "state_grads",
        functools.partial(state_grad_kernel, len(every)),
        (width // TILE,),
        xn_columns + piece_whole * 2 + [fixed((TILE, slots))] * len(every) + [fixed((8, slots))] * len(every) + few * 2,
        pl.BlockSpec((group, span + 16, 2 * head + 128), lambda j: (j, 0, 0)),
        shaped((n_seq, span + 16, 2 * head + 128), bf16),
        cost=cost(4 * rows * width * head, 2 * rows * width + 4 * rows * head + 4 * width * head),
    )(live.pop("xn"), *[lasts[key][i] for i in (0, 1, 2, 4, 5) for key in every], *[backs[key][9] for key in every])
    end(live.pop(("dxn_part", 1, 0)), ("ffn", 1, 1))
    start()
    attn_shares = lax.psum_scatter(live.pop("state_grads"), "seq", scatter_dimension=0)
    finish_out(0, 0)
    finish_out(0, 1)
    live["out"], live["down"] = outs[0], down_shares
    end(live.pop(("dxn_part", 1, 1)), ("dxn", 0, 0))
    start()
    outs[0], down_shares = live.pop("out"), live.pop("down")
    finish_out(1, 0)
    finish_out(1, 1)
    finish_grad(0, 0)
    live["out"], live["in_grad"] = outs[0], in_grads[0]
    end(None, ("dxn", 0, 1))
    start()
    in_grads[0] = live.pop("in_grad")
    finish_grad(0, 1)
    live["in_grad"] = in_grads[0]
    end(None, ("dxn", 1, 0))
    start()
    in_grads[0] = live.pop("in_grad")
    late = behind_of(attn_shares, in_grads[0]).astype(f32)
    gain1_total = late[:span, 2 * head + slots + 1]
    others = [lax.ppermute(gain1_total, "head", [(i, i ^ d) for i in range(n_head)]) for d in (1, 2, 3)]
    gain1_total = (gain1_total + others[0]) + (others[1] + others[2])
    finish_grad(1, 0)
    end(None, ("dxn", 1, 1), (gain1_total, in_grads[0]))
    finish_grad(1, 1)
    small_shares = late[:, 2 * head :]
    query_shares = down_shares[:, units:].astype(f32)

    return (
        live["out"],
        in_grads[0],
        gain1_total,
        query_shares[:, :head],
        late[:span, :head],
        late[:span, head : 2 * head],
        small_shares[:span, :slots],
        small_shares[span, :slots] + small_shares[span + 1, :slots],
        query_shares[:, head:].T,
        small_shares[:span, slots],
        wide_shares[0].astype(f32),
        wide_shares[1].astype(f32),
        down_shares[:, :units].astype(f32).T,
    )


def solution(mesh):
    rows, both = P(None, "seq", None), P("seq", "head")
    by_head, down = P(None, "head"), P("head", "seq")
    return jax.shard_map(
        on_device,
        mesh=mesh,
        in_specs=(rows, P(), by_head, by_head, by_head, by_head, P("head"), P("head", None), P(), both, both, down, rows),
        out_specs=(rows, rows, P("seq"), both, both, both, both, P("head"), down, P("seq"), both, both, down),
        check_vma=False,
    )
```

```python
import functools

import jax
import jax.numpy as jnp
from jax import lax
from jax.experimental import pallas as pl
from jax.experimental.pallas import tpu as pltpu
from jax.sharding import PartitionSpec as P

CHUNK = 128
TILE = 256
EPS = 1e-06
RATE = 0.5
MIB = 2**20
f32 = jnp.float32
bf16 = jnp.bfloat16
highest = lax.Precision.HIGHEST


def nn(a, b):
    return lax.dot_general(a, b, (((1,), (0,)), ((), ())), preferred_element_type=f32)


def nt(a, b):
    return lax.dot_general(a, b, (((1,), (1,)), ((), ())), preferred_element_type=f32)


def tn(a, b):
    return lax.dot_general(a, b, (((0,), (0,)), ((), ())), preferred_element_type=f32)


def exact(a, b, dims):
    return lax.dot_general(a, b, (dims, ((), ())), precision=highest, preferred_element_type=f32)


def halves(a):
    high = a.astype(bf16)
    return high, (a - high.astype(f32)).astype(bf16)


def call(name, kernel, grid, in_specs, out_specs, out_shape, scratch=(), vmem=24, cost=None, loose=(), loose_out=(),
         aliases=None):
    single = not isinstance(out_shape, list)
    shapes = [out_shape] if single else out_shape
    shapes = [s if i in loose_out else pltpu.HBM(s.shape, s.dtype) for i, s in enumerate(shapes)]
    function = pl.pallas_call(
        kernel,
        name=name,
        grid=grid,
        in_specs=in_specs,
        out_specs=out_specs,
        out_shape=shapes[0] if single else shapes,
        scratch_shapes=scratch,
        input_output_aliases=aliases or {},
        compiler_params=pltpu.CompilerParams(
            dimension_semantics=("arbitrary",) * len(grid), vmem_limit_bytes=vmem * MIB
        ),
        cost_estimate=cost,
    )

    def run(*operands):
        return function(*[
            o if i in loose or spec.memory_space == pltpu.SMEM else pltpu.with_memory_space_constraint(o, pltpu.HBM)
            for i, (o, spec) in enumerate(zip(operands, in_specs))
        ])

    return run


def cost(flops, data):
    return pl.CostEstimate(flops=int(flops), bytes_accessed=int(data), transcendentals=0)


def fixed(shape):
    zeros = (0,) * len(shape)
    return pl.BlockSpec(shape, lambda *_: zeros, pipeline_mode=pl.Buffered(1))


def shaped(shape, dtype):
    return jax.ShapeDtypeStruct(shape, dtype)


def triangle(lower):
    r = lax.broadcasted_iota(jnp.int32, (CHUNK, CHUNK), 0)
    c = lax.broadcasted_iota(jnp.int32, (CHUNK, CHUNK), 1)
    return r >= c if lower else r <= c


def gates(z):
    la = -RATE * lax.logistic(-z)
    y = -la
    taken = jnp.ones_like(y)
    for n in range(9, 1, -1):
        taken = 1.0 - y * (1.0 / n) * taken
    taken = y * taken
    cum = exact(triangle(True).astype(f32), la, ((1,), (0,)))
    return cum, jnp.exp(-cum) * taken


def turned_last(cum):
    return jnp.broadcast_to(cum[CHUNK - 1 :, :], cum.shape).T


def halves_sum(ones, values):
    high, low = halves(values)
    both = nn(ones.astype(bf16), jnp.concatenate([high, low], 1))
    width = values.shape[1]
    return both[:, :width] + both[:, width:]


def project_kernel(per_part, x_ref, gain_ref, wk_ref, wv_ref, wf_ref, bias_ref, gate_ref, up_ref, down_ref,
                   xn_ref, k_ref, v_ref, z_ref, cum_ref, in_ref, s_ref, d_ref, sent_ref, stacked_ref,
                   state, decay, down_rows, sems):
    step = pl.program_id(0)
    copies = [pltpu.make_async_copy(source, stacked_ref.at[i], sems.at[i])
              for i, source in enumerate((gate_ref, up_ref, down_rows))]

    @pl.when(step == 0)
    def _():
        copies[0].start()
        copies[1].start()
        down_rows[...] = down_ref[...].astype(f32).T.astype(bf16)
        copies[2].start()

    @pl.when(lax.rem(pl.program_id(0), per_part) == 0)
    def _():
        state[...] = jnp.zeros_like(state)
        decay[...] = jnp.zeros_like(decay)

    x = x_ref[...].astype(f32)
    r1 = lax.rsqrt(jnp.mean(x * x, axis=-1, keepdims=True) + EPS)
    xn = (x * r1 * gain_ref[...]).astype(bf16)
    xn_ref[...] = xn
    k_ref[...] = nn(xn, wk_ref[...]).astype(bf16)
    v_ref[...] = nn(xn, wv_ref[...]).astype(bf16)
    z_ref[...] = nt(xn, wf_ref[...]) + bias_ref[...]
    width = k_ref.shape[1]
    for c in range(x_ref.shape[0] // CHUNK):
        rows = pl.ds(c * CHUNK, CHUNK)
        cum, inflow = gates(z_ref[rows, :])
        cum_ref[rows, :] = cum
        in_ref[rows, :] = inflow
        total = turned_last(cum)
        spread = inflow.astype(bf16)
        keep = jnp.exp(total[:, :1])
        state[:, :width] = keep * (state[:, :width] + tn(spread, k_ref[rows, :]))
        state[:, width:] = keep * (state[:, width:] + tn(spread, v_ref[rows, :]))
        decay[...] += total
    s_ref[0] = state[...]
    d_ref[0] = jnp.exp(decay[...])
    pack(sent_ref, 0, jnp.exp(decay[...]), state[...])

    @pl.when(step == pl.num_programs(0) - 1)
    def _():
        for copy in copies:
            copy.wait()


def query_kernel(xn_ref, wq_ref, q_ref):
    q_ref[...] = nn(xn_ref[...], wq_ref[...]).astype(bf16)


def read_kernel(q_ref, k_ref, v_ref, cum_ref, in_ref, e0_ref, wo_ref, o_ref, p_ref, sc_ref, e_ref, left_ref, att_ref, state):
    @pl.when(pl.program_id(0) == 0)
    def _():
        state[...] = e0_ref[...]

    width = q_ref.shape[1]
    lower = triangle(True)
    q, k, v = q_ref[...], k_ref[...], v_ref[...]
    cum, inflow = cum_ref[...], in_ref[...]
    total = turned_last(cum)
    growth = jnp.exp(cum)
    e_ref[0] = state[...]
    i_hi, i_lo = halves(inflow)
    a_hi, a_lo = halves(jnp.where(lower, nt(q, k), 0.0))
    e_hi, e_lo = halves(state[:, :width])
    scores = growth * (nt(q, e_hi) + nt(q, e_lo) + nn(a_hi, i_hi) + (nn(a_hi, i_lo) + nn(a_lo, i_hi)))
    top = jnp.exp(scores - jnp.max(scores, axis=-1, keepdims=True))
    p = top / jnp.sum(top, axis=-1, keepdims=True)
    w = (p * growth).astype(bf16)
    mixing = jnp.where(lower, nt(w, i_hi), 0.0).astype(bf16)
    o = (nn(w, state[:, width:].astype(bf16)) + nn(mixing, v)).astype(bf16)
    o_ref[...] = o
    att_ref[...] = nn(o, wo_ref[...]).astype(bf16)
    p_ref[...] = p
    sc_ref[...] = scores
    keep = jnp.exp(total[:, :1])
    state[:, :width] = keep * (state[:, :width] + tn(i_hi, k))
    state[:, width:] = keep * (state[:, width:] + tn(i_hi, v))
    left_ref[...] = state[...]


def back_kernel(dhn_ref, hid_ref, cot_ref, gain_ref, wo_ref, q_ref, k_ref, v_ref, cum_ref, in_ref, p_ref, sc_ref,
                e_ref, datt_ref, dq_ref, dkl_ref, dvl_ref, h_ref, x1_ref, g_ref, s_ref, d_ref, gg_ref, state, decay):
    step = pl.program_id(0)

    @pl.when(step == 0)
    def _():
        state[...] = jnp.zeros_like(state)
        decay[...] = jnp.zeros_like(decay)
        gg_ref[...] = jnp.zeros_like(gg_ref)

    hidden = hid_ref[...].astype(f32)
    dhn = dhn_ref[...].astype(f32)
    r2 = lax.rsqrt(jnp.mean(hidden * hidden, axis=-1, keepdims=True) + EPS)
    gg_ref[...] += jnp.sum((dhn * hidden * r2).reshape(-1, 8, hidden.shape[1]), axis=0)
    u2 = gain_ref[...] * dhn
    dhid = (
        cot_ref[...].astype(f32)
        + r2 * u2
        - hidden * (r2 * r2 * r2) * jnp.mean(u2 * hidden, axis=-1, keepdims=True)
    )
    datt = dhid.astype(bf16)
    datt_ref[...] = datt
    width = q_ref.shape[1]
    do = nt(datt, wo_ref[...]).astype(bf16)
    lower, upper = triangle(True), triangle(False)
    q, k, v = q_ref[...], k_ref[...], v_ref[...]
    cum, inflow = cum_ref[...], in_ref[...]
    total = turned_last(cum)
    growth = jnp.exp(cum)
    p = p_ref[...]
    i_hi, i_lo = halves(inflow)
    b_hi, b_lo = halves(jnp.where(lower, nt(do, v), 0.0))
    ev_hi, ev_lo = halves(e_ref[0, :, width:])
    dp = growth * (nt(do, ev_hi) + nt(do, ev_lo) + nn(b_hi, i_hi) + (nn(b_hi, i_lo) + nn(b_lo, i_hi)))
    ds = p * (dp - jnp.sum(p * dp, axis=-1, keepdims=True))
    w = (p * growth).astype(bf16)
    gds = (growth * ds).astype(bf16)
    n = jnp.where(lower, nt(gds, i_hi), 0.0).astype(bf16)
    dq_ref[...] = (nn(gds, e_ref[0, :, :width].astype(bf16)) + nn(n, k)).astype(bf16)
    n_t = jnp.where(upper, nt(i_hi, gds), 0.0).astype(bf16)
    m_t = jnp.where(upper, nt(i_hi, w), 0.0).astype(bf16)
    dkl_ref[...] = nn(n_t, q)
    dvl_ref[...] = nn(m_t, do)
    h_ref[...] = ds * sc_ref[...] + p * dp
    a_t = jnp.where(upper, nt(k, q), 0.0).astype(bf16)
    b_t = jnp.where(upper, nt(v, do), 0.0).astype(bf16)
    x1_ref[...] = nn(a_t, gds) + nn(b_t, w)
    keep = jnp.exp(total[:, :1])
    g_k, g_v = tn(gds, q), tn(w, do)
    g_ref[0, :, :width] = g_k
    g_ref[0, :, width:] = g_v
    state[:, :width] = g_k + keep * state[:, :width]
    state[:, width:] = g_v + keep * state[:, width:]
    decay[...] += total
    s_ref[...] = state[...]
    d_ref[...] = jnp.exp(decay[...])


def last_kernel(l0_ref, k_ref, v_ref, z_ref, cum_ref, in_ref, e_ref, g_ref, dkl_ref, dvl_ref, h_ref, x1_ref, dq_ref, x_ref,
                wq_ref, wk_ref, wv_ref, wf_ref, dk_ref, dv_ref, dz_ref, dxn_ref, bias_ref, gg_ref,
                state, wq, wk, wv, wf, sems):
    step, steps = pl.program_id(0), pl.num_programs(0)
    loads = [pltpu.make_async_copy(source, target, sems.at[i])
             for i, (source, target) in enumerate(((wq_ref, wq), (wk_ref, wk), (wv_ref, wv), (wf_ref, wf)))]

    @pl.when(step == 0)
    def _():
        for load in loads:
            load.start()
        state[...] = l0_ref[...]
        bias_ref[...] = jnp.zeros_like(bias_ref)

    width = k_ref.shape[1]
    k, v, z = k_ref[...], v_ref[...], z_ref[...]
    cum, inflow = cum_ref[...], in_ref[...]
    total = turned_last(cum)
    i_hi = inflow.astype(bf16)
    keep = jnp.exp(total[:, :1])
    lg = keep * state[...]
    lg_k, lg_v = lg[:, :width].astype(bf16), lg[:, width:].astype(bf16)
    rows = pl.ds(pl.multiple_of((steps - 1 - step) * CHUNK, CHUNK), CHUNK)
    dk_ref[rows, :] = (dkl_ref[...] + nn(i_hi, lg_k)).astype(bf16)
    dv_ref[rows, :] = (dvl_ref[...] + nn(i_hi, lg_v)).astype(bf16)
    x1 = x1_ref[...]
    x2 = nt(k, lg_k) + nt(v, lg_v)
    met = jnp.broadcast_to(jnp.sum(lg * e_ref[0], axis=1, keepdims=True), (lg.shape[0], CHUNK)).T
    h, r1 = h_ref[...], inflow * x1
    dla = (
        halves_sum(triangle(False), h - r1)
        + r1
        + halves_sum(triangle(True), inflow * x2)
        + met
        - jnp.exp(-cum) * (x1 + x2)
    )
    rate = lax.logistic(-z)
    dz = (dla * RATE * rate * (1.0 - rate)).astype(bf16)
    dz_ref[rows, :] = dz
    bias_ref[...] += jnp.sum(dz.astype(f32).reshape(-1, 8, dz.shape[1]), axis=0)
    state[...] = g_ref[0] + lg

    @pl.when(step == steps - 1)
    def _():
        for load in loads:
            load.wait()
        dxn = nt(dq_ref[...], wq[...]) + nt(dk_ref[...], wk[...]) + nt(dv_ref[...], wv[...]) + nn(dz_ref[...], wf[...])
        dxn_ref[...] = dxn.astype(bf16)
        x = x_ref[...].astype(f32)
        r1 = lax.rsqrt(jnp.mean(x * x, axis=-1, keepdims=True) + EPS)
        gg_ref[...] = jnp.sum((dxn * x * r1).reshape(-1, 8, x.shape[1]), axis=0)


def out_kernel(hid_ref, ffn_ref, *refs):
    refs[-1][0] = (hid_ref[...].astype(f32) + ffn_ref[...].astype(f32)).astype(bf16)


def in_grad_kernel(dhid_ref, dxn_ref, x_ref, gain_ref, *refs):
    x = x_ref[...].astype(f32)
    r1 = lax.rsqrt(jnp.mean(x * x, axis=-1, keepdims=True) + EPS)
    u1 = gain_ref[...] * dxn_ref[...].astype(f32)
    refs[-1][0] = dhid_ref[...].astype(f32) + r1 * u1 - x * (r1 * r1 * r1) * jnp.mean(u1 * x, axis=-1, keepdims=True)


def feed_kernel(first_row, x_ref, att_ref, gain_ref, cot_ref, full_ref, hid_ref, hn_ref, act_ref, dg_ref, du_ref,
                ffn_ref, dhn_ref, weights, x, cot, hid, hn, act, dg, du, ffn, in_sems, out_sems, weight_sems):
    rows, width = x.shape
    units = act.shape[1]
    blocks, _, span, _ = weights.shape
    tiles = [(u, min(TILE, units - u)) for u in range(0, units, TILE)]
    here = pl.ds(first_row, rows)
    reads = [pltpu.make_async_copy(source.at[here, :], target, in_sems.at[i])
             for i, (source, target) in enumerate(((x_ref, x), (cot_ref, cot)))]
    loads = [pltpu.make_async_copy(full_ref.at[:, :, :, pl.ds(u, size)], weights.at[:, :, :, pl.ds(u, size)],
                                   weight_sems.at[i]) for i, (u, size) in enumerate(tiles)]
    writes = [pltpu.make_async_copy(source, target, out_sems.at[i])
              for i, (source, target) in enumerate(
                  ((hid, hid_ref), (hn, hn_ref), (act, act_ref), (dg, dg_ref), (du, du_ref), (ffn, ffn_ref)))]
    for copy in reads + loads:
        copy.start()
    for copy in reads:
        copy.wait()
    hidden = x[...].astype(f32) + att_ref[...].astype(f32)
    hid[...] = hidden.astype(bf16)
    r2 = lax.rsqrt(jnp.mean(hidden * hidden, axis=-1, keepdims=True) + EPS)
    hn[...] = (hidden * r2 * gain_ref[...]).astype(bf16)
    writes[0].start()
    writes[1].start()
    for (u, size), load in zip(tiles, loads):
        load.wait()
        gate, up, dact = (
            nn(left[...], weights[:, i, :, u : u + size].reshape(width, size))
            for i, left in enumerate((hn, hn, cot))
        )
        s = lax.logistic(gate)
        silu = gate * s
        act[:, u : u + size] = (silu * up).astype(bf16)
        dg[:, u : u + size] = (dact * up * s * (1.0 + gate * (1.0 - s))).astype(bf16)
        du[:, u : u + size] = (dact * silu).astype(bf16)
    for write in writes[2:5]:
        write.start()
    group = max(1, TILE // span)
    for b in range(0, blocks, group):
        columns = slice(b * span, (b + group) * span)
        w_gate, w_up, w_down = (weights[b : b + group, i].reshape(group * span, units) for i in range(3))
        ffn[:, columns] = nt(act[...], w_down).astype(bf16)
        dhn_ref[:, columns] = (nt(dg[...], w_gate) + nt(du[...], w_up)).astype(bf16)
    writes[5].start()
    for write in writes:
        write.wait()


def summed(pairs):
    total = tn(*pairs[0])
    for pair in pairs[1:]:
        total = total + tn(*pair)
    return total.astype(bf16)


def down_grad_kernel(*refs):
    cot_ref, act, out_ref = refs[0], refs[1:-1], refs[-1]
    rows = act[0].shape[0]
    block = summed([(cot_ref[i * rows : (i + 1) * rows, :], a[...]) for i, a in enumerate(act)])
    out_ref[...] = block.reshape(out_ref.shape)


def wide_grad_kernel(*refs):
    out_ref = refs[-1]
    count = (len(refs) - 1) // 3
    hn, dg, du = refs[:count], refs[count : 2 * count], refs[2 * count : 3 * count]
    blocks, _, width, units = out_ref.shape
    for i, grads in enumerate((dg, du)):
        block = summed([(h[...], g[...]) for h, g in zip(hn, grads)])
        out_ref[:, i] = block.reshape(blocks, width, units)


def query_grad_kernel(count, first_column, *refs):
    xn_ref, out_ref, block, sems = refs[0], refs[-3], refs[-2], refs[-1]
    datt, dq, o = (refs[1 + i * count : 1 + (i + 1) * count] for i in range(3))
    rows, width = dq[0].shape
    _, groups, span, columns = block.shape
    step, steps = pl.program_id(0), pl.num_programs(0)

    def copy(at):
        slot = lax.rem(at, 2)
        return pltpu.make_async_copy(
            block.at[slot], out_ref.at[pl.ds(at * groups, groups), :, pl.ds(first_column, columns)], sems.at[slot]
        )

    @pl.when(step >= 2)
    def _():
        copy(step - 2).wait()

    xn = [xn_ref[i * rows : (i + 1) * rows, :] for i in range(count)]
    slot = lax.rem(step, 2)
    query = summed([(x, g[...]) for x, g in zip(xn, dq)])
    block[slot, :, :, :width] = query.reshape(groups, span, width)
    output = summed([(d[...], r[...]) for d, r in zip(datt, o)])
    block[slot, :, :, width:] = output.reshape(groups, span, width)
    copy(step).start()

    @pl.when(step == steps - 1)
    def _():
        copy(step - 1).wait()
        copy(step).wait()


def state_grad_kernel(count, *refs):
    xn_ref, out_ref = refs[0], refs[-1]
    dk, dv, dz, bias, gain1, gain2 = (refs[1 + i * count : 1 + (i + 1) * count] for i in range(6))
    rows, width = dk[0].shape
    slots = dz[0].shape[1]
    groups, high, _ = out_ref.shape
    span = high - 16
    xn = [xn_ref[i * rows : (i + 1) * rows, :] for i in range(count)]
    for i, grads in enumerate((dk, dv)):
        block = summed([(x, g[...]) for x, g in zip(xn, grads)])
        out_ref[:, :span, i * width : (i + 1) * width] = block.reshape(groups, span, width)
    forget = tn(xn[0], dz[0][...])
    for x, g in zip(xn[1:], dz[1:]):
        forget = forget + tn(x, g[...])
    pad = 128 - slots % 128

    def padded(values):
        return jnp.concatenate([values, jnp.zeros((values.shape[0], pad), f32)], 1)

    def column(parts):
        total = parts[0][...]
        for part in parts[1:]:
            total = total + part[...]
        return jnp.sum(total.T, axis=1, keepdims=True)

    small = padded(forget)
    lane = lax.broadcasted_iota(jnp.int32, small.shape, 1)
    small = jnp.where(lane == slots, column(gain2), jnp.where(lane == slots + 1, column(gain1), small))
    out_ref[:, :span, 2 * width :] = small.astype(bf16).reshape(groups, span, slots + pad)
    total = bias[0][...]
    for part in bias[1:]:
        total = total + part[...]
    total = padded(jnp.broadcast_to(jnp.sum(total, axis=0, keepdims=True), (16, slots)))
    upper = total.astype(bf16).astype(f32)
    row = lax.broadcasted_iota(jnp.int32, total.shape, 0)
    tail = jnp.where(row == 0, upper, jnp.where(row == 1, total - upper, 0.0)).astype(bf16)
    for g in range(groups):
        out_ref[g, span:, : 2 * width] = jnp.zeros((16, 2 * width), bf16)
        out_ref[g, span:, 2 * width :] = tail


def pack(ref, m, decay, state):
    high, low = halves(decay)
    lane = lax.broadcasted_iota(jnp.int32, decay.shape, 1)
    width = state.shape[1]
    ref[m, :, :width] = state.astype(bf16)
    ref[m, :, width:] = jnp.where(lane == 0, high.astype(f32), low.astype(f32)).astype(bf16)


def fold_kernel(parts, pieces, *refs):
    s_refs, d_refs, (s_out, d_out, sent) = refs[: parts * pieces], refs[parts * pieces : -3], refs[-3:]
    for m in range(parts):
        s, d = s_refs[m * pieces + pieces - 1][...], d_refs[m * pieces + pieces - 1][...]
        for t in reversed(range(pieces - 1)):
            here = d_refs[m * pieces + t][...]
            s, d = s_refs[m * pieces + t][...] + here[:, :1] * s, here * d
        s_out[m], d_out[m] = s, d
        pack(sent, m, d, s)


def hop_kernel(bit, after, first, final, parts, pieces, *refs):
    refs = list(refs)
    s_ref, d_ref, got_ref = refs[:3]
    refs = refs[3:]
    if not first:
        part_s_ref, part_d_ref = refs[:2]
        refs = refs[2:]
    early = (lax.axis_index("seq") & bit) == 0
    takes = early if after else jnp.logical_not(early)
    width = s_ref.shape[2]
    found = []
    for m in range(parts):
        tail = got_ref[m, :, width:].astype(f32)
        there_d, there_s = tail[:, :1] + tail[:, 1:2], got_ref[m, :, :width].astype(f32)
        s, d = s_ref[m], d_ref[m]
        there_wide = jnp.broadcast_to(there_d, d.shape)
        new_s = jnp.where(takes, s + d[:, :1] * there_s, there_s + there_d * s)
        if first:
            part_s, part_d = jnp.where(takes, there_s, 0.0), jnp.where(takes, there_wide, 1.0)
        else:
            part_s, part_d = part_s_ref[m], part_d_ref[m]
            part_s = jnp.where(takes, part_s + part_d[:, :1] * there_s, part_s)
            part_d = jnp.where(takes, part_d * there_wide, part_d)
        found.append((new_s, d * there_wide, part_s, part_d))
    if not final:
        s_out, d_out, part_s_out, part_d_out, sent = refs
        for m, (s, d, part_s, part_d) in enumerate(found):
            s_out[m], d_out[m], part_s_out[m], part_d_out[m] = s, d, part_s, part_d
            pack(sent, m, d, s)
        return
    *own, out = refs
    arriving = jnp.zeros_like(found[0][0])
    for m in reversed(range(parts)) if after else range(parts):
        s, d, part_s, part_d = found[m]
        enters = part_s + part_d[:, :1] * arriving
        arriving = s + d[:, :1] * arriving
        for t in reversed(range(pieces)) if after else range(1):
            out[m * pieces + t if after else m] = enters
            if after and t:
                here = m * pieces + t
                enters = own[here][...] + own[parts * pieces + here][:, :1] * enters


def in_vmem(name, kernel, operands, shapes):
    return pl.pallas_call(
        kernel,
        name=name,
        in_specs=[pl.BlockSpec(memory_space=pltpu.VMEM)] * len(operands),
        out_specs=[pl.BlockSpec(memory_space=pltpu.VMEM)] * len(shapes),
        out_shape=shapes,
        compiler_params=pltpu.CompilerParams(vmem_limit_bytes=12 * MIB),
        cost_estimate=cost(0, 6 * MIB),
    )(*operands)


def scan_states(n, state, decay, sent, after, own=(), pieces=1, ties=()):
    parts, slots, width = state.shape
    part, bit, hops = [], 1, 0
    while bit < n:
        got = lax.ppermute(sent, "seq", [(i, i ^ bit) for i in range(n)])
        final = 2 * bit == n
        shapes = [shaped(state.shape, f32), shaped(decay.shape, f32)] * 2 + [shaped(sent.shape, bf16)]
        if final:
            shapes = [shaped((parts * pieces, slots, width), f32)]
        if hops < len(ties) and ties[hops] is not None:
            state = ties[hops](state, got)
        results = in_vmem(
            "hop",
            functools.partial(hop_kernel, bit, after, not part, final, parts, pieces),
            [state, decay, got, *part, *(own if final else ())],
            shapes,
        )
        if final:
            return results[0]
        state, decay, *part, sent = results
        bit, hops = 2 * bit, hops + 1


def behind_of(value, *first):
    return lax.optimization_barrier((value,) + first)[0]


def join_kernel(has, *refs):
    refs = iter(refs)
    piece, outer, pair, middle, total, coming = (next(refs) if h else None for h in has)
    makes = (piece is not None, pair is not None or coming is not None, total is not None)
    new_pair, new_total, done = (next(refs) if m else None for m in makes)
    me = lax.axis_index("head")
    end = (me == 0) | (me == 3)

    def each(work):
        @pl.loop(0, TILE // 32)
        def _(i):
            work(pl.ds(pl.multiple_of(i * 32, 32), 32))

    def both(a, b, rows):
        return a[rows, :] + b[rows, :]

    @pl.when(end)
    def _():
        def work(rows):
            if coming is not None:
                new_total[rows, :] = coming[rows, :]
            if done is not None:
                done[rows, :] = outer[rows, :]

        each(work)

    @pl.when(jnp.logical_not(end))
    def _():
        def work(rows):
            if piece is not None:
                new_pair[rows, :] = both(piece, outer, rows)
            if pair is not None:
                new_total[rows, :] = both(pair, middle, rows)
            if done is not None:
                done[rows, :] = total[rows, :]

        each(work)


class Line:
    INWARD, OUTWARD, MIDDLE = [(0, 1), (3, 2)], [(1, 0), (2, 3)], [(1, 2), (2, 1)]

    def __init__(self):
        self.piece = self.pair = self.payload = None
        self.returns = False

    def load(self, piece):
        self.piece = self.payload = piece

    def step(self, inputs):
        piece, pair, payload, returns = self.piece, self.pair, self.payload, self.returns
        values = [v for v in (payload, pair) if v is not None] + inputs
        values = list(lax.optimization_barrier(tuple(values)))
        outer = middle = None
        if payload is not None:
            payload = values.pop(0)
            way = (self.INWARD if piece is not None else []) + (self.OUTWARD if returns else [])
            outer = lax.ppermute(payload, "head", way)
        if pair is not None:
            pair = values.pop(0)
            middle = lax.ppermute(pair, "head", self.MIDDLE)
        self.waiting = (piece, outer, pair, middle, payload if returns else None)
        return values

    def join(self, coming=None, after=()):
        piece, outer, pair, middle, total = self.waiting
        if after:
            outer = behind_of(outer, *after)
        if piece is None and total is None:
            outer = None
        operands = [piece, outer, pair, middle, total, coming]
        makes = [piece is not None, pair is not None or coming is not None, total is not None]
        arrays = [o for o in operands if o is not None]
        results = in_vmem(
            "join",
            functools.partial(join_kernel, [o is not None for o in operands]),
            arrays,
            [shaped(arrays[0].shape, bf16)] * sum(makes),
        )
        results = iter(results)
        self.pair, self.payload, done = (next(results) if m else None for m in makes)
        self.returns = pair is not None
        self.piece = coming
        return done


def on_device(tokens, gain_attn, w_query, w_key, w_value, w_forget, forget_bias, w_out, gain_ffn, w_gate, w_up, w_down,
              cotangent):
    parts, part_rows, width = tokens.shape
    rows = parts * part_rows
    head = w_query.shape[1]
    slots = w_forget.shape[1]
    units = w_gate.shape[1]
    n_seq, n_head = lax.axis_size("seq"), lax.axis_size("head")
    span = w_gate.shape[0]
    per_part = pieces = part_rows // TILE
    chunks = TILE // CHUNK
    every = [(m, t) for m in range(parts) for t in range(pieces)]

    x = tokens.reshape(rows, width)
    cot = cotangent.reshape(rows, width)
    gain1 = gain_attn.reshape(1, width)
    gain2 = gain_ffn.reshape(1, width)
    state_scratch = pltpu.VMEM((slots, 2 * head), f32)
    decay_scratch = pltpu.VMEM((slots, 128), f32)
    anywhere = pl.BlockSpec(memory_space=pl.ANY)
    in_place = pl.BlockSpec(memory_space=pltpu.VMEM)

    all_rows = lambda c: pl.BlockSpec((TILE, c), lambda i: (i, 0))
    by_part = lambda c: pl.BlockSpec((1, slots, c), lambda i: (i // per_part, 0, 0))
    forget_rows = w_forget.T
    xn, k, v, z, cum, inflow, local, decay, sent, stacked = call(
        "project",
        functools.partial(project_kernel, per_part),
        (rows // TILE,),
        [all_rows(width), fixed((1, width))] + [fixed((width, head))] * 2 + [fixed((slots, width)), fixed((1, slots)), anywhere, anywhere,
                                                                        fixed((units, span))],
        [all_rows(width), all_rows(head), all_rows(head)] + [all_rows(slots)] * 3
        + [by_part(2 * head), by_part(128), by_part(2 * head + 128), anywhere],
        [shaped((rows, width), bf16)] + [shaped((rows, head), bf16)] * 2
        + [shaped((rows, slots), f32)] * 3 + [shaped((parts, slots, 2 * head), f32), shaped((parts, slots, 128), f32),
                                             shaped((parts, slots, 2 * head + 128), bf16), shaped((3, span, units), bf16)],
        [state_scratch, decay_scratch, pltpu.VMEM((span, units), bf16), pltpu.SemaphoreType.DMA((3,))],
        cost=cost(2 * rows * width * (2 * head + slots), 2 * rows * width * 3 + 2 * width * 2 * head),
        loose_out=(6, 7, 8),
    )(x, gain1, w_key, w_value, forget_rows, forget_bias.reshape(1, slots), w_gate, w_up, w_down)
    q = call(
        "query",
        query_kernel,
        (rows // TILE,),
        [all_rows(width), fixed((width, head))],
        all_rows(head),
        shaped((rows, head), bf16),
        cost=cost(2 * rows * width * head, 2 * rows * (width + head) + 2 * width * head),
    )(xn, w_query)
    full = lax.all_gather(stacked, "seq")
    entering = scan_states(n_seq, local, decay, sent, False)

    def chunk_rows(m, t, columns, back):
        start = (m * pieces + t) * chunks
        return pl.BlockSpec((CHUNK, columns), lambda i: (start + (chunks - 1 - i if back else i), 0))

    def own_rows(columns, back):
        return pl.BlockSpec((CHUNK, columns), lambda i: (chunks - 1 - i if back else i, 0))

    def chunk_state(back):
        return pl.BlockSpec((1, slots, 2 * head), lambda i: (chunks - 1 - i if back else i, 0, 0))

    def whole(shape):
        return pl.BlockSpec(shape, lambda i: (0,) * len(shape))

    def state_of(m):
        return pl.BlockSpec((None, slots, 2 * head), lambda i: (m, 0, 0))

    states_shape = shaped((chunks, slots, 2 * head), f32)

    def read(m, t, entering, which):
        return call(
            "read",
            read_kernel,
            (chunks,),
            [chunk_rows(m, t, head, False)] * 3 + [chunk_rows(m, t, slots, False)] * 2
            + [state_of(which), fixed((head, width))],
            [own_rows(head, False), own_rows(slots, False), own_rows(slots, False), chunk_state(False),
             pl.BlockSpec((None, slots, 2 * head), lambda i: (0, 0, 0)), own_rows(width, False)],
            [shaped((TILE, head), bf16), shaped((TILE, slots), f32), shaped((TILE, slots), f32), states_shape,
             shaped((1, slots, 2 * head), f32), shaped((TILE, width), bf16)],
            [state_scratch],
            cost=cost(2 * TILE * head * (600 + width), 2 * TILE * (head * 4 + width) + 2 * head * width),
            loose=(5,),
            loose_out=(4, 5),
        )(q, k, v, cum, inflow, entering, w_out)

    def feed(m, t, attended):
        tile_count = pl.cdiv(units, TILE)
        vmem = pltpu.VMEM
        return call(
            "feed",
            functools.partial(feed_kernel, (m * pieces + t) * TILE),
            (),
            [anywhere, in_place, in_place, anywhere, anywhere],
            [anywhere] * 6 + [in_place],
            [shaped((TILE, width), bf16)] * 2 + [shaped((TILE, units), bf16)] * 3
            + [shaped((TILE, width), bf16)] * 2,
            [vmem((n_seq, 3, span, units), bf16), vmem((TILE, width), bf16), vmem((TILE, width), bf16),
             vmem((TILE, width), bf16), vmem((TILE, width), bf16)] + [vmem((TILE, units), bf16)] * 3
            + [vmem((TILE, width), bf16), pltpu.SemaphoreType.DMA((2,)), pltpu.SemaphoreType.DMA((6,)),
               pltpu.SemaphoreType.DMA((tile_count,))],
            cost=cost(12 * TILE * width * units, 6 * width * units + TILE * width * 14),
            vmem=44,
            loose=(1, 2),
            loose_out=(6,),
        )(x, attended, gain2, cot, full)

    group = max(1, TILE // span)
    columns = group * span
    def down_grads(acts):
        return call(
            "down_grads",
            down_grad_kernel,
            (width // columns // 2,),
            [pl.BlockSpec((rows, 2 * columns), lambda j: (0, j))] + [fixed((TILE, units))] * len(acts),
            pl.BlockSpec((2 * group, span, units), lambda j: (j, 0, 0)),
            shaped((n_seq, span, units + 2 * head), bf16),
            cost=cost(2 * rows * width * units, 2 * (rows * width + rows * units + width * units)),
        )(cot, *acts)

    def wide_grads(normed, gates, ups):
        count = len(normed)
        return call(
            "wide_grads",
            wide_grad_kernel,
            (width // columns,),
            [pl.BlockSpec((TILE, columns), lambda j: (0, j))] * count
            + [fixed((TILE, units))] * (2 * count),
            pl.BlockSpec((group, 2, span, units), lambda j: (j, 0, 0, 0)),
            shaped((n_seq, 2, span, units), bf16),
            cost=cost(4 * rows * width * units, 2 * (rows * width + 2 * rows * units + 2 * width * units)),
        )(*normed, *gates, *ups)

    def back(m, t, dhn, hidden):
        o, p, scores, e_chunks = reads[m, t][:4]
        return call(
            "back",
            back_kernel,
            (chunks,),
            [own_rows(width, True), own_rows(width, True), chunk_rows(m, t, width, True), fixed((1, width)),
             fixed((head, width))]
            + [chunk_rows(m, t, head, True)] * 3 + [chunk_rows(m, t, slots, True)] * 2 + [own_rows(slots, True)] * 2
            + [chunk_state(True)],
            [own_rows(width, True)] + [own_rows(head, True)] * 3 + [own_rows(slots, True)] * 2
            + [chunk_state(True), whole((slots, 2 * head)), whole((slots, 128)), whole((8, width))],
            [shaped((TILE, width), bf16), shaped((TILE, head), bf16),
             shaped((TILE, head), f32), shaped((TILE, head), f32), shaped((TILE, slots), f32),
             shaped((TILE, slots), f32), states_shape, shaped((slots, 2 * head), f32), shaped((slots, 128), f32),
             shaped((8, width), f32)],
            [state_scratch, decay_scratch],
            cost=cost(2 * TILE * width * head + 2 * TILE * head * 1500, TILE * width * 14 + TILE * head * 20),
            loose=(0,),
            loose_out=(7, 8),
        )(dhn, hidden, cot, gain2, w_out, q, k, v, cum, inflow, p, scores, e_chunks)

    def last(m, t, leaving, saved):
        dq, dk_local, dv_local, h_sum, x_local, g_chunks = saved
        here = m * pieces + t
        return call(
            "last",
            last_kernel,
            (chunks,),
            [state_of(here), chunk_rows(m, t, head, True), chunk_rows(m, t, head, True),
             *[chunk_rows(m, t, slots, True)] * 3, chunk_state(True), chunk_state(True), own_rows(head, True),
             own_rows(head, True), own_rows(slots, True), own_rows(slots, True), whole((TILE, head)),
             pl.BlockSpec((TILE, width), lambda i: (here, 0))] + [anywhere] * 4,
            [whole((TILE, head)), whole((TILE, head)), whole((TILE, slots)), whole((TILE, width)), whole((8, slots)),
             whole((8, width))],
            [shaped((TILE, head), bf16), shaped((TILE, head), bf16), shaped((TILE, slots), bf16),
             shaped((TILE, width), bf16), shaped((8, slots), f32), shaped((8, width), f32)],
            [state_scratch] + [pltpu.VMEM((width, head), bf16)] * 3
            + [pltpu.VMEM((slots, width), bf16), pltpu.SemaphoreType.DMA((4,))],
            cost=cost(2 * TILE * width * (3 * head + slots), TILE * width * 8 + TILE * head * 20 + width * head * 6),
            loose=(0,),
            loose_out=(3,),
        )(leaving, k, v, z, cum, inflow, reads[m, t][3], g_chunks, dk_local, dv_local, h_sum, x_local, dq, x,
          w_query, w_key, w_value, forget_rows)

    line = Line()
    live = {}

    def start():
        names = list(live)
        live.update(zip(names, line.step([live[n] for n in names])))

    def end(coming=None, done=None, after=()):
        total = line.join(coming, after)
        if done is not None:
            live[done] = total

    reads, backs, lasts = {}, {}, {}
    outs, in_grads = [None], [None]
    eighth = TILE // 2

    def into(name, kernel, m, t, kept, dtype, inputs, specs):
        spec = pl.BlockSpec((1, eighth, width), lambda i: (m, 2 * t + i, 0))
        old = [] if kept[0] is None else [kept[0]]
        kept[0] = call(
            name,
            kernel,
            (2,),
            specs + [anywhere] * len(old),
            spec,
            shaped(tokens.shape, dtype),
            cost=cost(0, TILE * width * 10),
            loose=(1,),
            aliases={len(specs): 0} if old else None,
        )(*inputs, *old)

    piece_spec = pl.BlockSpec((eighth, width), lambda i: (i, 0))

    def finish_out(m, t):
        into("out", out_kernel, m, t, outs, bf16, [live.pop(("hidden", m, t)), live.pop(("ffn", m, t))],
             [piece_spec, piece_spec])

    def finish_grad(m, t):
        x_rows = pl.BlockSpec((eighth, width), lambda i: (2 * (m * pieces + t) + i, 0))
        into("in_grad", in_grad_kernel, m, t, in_grads, f32, [backs[m, t][0], live.pop(("dxn", m, t)), x, gain1],
             [piece_spec, piece_spec, x_rows, pl.BlockSpec((1, width), lambda i: (0, 0))])

    def go_read(m, t):
        before = live["entering"] if t == 0 else live.pop("left")
        reads[m, t] = read(m, t, before, m if t == 0 else 0)
        if t + 1 < pieces:
            live["left"] = reads[m, t][4]
        return reads[m, t][5]

    def go_feed(m, t):
        made = feed(m, t, live.pop(("att", m, t)))
        for name, value in zip(("hidden", "hn", "act", "dgate", "dup", "ffn_part"), made):
            live[name, m, t] = value
        return made[6]

    def go_back(m, t):
        backs[m, t] = back(m, t, live.pop(("dhn", m, t)), live["hidden", m, t])
        live["back", m, t] = backs[m, t][7]

    def go_last(m, t):
        lasts[m, t] = last(m, t, live["leaving"], backs[m, t][1:7])
        live["dxn_part", m, t] = lasts[m, t][3]

    def taken(name):
        return [live.pop((name, *key)) for key in every]

    live["entering"] = entering
    line.load(go_read(0, 0))
    start()
    end(go_read(0, 1))
    start()
    end(go_read(1, 0))
    start()
    end(go_read(1, 1), ("att", 0, 0))
    live.pop("entering")
    start()
    end(go_feed(0, 0), ("att", 0, 1))
    start()
    end(go_feed(0, 1), ("att", 1, 0))
    start()
    end(go_feed(1, 0), ("att", 1, 1))
    start()
    end(go_feed(1, 1), ("dhn", 0, 0))
    start()
    live["wide_grads"] = wide_grads(taken("hn"), taken("dgate"), taken("dup"))
    end(live.pop(("ffn_part", 0, 0)), ("dhn", 0, 1))
    start()
    wide_shares = lax.psum_scatter(live.pop("wide_grads"), "seq", scatter_dimension=0)
    go_back(0, 0)
    go_back(0, 1)
    end(live.pop(("ffn_part", 0, 1)), ("dhn", 1, 0))
    start()
    go_back(1, 0)
    live["down"] = down_grads(taken("act"))
    end(live.pop(("ffn_part", 1, 0)), ("dhn", 1, 1))
    start()
    go_back(1, 1)
    taken("back")
    own = [backs[key][7] for key in every] + [backs[key][8] for key in every]
    folded = in_vmem(
        "fold",
        functools.partial(fold_kernel, parts, pieces),
        own,
        [shaped(local.shape, f32), shaped(decay.shape, f32), shaped(sent.shape, bf16)],
    )

    xn_columns = [pl.BlockSpec((rows, TILE), lambda j: (0, j))]
    piece_columns = [pl.BlockSpec((TILE, TILE), lambda j: (0, j))] * len(every)
    piece_whole = [fixed((TILE, head))] * len(every)
    made = []

    def beside_first(state, got):
        live["xn"] = xn
        end(behind_of(live.pop(("ffn_part", 1, 1)), got), ("ffn", 0, 0))
        start()
        made.extend((live.pop("xn"), live.pop("down")))
        return state

    def beside_third(state, got):
        grads = call(
            "query_grads",
            functools.partial(query_grad_kernel, len(every), units),
            (width // columns,),
            xn_columns + piece_columns + piece_whole * 2 + [anywhere],
            anywhere,
            shaped((n_seq, span, units + 2 * head), bf16),
            [pltpu.VMEM((2, group, span, 2 * head), bf16), pltpu.SemaphoreType.DMA((2,))],
            cost=cost(4 * rows * width * head, 4 * rows * width + 4 * rows * head + 4 * width * head),
            aliases={1 + 3 * len(every): 0},
        )(behind_of(made[0], state), *[backs[key][0] for key in every], *[backs[key][1] for key in every],
          *[reads[key][0] for key in every], made[1])
        made.append(grads)
        return behind_of(state, grads)

    ties = [beside_first, None, beside_third]
    live["leaving"] = scan_states(n_seq, *folded, True, own, pieces, ties)
    live["query_grads"], live["wide"] = made[2], wide_shares
    go_last(0, 0)
    end(live.pop(("dxn_part", 0, 0)), ("ffn", 0, 1))
    start()
    wide_shares = live.pop("wide")
    down_shares = lax.psum_scatter(live.pop("query_grads"), "seq", scatter_dimension=0)
    go_last(0, 1)
    go_last(1, 0)
    live["xn"] = xn
    end(live.pop(("dxn_part", 0, 1)), ("ffn", 1, 0))
    start()
    go_last(1, 1)
    live.pop("leaving")
    few = [pl.BlockSpec((8, TILE), lambda j: (0, j))] * len(every)
    live["state_grads"] = call(
        "state_grads",
        functools.partial(state_grad_kernel, len(every)),
        (width // TILE,),
        xn_columns + piece_whole * 2 + [fixed((TILE, slots))] * len(every) + [fixed((8, slots))] * len(every) + few * 2,
        pl.BlockSpec((group, span + 16, 2 * head + 128), lambda j: (j, 0, 0)),
        shaped((n_seq, span + 16, 2 * head + 128), bf16),
        cost=cost(4 * rows * width * head, 2 * rows * width + 4 * rows * head + 4 * width * head),
    )(live.pop("xn"), *[lasts[key][i] for i in (0, 1, 2, 4, 5) for key in every], *[backs[key][9] for key in every])
    end(live.pop(("dxn_part", 1, 0)), ("ffn", 1, 1))
    start()
    attn_shares = lax.psum_scatter(live.pop("state_grads"), "seq", scatter_dimension=0)
    finish_out(0, 0)
    finish_out(0, 1)
    live["out"], live["down"] = outs[0], down_shares
    end(live.pop(("dxn_part", 1, 1)), ("dxn", 0, 0))
    start()
    outs[0], down_shares = live.pop("out"), live.pop("down")
    finish_out(1, 0)
    finish_out(1, 1)
    finish_grad(0, 0)
    live["out"], live["in_grad"] = outs[0], in_grads[0]
    end(None, ("dxn", 0, 1))
    start()
    in_grads[0] = live.pop("in_grad")
    finish_grad(0, 1)
    live["in_grad"] = in_grads[0]
    end(None, ("dxn", 1, 0))
    start()
    in_grads[0] = live.pop("in_grad")
    late = behind_of(attn_shares, in_grads[0]).astype(f32)
    gain1_total = late[:span, 2 * head + slots + 1]
    others = [lax.ppermute(gain1_total, "head", [(i, i ^ d) for i in range(n_head)]) for d in (1, 2, 3)]
    gain1_total = (gain1_total + others[0]) + (others[1] + others[2])
    finish_grad(1, 0)
    end(None, ("dxn", 1, 1), (gain1_total, in_grads[0]))
    finish_grad(1, 1)
    small_shares = late[:, 2 * head :]
    query_shares = down_shares[:, units:].astype(f32)

    return (
        live["out"],
        in_grads[0],
        gain1_total,
        query_shares[:, :head],
        late[:span, :head],
        late[:span, head : 2 * head],
        small_shares[:span, :slots],
        small_shares[span, :slots] + small_shares[span + 1, :slots],
        query_shares[:, head:].T,
        small_shares[:span, slots],
        wide_shares[0].astype(f32),
        wide_shares[1].astype(f32),
        down_shares[:, :units].astype(f32).T,
    )


def solution(mesh):
    rows, both = P(None, "seq", None), P("seq", "head")
    by_head, down = P(None, "head"), P("head", "seq")
    return jax.shard_map(
        on_device,
        mesh=mesh,
        in_specs=(rows, P(), by_head, by_head, by_head, by_head, P("head"), P("head", None), P(), both, both, down, rows),
        out_specs=(rows, rows, P("seq"), both, both, both, both, P("head"), down, P("seq"), both, both, down),
        check_vma=False,
    )
```

```python
import functools

import jax
import jax.numpy as jnp
from jax import lax
from jax.experimental import pallas as pl
from jax.experimental.pallas import tpu as pltpu
from jax.sharding import PartitionSpec as P

CHUNK = 128
TILE = 256
EPS = 1e-06
RATE = 0.5
MIB = 2**20
f32 = jnp.float32
bf16 = jnp.bfloat16
highest = lax.Precision.HIGHEST


def nn(a, b):
    return lax.dot_general(a, b, (((1,), (0,)), ((), ())), preferred_element_type=f32)


def nt(a, b):
    return lax.dot_general(a, b, (((1,), (1,)), ((), ())), preferred_element_type=f32)


def tn(a, b):
    return lax.dot_general(a, b, (((0,), (0,)), ((), ())), preferred_element_type=f32)


def exact(a, b, dims):
    return lax.dot_general(a, b, (dims, ((), ())), precision=highest, preferred_element_type=f32)


def halves(a):
    high = a.astype(bf16)
    return high, (a - high.astype(f32)).astype(bf16)


def call(name, kernel, grid, in_specs, out_specs, out_shape, scratch=(), vmem=24, cost=None, loose=(), loose_out=(),
         aliases=None):
    single = not isinstance(out_shape, list)
    shapes = [out_shape] if single else out_shape
    shapes = [s if i in loose_out else pltpu.HBM(s.shape, s.dtype) for i, s in enumerate(shapes)]
    function = pl.pallas_call(
        kernel,
        name=name,
        grid=grid,
        in_specs=in_specs,
        out_specs=out_specs,
        out_shape=shapes[0] if single else shapes,
        scratch_shapes=scratch,
        input_output_aliases=aliases or {},
        compiler_params=pltpu.CompilerParams(
            dimension_semantics=("arbitrary",) * len(grid), vmem_limit_bytes=vmem * MIB
        ),
        cost_estimate=cost,
    )

    def run(*operands):
        return function(*[
            o if i in loose or spec.memory_space == pltpu.SMEM else pltpu.with_memory_space_constraint(o, pltpu.HBM)
            for i, (o, spec) in enumerate(zip(operands, in_specs))
        ])

    return run


def cost(flops, data):
    return pl.CostEstimate(flops=int(flops), bytes_accessed=int(data), transcendentals=0)


def fixed(shape):
    zeros = (0,) * len(shape)
    return pl.BlockSpec(shape, lambda *_: zeros, pipeline_mode=pl.Buffered(1))


def shaped(shape, dtype):
    return jax.ShapeDtypeStruct(shape, dtype)


def triangle(lower):
    r = lax.broadcasted_iota(jnp.int32, (CHUNK, CHUNK), 0)
    c = lax.broadcasted_iota(jnp.int32, (CHUNK, CHUNK), 1)
    return r >= c if lower else r <= c


def gates(z):
    la = -RATE * lax.logistic(-z)
    y = -la
    taken = jnp.ones_like(y)
    for n in range(9, 1, -1):
        taken = 1.0 - y * (1.0 / n) * taken
    taken = y * taken
    cum = exact(triangle(True).astype(f32), la, ((1,), (0,)))
    return cum, jnp.exp(-cum) * taken


def turned_last(cum):
    return jnp.broadcast_to(cum[CHUNK - 1 :, :], cum.shape).T


def halves_sum(ones, values):
    high, low = halves(values)
    both = nn(ones.astype(bf16), jnp.concatenate([high, low], 1))
    width = values.shape[1]
    return both[:, :width] + both[:, width:]


def project_kernel(per_part, x_ref, gain_ref, wk_ref, wv_ref, wf_ref, bias_ref,
                   xn_ref, k_ref, v_ref, z_ref, cum_ref, in_ref, s_ref, d_ref, sent_ref, state, decay):
    @pl.when(lax.rem(pl.program_id(0), per_part) == 0)
    def _():
        state[...] = jnp.zeros_like(state)
        decay[...] = jnp.zeros_like(decay)

    x = x_ref[...].astype(f32)
    r1 = lax.rsqrt(jnp.mean(x * x, axis=-1, keepdims=True) + EPS)
    xn = (x * r1 * gain_ref[...]).astype(bf16)
    xn_ref[...] = xn
    k_ref[...] = nn(xn, wk_ref[...]).astype(bf16)
    v_ref[...] = nn(xn, wv_ref[...]).astype(bf16)
    z_ref[...] = nt(xn, wf_ref[...]) + bias_ref[...]
    width = k_ref.shape[1]
    for c in range(x_ref.shape[0] // CHUNK):
        rows = pl.ds(c * CHUNK, CHUNK)
        cum, inflow = gates(z_ref[rows, :])
        cum_ref[rows, :] = cum
        in_ref[rows, :] = inflow
        total = turned_last(cum)
        spread = inflow.astype(bf16)
        keep = jnp.exp(total[:, :1])
        state[:, :width] = keep * (state[:, :width] + tn(spread, k_ref[rows, :]))
        state[:, width:] = keep * (state[:, width:] + tn(spread, v_ref[rows, :]))
        decay[...] += total
    s_ref[0] = state[...]
    d_ref[0] = jnp.exp(decay[...])
    pack(sent_ref, 0, jnp.exp(decay[...]), state[...])


def query_kernel(xn_ref, wq_ref, q_ref):
    q_ref[...] = nn(xn_ref[...], wq_ref[...]).astype(bf16)


def read_kernel(q_ref, k_ref, v_ref, cum_ref, in_ref, e0_ref, wo_ref, o_ref, p_ref, sc_ref, e_ref, left_ref, att_ref, state):
    @pl.when(pl.program_id(0) == 0)
    def _():
        state[...] = e0_ref[...]

    width = q_ref.shape[1]
    lower = triangle(True)
    q, k, v = q_ref[...], k_ref[...], v_ref[...]
    cum, inflow = cum_ref[...], in_ref[...]
    total = turned_last(cum)
    growth = jnp.exp(cum)
    e_ref[0] = state[...]
    i_hi, i_lo = halves(inflow)
    a_hi, a_lo = halves(jnp.where(lower, nt(q, k), 0.0))
    e_hi, e_lo = halves(state[:, :width])
    scores = growth * (nt(q, e_hi) + nt(q, e_lo) + nn(a_hi, i_hi) + (nn(a_hi, i_lo) + nn(a_lo, i_hi)))
    top = jnp.exp(scores - jnp.max(scores, axis=-1, keepdims=True))
    p = top / jnp.sum(top, axis=-1, keepdims=True)
    w = (p * growth).astype(bf16)
    mixing = jnp.where(lower, nt(w, i_hi), 0.0).astype(bf16)
    o = (nn(w, state[:, width:].astype(bf16)) + nn(mixing, v)).astype(bf16)
    o_ref[...] = o
    att_ref[...] = nn(o, wo_ref[...]).astype(bf16)
    p_ref[...] = p
    sc_ref[...] = scores
    keep = jnp.exp(total[:, :1])
    state[:, :width] = keep * (state[:, :width] + tn(i_hi, k))
    state[:, width:] = keep * (state[:, width:] + tn(i_hi, v))
    left_ref[...] = state[...]


def back_kernel(dhn_ref, hid_ref, cot_ref, gain_ref, wo_ref, q_ref, k_ref, v_ref, cum_ref, in_ref, p_ref, sc_ref,
                e_ref, datt_ref, dq_ref, dkl_ref, dvl_ref, h_ref, x1_ref, g_ref, s_ref, d_ref, gg_ref, state, decay):
    step = pl.program_id(0)

    @pl.when(step == 0)
    def _():
        state[...] = jnp.zeros_like(state)
        decay[...] = jnp.zeros_like(decay)
        gg_ref[...] = jnp.zeros_like(gg_ref)

    hidden = hid_ref[...].astype(f32)
    dhn = dhn_ref[...].astype(f32)
    r2 = lax.rsqrt(jnp.mean(hidden * hidden, axis=-1, keepdims=True) + EPS)
    gg_ref[...] += jnp.sum((dhn * hidden * r2).reshape(-1, 8, hidden.shape[1]), axis=0)
    u2 = gain_ref[...] * dhn
    dhid = (
        cot_ref[...].astype(f32)
        + r2 * u2
        - hidden * (r2 * r2 * r2) * jnp.mean(u2 * hidden, axis=-1, keepdims=True)
    )
    datt = dhid.astype(bf16)
    datt_ref[...] = datt
    width = q_ref.shape[1]
    do = nt(datt, wo_ref[...]).astype(bf16)
    lower, upper = triangle(True), triangle(False)
    q, k, v = q_ref[...], k_ref[...], v_ref[...]
    cum, inflow = cum_ref[...], in_ref[...]
    total = turned_last(cum)
    growth = jnp.exp(cum)
    p = p_ref[...]
    i_hi, i_lo = halves(inflow)
    b_hi, b_lo = halves(jnp.where(lower, nt(do, v), 0.0))
    ev_hi, ev_lo = halves(e_ref[0, :, width:])
    dp = growth * (nt(do, ev_hi) + nt(do, ev_lo) + nn(b_hi, i_hi) + (nn(b_hi, i_lo) + nn(b_lo, i_hi)))
    ds = p * (dp - jnp.sum(p * dp, axis=-1, keepdims=True))
    w = (p * growth).astype(bf16)
    gds = (growth * ds).astype(bf16)
    n = jnp.where(lower, nt(gds, i_hi), 0.0).astype(bf16)
    dq_ref[...] = (nn(gds, e_ref[0, :, :width].astype(bf16)) + nn(n, k)).astype(bf16)
    n_t = jnp.where(upper, nt(i_hi, gds), 0.0).astype(bf16)
    m_t = jnp.where(upper, nt(i_hi, w), 0.0).astype(bf16)
    dkl_ref[...] = nn(n_t, q)
    dvl_ref[...] = nn(m_t, do)
    h_ref[...] = ds * sc_ref[...] + p * dp
    a_t = jnp.where(upper, nt(k, q), 0.0).astype(bf16)
    b_t = jnp.where(upper, nt(v, do), 0.0).astype(bf16)
    x1_ref[...] = nn(a_t, gds) + nn(b_t, w)
    keep = jnp.exp(total[:, :1])
    g_k, g_v = tn(gds, q), tn(w, do)
    g_ref[0, :, :width] = g_k
    g_ref[0, :, width:] = g_v
    state[:, :width] = g_k + keep * state[:, :width]
    state[:, width:] = g_v + keep * state[:, width:]
    decay[...] += total
    s_ref[...] = state[...]
    d_ref[...] = jnp.exp(decay[...])


def last_kernel(l0_ref, k_ref, v_ref, z_ref, cum_ref, in_ref, e_ref, g_ref, dkl_ref, dvl_ref, h_ref, x1_ref, dq_ref, x_ref,
                wq_ref, wk_ref, wv_ref, wf_ref, dk_ref, dv_ref, dz_ref, dxn_ref, bias_ref, gg_ref,
                state, wq, wk, wv, wf, sems):
    step, steps = pl.program_id(0), pl.num_programs(0)
    loads = [pltpu.make_async_copy(source, target, sems.at[i])
             for i, (source, target) in enumerate(((wq_ref, wq), (wk_ref, wk), (wv_ref, wv), (wf_ref, wf)))]

    @pl.when(step == 0)
    def _():
        for load in loads:
            load.start()
        state[...] = l0_ref[...]
        bias_ref[...] = jnp.zeros_like(bias_ref)

    width = k_ref.shape[1]
    k, v, z = k_ref[...], v_ref[...], z_ref[...]
    cum, inflow = cum_ref[...], in_ref[...]
    total = turned_last(cum)
    i_hi = inflow.astype(bf16)
    keep = jnp.exp(total[:, :1])
    lg = keep * state[...]
    lg_k, lg_v = lg[:, :width].astype(bf16), lg[:, width:].astype(bf16)
    rows = pl.ds(pl.multiple_of((steps - 1 - step) * CHUNK, CHUNK), CHUNK)
    dk_ref[rows, :] = (dkl_ref[...] + nn(i_hi, lg_k)).astype(bf16)
    dv_ref[rows, :] = (dvl_ref[...] + nn(i_hi, lg_v)).astype(bf16)
    x1 = x1_ref[...]
    x2 = nt(k, lg_k) + nt(v, lg_v)
    met = jnp.broadcast_to(jnp.sum(lg * e_ref[0], axis=1, keepdims=True), (lg.shape[0], CHUNK)).T
    h, r1 = h_ref[...], inflow * x1
    dla = (
        halves_sum(triangle(False), h - r1)
        + r1
        + halves_sum(triangle(True), inflow * x2)
        + met
        - jnp.exp(-cum) * (x1 + x2)
    )
    rate = lax.logistic(-z)
    dz = (dla * RATE * rate * (1.0 - rate)).astype(bf16)
    dz_ref[rows, :] = dz
    bias_ref[...] += jnp.sum(dz.astype(f32).reshape(-1, 8, dz.shape[1]), axis=0)
    state[...] = g_ref[0] + lg

    @pl.when(step == steps - 1)
    def _():
        for load in loads:
            load.wait()
        dxn = nt(dq_ref[...], wq[...]) + nt(dk_ref[...], wk[...]) + nt(dv_ref[...], wv[...]) + nn(dz_ref[...], wf[...])
        dxn_ref[...] = dxn.astype(bf16)
        x = x_ref[...].astype(f32)
        r1 = lax.rsqrt(jnp.mean(x * x, axis=-1, keepdims=True) + EPS)
        gg_ref[...] = jnp.sum((dxn * x * r1).reshape(-1, 8, x.shape[1]), axis=0)


def out_kernel(hid_ref, ffn_ref, *refs):
    refs[-1][0] = (hid_ref[...].astype(f32) + ffn_ref[...].astype(f32)).astype(bf16)


def in_grad_kernel(dhid_ref, dxn_ref, x_ref, gain_ref, *refs):
    x = x_ref[...].astype(f32)
    r1 = lax.rsqrt(jnp.mean(x * x, axis=-1, keepdims=True) + EPS)
    u1 = gain_ref[...] * dxn_ref[...].astype(f32)
    refs[-1][0] = dhid_ref[...].astype(f32) + r1 * u1 - x * (r1 * r1 * r1) * jnp.mean(u1 * x, axis=-1, keepdims=True)


def feed_kernel(first_row, x_ref, att_ref, gain_ref, cot_ref, full_ref, hid_ref, hn_ref, act_ref, dg_ref, du_ref,
                ffn_ref, dhn_ref, weights, x, cot, hid, hn, act, dg, du, ffn, in_sems, out_sems, weight_sems):
    rows, width = x.shape
    units = act.shape[1]
    blocks, _, span, _ = weights.shape
    tiles = [(u, min(TILE, units - u)) for u in range(0, units, TILE)]
    here = pl.ds(first_row, rows)
    reads = [pltpu.make_async_copy(source.at[here, :], target, in_sems.at[i])
             for i, (source, target) in enumerate(((x_ref, x), (cot_ref, cot)))]
    loads = [pltpu.make_async_copy(full_ref.at[:, :, :, pl.ds(u, size)], weights.at[:, :, :, pl.ds(u, size)],
                                   weight_sems.at[i]) for i, (u, size) in enumerate(tiles)]
    writes = [pltpu.make_async_copy(source, target, out_sems.at[i])
              for i, (source, target) in enumerate(
                  ((hid, hid_ref), (hn, hn_ref), (act, act_ref), (dg, dg_ref), (du, du_ref), (ffn, ffn_ref)))]
    for copy in reads + loads:
        copy.start()
    for copy in reads:
        copy.wait()
    hidden = x[...].astype(f32) + att_ref[...].astype(f32)
    hid[...] = hidden.astype(bf16)
    r2 = lax.rsqrt(jnp.mean(hidden * hidden, axis=-1, keepdims=True) + EPS)
    hn[...] = (hidden * r2 * gain_ref[...]).astype(bf16)
    writes[0].start()
    writes[1].start()
    for (u, size), load in zip(tiles, loads):
        load.wait()
        gate, up, dact = (
            nn(left[...], weights[:, i, :, u : u + size].reshape(width, size))
            for i, left in enumerate((hn, hn, cot))
        )
        s = lax.logistic(gate)
        silu = gate * s
        act[:, u : u + size] = (silu * up).astype(bf16)
        dg[:, u : u + size] = (dact * up * s * (1.0 + gate * (1.0 - s))).astype(bf16)
        du[:, u : u + size] = (dact * silu).astype(bf16)
    for write in writes[2:5]:
        write.start()
    group = max(1, TILE // span)
    for b in range(0, blocks, group):
        columns = slice(b * span, (b + group) * span)
        w_gate, w_up, w_down = (weights[b : b + group, i].reshape(group * span, units) for i in range(3))
        ffn[:, columns] = nt(act[...], w_down).astype(bf16)
        dhn_ref[:, columns] = (nt(dg[...], w_gate) + nt(du[...], w_up)).astype(bf16)
    writes[5].start()
    for write in writes:
        write.wait()


def summed(pairs):
    total = tn(*pairs[0])
    for pair in pairs[1:]:
        total = total + tn(*pair)
    return total.astype(bf16)


def down_grad_kernel(*refs):
    cot_ref, act, out_ref = refs[0], refs[1:-1], refs[-1]
    rows = act[0].shape[0]
    block = summed([(cot_ref[i * rows : (i + 1) * rows, :], a[...]) for i, a in enumerate(act)])
    out_ref[...] = block.reshape(out_ref.shape)


def wide_grad_kernel(*refs):
    out_ref = refs[-1]
    count = (len(refs) - 1) // 3
    hn, dg, du = refs[:count], refs[count : 2 * count], refs[2 * count : 3 * count]
    blocks, _, width, units = out_ref.shape
    for i, grads in enumerate((dg, du)):
        block = summed([(h[...], g[...]) for h, g in zip(hn, grads)])
        out_ref[:, i] = block.reshape(blocks, width, units)


def query_grad_kernel(count, first_column, *refs):
    xn_ref, out_ref, block, sems = refs[0], refs[-3], refs[-2], refs[-1]
    datt, dq, o = (refs[1 + i * count : 1 + (i + 1) * count] for i in range(3))
    rows, width = dq[0].shape
    _, groups, span, columns = block.shape
    step, steps = pl.program_id(0), pl.num_programs(0)

    def copy(at):
        slot = lax.rem(at, 2)
        return pltpu.make_async_copy(
            block.at[slot], out_ref.at[pl.ds(at * groups, groups), :, pl.ds(first_column, columns)], sems.at[slot]
        )

    @pl.when(step >= 2)
    def _():
        copy(step - 2).wait()

    xn = [xn_ref[i * rows : (i + 1) * rows, :] for i in range(count)]
    slot = lax.rem(step, 2)
    query = summed([(x, g[...]) for x, g in zip(xn, dq)])
    block[slot, :, :, :width] = query.reshape(groups, span, width)
    output = summed([(d[...], r[...]) for d, r in zip(datt, o)])
    block[slot, :, :, width:] = output.reshape(groups, span, width)
    copy(step).start()

    @pl.when(step == steps - 1)
    def _():
        copy(step - 1).wait()
        copy(step).wait()


def state_grad_kernel(count, *refs):
    xn_ref, out_ref = refs[0], refs[-1]
    dk, dv, dz, bias, gain1, gain2 = (refs[1 + i * count : 1 + (i + 1) * count] for i in range(6))
    rows, width = dk[0].shape
    slots = dz[0].shape[1]
    groups, high, _ = out_ref.shape
    span = high - 16
    xn = [xn_ref[i * rows : (i + 1) * rows, :] for i in range(count)]
    for i, grads in enumerate((dk, dv)):
        block = summed([(x, g[...]) for x, g in zip(xn, grads)])
        out_ref[:, :span, i * width : (i + 1) * width] = block.reshape(groups, span, width)
    forget = tn(xn[0], dz[0][...])
    for x, g in zip(xn[1:], dz[1:]):
        forget = forget + tn(x, g[...])
    pad = 128 - slots % 128

    def padded(values):
        return jnp.concatenate([values, jnp.zeros((values.shape[0], pad), f32)], 1)

    def column(parts):
        total = parts[0][...]
        for part in parts[1:]:
            total = total + part[...]
        return jnp.sum(total.T, axis=1, keepdims=True)

    small = padded(forget)
    lane = lax.broadcasted_iota(jnp.int32, small.shape, 1)
    small = jnp.where(lane == slots, column(gain2), jnp.where(lane == slots + 1, column(gain1), small))
    out_ref[:, :span, 2 * width :] = small.astype(bf16).reshape(groups, span, slots + pad)
    total = bias[0][...]
    for part in bias[1:]:
        total = total + part[...]
    total = padded(jnp.broadcast_to(jnp.sum(total, axis=0, keepdims=True), (16, slots)))
    upper = total.astype(bf16).astype(f32)
    row = lax.broadcasted_iota(jnp.int32, total.shape, 0)
    tail = jnp.where(row == 0, upper, jnp.where(row == 1, total - upper, 0.0)).astype(bf16)
    for g in range(groups):
        out_ref[g, span:, : 2 * width] = jnp.zeros((16, 2 * width), bf16)
        out_ref[g, span:, 2 * width :] = tail


def pack(ref, m, decay, state):
    high, low = halves(decay)
    lane = lax.broadcasted_iota(jnp.int32, decay.shape, 1)
    width = state.shape[1]
    ref[m, :, :width] = state.astype(bf16)
    ref[m, :, width:] = jnp.where(lane == 0, high.astype(f32), low.astype(f32)).astype(bf16)


def fold_kernel(parts, pieces, *refs):
    s_refs, d_refs, (s_out, d_out, sent) = refs[: parts * pieces], refs[parts * pieces : -3], refs[-3:]
    for m in range(parts):
        s, d = s_refs[m * pieces + pieces - 1][...], d_refs[m * pieces + pieces - 1][...]
        for t in reversed(range(pieces - 1)):
            here = d_refs[m * pieces + t][...]
            s, d = s_refs[m * pieces + t][...] + here[:, :1] * s, here * d
        s_out[m], d_out[m] = s, d
        pack(sent, m, d, s)


def hop_kernel(bit, after, first, final, parts, pieces, *refs):
    refs = list(refs)
    s_ref, d_ref, got_ref = refs[:3]
    refs = refs[3:]
    if not first:
        part_s_ref, part_d_ref = refs[:2]
        refs = refs[2:]
    early = (lax.axis_index("seq") & bit) == 0
    takes = early if after else jnp.logical_not(early)
    width = s_ref.shape[2]
    found = []
    for m in range(parts):
        tail = got_ref[m, :, width:].astype(f32)
        there_d, there_s = tail[:, :1] + tail[:, 1:2], got_ref[m, :, :width].astype(f32)
        s, d = s_ref[m], d_ref[m]
        there_wide = jnp.broadcast_to(there_d, d.shape)
        new_s = jnp.where(takes, s + d[:, :1] * there_s, there_s + there_d * s)
        if first:
            part_s, part_d = jnp.where(takes, there_s, 0.0), jnp.where(takes, there_wide, 1.0)
        else:
            part_s, part_d = part_s_ref[m], part_d_ref[m]
            part_s = jnp.where(takes, part_s + part_d[:, :1] * there_s, part_s)
            part_d = jnp.where(takes, part_d * there_wide, part_d)
        found.append((new_s, d * there_wide, part_s, part_d))
    if not final:
        s_out, d_out, part_s_out, part_d_out, sent = refs
        for m, (s, d, part_s, part_d) in enumerate(found):
            s_out[m], d_out[m], part_s_out[m], part_d_out[m] = s, d, part_s, part_d
            pack(sent, m, d, s)
        return
    *own, out = refs
    arriving = jnp.zeros_like(found[0][0])
    for m in reversed(range(parts)) if after else range(parts):
        s, d, part_s, part_d = found[m]
        enters = part_s + part_d[:, :1] * arriving
        arriving = s + d[:, :1] * arriving
        for t in reversed(range(pieces)) if after else range(1):
            out[m * pieces + t if after else m] = enters
            if after and t:
                here = m * pieces + t
                enters = own[here][...] + own[parts * pieces + here][:, :1] * enters


def in_vmem(name, kernel, operands, shapes):
    return pl.pallas_call(
        kernel,
        name=name,
        in_specs=[pl.BlockSpec(memory_space=pltpu.VMEM)] * len(operands),
        out_specs=[pl.BlockSpec(memory_space=pltpu.VMEM)] * len(shapes),
        out_shape=shapes,
        compiler_params=pltpu.CompilerParams(vmem_limit_bytes=12 * MIB),
        cost_estimate=cost(0, 6 * MIB),
    )(*operands)


def scan_states(n, state, decay, sent, after, own=(), pieces=1, ties=()):
    parts, slots, width = state.shape
    part, bit, hops = [], 1, 0
    while bit < n:
        got = lax.ppermute(sent, "seq", [(i, i ^ bit) for i in range(n)])
        final = 2 * bit == n
        shapes = [shaped(state.shape, f32), shaped(decay.shape, f32)] * 2 + [shaped(sent.shape, bf16)]
        if final:
            shapes = [shaped((parts * pieces, slots, width), f32)]
        if hops < len(ties) and ties[hops] is not None:
            state = ties[hops](state, got)
        results = in_vmem(
            "hop",
            functools.partial(hop_kernel, bit, after, not part, final, parts, pieces),
            [state, decay, got, *part, *(own if final else ())],
            shapes,
        )
        if final:
            return results[0]
        state, decay, *part, sent = results
        bit, hops = 2 * bit, hops + 1


def behind_of(value, *first):
    return lax.optimization_barrier((value,) + first)[0]


def join_kernel(has, *refs):
    refs = iter(refs)
    piece, outer, pair, middle, total, coming = (next(refs) if h else None for h in has)
    makes = (piece is not None, pair is not None or coming is not None, total is not None)
    new_pair, new_total, done = (next(refs) if m else None for m in makes)
    me = lax.axis_index("head")
    end = (me == 0) | (me == 3)

    def each(work):
        @pl.loop(0, TILE // 32)
        def _(i):
            work(pl.ds(pl.multiple_of(i * 32, 32), 32))

    def both(a, b, rows):
        return a[rows, :] + b[rows, :]

    @pl.when(end)
    def _():
        def work(rows):
            if coming is not None:
                new_total[rows, :] = coming[rows, :]
            if done is not None:
                done[rows, :] = outer[rows, :]

        each(work)

    @pl.when(jnp.logical_not(end))
    def _():
        def work(rows):
            if piece is not None:
                new_pair[rows, :] = both(piece, outer, rows)
            if pair is not None:
                new_total[rows, :] = both(pair, middle, rows)
            if done is not None:
                done[rows, :] = total[rows, :]

        each(work)


class Line:
    INWARD, OUTWARD, MIDDLE = [(0, 1), (3, 2)], [(1, 0), (2, 3)], [(1, 2), (2, 1)]

    def __init__(self):
        self.piece = self.pair = self.payload = None
        self.returns = False

    def load(self, piece):
        self.piece = self.payload = piece

    def step(self, inputs):
        piece, pair, payload, returns = self.piece, self.pair, self.payload, self.returns
        values = [v for v in (payload, pair) if v is not None] + inputs
        values = list(lax.optimization_barrier(tuple(values)))
        outer = middle = None
        if payload is not None:
            payload = values.pop(0)
            way = (self.INWARD if piece is not None else []) + (self.OUTWARD if returns else [])
            outer = lax.ppermute(payload, "head", way)
        if pair is not None:
            pair = values.pop(0)
            middle = lax.ppermute(pair, "head", self.MIDDLE)
        self.waiting = (piece, outer, pair, middle, payload if returns else None)
        return values

    def join(self, coming=None, after=()):
        piece, outer, pair, middle, total = self.waiting
        if after:
            outer = behind_of(outer, *after)
        if piece is None and total is None:
            outer = None
        operands = [piece, outer, pair, middle, total, coming]
        makes = [piece is not None, pair is not None or coming is not None, total is not None]
        arrays = [o for o in operands if o is not None]
        results = in_vmem(
            "join",
            functools.partial(join_kernel, [o is not None for o in operands]),
            arrays,
            [shaped(arrays[0].shape, bf16)] * sum(makes),
        )
        results = iter(results)
        self.pair, self.payload, done = (next(results) if m else None for m in makes)
        self.returns = pair is not None
        self.piece = coming
        return done


def on_device(tokens, gain_attn, w_query, w_key, w_value, w_forget, forget_bias, w_out, gain_ffn, w_gate, w_up, w_down,
              cotangent):
    parts, part_rows, width = tokens.shape
    rows = parts * part_rows
    head = w_query.shape[1]
    slots = w_forget.shape[1]
    units = w_gate.shape[1]
    n_seq, n_head = lax.axis_size("seq"), lax.axis_size("head")
    span = w_gate.shape[0]
    per_part = pieces = part_rows // TILE
    chunks = TILE // CHUNK
    every = [(m, t) for m in range(parts) for t in range(pieces)]

    x = tokens.reshape(rows, width)
    cot = cotangent.reshape(rows, width)
    gain1 = gain_attn.reshape(1, width)
    gain2 = gain_ffn.reshape(1, width)
    state_scratch = pltpu.VMEM((slots, 2 * head), f32)
    decay_scratch = pltpu.VMEM((slots, 128), f32)
    anywhere = pl.BlockSpec(memory_space=pl.ANY)
    in_place = pl.BlockSpec(memory_space=pltpu.VMEM)

    all_rows = lambda c: pl.BlockSpec((TILE, c), lambda i: (i, 0))
    by_part = lambda c: pl.BlockSpec((1, slots, c), lambda i: (i // per_part, 0, 0))
    forget_rows = w_forget.T
    xn, k, v, z, cum, inflow, local, decay, sent = call(
        "project",
        functools.partial(project_kernel, per_part),
        (rows // TILE,),
        [all_rows(width), fixed((1, width))] + [fixed((width, head))] * 2 + [fixed((slots, width)), fixed((1, slots))],
        [all_rows(width), all_rows(head), all_rows(head)] + [all_rows(slots)] * 3
        + [by_part(2 * head), by_part(128), by_part(2 * head + 128)],
        [shaped((rows, width), bf16)] + [shaped((rows, head), bf16)] * 2
        + [shaped((rows, slots), f32)] * 3 + [shaped((parts, slots, 2 * head), f32), shaped((parts, slots, 128), f32),
                                             shaped((parts, slots, 2 * head + 128), bf16)],
        [state_scratch, decay_scratch],
        cost=cost(2 * rows * width * (2 * head + slots), 2 * rows * width * 3 + 2 * width * 2 * head),
        loose_out=(6, 7, 8),
    )(x, gain1, w_key, w_value, forget_rows, forget_bias.reshape(1, slots))
    q = call(
        "query",
        query_kernel,
        (rows // TILE,),
        [all_rows(width), fixed((width, head))],
        all_rows(head),
        shaped((rows, head), bf16),
        cost=cost(2 * rows * width * head, 2 * rows * (width + head) + 2 * width * head),
    )(xn, w_query)
    stacked = []

    def stack_weights(state, got):
        gate, down, _ = lax.optimization_barrier((w_gate, w_down, got))
        stacked.append(jnp.stack([gate, w_up, down.T]))
        return state

    entering = scan_states(n_seq, local, decay, sent, False, ties=[stack_weights])
    full = lax.all_gather(stacked[0], "seq")

    def chunk_rows(m, t, columns, back):
        start = (m * pieces + t) * chunks
        return pl.BlockSpec((CHUNK, columns), lambda i: (start + (chunks - 1 - i if back else i), 0))

    def own_rows(columns, back):
        return pl.BlockSpec((CHUNK, columns), lambda i: (chunks - 1 - i if back else i, 0))

    def chunk_state(back):
        return pl.BlockSpec((1, slots, 2 * head), lambda i: (chunks - 1 - i if back else i, 0, 0))

    def whole(shape):
        return pl.BlockSpec(shape, lambda i: (0,) * len(shape))

    def state_of(m):
        return pl.BlockSpec((None, slots, 2 * head), lambda i: (m, 0, 0))

    states_shape = shaped((chunks, slots, 2 * head), f32)

    def read(m, t, entering, which):
        return call(
            "read",
            read_kernel,
            (chunks,),
            [chunk_rows(m, t, head, False)] * 3 + [chunk_rows(m, t, slots, False)] * 2
            + [state_of(which), fixed((head, width))],
            [own_rows(head, False), own_rows(slots, False), own_rows(slots, False), chunk_state(False),
             pl.BlockSpec((None, slots, 2 * head), lambda i: (0, 0, 0)), own_rows(width, False)],
            [shaped((TILE, head), bf16), shaped((TILE, slots), f32), shaped((TILE, slots), f32), states_shape,
             shaped((1, slots, 2 * head), f32), shaped((TILE, width), bf16)],
            [state_scratch],
            cost=cost(2 * TILE * head * (600 + width), 2 * TILE * (head * 4 + width) + 2 * head * width),
            loose=(5,),
            loose_out=(4, 5),
        )(q, k, v, cum, inflow, entering, w_out)

    def feed(m, t, attended):
        tile_count = pl.cdiv(units, TILE)
        vmem = pltpu.VMEM
        return call(
            "feed",
            functools.partial(feed_kernel, (m * pieces + t) * TILE),
            (),
            [anywhere, in_place, in_place, anywhere, anywhere],
            [anywhere] * 6 + [in_place],
            [shaped((TILE, width), bf16)] * 2 + [shaped((TILE, units), bf16)] * 3
            + [shaped((TILE, width), bf16)] * 2,
            [vmem((n_seq, 3, span, units), bf16), vmem((TILE, width), bf16), vmem((TILE, width), bf16),
             vmem((TILE, width), bf16), vmem((TILE, width), bf16)] + [vmem((TILE, units), bf16)] * 3
            + [vmem((TILE, width), bf16), pltpu.SemaphoreType.DMA((2,)), pltpu.SemaphoreType.DMA((6,)),
               pltpu.SemaphoreType.DMA((tile_count,))],
            cost=cost(12 * TILE * width * units, 6 * width * units + TILE * width * 14),
            vmem=44,
            loose=(1, 2),
            loose_out=(6,),
        )(x, attended, gain2, cot, full)

    group = max(1, TILE // span)
    columns = group * span
    def down_grads(acts):
        return call(
            "down_grads",
            down_grad_kernel,
            (width // columns // 2,),
            [pl.BlockSpec((rows, 2 * columns), lambda j: (0, j))] + [fixed((TILE, units))] * len(acts),
            pl.BlockSpec((2 * group, span, units), lambda j: (j, 0, 0)),
            shaped((n_seq, span, units + 2 * head), bf16),
            cost=cost(2 * rows * width * units, 2 * (rows * width + rows * units + width * units)),
        )(cot, *acts)

    def wide_grads(normed, gates, ups):
        count = len(normed)
        return call(
            "wide_grads",
            wide_grad_kernel,
            (width // columns,),
            [pl.BlockSpec((TILE, columns), lambda j: (0, j))] * count
            + [fixed((TILE, units))] * (2 * count),
            pl.BlockSpec((group, 2, span, units), lambda j: (j, 0, 0, 0)),
            shaped((n_seq, 2, span, units), bf16),
            cost=cost(4 * rows * width * units, 2 * (rows * width + 2 * rows * units + 2 * width * units)),
        )(*normed, *gates, *ups)

    def back(m, t, dhn, hidden):
        o, p, scores, e_chunks = reads[m, t][:4]
        return call(
            "back",
            back_kernel,
            (chunks,),
            [own_rows(width, True), own_rows(width, True), chunk_rows(m, t, width, True), fixed((1, width)),
             fixed((head, width))]
            + [chunk_rows(m, t, head, True)] * 3 + [chunk_rows(m, t, slots, True)] * 2 + [own_rows(slots, True)] * 2
            + [chunk_state(True)],
            [own_rows(width, True)] + [own_rows(head, True)] * 3 + [own_rows(slots, True)] * 2
            + [chunk_state(True), whole((slots, 2 * head)), whole((slots, 128)), whole((8, width))],
            [shaped((TILE, width), bf16), shaped((TILE, head), bf16),
             shaped((TILE, head), f32), shaped((TILE, head), f32), shaped((TILE, slots), f32),
             shaped((TILE, slots), f32), states_shape, shaped((slots, 2 * head), f32), shaped((slots, 128), f32),
             shaped((8, width), f32)],
            [state_scratch, decay_scratch],
            cost=cost(2 * TILE * width * head + 2 * TILE * head * 1500, TILE * width * 14 + TILE * head * 20),
            loose=(0,),
            loose_out=(7, 8),
        )(dhn, hidden, cot, gain2, w_out, q, k, v, cum, inflow, p, scores, e_chunks)

    def last(m, t, leaving, saved):
        dq, dk_local, dv_local, h_sum, x_local, g_chunks = saved
        here = m * pieces + t
        return call(
            "last",
            last_kernel,
            (chunks,),
            [state_of(here), chunk_rows(m, t, head, True), chunk_rows(m, t, head, True),
             *[chunk_rows(m, t, slots, True)] * 3, chunk_state(True), chunk_state(True), own_rows(head, True),
             own_rows(head, True), own_rows(slots, True), own_rows(slots, True), whole((TILE, head)),
             pl.BlockSpec((TILE, width), lambda i: (here, 0))] + [anywhere] * 4,
            [whole((TILE, head)), whole((TILE, head)), whole((TILE, slots)), whole((TILE, width)), whole((8, slots)),
             whole((8, width))],
            [shaped((TILE, head), bf16), shaped((TILE, head), bf16), shaped((TILE, slots), bf16),
             shaped((TILE, width), bf16), shaped((8, slots), f32), shaped((8, width), f32)],
            [state_scratch] + [pltpu.VMEM((width, head), bf16)] * 3
            + [pltpu.VMEM((slots, width), bf16), pltpu.SemaphoreType.DMA((4,))],
            cost=cost(2 * TILE * width * (3 * head + slots), TILE * width * 8 + TILE * head * 20 + width * head * 6),
            loose=(0,),
            loose_out=(3,),
        )(leaving, k, v, z, cum, inflow, reads[m, t][3], g_chunks, dk_local, dv_local, h_sum, x_local, dq, x,
          w_query, w_key, w_value, forget_rows)

    line = Line()
    live = {}

    def start():
        names = list(live)
        live.update(zip(names, line.step([live[n] for n in names])))

    def end(coming=None, done=None, after=()):
        total = line.join(coming, after)
        if done is not None:
            live[done] = total

    reads, backs, lasts = {}, {}, {}
    outs, in_grads = [None], [None]
    eighth = TILE // 2

    def into(name, kernel, m, t, kept, dtype, inputs, specs):
        spec = pl.BlockSpec((1, eighth, width), lambda i: (m, 2 * t + i, 0))
        old = [] if kept[0] is None else [kept[0]]
        kept[0] = call(
            name,
            kernel,
            (2,),
            specs + [anywhere] * len(old),
            spec,
            shaped(tokens.shape, dtype),
            cost=cost(0, TILE * width * 10),
            loose=(1,),
            aliases={len(specs): 0} if old else None,
        )(*inputs, *old)

    piece_spec = pl.BlockSpec((eighth, width), lambda i: (i, 0))

    def finish_out(m, t):
        into("out", out_kernel, m, t, outs, bf16, [live.pop(("hidden", m, t)), live.pop(("ffn", m, t))],
             [piece_spec, piece_spec])

    def finish_grad(m, t):
        x_rows = pl.BlockSpec((eighth, width), lambda i: (2 * (m * pieces + t) + i, 0))
        into("in_grad", in_grad_kernel, m, t, in_grads, f32, [backs[m, t][0], live.pop(("dxn", m, t)), x, gain1],
             [piece_spec, piece_spec, x_rows, pl.BlockSpec((1, width), lambda i: (0, 0))])

    def go_read(m, t):
        before = live["entering"] if t == 0 else live.pop("left")
        reads[m, t] = read(m, t, before, m if t == 0 else 0)
        if t + 1 < pieces:
            live["left"] = reads[m, t][4]
        return reads[m, t][5]

    def go_feed(m, t):
        made = feed(m, t, live.pop(("att", m, t)))
        for name, value in zip(("hidden", "hn", "act", "dgate", "dup", "ffn_part"), made):
            live[name, m, t] = value
        return made[6]

    def go_back(m, t):
        backs[m, t] = back(m, t, live.pop(("dhn", m, t)), live["hidden", m, t])
        live["back", m, t] = backs[m, t][7]

    def go_last(m, t):
        lasts[m, t] = last(m, t, live["leaving"], backs[m, t][1:7])
        live["dxn_part", m, t] = lasts[m, t][3]

    def taken(name):
        return [live.pop((name, *key)) for key in every]

    live["entering"] = entering
    line.load(go_read(0, 0))
    start()
    end(go_read(0, 1))
    start()
    end(go_read(1, 0))
    start()
    end(go_read(1, 1), ("att", 0, 0))
    live.pop("entering")
    start()
    end(go_feed(0, 0), ("att", 0, 1))
    start()
    end(go_feed(0, 1), ("att", 1, 0))
    start()
    end(go_feed(1, 0), ("att", 1, 1))
    start()
    end(go_feed(1, 1), ("dhn", 0, 0))
    start()
    live["wide_grads"] = wide_grads(taken("hn"), taken("dgate"), taken("dup"))
    end(live.pop(("ffn_part", 0, 0)), ("dhn", 0, 1))
    start()
    wide_shares = lax.psum_scatter(live.pop("wide_grads"), "seq", scatter_dimension=0)
    go_back(0, 0)
    go_back(0, 1)
    end(live.pop(("ffn_part", 0, 1)), ("dhn", 1, 0))
    start()
    go_back(1, 0)
    live["down"] = down_grads(taken("act"))
    end(live.pop(("ffn_part", 1, 0)), ("dhn", 1, 1))
    start()
    go_back(1, 1)
    taken("back")
    own = [backs[key][7] for key in every] + [backs[key][8] for key in every]
    folded = in_vmem(
        "fold",
        functools.partial(fold_kernel, parts, pieces),
        own,
        [shaped(local.shape, f32), shaped(decay.shape, f32), shaped(sent.shape, bf16)],
    )

    xn_columns = [pl.BlockSpec((rows, TILE), lambda j: (0, j))]
    piece_columns = [pl.BlockSpec((TILE, TILE), lambda j: (0, j))] * len(every)
    piece_whole = [fixed((TILE, head))] * len(every)
    made = []

    def beside_first(state, got):
        live["xn"] = xn
        end(behind_of(live.pop(("ffn_part", 1, 1)), got), ("ffn", 0, 0))
        start()
        made.extend((live.pop("xn"), live.pop("down")))
        return state

    def beside_second(state, got):
        grads = call(
            "query_grads",
            functools.partial(query_grad_kernel, len(every), units),
            (width // columns,),
            xn_columns + piece_columns + piece_whole * 2 + [anywhere],
            anywhere,
            shaped((n_seq, span, units + 2 * head), bf16),
            [pltpu.VMEM((2, group, span, 2 * head), bf16), pltpu.SemaphoreType.DMA((2,))],
            cost=cost(12 * rows * width * head, 3 * (4 * rows * width + 4 * rows * head + 4 * width * head)),
            aliases={1 + 3 * len(every): 0},
        )(behind_of(made[0], state), *[backs[key][0] for key in every], *[backs[key][1] for key in every],
          *[reads[key][0] for key in every], made[1])
        made.append(grads)
        return behind_of(state, grads)

    ties = [beside_first, beside_second]
    live["leaving"] = scan_states(n_seq, *folded, True, own, pieces, ties)
    live["query_grads"], live["wide"] = made[2], wide_shares
    go_last(0, 0)
    end(live.pop(("dxn_part", 0, 0)), ("ffn", 0, 1))
    start()
    wide_shares = live.pop("wide")
    down_shares = lax.psum_scatter(live.pop("query_grads"), "seq", scatter_dimension=0)
    go_last(0, 1)
    go_last(1, 0)
    live["xn"] = xn
    end(live.pop(("dxn_part", 0, 1)), ("ffn", 1, 0))
    start()
    go_last(1, 1)
    live.pop("leaving")
    few = [pl.BlockSpec((8, TILE), lambda j: (0, j))] * len(every)
    live["state_grads"] = call(
        "state_grads",
        functools.partial(state_grad_kernel, len(every)),
        (width // TILE,),
        xn_columns + piece_whole * 2 + [fixed((TILE, slots))] * len(every) + [fixed((8, slots))] * len(every) + few * 2,
        pl.BlockSpec((group, span + 16, 2 * head + 128), lambda j: (j, 0, 0)),
        shaped((n_seq, span + 16, 2 * head + 128), bf16),
        cost=cost(4 * rows * width * head, 2 * rows * width + 4 * rows * head + 4 * width * head),
    )(live.pop("xn"), *[lasts[key][i] for i in (0, 1, 2, 4, 5) for key in every], *[backs[key][9] for key in every])
    end(live.pop(("dxn_part", 1, 0)), ("ffn", 1, 1))
    start()
    attn_shares = lax.psum_scatter(live.pop("state_grads"), "seq", scatter_dimension=0)
    finish_out(0, 0)
    finish_out(0, 1)
    live["out"], live["down"] = outs[0], down_shares
    end(live.pop(("dxn_part", 1, 1)), ("dxn", 0, 0))
    start()
    outs[0], down_shares = live.pop("out"), live.pop("down")
    finish_out(1, 0)
    finish_out(1, 1)
    finish_grad(0, 0)
    live["out"], live["in_grad"] = outs[0], in_grads[0]
    end(None, ("dxn", 0, 1))
    start()
    in_grads[0] = live.pop("in_grad")
    finish_grad(0, 1)
    live["in_grad"] = in_grads[0]
    end(None, ("dxn", 1, 0))
    start()
    in_grads[0] = live.pop("in_grad")
    late = behind_of(attn_shares, in_grads[0]).astype(f32)
    gain1_total = late[:span, 2 * head + slots + 1]
    others = [lax.ppermute(gain1_total, "head", [(i, i ^ d) for i in range(n_head)]) for d in (1, 2, 3)]
    gain1_total = (gain1_total + others[0]) + (others[1] + others[2])
    finish_grad(1, 0)
    end(None, ("dxn", 1, 1), (gain1_total, in_grads[0]))
    finish_grad(1, 1)
    small_shares = late[:, 2 * head :]
    query_shares = down_shares[:, units:].astype(f32)

    return (
        live["out"],
        in_grads[0],
        gain1_total,
        query_shares[:, :head],
        late[:span, :head],
        late[:span, head : 2 * head],
        small_shares[:span, :slots],
        small_shares[span, :slots] + small_shares[span + 1, :slots],
        query_shares[:, head:].T,
        small_shares[:span, slots],
        wide_shares[0].astype(f32),
        wide_shares[1].astype(f32),
        down_shares[:, :units].astype(f32).T,
    )


def solution(mesh):
    rows, both = P(None, "seq", None), P("seq", "head")
    by_head, down = P(None, "head"), P("head", "seq")
    return jax.shard_map(
        on_device,
        mesh=mesh,
        in_specs=(rows, P(), by_head, by_head, by_head, by_head, P("head"), P("head", None), P(), both, both, down, rows),
        out_specs=(rows, rows, P("seq"), both, both, both, both, P("head"), down, P("seq"), both, both, down),
        check_vma=False,
    )
```

```python
import functools

import jax
import jax.numpy as jnp
from jax import lax
from jax.experimental import pallas as pl
from jax.experimental.pallas import tpu as pltpu
from jax.sharding import PartitionSpec as P

CHUNK = 128
TILE = 256
EPS = 1e-06
RATE = 0.5
MIB = 2**20
f32 = jnp.float32
bf16 = jnp.bfloat16
highest = lax.Precision.HIGHEST


def nn(a, b):
    return lax.dot_general(a, b, (((1,), (0,)), ((), ())), preferred_element_type=f32)


def nt(a, b):
    return lax.dot_general(a, b, (((1,), (1,)), ((), ())), preferred_element_type=f32)


def tn(a, b):
    return lax.dot_general(a, b, (((0,), (0,)), ((), ())), preferred_element_type=f32)


def exact(a, b, dims):
    return lax.dot_general(a, b, (dims, ((), ())), precision=highest, preferred_element_type=f32)


def halves(a):
    high = a.astype(bf16)
    return high, (a - high.astype(f32)).astype(bf16)


def call(name, kernel, grid, in_specs, out_specs, out_shape, scratch=(), vmem=24, cost=None, loose=(), loose_out=(),
         aliases=None):
    single = not isinstance(out_shape, list)
    shapes = [out_shape] if single else out_shape
    shapes = [s if i in loose_out else pltpu.HBM(s.shape, s.dtype) for i, s in enumerate(shapes)]
    function = pl.pallas_call(
        kernel,
        name=name,
        grid=grid,
        in_specs=in_specs,
        out_specs=out_specs,
        out_shape=shapes[0] if single else shapes,
        scratch_shapes=scratch,
        input_output_aliases=aliases or {},
        compiler_params=pltpu.CompilerParams(
            dimension_semantics=("arbitrary",) * len(grid), vmem_limit_bytes=vmem * MIB
        ),
        cost_estimate=cost,
    )

    def run(*operands):
        return function(*[
            o if i in loose or spec.memory_space == pltpu.SMEM else pltpu.with_memory_space_constraint(o, pltpu.HBM)
            for i, (o, spec) in enumerate(zip(operands, in_specs))
        ])

    return run


def cost(flops, data):
    return pl.CostEstimate(flops=int(flops), bytes_accessed=int(data), transcendentals=0)


def fixed(shape):
    zeros = (0,) * len(shape)
    return pl.BlockSpec(shape, lambda *_: zeros, pipeline_mode=pl.Buffered(1))


def shaped(shape, dtype):
    return jax.ShapeDtypeStruct(shape, dtype)


def triangle(lower):
    r = lax.broadcasted_iota(jnp.int32, (CHUNK, CHUNK), 0)
    c = lax.broadcasted_iota(jnp.int32, (CHUNK, CHUNK), 1)
    return r >= c if lower else r <= c


def gates(z):
    la = -RATE * lax.logistic(-z)
    y = -la
    taken = jnp.ones_like(y)
    for n in range(9, 1, -1):
        taken = 1.0 - y * (1.0 / n) * taken
    taken = y * taken
    cum = exact(triangle(True).astype(f32), la, ((1,), (0,)))
    return cum, jnp.exp(-cum) * taken


def turned_last(cum):
    return jnp.broadcast_to(cum[CHUNK - 1 :, :], cum.shape).T


def halves_sum(ones, values):
    high, low = halves(values)
    both = nn(ones.astype(bf16), jnp.concatenate([high, low], 1))
    width = values.shape[1]
    return both[:, :width] + both[:, width:]


def project_kernel(per_part, x_ref, gain_ref, wk_ref, wv_ref, wf_ref, bias_ref,
                   xn_ref, k_ref, v_ref, z_ref, cum_ref, in_ref, s_ref, d_ref, sent_ref, state, decay, wk, wv, sems):
    first = pl.program_id(0) == 0
    loads = [pltpu.make_async_copy(wk_ref, wk, sems.at[0]), pltpu.make_async_copy(wv_ref, wv, sems.at[1])]

    @pl.when(first)
    def _():
        for load in loads:
            load.start()

    @pl.when(lax.rem(pl.program_id(0), per_part) == 0)
    def _():
        state[...] = jnp.zeros_like(state)
        decay[...] = jnp.zeros_like(decay)

    x = x_ref[...].astype(f32)
    r1 = lax.rsqrt(jnp.mean(x * x, axis=-1, keepdims=True) + EPS)
    xn = (x * r1 * gain_ref[...]).astype(bf16)
    xn_ref[...] = xn

    @pl.when(first)
    def _():
        for load in loads:
            load.wait()

    k_ref[...] = nn(xn, wk[...]).astype(bf16)
    v_ref[...] = nn(xn, wv[...]).astype(bf16)
    z_ref[...] = nt(xn, wf_ref[...]) + bias_ref[...]
    width = k_ref.shape[1]
    for c in range(x_ref.shape[0] // CHUNK):
        rows = pl.ds(c * CHUNK, CHUNK)
        cum, inflow = gates(z_ref[rows, :])
        cum_ref[rows, :] = cum
        in_ref[rows, :] = inflow
        total = turned_last(cum)
        spread = inflow.astype(bf16)
        keep = jnp.exp(total[:, :1])
        state[:, :width] = keep * (state[:, :width] + tn(spread, k_ref[rows, :]))
        state[:, width:] = keep * (state[:, width:] + tn(spread, v_ref[rows, :]))
        decay[...] += total
    s_ref[0] = state[...]
    d_ref[0] = jnp.exp(decay[...])
    pack(sent_ref, 0, jnp.exp(decay[...]), state[...])


def query_kernel(xn_ref, wq_ref, q_ref):
    q_ref[...] = nn(xn_ref[...], wq_ref[...]).astype(bf16)


def read_kernel(q_ref, k_ref, v_ref, cum_ref, in_ref, e0_ref, wo_ref, o_ref, p_ref, sc_ref, e_ref, left_ref, att_ref,
                state, wo, sem):
    first = pl.program_id(0) == 0
    load = pltpu.make_async_copy(wo_ref, wo, sem.at[0])

    @pl.when(first)
    def _():
        load.start()
        state[...] = e0_ref[...]

    width = q_ref.shape[1]
    lower = triangle(True)
    q, k, v = q_ref[...], k_ref[...], v_ref[...]
    cum, inflow = cum_ref[...], in_ref[...]
    total = turned_last(cum)
    growth = jnp.exp(cum)
    e_ref[0] = state[...]
    i_hi, i_lo = halves(inflow)
    a_hi, a_lo = halves(jnp.where(lower, nt(q, k), 0.0))
    e_hi, e_lo = halves(state[:, :width])
    scores = growth * (nt(q, e_hi) + nt(q, e_lo) + nn(a_hi, i_hi) + (nn(a_hi, i_lo) + nn(a_lo, i_hi)))
    top = jnp.exp(scores - jnp.max(scores, axis=-1, keepdims=True))
    p = top / jnp.sum(top, axis=-1, keepdims=True)
    w = (p * growth).astype(bf16)
    mixing = jnp.where(lower, nt(w, i_hi), 0.0).astype(bf16)
    o = (nn(w, state[:, width:].astype(bf16)) + nn(mixing, v)).astype(bf16)
    o_ref[...] = o

    @pl.when(first)
    def _():
        load.wait()

    att_ref[...] = nn(o, wo[...]).astype(bf16)
    p_ref[...] = p
    sc_ref[...] = scores
    keep = jnp.exp(total[:, :1])
    state[:, :width] = keep * (state[:, :width] + tn(i_hi, k))
    state[:, width:] = keep * (state[:, width:] + tn(i_hi, v))
    left_ref[...] = state[...]


def back_kernel(dhn_ref, hid_ref, cot_ref, gain_ref, wo_ref, q_ref, k_ref, v_ref, cum_ref, in_ref, p_ref, sc_ref,
                e_ref, datt_ref, dq_ref, dkl_ref, dvl_ref, h_ref, x1_ref, g_ref, s_ref, d_ref, gg_ref, state, decay,
                wo, sem):
    step = pl.program_id(0)
    load = pltpu.make_async_copy(wo_ref, wo, sem.at[0])

    @pl.when(step == 0)
    def _():
        load.start()
        state[...] = jnp.zeros_like(state)
        decay[...] = jnp.zeros_like(decay)
        gg_ref[...] = jnp.zeros_like(gg_ref)

    hidden = hid_ref[...].astype(f32)
    dhn = dhn_ref[...].astype(f32)
    r2 = lax.rsqrt(jnp.mean(hidden * hidden, axis=-1, keepdims=True) + EPS)
    gg_ref[...] += jnp.sum((dhn * hidden * r2).reshape(-1, 8, hidden.shape[1]), axis=0)
    u2 = gain_ref[...] * dhn
    dhid = (
        cot_ref[...].astype(f32)
        + r2 * u2
        - hidden * (r2 * r2 * r2) * jnp.mean(u2 * hidden, axis=-1, keepdims=True)
    )
    datt = dhid.astype(bf16)
    datt_ref[...] = datt
    width = q_ref.shape[1]

    @pl.when(step == 0)
    def _():
        load.wait()

    do = nt(datt, wo[...]).astype(bf16)
    lower, upper = triangle(True), triangle(False)
    q, k, v = q_ref[...], k_ref[...], v_ref[...]
    cum, inflow = cum_ref[...], in_ref[...]
    total = turned_last(cum)
    growth = jnp.exp(cum)
    p = p_ref[...]
    i_hi, i_lo = halves(inflow)
    b_hi, b_lo = halves(jnp.where(lower, nt(do, v), 0.0))
    ev_hi, ev_lo = halves(e_ref[0, :, width:])
    dp = growth * (nt(do, ev_hi) + nt(do, ev_lo) + nn(b_hi, i_hi) + (nn(b_hi, i_lo) + nn(b_lo, i_hi)))
    ds = p * (dp - jnp.sum(p * dp, axis=-1, keepdims=True))
    w = (p * growth).astype(bf16)
    gds = (growth * ds).astype(bf16)
    n = jnp.where(lower, nt(gds, i_hi), 0.0).astype(bf16)
    dq_ref[...] = (nn(gds, e_ref[0, :, :width].astype(bf16)) + nn(n, k)).astype(bf16)
    n_t = jnp.where(upper, nt(i_hi, gds), 0.0).astype(bf16)
    m_t = jnp.where(upper, nt(i_hi, w), 0.0).astype(bf16)
    dkl_ref[...] = nn(n_t, q)
    dvl_ref[...] = nn(m_t, do)
    h_ref[...] = ds * sc_ref[...] + p * dp
    a_t = jnp.where(upper, nt(k, q), 0.0).astype(bf16)
    b_t = jnp.where(upper, nt(v, do), 0.0).astype(bf16)
    x1_ref[...] = nn(a_t, gds) + nn(b_t, w)
    keep = jnp.exp(total[:, :1])
    g_k, g_v = tn(gds, q), tn(w, do)
    g_ref[0, :, :width] = g_k
    g_ref[0, :, width:] = g_v
    state[:, :width] = g_k + keep * state[:, :width]
    state[:, width:] = g_v + keep * state[:, width:]
    decay[...] += total
    s_ref[...] = state[...]
    d_ref[...] = jnp.exp(decay[...])


def last_kernel(l0_ref, k_ref, v_ref, z_ref, cum_ref, in_ref, e_ref, g_ref, dkl_ref, dvl_ref, h_ref, x1_ref, dq_ref, x_ref,
                wq_ref, wk_ref, wv_ref, wf_ref, dk_ref, dv_ref, dz_ref, dxn_ref, bias_ref, gg_ref,
                state, wq, wk, wv, wf, sems):
    step, steps = pl.program_id(0), pl.num_programs(0)
    loads = [pltpu.make_async_copy(source, target, sems.at[i])
             for i, (source, target) in enumerate(((wq_ref, wq), (wk_ref, wk), (wv_ref, wv), (wf_ref, wf)))]

    @pl.when(step == 0)
    def _():
        for load in loads:
            load.start()
        state[...] = l0_ref[...]
        bias_ref[...] = jnp.zeros_like(bias_ref)

    width = k_ref.shape[1]
    k, v, z = k_ref[...], v_ref[...], z_ref[...]
    cum, inflow = cum_ref[...], in_ref[...]
    total = turned_last(cum)
    i_hi = inflow.astype(bf16)
    keep = jnp.exp(total[:, :1])
    lg = keep * state[...]
    lg_k, lg_v = lg[:, :width].astype(bf16), lg[:, width:].astype(bf16)
    rows = pl.ds(pl.multiple_of((steps - 1 - step) * CHUNK, CHUNK), CHUNK)
    dk_ref[rows, :] = (dkl_ref[...] + nn(i_hi, lg_k)).astype(bf16)
    dv_ref[rows, :] = (dvl_ref[...] + nn(i_hi, lg_v)).astype(bf16)
    x1 = x1_ref[...]
    x2 = nt(k, lg_k) + nt(v, lg_v)
    met = jnp.broadcast_to(jnp.sum(lg * e_ref[0], axis=1, keepdims=True), (lg.shape[0], CHUNK)).T
    h, r1 = h_ref[...], inflow * x1
    dla = (
        halves_sum(triangle(False), h - r1)
        + r1
        + halves_sum(triangle(True), inflow * x2)
        + met
        - jnp.exp(-cum) * (x1 + x2)
    )
    rate = lax.logistic(-z)
    dz = (dla * RATE * rate * (1.0 - rate)).astype(bf16)
    dz_ref[rows, :] = dz
    bias_ref[...] += jnp.sum(dz.astype(f32).reshape(-1, 8, dz.shape[1]), axis=0)
    state[...] = g_ref[0] + lg

    @pl.when(step == steps - 1)
    def _():
        for load in loads:
            load.wait()
        dxn = nt(dq_ref[...], wq[...]) + nt(dk_ref[...], wk[...]) + nt(dv_ref[...], wv[...]) + nn(dz_ref[...], wf[...])
        dxn_ref[...] = dxn.astype(bf16)
        x = x_ref[...].astype(f32)
        r1 = lax.rsqrt(jnp.mean(x * x, axis=-1, keepdims=True) + EPS)
        gg_ref[...] = jnp.sum((dxn * x * r1).reshape(-1, 8, x.shape[1]), axis=0)


def out_kernel(hid_ref, ffn_ref, *refs):
    refs[-1][0] = (hid_ref[...].astype(f32) + ffn_ref[...].astype(f32)).astype(bf16)


def in_grad_kernel(dhid_ref, dxn_ref, x_ref, gain_ref, *refs):
    x = x_ref[...].astype(f32)
    r1 = lax.rsqrt(jnp.mean(x * x, axis=-1, keepdims=True) + EPS)
    u1 = gain_ref[...] * dxn_ref[...].astype(f32)
    refs[-1][0] = dhid_ref[...].astype(f32) + r1 * u1 - x * (r1 * r1 * r1) * jnp.mean(u1 * x, axis=-1, keepdims=True)


def feed_kernel(first_row, x_ref, att_ref, gain_ref, cot_ref, full_ref, hid_ref, hn_ref, act_ref, dg_ref, du_ref,
                ffn_ref, dhn_ref, weights, x, cot, hid, hn, act, dg, du, ffn, in_sems, out_sems, weight_sems):
    rows, width = x.shape
    units = act.shape[1]
    blocks, _, span, _ = weights.shape
    tiles = [(u, min(TILE, units - u)) for u in range(0, units, TILE)]
    here = pl.ds(first_row, rows)
    reads = [pltpu.make_async_copy(source.at[here, :], target, in_sems.at[i])
             for i, (source, target) in enumerate(((x_ref, x), (cot_ref, cot)))]
    loads = [pltpu.make_async_copy(full_ref.at[:, :, :, pl.ds(u, size)], weights.at[:, :, :, pl.ds(u, size)],
                                   weight_sems.at[i]) for i, (u, size) in enumerate(tiles)]
    writes = [pltpu.make_async_copy(source, target, out_sems.at[i])
              for i, (source, target) in enumerate(
                  ((hid, hid_ref), (hn, hn_ref), (act, act_ref), (dg, dg_ref), (du, du_ref), (ffn, ffn_ref)))]
    for copy in reads + loads:
        copy.start()
    for copy in reads:
        copy.wait()
    hidden = x[...].astype(f32) + att_ref[...].astype(f32)
    hid[...] = hidden.astype(bf16)
    r2 = lax.rsqrt(jnp.mean(hidden * hidden, axis=-1, keepdims=True) + EPS)
    hn[...] = (hidden * r2 * gain_ref[...]).astype(bf16)
    writes[0].start()
    writes[1].start()
    for (u, size), load in zip(tiles, loads):
        load.wait()
        gate, up, dact = (
            nn(left[...], weights[:, i, :, u : u + size].reshape(width, size))
            for i, left in enumerate((hn, hn, cot))
        )
        s = lax.logistic(gate)
        silu = gate * s
        act[:, u : u + size] = (silu * up).astype(bf16)
        dg[:, u : u + size] = (dact * up * s * (1.0 + gate * (1.0 - s))).astype(bf16)
        du[:, u : u + size] = (dact * silu).astype(bf16)
    for write in writes[2:5]:
        write.start()
    group = max(1, TILE // span)
    for b in range(0, blocks, group):
        columns = slice(b * span, (b + group) * span)
        w_gate, w_up, w_down = (weights[b : b + group, i].reshape(group * span, units) for i in range(3))
        ffn[:, columns] = nt(act[...], w_down).astype(bf16)
        dhn_ref[:, columns] = (nt(dg[...], w_gate) + nt(du[...], w_up)).astype(bf16)
    writes[5].start()
    for write in writes:
        write.wait()


def summed(pairs):
    total = tn(*pairs[0])
    for pair in pairs[1:]:
        total = total + tn(*pair)
    return total.astype(bf16)


def down_grad_kernel(*refs):
    cot_ref, act, out_ref = refs[0], refs[1:-1], refs[-1]
    rows = act[0].shape[0]
    block = summed([(cot_ref[i * rows : (i + 1) * rows, :], a[...]) for i, a in enumerate(act)])
    out_ref[...] = block.reshape(out_ref.shape)


def wide_grad_kernel(*refs):
    out_ref = refs[-1]
    count = (len(refs) - 1) // 3
    hn, dg, du = refs[:count], refs[count : 2 * count], refs[2 * count : 3 * count]
    blocks, _, width, units = out_ref.shape
    for i, grads in enumerate((dg, du)):
        block = summed([(h[...], g[...]) for h, g in zip(hn, grads)])
        out_ref[:, i] = block.reshape(blocks, width, units)


def query_grad_kernel(count, first_column, *refs):
    xn_ref, out_ref, block, sems = refs[0], refs[-3], refs[-2], refs[-1]
    datt, dq, o = (refs[1 + i * count : 1 + (i + 1) * count] for i in range(3))
    rows, width = dq[0].shape
    _, groups, span, columns = block.shape
    step, steps = pl.program_id(0), pl.num_programs(0)

    def copy(at):
        slot = lax.rem(at, 2)
        return pltpu.make_async_copy(
            block.at[slot], out_ref.at[pl.ds(at * groups, groups), :, pl.ds(first_column, columns)], sems.at[slot]
        )

    @pl.when(step >= 2)
    def _():
        copy(step - 2).wait()

    xn = [xn_ref[i * rows : (i + 1) * rows, :] for i in range(count)]
    slot = lax.rem(step, 2)
    query = summed([(x, g[...]) for x, g in zip(xn, dq)])
    block[slot, :, :, :width] = query.reshape(groups, span, width)
    output = summed([(d[...], r[...]) for d, r in zip(datt, o)])
    block[slot, :, :, width:] = output.reshape(groups, span, width)
    copy(step).start()

    @pl.when(step == steps - 1)
    def _():
        copy(step - 1).wait()
        copy(step).wait()


def state_grad_kernel(count, *refs):
    xn_ref, out_ref = refs[0], refs[-1]
    dk, dv, dz, bias, gain1, gain2 = (refs[1 + i * count : 1 + (i + 1) * count] for i in range(6))
    rows, width = dk[0].shape
    slots = dz[0].shape[1]
    groups, high, _ = out_ref.shape
    span = high - 16
    xn = [xn_ref[i * rows : (i + 1) * rows, :] for i in range(count)]
    for i, grads in enumerate((dk, dv)):
        block = summed([(x, g[...]) for x, g in zip(xn, grads)])
        out_ref[:, :span, i * width : (i + 1) * width] = block.reshape(groups, span, width)
    forget = tn(xn[0], dz[0][...])
    for x, g in zip(xn[1:], dz[1:]):
        forget = forget + tn(x, g[...])
    pad = 128 - slots % 128

    def padded(values):
        return jnp.concatenate([values, jnp.zeros((values.shape[0], pad), f32)], 1)

    def column(parts):
        total = parts[0][...]
        for part in parts[1:]:
            total = total + part[...]
        return jnp.sum(total.T, axis=1, keepdims=True)

    small = padded(forget)
    lane = lax.broadcasted_iota(jnp.int32, small.shape, 1)
    small = jnp.where(lane == slots, column(gain2), jnp.where(lane == slots + 1, column(gain1), small))
    out_ref[:, :span, 2 * width :] = small.astype(bf16).reshape(groups, span, slots + pad)
    total = bias[0][...]
    for part in bias[1:]:
        total = total + part[...]
    total = padded(jnp.broadcast_to(jnp.sum(total, axis=0, keepdims=True), (16, slots)))
    upper = total.astype(bf16).astype(f32)
    row = lax.broadcasted_iota(jnp.int32, total.shape, 0)
    tail = jnp.where(row == 0, upper, jnp.where(row == 1, total - upper, 0.0)).astype(bf16)
    for g in range(groups):
        out_ref[g, span:, : 2 * width] = jnp.zeros((16, 2 * width), bf16)
        out_ref[g, span:, 2 * width :] = tail


def pack(ref, m, decay, state):
    high, low = halves(decay)
    lane = lax.broadcasted_iota(jnp.int32, decay.shape, 1)
    width = state.shape[1]
    ref[m, :, :width] = state.astype(bf16)
    ref[m, :, width:] = jnp.where(lane == 0, high.astype(f32), low.astype(f32)).astype(bf16)


def fold_kernel(parts, pieces, *refs):
    s_refs, d_refs, (s_out, d_out, sent) = refs[: parts * pieces], refs[parts * pieces : -3], refs[-3:]
    for m in range(parts):
        s, d = s_refs[m * pieces + pieces - 1][...], d_refs[m * pieces + pieces - 1][...]
        for t in reversed(range(pieces - 1)):
            here = d_refs[m * pieces + t][...]
            s, d = s_refs[m * pieces + t][...] + here[:, :1] * s, here * d
        s_out[m], d_out[m] = s, d
        pack(sent, m, d, s)


def hop_kernel(bit, after, first, final, parts, pieces, *refs):
    refs = list(refs)
    s_ref, d_ref, got_ref = refs[:3]
    refs = refs[3:]
    if not first:
        part_s_ref, part_d_ref = refs[:2]
        refs = refs[2:]
    early = (lax.axis_index("seq") & bit) == 0
    takes = early if after else jnp.logical_not(early)
    width = s_ref.shape[2]
    found = []
    for m in range(parts):
        tail = got_ref[m, :, width:].astype(f32)
        there_d, there_s = tail[:, :1] + tail[:, 1:2], got_ref[m, :, :width].astype(f32)
        s, d = s_ref[m], d_ref[m]
        there_wide = jnp.broadcast_to(there_d, d.shape)
        new_s = jnp.where(takes, s + d[:, :1] * there_s, there_s + there_d * s)
        if first:
            part_s, part_d = jnp.where(takes, there_s, 0.0), jnp.where(takes, there_wide, 1.0)
        else:
            part_s, part_d = part_s_ref[m], part_d_ref[m]
            part_s = jnp.where(takes, part_s + part_d[:, :1] * there_s, part_s)
            part_d = jnp.where(takes, part_d * there_wide, part_d)
        found.append((new_s, d * there_wide, part_s, part_d))
    if not final:
        s_out, d_out, part_s_out, part_d_out, sent = refs
        for m, (s, d, part_s, part_d) in enumerate(found):
            s_out[m], d_out[m], part_s_out[m], part_d_out[m] = s, d, part_s, part_d
            pack(sent, m, d, s)
        return
    *own, out = refs
    arriving = jnp.zeros_like(found[0][0])
    for m in reversed(range(parts)) if after else range(parts):
        s, d, part_s, part_d = found[m]
        enters = part_s + part_d[:, :1] * arriving
        arriving = s + d[:, :1] * arriving
        for t in reversed(range(pieces)) if after else range(1):
            out[m * pieces + t if after else m] = enters
            if after and t:
                here = m * pieces + t
                enters = own[here][...] + own[parts * pieces + here][:, :1] * enters


def in_vmem(name, kernel, operands, shapes):
    return pl.pallas_call(
        kernel,
        name=name,
        in_specs=[pl.BlockSpec(memory_space=pltpu.VMEM)] * len(operands),
        out_specs=[pl.BlockSpec(memory_space=pltpu.VMEM)] * len(shapes),
        out_shape=shapes,
        compiler_params=pltpu.CompilerParams(vmem_limit_bytes=12 * MIB),
        cost_estimate=cost(0, 6 * MIB),
    )(*operands)


def scan_states(n, state, decay, sent, after, own=(), pieces=1, ties=()):
    parts, slots, width = state.shape
    part, bit, hops = [], 1, 0
    while bit < n:
        got = lax.ppermute(sent, "seq", [(i, i ^ bit) for i in range(n)])
        final = 2 * bit == n
        shapes = [shaped(state.shape, f32), shaped(decay.shape, f32)] * 2 + [shaped(sent.shape, bf16)]
        if final:
            shapes = [shaped((parts * pieces, slots, width), f32)]
        if hops < len(ties) and ties[hops] is not None:
            state = ties[hops](state, got)
        results = in_vmem(
            "hop",
            functools.partial(hop_kernel, bit, after, not part, final, parts, pieces),
            [state, decay, got, *part, *(own if final else ())],
            shapes,
        )
        if final:
            return results[0]
        state, decay, *part, sent = results
        bit, hops = 2 * bit, hops + 1


def behind_of(value, *first):
    return lax.optimization_barrier((value,) + first)[0]


def join_kernel(has, *refs):
    refs = iter(refs)
    piece, outer, pair, middle, total, coming = (next(refs) if h else None for h in has)
    makes = (piece is not None, pair is not None or coming is not None, total is not None)
    new_pair, new_total, done = (next(refs) if m else None for m in makes)
    me = lax.axis_index("head")
    end = (me == 0) | (me == 3)

    def each(work):
        @pl.loop(0, TILE // 32)
        def _(i):
            work(pl.ds(pl.multiple_of(i * 32, 32), 32))

    def both(a, b, rows):
        return a[rows, :] + b[rows, :]

    @pl.when(end)
    def _():
        def work(rows):
            if coming is not None:
                new_total[rows, :] = coming[rows, :]
            if done is not None:
                done[rows, :] = outer[rows, :]

        each(work)

    @pl.when(jnp.logical_not(end))
    def _():
        def work(rows):
            if piece is not None:
                new_pair[rows, :] = both(piece, outer, rows)
            if pair is not None:
                new_total[rows, :] = both(pair, middle, rows)
            if done is not None:
                done[rows, :] = total[rows, :]

        each(work)


class Line:
    INWARD, OUTWARD, MIDDLE = [(0, 1), (3, 2)], [(1, 0), (2, 3)], [(1, 2), (2, 1)]

    def __init__(self):
        self.piece = self.pair = self.payload = None
        self.returns = False

    def load(self, piece):
        self.piece = self.payload = piece

    def step(self, inputs):
        piece, pair, payload, returns = self.piece, self.pair, self.payload, self.returns
        values = [v for v in (payload, pair) if v is not None] + inputs
        values = list(lax.optimization_barrier(tuple(values)))
        outer = middle = None
        if payload is not None:
            payload = values.pop(0)
            way = (self.INWARD if piece is not None else []) + (self.OUTWARD if returns else [])
            outer = lax.ppermute(payload, "head", way)
        if pair is not None:
            pair = values.pop(0)
            middle = lax.ppermute(pair, "head", self.MIDDLE)
        self.waiting = (piece, outer, pair, middle, payload if returns else None)
        return values

    def join(self, coming=None, after=()):
        piece, outer, pair, middle, total = self.waiting
        if after:
            outer = behind_of(outer, *after)
        if piece is None and total is None:
            outer = None
        operands = [piece, outer, pair, middle, total, coming]
        makes = [piece is not None, pair is not None or coming is not None, total is not None]
        arrays = [o for o in operands if o is not None]
        results = in_vmem(
            "join",
            functools.partial(join_kernel, [o is not None for o in operands]),
            arrays,
            [shaped(arrays[0].shape, bf16)] * sum(makes),
        )
        results = iter(results)
        self.pair, self.payload, done = (next(results) if m else None for m in makes)
        self.returns = pair is not None
        self.piece = coming
        return done


def on_device(tokens, gain_attn, w_query, w_key, w_value, w_forget, forget_bias, w_out, gain_ffn, w_gate, w_up, w_down,
              cotangent):
    parts, part_rows, width = tokens.shape
    rows = parts * part_rows
    head = w_query.shape[1]
    slots = w_forget.shape[1]
    units = w_gate.shape[1]
    n_seq, n_head = lax.axis_size("seq"), lax.axis_size("head")
    span = w_gate.shape[0]
    per_part = pieces = part_rows // TILE
    chunks = TILE // CHUNK
    every = [(m, t) for m in range(parts) for t in range(pieces)]

    x = tokens.reshape(rows, width)
    cot = cotangent.reshape(rows, width)
    gain1 = gain_attn.reshape(1, width)
    gain2 = gain_ffn.reshape(1, width)
    state_scratch = pltpu.VMEM((slots, 2 * head), f32)
    decay_scratch = pltpu.VMEM((slots, 128), f32)
    anywhere = pl.BlockSpec(memory_space=pl.ANY)
    in_place = pl.BlockSpec(memory_space=pltpu.VMEM)

    all_rows = lambda c: pl.BlockSpec((TILE, c), lambda i: (i, 0))
    by_part = lambda c: pl.BlockSpec((1, slots, c), lambda i: (i // per_part, 0, 0))
    forget_rows = w_forget.T
    xn, k, v, z, cum, inflow, local, decay, sent = call(
        "project",
        functools.partial(project_kernel, per_part),
        (rows // TILE,),
        [all_rows(width), fixed((1, width))] + [anywhere] * 2 + [fixed((slots, width)), fixed((1, slots))],
        [all_rows(width), all_rows(head), all_rows(head)] + [all_rows(slots)] * 3
        + [by_part(2 * head), by_part(128), by_part(2 * head + 128)],
        [shaped((rows, width), bf16)] + [shaped((rows, head), bf16)] * 2
        + [shaped((rows, slots), f32)] * 3 + [shaped((parts, slots, 2 * head), f32), shaped((parts, slots, 128), f32),
                                             shaped((parts, slots, 2 * head + 128), bf16)],
        [state_scratch, decay_scratch] + [pltpu.VMEM((width, head), bf16)] * 2 + [pltpu.SemaphoreType.DMA((2,))],
        cost=cost(2 * rows * width * (2 * head + slots), 2 * rows * width * 3 + 2 * width * 2 * head),
        loose_out=(6, 7, 8),
    )(x, gain1, w_key, w_value, forget_rows, forget_bias.reshape(1, slots))
    q = call(
        "query",
        query_kernel,
        (rows // TILE,),
        [all_rows(width), fixed((width, head))],
        all_rows(head),
        shaped((rows, head), bf16),
        cost=cost(2 * rows * width * head, 2 * rows * (width + head) + 2 * width * head),
    )(xn, w_query)
    stacked = []

    def stack_weights(state, got):
        gate, down, _ = lax.optimization_barrier((w_gate, w_down, got))
        stacked.append(jnp.stack([gate, w_up, down.T]))
        return state

    entering = scan_states(n_seq, local, decay, sent, False, ties=[stack_weights])
    full = lax.all_gather(stacked[0], "seq")

    def chunk_rows(m, t, columns, back):
        start = (m * pieces + t) * chunks
        return pl.BlockSpec((CHUNK, columns), lambda i: (start + (chunks - 1 - i if back else i), 0))

    def own_rows(columns, back):
        return pl.BlockSpec((CHUNK, columns), lambda i: (chunks - 1 - i if back else i, 0))

    def chunk_state(back):
        return pl.BlockSpec((1, slots, 2 * head), lambda i: (chunks - 1 - i if back else i, 0, 0))

    def whole(shape):
        return pl.BlockSpec(shape, lambda i: (0,) * len(shape))

    def state_of(m):
        return pl.BlockSpec((None, slots, 2 * head), lambda i: (m, 0, 0))

    states_shape = shaped((chunks, slots, 2 * head), f32)

    def read(m, t, entering, which):
        return call(
            "read",
            read_kernel,
            (chunks,),
            [chunk_rows(m, t, head, False)] * 3 + [chunk_rows(m, t, slots, False)] * 2
            + [state_of(which), anywhere],
            [own_rows(head, False), own_rows(slots, False), own_rows(slots, False), chunk_state(False),
             pl.BlockSpec((None, slots, 2 * head), lambda i: (0, 0, 0)), own_rows(width, False)],
            [shaped((TILE, head), bf16), shaped((TILE, slots), f32), shaped((TILE, slots), f32), states_shape,
             shaped((1, slots, 2 * head), f32), shaped((TILE, width), bf16)],
            [state_scratch, pltpu.VMEM((head, width), bf16), pltpu.SemaphoreType.DMA((1,))],
            cost=cost(2 * TILE * head * (600 + width), 2 * TILE * (head * 4 + width) + 2 * head * width),
            loose=(5,),
            loose_out=(4, 5),
        )(q, k, v, cum, inflow, entering, w_out)

    def feed(m, t, attended):
        tile_count = pl.cdiv(units, TILE)
        vmem = pltpu.VMEM
        return call(
            "feed",
            functools.partial(feed_kernel, (m * pieces + t) * TILE),
            (),
            [anywhere, in_place, in_place, anywhere, anywhere],
            [anywhere] * 6 + [in_place],
            [shaped((TILE, width), bf16)] * 2 + [shaped((TILE, units), bf16)] * 3
            + [shaped((TILE, width), bf16)] * 2,
            [vmem((n_seq, 3, span, units), bf16), vmem((TILE, width), bf16), vmem((TILE, width), bf16),
             vmem((TILE, width), bf16), vmem((TILE, width), bf16)] + [vmem((TILE, units), bf16)] * 3
            + [vmem((TILE, width), bf16), pltpu.SemaphoreType.DMA((2,)), pltpu.SemaphoreType.DMA((6,)),
               pltpu.SemaphoreType.DMA((tile_count,))],
            cost=cost(12 * TILE * width * units, 6 * width * units + TILE * width * 14),
            vmem=44,
            loose=(1, 2),
            loose_out=(6,),
        )(x, attended, gain2, cot, full)

    group = max(1, TILE // span)
    columns = group * span
    def down_grads(acts):
        return call(
            "down_grads",
            down_grad_kernel,
            (width // columns // 2,),
            [pl.BlockSpec((rows, 2 * columns), lambda j: (0, j))] + [fixed((TILE, units))] * len(acts),
            pl.BlockSpec((2 * group, span, units), lambda j: (j, 0, 0)),
            shaped((n_seq, span, units + 2 * head), bf16),
            cost=cost(2 * rows * width * units, 2 * (rows * width + rows * units + width * units)),
        )(cot, *acts)

    def wide_grads(normed, gates, ups):
        count = len(normed)
        return call(
            "wide_grads",
            wide_grad_kernel,
            (width // columns,),
            [pl.BlockSpec((TILE, columns), lambda j: (0, j))] * count
            + [fixed((TILE, units))] * (2 * count),
            pl.BlockSpec((group, 2, span, units), lambda j: (j, 0, 0, 0)),
            shaped((n_seq, 2, span, units), bf16),
            cost=cost(4 * rows * width * units, 2 * (rows * width + 2 * rows * units + 2 * width * units)),
        )(*normed, *gates, *ups)

    def back(m, t, dhn, hidden):
        o, p, scores, e_chunks = reads[m, t][:4]
        return call(
            "back",
            back_kernel,
            (chunks,),
            [own_rows(width, True), own_rows(width, True), chunk_rows(m, t, width, True), fixed((1, width)),
             anywhere]
            + [chunk_rows(m, t, head, True)] * 3 + [chunk_rows(m, t, slots, True)] * 2 + [own_rows(slots, True)] * 2
            + [chunk_state(True)],
            [own_rows(width, True)] + [own_rows(head, True)] * 3 + [own_rows(slots, True)] * 2
            + [chunk_state(True), whole((slots, 2 * head)), whole((slots, 128)), whole((8, width))],
            [shaped((TILE, width), bf16), shaped((TILE, head), bf16),
             shaped((TILE, head), f32), shaped((TILE, head), f32), shaped((TILE, slots), f32),
             shaped((TILE, slots), f32), states_shape, shaped((slots, 2 * head), f32), shaped((slots, 128), f32),
             shaped((8, width), f32)],
            [state_scratch, decay_scratch, pltpu.VMEM((head, width), bf16), pltpu.SemaphoreType.DMA((1,))],
            cost=cost(2 * TILE * width * head + 2 * TILE * head * 1500, TILE * width * 14 + TILE * head * 20),
            loose=(0,),
            loose_out=(7, 8),
        )(dhn, hidden, cot, gain2, w_out, q, k, v, cum, inflow, p, scores, e_chunks)

    def last(m, t, leaving, saved):
        dq, dk_local, dv_local, h_sum, x_local, g_chunks = saved
        here = m * pieces + t
        return call(
            "last",
            last_kernel,
            (chunks,),
            [state_of(here), chunk_rows(m, t, head, True), chunk_rows(m, t, head, True),
             *[chunk_rows(m, t, slots, True)] * 3, chunk_state(True), chunk_state(True), own_rows(head, True),
             own_rows(head, True), own_rows(slots, True), own_rows(slots, True), whole((TILE, head)),
             pl.BlockSpec((TILE, width), lambda i: (here, 0))] + [anywhere] * 4,
            [whole((TILE, head)), whole((TILE, head)), whole((TILE, slots)), whole((TILE, width)), whole((8, slots)),
             whole((8, width))],
            [shaped((TILE, head), bf16), shaped((TILE, head), bf16), shaped((TILE, slots), bf16),
             shaped((TILE, width), bf16), shaped((8, slots), f32), shaped((8, width), f32)],
            [state_scratch] + [pltpu.VMEM((width, head), bf16)] * 3
            + [pltpu.VMEM((slots, width), bf16), pltpu.SemaphoreType.DMA((4,))],
            cost=cost(2 * TILE * width * (3 * head + slots), TILE * width * 8 + TILE * head * 20 + width * head * 6),
            loose=(0,),
            loose_out=(3,),
        )(leaving, k, v, z, cum, inflow, reads[m, t][3], g_chunks, dk_local, dv_local, h_sum, x_local, dq, x,
          w_query, w_key, w_value, forget_rows)

    line = Line()
    live = {}

    def start():
        names = list(live)
        live.update(zip(names, line.step([live[n] for n in names])))

    def end(coming=None, done=None, after=()):
        total = line.join(coming, after)
        if done is not None:
            live[done] = total

    reads, backs, lasts = {}, {}, {}
    outs, in_grads = [None], [None]
    blocks = 4
    eighth = TILE // blocks

    def into(name, kernel, m, t, kept, dtype, inputs, specs):
        spec = pl.BlockSpec((1, eighth, width), lambda i: (m, blocks * t + i, 0))
        old = [] if kept[0] is None else [kept[0]]
        kept[0] = call(
            name,
            kernel,
            (blocks,),
            specs + [anywhere] * len(old),
            spec,
            shaped(tokens.shape, dtype),
            cost=cost(0, TILE * width * 10),
            loose=(1,),
            aliases={len(specs): 0} if old else None,
        )(*inputs, *old)

    piece_spec = pl.BlockSpec((eighth, width), lambda i: (i, 0))

    def finish_out(m, t):
        into("out", out_kernel, m, t, outs, bf16, [live.pop(("hidden", m, t)), live.pop(("ffn", m, t))],
             [piece_spec, piece_spec])

    def finish_grad(m, t):
        x_rows = pl.BlockSpec((eighth, width), lambda i: (blocks * (m * pieces + t) + i, 0))
        into("in_grad", in_grad_kernel, m, t, in_grads, f32, [backs[m, t][0], live.pop(("dxn", m, t)), x, gain1],
             [piece_spec, piece_spec, x_rows, pl.BlockSpec((1, width), lambda i: (0, 0))])

    def go_read(m, t):
        before = live["entering"] if t == 0 else live.pop("left")
        reads[m, t] = read(m, t, before, m if t == 0 else 0)
        if t + 1 < pieces:
            live["left"] = reads[m, t][4]
        return reads[m, t][5]

    def go_feed(m, t):
        made = feed(m, t, live.pop(("att", m, t)))
        for name, value in zip(("hidden", "hn", "act", "dgate", "dup", "ffn_part"), made):
            live[name, m, t] = value
        return made[6]

    def go_back(m, t):
        backs[m, t] = back(m, t, live.pop(("dhn", m, t)), live["hidden", m, t])
        live["back", m, t] = backs[m, t][7]

    def go_last(m, t):
        lasts[m, t] = last(m, t, live["leaving"], backs[m, t][1:7])
        live["dxn_part", m, t] = lasts[m, t][3]

    def taken(name):
        return [live.pop((name, *key)) for key in every]

    live["entering"] = entering
    line.load(go_read(0, 0))
    start()
    end(go_read(0, 1))
    start()
    end(go_read(1, 0))
    start()
    end(go_read(1, 1), ("att", 0, 0))
    live.pop("entering")
    start()
    end(go_feed(0, 0), ("att", 0, 1))
    start()
    end(go_feed(0, 1), ("att", 1, 0))
    start()
    end(go_feed(1, 0), ("att", 1, 1))
    start()
    end(go_feed(1, 1), ("dhn", 0, 0))
    start()
    live["wide_grads"] = wide_grads(taken("hn"), taken("dgate"), taken("dup"))
    end(live.pop(("ffn_part", 0, 0)), ("dhn", 0, 1))
    start()
    wide_shares = lax.psum_scatter(live.pop("wide_grads"), "seq", scatter_dimension=0)
    go_back(0, 0)
    go_back(0, 1)
    end(live.pop(("ffn_part", 0, 1)), ("dhn", 1, 0))
    start()
    go_back(1, 0)
    live["down"] = down_grads(taken("act"))
    end(live.pop(("ffn_part", 1, 0)), ("dhn", 1, 1))
    start()
    go_back(1, 1)
    taken("back")
    own = [backs[key][7] for key in every] + [backs[key][8] for key in every]
    folded = in_vmem(
        "fold",
        functools.partial(fold_kernel, parts, pieces),
        own,
        [shaped(local.shape, f32), shaped(decay.shape, f32), shaped(sent.shape, bf16)],
    )

    xn_columns = [pl.BlockSpec((rows, TILE), lambda j: (0, j))]
    piece_columns = [pl.BlockSpec((TILE, TILE), lambda j: (0, j))] * len(every)
    piece_whole = [fixed((TILE, head))] * len(every)
    made = []

    def beside_first(state, got):
        live["xn"] = xn
        end(behind_of(live.pop(("ffn_part", 1, 1)), got), ("ffn", 0, 0))
        start()
        made.extend((live.pop("xn"), live.pop("down")))
        return state

    def beside_second(state, got):
        grads = call(
            "query_grads",
            functools.partial(query_grad_kernel, len(every), units),
            (width // columns,),
            xn_columns + piece_columns + piece_whole * 2 + [anywhere],
            anywhere,
            shaped((n_seq, span, units + 2 * head), bf16),
            [pltpu.VMEM((2, group, span, 2 * head), bf16), pltpu.SemaphoreType.DMA((2,))],
            cost=cost(12 * rows * width * head, 3 * (4 * rows * width + 4 * rows * head + 4 * width * head)),
            aliases={1 + 3 * len(every): 0},
        )(behind_of(made[0], state), *[backs[key][0] for key in every], *[backs[key][1] for key in every],
          *[reads[key][0] for key in every], made[1])
        made.append(grads)
        return behind_of(state, grads)

    ties = [beside_first, beside_second]
    live["leaving"] = scan_states(n_seq, *folded, True, own, pieces, ties)
    live["query_grads"], live["wide"] = made[2], wide_shares
    go_last(0, 0)
    end(live.pop(("dxn_part", 0, 0)), ("ffn", 0, 1))
    start()
    wide_shares = live.pop("wide")
    down_shares = lax.psum_scatter(live.pop("query_grads"), "seq", scatter_dimension=0)
    go_last(0, 1)
    go_last(1, 0)
    live["xn"] = xn
    end(live.pop(("dxn_part", 0, 1)), ("ffn", 1, 0))
    start()
    go_last(1, 1)
    live.pop("leaving")
    few = [pl.BlockSpec((8, TILE), lambda j: (0, j))] * len(every)
    live["state_grads"] = call(
        "state_grads",
        functools.partial(state_grad_kernel, len(every)),
        (width // TILE,),
        xn_columns + piece_whole * 2 + [fixed((TILE, slots))] * len(every) + [fixed((8, slots))] * len(every) + few * 2,
        pl.BlockSpec((group, span + 16, 2 * head + 128), lambda j: (j, 0, 0)),
        shaped((n_seq, span + 16, 2 * head + 128), bf16),
        cost=cost(4 * rows * width * head, 2 * rows * width + 4 * rows * head + 4 * width * head),
    )(live.pop("xn"), *[lasts[key][i] for i in (0, 1, 2, 4, 5) for key in every], *[backs[key][9] for key in every])
    end(live.pop(("dxn_part", 1, 0)), ("ffn", 1, 1))
    start()
    attn_shares = lax.psum_scatter(live.pop("state_grads"), "seq", scatter_dimension=0)
    finish_out(0, 0)
    finish_out(0, 1)
    live["out"], live["down"] = outs[0], down_shares
    end(live.pop(("dxn_part", 1, 1)), ("dxn", 0, 0))
    start()
    outs[0], down_shares = live.pop("out"), live.pop("down")
    finish_out(1, 0)
    finish_out(1, 1)
    finish_grad(0, 0)
    live["out"], live["in_grad"] = outs[0], in_grads[0]
    end(None, ("dxn", 0, 1))
    start()
    in_grads[0] = live.pop("in_grad")
    finish_grad(0, 1)
    live["in_grad"] = in_grads[0]
    end(None, ("dxn", 1, 0))
    start()
    in_grads[0] = live.pop("in_grad")
    late = behind_of(attn_shares, in_grads[0]).astype(f32)
    gain1_total = late[:span, 2 * head + slots + 1]
    others = [lax.ppermute(gain1_total, "head", [(i, i ^ d) for i in range(n_head)]) for d in (1, 2, 3)]
    gain1_total = (gain1_total + others[0]) + (others[1] + others[2])
    finish_grad(1, 0)
    end(None, ("dxn", 1, 1), (gain1_total, in_grads[0]))
    finish_grad(1, 1)
    small_shares = late[:, 2 * head :]
    query_shares = down_shares[:, units:].astype(f32)

    return (
        live["out"],
        in_grads[0],
        gain1_total,
        query_shares[:, :head],
        late[:span, :head],
        late[:span, head : 2 * head],
        small_shares[:span, :slots],
        small_shares[span, :slots] + small_shares[span + 1, :slots],
        query_shares[:, head:].T,
        small_shares[:span, slots],
        wide_shares[0].astype(f32),
        wide_shares[1].astype(f32),
        down_shares[:, :units].astype(f32).T,
    )


def solution(mesh):
    rows, both = P(None, "seq", None), P("seq", "head")
    by_head, down = P(None, "head"), P("head", "seq")
    return jax.shard_map(
        on_device,
        mesh=mesh,
        in_specs=(rows, P(), by_head, by_head, by_head, by_head, P("head"), P("head", None), P(), both, both, down, rows),
        out_specs=(rows, rows, P("seq"), both, both, both, both, P("head"), down, P("seq"), both, both, down),
        check_vma=False,
    )
```

```python
import functools

import jax
import jax.numpy as jnp
from jax import lax
from jax.experimental import pallas as pl
from jax.experimental.pallas import tpu as pltpu
from jax.sharding import PartitionSpec as P

CHUNK = 128
TILE = 256
EPS = 1e-06
RATE = 0.5
MIB = 2**20
f32 = jnp.float32
bf16 = jnp.bfloat16
highest = lax.Precision.HIGHEST


def nn(a, b):
    return lax.dot_general(a, b, (((1,), (0,)), ((), ())), preferred_element_type=f32)


def nt(a, b):
    return lax.dot_general(a, b, (((1,), (1,)), ((), ())), preferred_element_type=f32)


def tn(a, b):
    return lax.dot_general(a, b, (((0,), (0,)), ((), ())), preferred_element_type=f32)


def exact(a, b, dims):
    return lax.dot_general(a, b, (dims, ((), ())), precision=highest, preferred_element_type=f32)


def halves(a):
    high = a.astype(bf16)
    return high, (a - high.astype(f32)).astype(bf16)


def call(name, kernel, grid, in_specs, out_specs, out_shape, scratch=(), vmem=24, cost=None, loose=(), loose_out=(),
         aliases=None):
    single = not isinstance(out_shape, list)
    shapes = [out_shape] if single else out_shape
    shapes = [s if i in loose_out else pltpu.HBM(s.shape, s.dtype) for i, s in enumerate(shapes)]
    function = pl.pallas_call(
        kernel,
        name=name,
        grid=grid,
        in_specs=in_specs,
        out_specs=out_specs,
        out_shape=shapes[0] if single else shapes,
        scratch_shapes=scratch,
        input_output_aliases=aliases or {},
        compiler_params=pltpu.CompilerParams(
            dimension_semantics=("arbitrary",) * len(grid), vmem_limit_bytes=vmem * MIB
        ),
        cost_estimate=cost,
    )

    def run(*operands):
        return function(*[
            o if i in loose or spec.memory_space == pltpu.SMEM else pltpu.with_memory_space_constraint(o, pltpu.HBM)
            for i, (o, spec) in enumerate(zip(operands, in_specs))
        ])

    return run


def cost(flops, data):
    return pl.CostEstimate(flops=int(flops), bytes_accessed=int(data), transcendentals=0)


def fixed(shape):
    zeros = (0,) * len(shape)
    return pl.BlockSpec(shape, lambda *_: zeros, pipeline_mode=pl.Buffered(1))


def shaped(shape, dtype):
    return jax.ShapeDtypeStruct(shape, dtype)


def triangle(lower):
    r = lax.broadcasted_iota(jnp.int32, (CHUNK, CHUNK), 0)
    c = lax.broadcasted_iota(jnp.int32, (CHUNK, CHUNK), 1)
    return r >= c if lower else r <= c


def gates(z):
    la = -RATE * lax.logistic(-z)
    y = -la
    taken = jnp.ones_like(y)
    for n in range(9, 1, -1):
        taken = 1.0 - y * (1.0 / n) * taken
    taken = y * taken
    cum = exact(triangle(True).astype(f32), la, ((1,), (0,)))
    return cum, jnp.exp(-cum) * taken


def turned_last(cum):
    return jnp.broadcast_to(cum[CHUNK - 1 :, :], cum.shape).T


def halves_sum(ones, values):
    high, low = halves(values)
    both = nn(ones.astype(bf16), jnp.concatenate([high, low], 1))
    width = values.shape[1]
    return both[:, :width] + both[:, width:]


def project_kernel(per_part, x_ref, gain_ref, wk_ref, wv_ref, wf_ref, bias_ref,
                   xn_ref, k_ref, v_ref, z_ref, cum_ref, in_ref, s_ref, d_ref, sent_ref, state, decay):
    @pl.when(lax.rem(pl.program_id(0), per_part) == 0)
    def _():
        state[...] = jnp.zeros_like(state)
        decay[...] = jnp.zeros_like(decay)

    x = x_ref[...].astype(f32)
    r1 = lax.rsqrt(jnp.mean(x * x, axis=-1, keepdims=True) + EPS)
    xn = (x * r1 * gain_ref[...]).astype(bf16)
    xn_ref[...] = xn
    k_ref[...] = nn(xn, wk_ref[...]).astype(bf16)
    v_ref[...] = nn(xn, wv_ref[...]).astype(bf16)
    z_ref[...] = nt(xn, wf_ref[...]) + bias_ref[...]
    width = k_ref.shape[1]
    for c in range(x_ref.shape[0] // CHUNK):
        rows = pl.ds(c * CHUNK, CHUNK)
        cum, inflow = gates(z_ref[rows, :])
        cum_ref[rows, :] = cum
        in_ref[rows, :] = inflow
        total = turned_last(cum)
        spread = inflow.astype(bf16)
        keep = jnp.exp(total[:, :1])
        state[:, :width] = keep * (state[:, :width] + tn(spread, k_ref[rows, :]))
        state[:, width:] = keep * (state[:, width:] + tn(spread, v_ref[rows, :]))
        decay[...] += total
    s_ref[0] = state[...]
    d_ref[0] = jnp.exp(decay[...])
    pack(sent_ref, 0, jnp.exp(decay[...]), state[...])


def query_kernel(xn_ref, wq_ref, q_ref):
    q_ref[...] = nn(xn_ref[...], wq_ref[...]).astype(bf16)


def read_kernel(q_ref, k_ref, v_ref, cum_ref, in_ref, e0_ref, wo_ref, o_ref, p_ref, sc_ref, e_ref, left_ref, att_ref, state):
    @pl.when(pl.program_id(0) == 0)
    def _():
        state[...] = e0_ref[...]

    width = q_ref.shape[1]
    lower = triangle(True)
    q, k, v = q_ref[...], k_ref[...], v_ref[...]
    cum, inflow = cum_ref[...], in_ref[...]
    total = turned_last(cum)
    growth = jnp.exp(cum)
    e_ref[0] = state[...]
    i_hi, i_lo = halves(inflow)
    a_hi, a_lo = halves(jnp.where(lower, nt(q, k), 0.0))
    e_hi, e_lo = halves(state[:, :width])
    scores = growth * (nt(q, e_hi) + nt(q, e_lo) + nn(a_hi, i_hi) + (nn(a_hi, i_lo) + nn(a_lo, i_hi)))
    top = jnp.exp(scores - jnp.max(scores, axis=-1, keepdims=True))
    p = top / jnp.sum(top, axis=-1, keepdims=True)
    w = (p * growth).astype(bf16)
    mixing = jnp.where(lower, nt(w, i_hi), 0.0).astype(bf16)
    o = (nn(w, state[:, width:].astype(bf16)) + nn(mixing, v)).astype(bf16)
    o_ref[...] = o
    att_ref[...] = nn(o, wo_ref[...]).astype(bf16)
    p_ref[...] = p
    sc_ref[...] = scores
    keep = jnp.exp(total[:, :1])
    state[:, :width] = keep * (state[:, :width] + tn(i_hi, k))
    state[:, width:] = keep * (state[:, width:] + tn(i_hi, v))
    left_ref[...] = state[...]


def back_kernel(dhn_ref, hid_ref, cot_ref, gain_ref, wo_ref, q_ref, k_ref, v_ref, cum_ref, in_ref, p_ref, sc_ref,
                e_ref, datt_ref, dq_ref, dkl_ref, dvl_ref, h_ref, x1_ref, g_ref, s_ref, d_ref, gg_ref, state, decay):
    step = pl.program_id(0)

    @pl.when(step == 0)
    def _():
        state[...] = jnp.zeros_like(state)
        decay[...] = jnp.zeros_like(decay)
        gg_ref[...] = jnp.zeros_like(gg_ref)

    hidden = hid_ref[...].astype(f32)
    dhn = dhn_ref[...].astype(f32)
    r2 = lax.rsqrt(jnp.mean(hidden * hidden, axis=-1, keepdims=True) + EPS)
    gg_ref[...] += jnp.sum((dhn * hidden * r2).reshape(-1, 8, hidden.shape[1]), axis=0)
    u2 = gain_ref[...] * dhn
    dhid = (
        cot_ref[...].astype(f32)
        + r2 * u2
        - hidden * (r2 * r2 * r2) * jnp.mean(u2 * hidden, axis=-1, keepdims=True)
    )
    datt = dhid.astype(bf16)
    datt_ref[...] = datt
    width = q_ref.shape[1]
    do = nt(datt, wo_ref[...]).astype(bf16)
    lower, upper = triangle(True), triangle(False)
    q, k, v = q_ref[...], k_ref[...], v_ref[...]
    cum, inflow = cum_ref[...], in_ref[...]
    total = turned_last(cum)
    growth = jnp.exp(cum)
    p = p_ref[...]
    i_hi, i_lo = halves(inflow)
    b_hi, b_lo = halves(jnp.where(lower, nt(do, v), 0.0))
    ev_hi, ev_lo = halves(e_ref[0, :, width:])
    dp = growth * (nt(do, ev_hi) + nt(do, ev_lo) + nn(b_hi, i_hi) + (nn(b_hi, i_lo) + nn(b_lo, i_hi)))
    ds = p * (dp - jnp.sum(p * dp, axis=-1, keepdims=True))
    w = (p * growth).astype(bf16)
    gds = (growth * ds).astype(bf16)
    n = jnp.where(lower, nt(gds, i_hi), 0.0).astype(bf16)
    dq_ref[...] = (nn(gds, e_ref[0, :, :width].astype(bf16)) + nn(n, k)).astype(bf16)
    n_t = jnp.where(upper, nt(i_hi, gds), 0.0).astype(bf16)
    m_t = jnp.where(upper, nt(i_hi, w), 0.0).astype(bf16)
    dkl_ref[...] = nn(n_t, q)
    dvl_ref[...] = nn(m_t, do)
    h_ref[...] = ds * sc_ref[...] + p * dp
    a_t = jnp.where(upper, nt(k, q), 0.0).astype(bf16)
    b_t = jnp.where(upper, nt(v, do), 0.0).astype(bf16)
    x1_ref[...] = nn(a_t, gds) + nn(b_t, w)
    keep = jnp.exp(total[:, :1])
    g_k, g_v = tn(gds, q), tn(w, do)
    g_ref[0, :, :width] = g_k
    g_ref[0, :, width:] = g_v
    state[:, :width] = g_k + keep * state[:, :width]
    state[:, width:] = g_v + keep * state[:, width:]
    decay[...] += total
    s_ref[...] = state[...]
    d_ref[...] = jnp.exp(decay[...])


def last_kernel(l0_ref, k_ref, v_ref, z_ref, cum_ref, in_ref, e_ref, g_ref, dkl_ref, dvl_ref, h_ref, x1_ref, dq_ref, x_ref,
                wq_ref, wk_ref, wv_ref, wf_ref, dk_ref, dv_ref, dz_ref, dxn_ref, bias_ref, gg_ref,
                state, wq, wk, wv, wf, sems):
    step, steps = pl.program_id(0), pl.num_programs(0)
    loads = [pltpu.make_async_copy(source, target, sems.at[i])
             for i, (source, target) in enumerate(((wq_ref, wq), (wk_ref, wk), (wv_ref, wv), (wf_ref, wf)))]

    @pl.when(step == 0)
    def _():
        for load in loads:
            load.start()
        state[...] = l0_ref[...]
        bias_ref[...] = jnp.zeros_like(bias_ref)

    width = k_ref.shape[1]
    k, v, z = k_ref[...], v_ref[...], z_ref[...]
    cum, inflow = cum_ref[...], in_ref[...]
    total = turned_last(cum)
    i_hi = inflow.astype(bf16)
    keep = jnp.exp(total[:, :1])
    lg = keep * state[...]
    lg_k, lg_v = lg[:, :width].astype(bf16), lg[:, width:].astype(bf16)
    rows = pl.ds(pl.multiple_of((steps - 1 - step) * CHUNK, CHUNK), CHUNK)
    dk_ref[rows, :] = (dkl_ref[...] + nn(i_hi, lg_k)).astype(bf16)
    dv_ref[rows, :] = (dvl_ref[...] + nn(i_hi, lg_v)).astype(bf16)
    x1 = x1_ref[...]
    x2 = nt(k, lg_k) + nt(v, lg_v)
    met = jnp.broadcast_to(jnp.sum(lg * e_ref[0], axis=1, keepdims=True), (lg.shape[0], CHUNK)).T
    h, r1 = h_ref[...], inflow * x1
    dla = (
        halves_sum(triangle(False), h - r1)
        + r1
        + halves_sum(triangle(True), inflow * x2)
        + met
        - jnp.exp(-cum) * (x1 + x2)
    )
    rate = lax.logistic(-z)
    dz = (dla * RATE * rate * (1.0 - rate)).astype(bf16)
    dz_ref[rows, :] = dz
    bias_ref[...] += jnp.sum(dz.astype(f32).reshape(-1, 8, dz.shape[1]), axis=0)
    state[...] = g_ref[0] + lg

    @pl.when(step == steps - 1)
    def _():
        for load in loads:
            load.wait()
        dxn = nt(dq_ref[...], wq[...]) + nt(dk_ref[...], wk[...]) + nt(dv_ref[...], wv[...]) + nn(dz_ref[...], wf[...])
        dxn_ref[...] = dxn.astype(bf16)
        x = x_ref[...].astype(f32)
        r1 = lax.rsqrt(jnp.mean(x * x, axis=-1, keepdims=True) + EPS)
        gg_ref[...] = jnp.sum((dxn * x * r1).reshape(-1, 8, x.shape[1]), axis=0)


def out_kernel(hid_ref, ffn_ref, *refs):
    refs[-1][0] = (hid_ref[...].astype(f32) + ffn_ref[...].astype(f32)).astype(bf16)


def in_grad_kernel(dhid_ref, dxn_ref, x_ref, gain_ref, *refs):
    x = x_ref[...].astype(f32)
    r1 = lax.rsqrt(jnp.mean(x * x, axis=-1, keepdims=True) + EPS)
    u1 = gain_ref[...] * dxn_ref[...].astype(f32)
    refs[-1][0] = dhid_ref[...].astype(f32) + r1 * u1 - x * (r1 * r1 * r1) * jnp.mean(u1 * x, axis=-1, keepdims=True)


def feed_kernel(first_row, x_ref, att_ref, gain_ref, cot_ref, full_ref, hid_ref, hn_ref, act_ref, dg_ref, du_ref,
                ffn_ref, dhn_ref, weights, x, cot, hid, hn, act, dg, du, ffn, in_sems, out_sems, weight_sems):
    rows, width = x.shape
    units = act.shape[1]
    blocks, _, span, _ = weights.shape
    tiles = [(u, min(TILE, units - u)) for u in range(0, units, TILE)]
    here = pl.ds(first_row, rows)
    reads = [pltpu.make_async_copy(source.at[here, :], target, in_sems.at[i])
             for i, (source, target) in enumerate(((x_ref, x), (cot_ref, cot)))]
    loads = [pltpu.make_async_copy(full_ref.at[:, :, :, pl.ds(u, size)], weights.at[:, :, :, pl.ds(u, size)],
                                   weight_sems.at[i]) for i, (u, size) in enumerate(tiles)]
    writes = [pltpu.make_async_copy(source, target, out_sems.at[i])
              for i, (source, target) in enumerate(
                  ((hid, hid_ref), (hn, hn_ref), (act, act_ref), (dg, dg_ref), (du, du_ref), (ffn, ffn_ref)))]
    for copy in reads + loads:
        copy.start()
    for copy in reads:
        copy.wait()
    hidden = x[...].astype(f32) + att_ref[...].astype(f32)
    hid[...] = hidden.astype(bf16)
    r2 = lax.rsqrt(jnp.mean(hidden * hidden, axis=-1, keepdims=True) + EPS)
    hn[...] = (hidden * r2 * gain_ref[...]).astype(bf16)
    writes[0].start()
    writes[1].start()
    for (u, size), load in zip(tiles, loads):
        load.wait()
        gate, up, dact = (
            nn(left[...], weights[:, i, :, u : u + size].reshape(width, size))
            for i, left in enumerate((hn, hn, cot))
        )
        s = lax.logistic(gate)
        silu = gate * s
        act[:, u : u + size] = (silu * up).astype(bf16)
        dg[:, u : u + size] = (dact * up * s * (1.0 + gate * (1.0 - s))).astype(bf16)
        du[:, u : u + size] = (dact * silu).astype(bf16)
    for write in writes[2:5]:
        write.start()
    group = max(1, TILE // span)
    for b in range(0, blocks, group):
        columns = slice(b * span, (b + group) * span)
        w_gate, w_up, w_down = (weights[b : b + group, i].reshape(group * span, units) for i in range(3))
        ffn[:, columns] = nt(act[...], w_down).astype(bf16)
        dhn_ref[:, columns] = (nt(dg[...], w_gate) + nt(du[...], w_up)).astype(bf16)
    writes[5].start()
    for write in writes:
        write.wait()


def summed(pairs):
    total = tn(*pairs[0])
    for pair in pairs[1:]:
        total = total + tn(*pair)
    return total.astype(bf16)


def down_grad_kernel(*refs):
    cot_ref, act, out_ref = refs[0], refs[1:-1], refs[-1]
    rows = act[0].shape[0]
    block = summed([(cot_ref[i * rows : (i + 1) * rows, :], a[...]) for i, a in enumerate(act)])
    out_ref[...] = block.reshape(out_ref.shape)


def wide_grad_kernel(*refs):
    out_ref = refs[-1]
    count = (len(refs) - 1) // 3
    hn, dg, du = refs[:count], refs[count : 2 * count], refs[2 * count : 3 * count]
    blocks, _, width, units = out_ref.shape
    for i, grads in enumerate((dg, du)):
        block = summed([(h[...], g[...]) for h, g in zip(hn, grads)])
        out_ref[:, i] = block.reshape(blocks, width, units)


def query_grad_kernel(count, first_column, *refs):
    xn_ref, out_ref, block, sems = refs[0], refs[-3], refs[-2], refs[-1]
    datt, dq, o = (refs[1 + i * count : 1 + (i + 1) * count] for i in range(3))
    rows, width = dq[0].shape
    _, groups, span, columns = block.shape
    step, steps = pl.program_id(0), pl.num_programs(0)

    def copy(at):
        slot = lax.rem(at, 2)
        return pltpu.make_async_copy(
            block.at[slot], out_ref.at[pl.ds(at * groups, groups), :, pl.ds(first_column, columns)], sems.at[slot]
        )

    @pl.when(step >= 2)
    def _():
        copy(step - 2).wait()

    xn = [xn_ref[i * rows : (i + 1) * rows, :] for i in range(count)]
    slot = lax.rem(step, 2)
    query = summed([(x, g[...]) for x, g in zip(xn, dq)])
    block[slot, :, :, :width] = query.reshape(groups, span, width)
    output = summed([(d[...], r[...]) for d, r in zip(datt, o)])
    block[slot, :, :, width:] = output.reshape(groups, span, width)
    copy(step).start()

    @pl.when(step == steps - 1)
    def _():
        copy(step - 1).wait()
        copy(step).wait()


def state_grad_kernel(count, *refs):
    xn_ref, out_ref = refs[0], refs[-1]
    dk, dv, dz, bias, gain1, gain2 = (refs[1 + i * count : 1 + (i + 1) * count] for i in range(6))
    rows, width = dk[0].shape
    slots = dz[0].shape[1]
    groups, high, _ = out_ref.shape
    span = high - 16
    xn = [xn_ref[i * rows : (i + 1) * rows, :] for i in range(count)]
    for i, grads in enumerate((dk, dv)):
        block = summed([(x, g[...]) for x, g in zip(xn, grads)])
        out_ref[:, :span, i * width : (i + 1) * width] = block.reshape(groups, span, width)
    forget = tn(xn[0], dz[0][...])
    for x, g in zip(xn[1:], dz[1:]):
        forget = forget + tn(x, g[...])
    pad = 128 - slots % 128

    def padded(values):
        return jnp.concatenate([values, jnp.zeros((values.shape[0], pad), f32)], 1)

    def column(parts):
        total = parts[0][...]
        for part in parts[1:]:
            total = total + part[...]
        return jnp.sum(total.T, axis=1, keepdims=True)

    small = padded(forget)
    lane = lax.broadcasted_iota(jnp.int32, small.shape, 1)
    small = jnp.where(lane == slots, column(gain2), jnp.where(lane == slots + 1, column(gain1), small))
    out_ref[:, :span, 2 * width :] = small.astype(bf16).reshape(groups, span, slots + pad)
    total = bias[0][...]
    for part in bias[1:]:
        total = total + part[...]
    total = padded(jnp.broadcast_to(jnp.sum(total, axis=0, keepdims=True), (16, slots)))
    upper = total.astype(bf16).astype(f32)
    row = lax.broadcasted_iota(jnp.int32, total.shape, 0)
    tail = jnp.where(row == 0, upper, jnp.where(row == 1, total - upper, 0.0)).astype(bf16)
    for g in range(groups):
        out_ref[g, span:, : 2 * width] = jnp.zeros((16, 2 * width), bf16)
        out_ref[g, span:, 2 * width :] = tail


def pack(ref, m, decay, state):
    high, low = halves(decay)
    lane = lax.broadcasted_iota(jnp.int32, decay.shape, 1)
    width = state.shape[1]
    ref[m, :, :width] = state.astype(bf16)
    ref[m, :, width:] = jnp.where(lane == 0, high.astype(f32), low.astype(f32)).astype(bf16)


def fold_kernel(parts, pieces, *refs):
    s_refs, d_refs, (s_out, d_out, sent) = refs[: parts * pieces], refs[parts * pieces : -3], refs[-3:]
    for m in range(parts):
        s, d = s_refs[m * pieces + pieces - 1][...], d_refs[m * pieces + pieces - 1][...]
        for t in reversed(range(pieces - 1)):
            here = d_refs[m * pieces + t][...]
            s, d = s_refs[m * pieces + t][...] + here[:, :1] * s, here * d
        s_out[m], d_out[m] = s, d
        pack(sent, m, d, s)


def hop_kernel(bit, after, first, final, parts, pieces, *refs):
    refs = list(refs)
    s_ref, d_ref, got_ref = refs[:3]
    refs = refs[3:]
    if not first:
        part_s_ref, part_d_ref = refs[:2]
        refs = refs[2:]
    early = (lax.axis_index("seq") & bit) == 0
    takes = early if after else jnp.logical_not(early)
    width = s_ref.shape[2]
    found = []
    for m in range(parts):
        tail = got_ref[m, :, width:].astype(f32)
        there_d, there_s = tail[:, :1] + tail[:, 1:2], got_ref[m, :, :width].astype(f32)
        s, d = s_ref[m], d_ref[m]
        there_wide = jnp.broadcast_to(there_d, d.shape)
        new_s = jnp.where(takes, s + d[:, :1] * there_s, there_s + there_d * s)
        if first:
            part_s, part_d = jnp.where(takes, there_s, 0.0), jnp.where(takes, there_wide, 1.0)
        else:
            part_s, part_d = part_s_ref[m], part_d_ref[m]
            part_s = jnp.where(takes, part_s + part_d[:, :1] * there_s, part_s)
            part_d = jnp.where(takes, part_d * there_wide, part_d)
        found.append((new_s, d * there_wide, part_s, part_d))
    if not final:
        s_out, d_out, part_s_out, part_d_out, sent = refs
        for m, (s, d, part_s, part_d) in enumerate(found):
            s_out[m], d_out[m], part_s_out[m], part_d_out[m] = s, d, part_s, part_d
            pack(sent, m, d, s)
        return
    *own, out = refs
    arriving = jnp.zeros_like(found[0][0])
    for m in reversed(range(parts)) if after else range(parts):
        s, d, part_s, part_d = found[m]
        enters = part_s + part_d[:, :1] * arriving
        arriving = s + d[:, :1] * arriving
        for t in reversed(range(pieces)) if after else range(1):
            out[m * pieces + t if after else m] = enters
            if after and t:
                here = m * pieces + t
                enters = own[here][...] + own[parts * pieces + here][:, :1] * enters


def in_vmem(name, kernel, operands, shapes):
    return pl.pallas_call(
        kernel,
        name=name,
        in_specs=[pl.BlockSpec(memory_space=pltpu.VMEM)] * len(operands),
        out_specs=[pl.BlockSpec(memory_space=pltpu.VMEM)] * len(shapes),
        out_shape=shapes,
        compiler_params=pltpu.CompilerParams(vmem_limit_bytes=12 * MIB),
        cost_estimate=cost(0, 6 * MIB),
    )(*operands)


def scan_states(n, state, decay, sent, after, own=(), pieces=1, ties=()):
    parts, slots, width = state.shape
    part, bit, hops = [], 1, 0
    while bit < n:
        got = lax.ppermute(sent, "seq", [(i, i ^ bit) for i in range(n)])
        final = 2 * bit == n
        shapes = [shaped(state.shape, f32), shaped(decay.shape, f32)] * 2 + [shaped(sent.shape, bf16)]
        if final:
            shapes = [shaped((parts * pieces, slots, width), f32)]
        if hops < len(ties) and ties[hops] is not None:
            state = ties[hops](state, got)
        results = in_vmem(
            "hop",
            functools.partial(hop_kernel, bit, after, not part, final, parts, pieces),
            [state, decay, got, *part, *(own if final else ())],
            shapes,
        )
        if final:
            return results[0]
        state, decay, *part, sent = results
        bit, hops = 2 * bit, hops + 1


def behind_of(value, *first):
    return lax.optimization_barrier((value,) + first)[0]


def join_kernel(has, *refs):
    refs = iter(refs)
    piece, outer, pair, middle, total, coming = (next(refs) if h else None for h in has)
    makes = (piece is not None, pair is not None or coming is not None, total is not None)
    new_pair, new_total, done = (next(refs) if m else None for m in makes)
    me = lax.axis_index("head")
    end = (me == 0) | (me == 3)

    def each(work):
        @pl.loop(0, TILE // 32)
        def _(i):
            work(pl.ds(pl.multiple_of(i * 32, 32), 32))

    def both(a, b, rows):
        return a[rows, :] + b[rows, :]

    @pl.when(end)
    def _():
        def work(rows):
            if coming is not None:
                new_total[rows, :] = coming[rows, :]
            if done is not None:
                done[rows, :] = outer[rows, :]

        each(work)

    @pl.when(jnp.logical_not(end))
    def _():
        def work(rows):
            if piece is not None:
                new_pair[rows, :] = both(piece, outer, rows)
            if pair is not None:
                new_total[rows, :] = both(pair, middle, rows)
            if done is not None:
                done[rows, :] = total[rows, :]

        each(work)


class Line:
    INWARD, OUTWARD, MIDDLE = [(0, 1), (3, 2)], [(1, 0), (2, 3)], [(1, 2), (2, 1)]

    def __init__(self):
        self.piece = self.pair = self.payload = None
        self.returns = False

    def load(self, piece):
        self.piece = self.payload = piece

    def step(self, inputs):
        piece, pair, payload, returns = self.piece, self.pair, self.payload, self.returns
        values = [v for v in (payload, pair) if v is not None] + inputs
        values = list(lax.optimization_barrier(tuple(values)))
        outer = middle = None
        if payload is not None:
            payload = values.pop(0)
            way = (self.INWARD if piece is not None else []) + (self.OUTWARD if returns else [])
            outer = lax.ppermute(payload, "head", way)
        if pair is not None:
            pair = values.pop(0)
            middle = lax.ppermute(pair, "head", self.MIDDLE)
        self.waiting = (piece, outer, pair, middle, payload if returns else None)
        return values

    def join(self, coming=None, after=()):
        piece, outer, pair, middle, total = self.waiting
        if after:
            outer = behind_of(outer, *after)
        if piece is None and total is None:
            outer = None
        operands = [piece, outer, pair, middle, total, coming]
        makes = [piece is not None, pair is not None or coming is not None, total is not None]
        arrays = [o for o in operands if o is not None]
        results = in_vmem(
            "join",
            functools.partial(join_kernel, [o is not None for o in operands]),
            arrays,
            [shaped(arrays[0].shape, bf16)] * sum(makes),
        )
        results = iter(results)
        self.pair, self.payload, done = (next(results) if m else None for m in makes)
        self.returns = pair is not None
        self.piece = coming
        return done


def on_device(tokens, gain_attn, w_query, w_key, w_value, w_forget, forget_bias, w_out, gain_ffn, w_gate, w_up, w_down,
              cotangent):
    parts, part_rows, width = tokens.shape
    rows = parts * part_rows
    head = w_query.shape[1]
    slots = w_forget.shape[1]
    units = w_gate.shape[1]
    n_seq, n_head = lax.axis_size("seq"), lax.axis_size("head")
    span = w_gate.shape[0]
    per_part = pieces = part_rows // TILE
    chunks = TILE // CHUNK
    every = [(m, t) for m in range(parts) for t in range(pieces)]

    x = tokens.reshape(rows, width)
    cot = cotangent.reshape(rows, width)
    gain1 = gain_attn.reshape(1, width)
    gain2 = gain_ffn.reshape(1, width)
    state_scratch = pltpu.VMEM((slots, 2 * head), f32)
    decay_scratch = pltpu.VMEM((slots, 128), f32)
    anywhere = pl.BlockSpec(memory_space=pl.ANY)
    in_place = pl.BlockSpec(memory_space=pltpu.VMEM)

    all_rows = lambda c: pl.BlockSpec((TILE, c), lambda i: (i, 0))
    by_part = lambda c: pl.BlockSpec((1, slots, c), lambda i: (i // per_part, 0, 0))
    forget_rows = w_forget.T
    xn, k, v, z, cum, inflow, local, decay, sent = call(
        "project",
        functools.partial(project_kernel, per_part),
        (rows // TILE,),
        [all_rows(width), fixed((1, width))] + [fixed((width, head))] * 2 + [fixed((slots, width)), fixed((1, slots))],
        [all_rows(width), all_rows(head), all_rows(head)] + [all_rows(slots)] * 3
        + [by_part(2 * head), by_part(128), by_part(2 * head + 128)],
        [shaped((rows, width), bf16)] + [shaped((rows, head), bf16)] * 2
        + [shaped((rows, slots), f32)] * 3 + [shaped((parts, slots, 2 * head), f32), shaped((parts, slots, 128), f32),
                                             shaped((parts, slots, 2 * head + 128), bf16)],
        [state_scratch, decay_scratch],
        cost=cost(2 * rows * width * (2 * head + slots), 2 * rows * width * 3 + 2 * width * 2 * head),
        loose_out=(6, 7, 8),
    )(x, gain1, w_key, w_value, forget_rows, forget_bias.reshape(1, slots))
    q = call(
        "query",
        query_kernel,
        (rows // TILE,),
        [all_rows(width), fixed((width, head))],
        all_rows(head),
        shaped((rows, head), bf16),
        cost=cost(2 * rows * width * head, 2 * rows * (width + head) + 2 * width * head),
    )(xn, w_query)
    stacked = []

    def stack_weights(state, got):
        gate, down, _ = lax.optimization_barrier((w_gate, w_down, got))
        stacked.append(jnp.stack([gate, w_up, down.T]))
        return state

    entering = scan_states(n_seq, local, decay, sent, False, ties=[stack_weights])
    full = lax.all_gather(stacked[0], "seq")

    def chunk_rows(m, t, columns, back):
        start = (m * pieces + t) * chunks
        return pl.BlockSpec((CHUNK, columns), lambda i: (start + (chunks - 1 - i if back else i), 0))

    def own_rows(columns, back):
        return pl.BlockSpec((CHUNK, columns), lambda i: (chunks - 1 - i if back else i, 0))

    def chunk_state(back):
        return pl.BlockSpec((1, slots, 2 * head), lambda i: (chunks - 1 - i if back else i, 0, 0))

    def whole(shape):
        return pl.BlockSpec(shape, lambda i: (0,) * len(shape))

    def state_of(m):
        return pl.BlockSpec((None, slots, 2 * head), lambda i: (m, 0, 0))

    states_shape = shaped((chunks, slots, 2 * head), f32)

    def read(m, t, entering, which):
        return call(
            "read",
            read_kernel,
            (chunks,),
            [chunk_rows(m, t, head, False)] * 3 + [chunk_rows(m, t, slots, False)] * 2
            + [state_of(which), fixed((head, width))],
            [own_rows(head, False), own_rows(slots, False), own_rows(slots, False), chunk_state(False),
             pl.BlockSpec((None, slots, 2 * head), lambda i: (0, 0, 0)), own_rows(width, False)],
            [shaped((TILE, head), bf16), shaped((TILE, slots), f32), shaped((TILE, slots), f32), states_shape,
             shaped((1, slots, 2 * head), f32), shaped((TILE, width), bf16)],
            [state_scratch],
            cost=cost(2 * TILE * head * (600 + width), 2 * TILE * (head * 4 + width) + 2 * head * width),
            loose=(5,),
            loose_out=(4, 5),
        )(q, k, v, cum, inflow, entering, w_out)

    def feed(m, t, attended):
        tile_count = pl.cdiv(units, TILE)
        vmem = pltpu.VMEM
        return call(
            "feed",
            functools.partial(feed_kernel, (m * pieces + t) * TILE),
            (),
            [anywhere, in_place, in_place, anywhere, anywhere],
            [anywhere] * 6 + [in_place],
            [shaped((TILE, width), bf16)] * 2 + [shaped((TILE, units), bf16)] * 3
            + [shaped((TILE, width), bf16)] * 2,
            [vmem((n_seq, 3, span, units), bf16), vmem((TILE, width), bf16), vmem((TILE, width), bf16),
             vmem((TILE, width), bf16), vmem((TILE, width), bf16)] + [vmem((TILE, units), bf16)] * 3
            + [vmem((TILE, width), bf16), pltpu.SemaphoreType.DMA((2,)), pltpu.SemaphoreType.DMA((6,)),
               pltpu.SemaphoreType.DMA((tile_count,))],
            cost=cost(12 * TILE * width * units, 6 * width * units + TILE * width * 14),
            vmem=44,
            loose=(1, 2),
            loose_out=(6,),
        )(x, attended, gain2, cot, full)

    group = max(1, TILE // span)
    columns = group * span
    def down_grads(acts):
        return call(
            "down_grads",
            down_grad_kernel,
            (width // columns // 2,),
            [pl.BlockSpec((rows, 2 * columns), lambda j: (0, j))] + [fixed((TILE, units))] * len(acts),
            pl.BlockSpec((2 * group, span, units), lambda j: (j, 0, 0)),
            shaped((n_seq, span, units + 2 * head), bf16),
            cost=cost(2 * rows * width * units, 2 * (rows * width + rows * units + width * units)),
        )(cot, *acts)

    def wide_grads(normed, gates, ups):
        count = len(normed)
        return call(
            "wide_grads",
            wide_grad_kernel,
            (width // columns,),
            [pl.BlockSpec((TILE, columns), lambda j: (0, j))] * count
            + [fixed((TILE, units))] * (2 * count),
            pl.BlockSpec((group, 2, span, units), lambda j: (j, 0, 0, 0)),
            shaped((n_seq, 2, span, units), bf16),
            cost=cost(4 * rows * width * units, 2 * (rows * width + 2 * rows * units + 2 * width * units)),
        )(*normed, *gates, *ups)

    def back(m, t, dhn, hidden):
        o, p, scores, e_chunks = reads[m, t][:4]
        return call(
            "back",
            back_kernel,
            (chunks,),
            [own_rows(width, True), own_rows(width, True), chunk_rows(m, t, width, True), fixed((1, width)),
             fixed((head, width))]
            + [chunk_rows(m, t, head, True)] * 3 + [chunk_rows(m, t, slots, True)] * 2 + [own_rows(slots, True)] * 2
            + [chunk_state(True)],
            [own_rows(width, True)] + [own_rows(head, True)] * 3 + [own_rows(slots, True)] * 2
            + [chunk_state(True), whole((slots, 2 * head)), whole((slots, 128)), whole((8, width))],
            [shaped((TILE, width), bf16), shaped((TILE, head), bf16),
             shaped((TILE, head), f32), shaped((TILE, head), f32), shaped((TILE, slots), f32),
             shaped((TILE, slots), f32), states_shape, shaped((slots, 2 * head), f32), shaped((slots, 128), f32),
             shaped((8, width), f32)],
            [state_scratch, decay_scratch],
            cost=cost(2 * TILE * width * head + 2 * TILE * head * 1500, TILE * width * 14 + TILE * head * 20),
            loose=(0,),
            loose_out=(7, 8),
        )(dhn, hidden, cot, gain2, w_out, q, k, v, cum, inflow, p, scores, e_chunks)

    def last(m, t, leaving, saved):
        dq, dk_local, dv_local, h_sum, x_local, g_chunks = saved
        here = m * pieces + t
        return call(
            "last",
            last_kernel,
            (chunks,),
            [state_of(here), chunk_rows(m, t, head, True), chunk_rows(m, t, head, True),
             *[chunk_rows(m, t, slots, True)] * 3, chunk_state(True), chunk_state(True), own_rows(head, True),
             own_rows(head, True), own_rows(slots, True), own_rows(slots, True), whole((TILE, head)),
             pl.BlockSpec((TILE, width), lambda i: (here, 0))] + [anywhere] * 4,
            [whole((TILE, head)), whole((TILE, head)), whole((TILE, slots)), whole((TILE, width)), whole((8, slots)),
             whole((8, width))],
            [shaped((TILE, head), bf16), shaped((TILE, head), bf16), shaped((TILE, slots), bf16),
             shaped((TILE, width), bf16), shaped((8, slots), f32), shaped((8, width), f32)],
            [state_scratch] + [pltpu.VMEM((width, head), bf16)] * 3
            + [pltpu.VMEM((slots, width), bf16), pltpu.SemaphoreType.DMA((4,))],
            cost=cost(2 * TILE * width * (3 * head + slots), TILE * width * 8 + TILE * head * 20 + width * head * 6),
            loose=(0,),
            loose_out=(3,),
        )(leaving, k, v, z, cum, inflow, reads[m, t][3], g_chunks, dk_local, dv_local, h_sum, x_local, dq, x,
          w_query, w_key, w_value, forget_rows)

    line = Line()
    live = {}

    def start():
        names = list(live)
        live.update(zip(names, line.step([live[n] for n in names])))

    def end(coming=None, done=None, after=()):
        total = line.join(coming, after)
        if done is not None:
            live[done] = total

    reads, backs, lasts = {}, {}, {}
    outs, in_grads = [None], [None]
    eighth = TILE // 2

    def into(name, kernel, m, t, kept, dtype, inputs, specs):
        spec = pl.BlockSpec((1, eighth, width), lambda i: (m, 2 * t + i, 0))
        old = [] if kept[0] is None else [kept[0]]
        kept[0] = call(
            name,
            kernel,
            (2,),
            specs + [anywhere] * len(old),
            spec,
            shaped(tokens.shape, dtype),
            cost=cost(0, TILE * width * 10),
            loose=(1,),
            aliases={len(specs): 0} if old else None,
        )(*inputs, *old)

    piece_spec = pl.BlockSpec((eighth, width), lambda i: (i, 0))

    def finish_out(m, t):
        into("out", out_kernel, m, t, outs, bf16, [live.pop(("hidden", m, t)), live.pop(("ffn", m, t))],
             [piece_spec, piece_spec])

    def finish_grad(m, t):
        x_rows = pl.BlockSpec((eighth, width), lambda i: (2 * (m * pieces + t) + i, 0))
        into("in_grad", in_grad_kernel, m, t, in_grads, f32, [backs[m, t][0], live.pop(("dxn", m, t)), x, gain1],
             [piece_spec, piece_spec, x_rows, pl.BlockSpec((1, width), lambda i: (0, 0))])

    def go_read(m, t):
        before = live["entering"] if t == 0 else live.pop("left")
        reads[m, t] = read(m, t, before, m if t == 0 else 0)
        if t + 1 < pieces:
            live["left"] = reads[m, t][4]
        return reads[m, t][5]

    def go_feed(m, t):
        made = feed(m, t, live.pop(("att", m, t)))
        for name, value in zip(("hidden", "hn", "act", "dgate", "dup", "ffn_part"), made):
            live[name, m, t] = value
        return made[6]

    def go_back(m, t):
        backs[m, t] = back(m, t, live.pop(("dhn", m, t)), live["hidden", m, t])
        live["back", m, t] = backs[m, t][7]

    def go_last(m, t):
        lasts[m, t] = last(m, t, live["leaving"], backs[m, t][1:7])
        live["dxn_part", m, t] = lasts[m, t][3]

    def taken(name):
        return [live.pop((name, *key)) for key in every]

    live["entering"] = entering
    line.load(go_read(0, 0))
    start()
    end(go_read(0, 1))
    start()
    end(go_read(1, 0))
    start()
    end(go_read(1, 1), ("att", 0, 0))
    live.pop("entering")
    start()
    end(go_feed(0, 0), ("att", 0, 1))
    start()
    end(go_feed(0, 1), ("att", 1, 0))
    start()
    end(go_feed(1, 0), ("att", 1, 1))
    start()
    end(go_feed(1, 1), ("dhn", 0, 0))
    start()
    live["wide_grads"] = wide_grads(taken("hn"), taken("dgate"), taken("dup"))
    end(live.pop(("ffn_part", 0, 0)), ("dhn", 0, 1))
    start()
    wide_shares = lax.psum_scatter(live.pop("wide_grads"), "seq", scatter_dimension=0)
    go_back(0, 0)
    go_back(0, 1)
    end(live.pop(("ffn_part", 0, 1)), ("dhn", 1, 0))
    start()
    go_back(1, 0)
    live["down"] = down_grads(taken("act"))
    end(live.pop(("ffn_part", 1, 0)), ("dhn", 1, 1))
    start()
    go_back(1, 1)
    taken("back")
    own = [backs[key][7] for key in every] + [backs[key][8] for key in every]
    folded = in_vmem(
        "fold",
        functools.partial(fold_kernel, parts, pieces),
        own,
        [shaped(local.shape, f32), shaped(decay.shape, f32), shaped(sent.shape, bf16)],
    )

    xn_columns = [pl.BlockSpec((rows, 2 * columns), lambda j: (0, j))]
    piece_columns = [pl.BlockSpec((TILE, 2 * columns), lambda j: (0, j))] * len(every)
    piece_whole = [fixed((TILE, head))] * len(every)
    made = []

    def beside_first(state, got):
        live["xn"] = xn
        end(behind_of(live.pop(("ffn_part", 1, 1)), got), ("ffn", 0, 0))
        start()
        made.extend((live.pop("xn"), live.pop("down")))
        return state

    def beside_second(state, got):
        grads = call(
            "query_grads",
            functools.partial(query_grad_kernel, len(every), units),
            (width // columns // 2,),
            xn_columns + piece_columns + piece_whole * 2 + [anywhere],
            anywhere,
            shaped((n_seq, span, units + 2 * head), bf16),
            [pltpu.VMEM((2, 2 * group, span, 2 * head), bf16), pltpu.SemaphoreType.DMA((2,))],
            cost=cost(12 * rows * width * head, 3 * (4 * rows * width + 4 * rows * head + 4 * width * head)),
            aliases={1 + 3 * len(every): 0},
        )(behind_of(made[0], state), *[backs[key][0] for key in every], *[backs[key][1] for key in every],
          *[reads[key][0] for key in every], made[1])
        made.append(grads)
        return behind_of(state, grads)

    ties = [beside_first, beside_second]
    live["leaving"] = scan_states(n_seq, *folded, True, own, pieces, ties)
    live["query_grads"], live["wide"] = made[2], wide_shares
    go_last(0, 0)
    end(live.pop(("dxn_part", 0, 0)), ("ffn", 0, 1))
    start()
    wide_shares = live.pop("wide")
    down_shares = lax.psum_scatter(live.pop("query_grads"), "seq", scatter_dimension=0)
    go_last(0, 1)
    go_last(1, 0)
    live["xn"] = xn
    end(live.pop(("dxn_part", 0, 1)), ("ffn", 1, 0))
    start()
    go_last(1, 1)
    live.pop("leaving")
    few = [pl.BlockSpec((8, 2 * columns), lambda j: (0, j))] * len(every)
    live["state_grads"] = call(
        "state_grads",
        functools.partial(state_grad_kernel, len(every)),
        (width // columns // 2,),
        xn_columns + piece_whole * 2 + [fixed((TILE, slots))] * len(every) + [fixed((8, slots))] * len(every) + few * 2,
        pl.BlockSpec((2 * group, span + 16, 2 * head + 128), lambda j: (j, 0, 0)),
        shaped((n_seq, span + 16, 2 * head + 128), bf16),
        cost=cost(4 * rows * width * head, 2 * rows * width + 4 * rows * head + 4 * width * head),
    )(live.pop("xn"), *[lasts[key][i] for i in (0, 1, 2, 4, 5) for key in every], *[backs[key][9] for key in every])
    end(live.pop(("dxn_part", 1, 0)), ("ffn", 1, 1))
    start()
    attn_shares = lax.psum_scatter(live.pop("state_grads"), "seq", scatter_dimension=0)
    finish_out(0, 0)
    finish_out(0, 1)
    live["out"], live["down"] = outs[0], down_shares
    end(live.pop(("dxn_part", 1, 1)), ("dxn", 0, 0))
    start()
    outs[0], down_shares = live.pop("out"), live.pop("down")
    finish_out(1, 0)
    finish_out(1, 1)
    finish_grad(0, 0)
    live["out"], live["in_grad"] = outs[0], in_grads[0]
    end(None, ("dxn", 0, 1))
    start()
    in_grads[0] = live.pop("in_grad")
    finish_grad(0, 1)
    live["in_grad"] = in_grads[0]
    end(None, ("dxn", 1, 0))
    start()
    in_grads[0] = live.pop("in_grad")
    late = behind_of(attn_shares, in_grads[0]).astype(f32)
    gain1_total = late[:span, 2 * head + slots + 1]
    others = [lax.ppermute(gain1_total, "head", [(i, i ^ d) for i in range(n_head)]) for d in (1, 2, 3)]
    gain1_total = (gain1_total + others[0]) + (others[1] + others[2])
    finish_grad(1, 0)
    end(None, ("dxn", 1, 1), (gain1_total, in_grads[0]))
    finish_grad(1, 1)
    small_shares = late[:, 2 * head :]
    query_shares = down_shares[:, units:].astype(f32)

    return (
        live["out"],
        in_grads[0],
        gain1_total,
        query_shares[:, :head],
        late[:span, :head],
        late[:span, head : 2 * head],
        small_shares[:span, :slots],
        small_shares[span, :slots] + small_shares[span + 1, :slots],
        query_shares[:, head:].T,
        small_shares[:span, slots],
        wide_shares[0].astype(f32),
        wide_shares[1].astype(f32),
        down_shares[:, :units].astype(f32).T,
    )


def solution(mesh):
    rows, both = P(None, "seq", None), P("seq", "head")
    by_head, down = P(None, "head"), P("head", "seq")
    return jax.shard_map(
        on_device,
        mesh=mesh,
        in_specs=(rows, P(), by_head, by_head, by_head, by_head, P("head"), P("head", None), P(), both, both, down, rows),
        out_specs=(rows, rows, P("seq"), both, both, both, both, P("head"), down, P("seq"), both, both, down),
        check_vma=False,
    )
```

```python
import functools

import jax
import jax.numpy as jnp
from jax import lax
from jax.experimental import pallas as pl
from jax.experimental.pallas import tpu as pltpu
from jax.sharding import PartitionSpec as P

CHUNK = 128
TILE = 256
EPS = 1e-06
RATE = 0.5
MIB = 2**20
f32 = jnp.float32
bf16 = jnp.bfloat16
highest = lax.Precision.HIGHEST


def nn(a, b):
    return lax.dot_general(a, b, (((1,), (0,)), ((), ())), preferred_element_type=f32)


def nt(a, b):
    return lax.dot_general(a, b, (((1,), (1,)), ((), ())), preferred_element_type=f32)


def tn(a, b):
    return lax.dot_general(a, b, (((0,), (0,)), ((), ())), preferred_element_type=f32)


def exact(a, b, dims):
    return lax.dot_general(a, b, (dims, ((), ())), precision=highest, preferred_element_type=f32)


def halves(a):
    high = a.astype(bf16)
    return high, (a - high.astype(f32)).astype(bf16)


def call(name, kernel, grid, in_specs, out_specs, out_shape, scratch=(), vmem=24, cost=None, loose=(), loose_out=(),
         aliases=None):
    single = not isinstance(out_shape, list)
    shapes = [out_shape] if single else out_shape
    shapes = [s if i in loose_out else pltpu.HBM(s.shape, s.dtype) for i, s in enumerate(shapes)]
    function = pl.pallas_call(
        kernel,
        name=name,
        grid=grid,
        in_specs=in_specs,
        out_specs=out_specs,
        out_shape=shapes[0] if single else shapes,
        scratch_shapes=scratch,
        input_output_aliases=aliases or {},
        compiler_params=pltpu.CompilerParams(
            dimension_semantics=("arbitrary",) * len(grid), vmem_limit_bytes=vmem * MIB
        ),
        cost_estimate=cost,
    )

    def run(*operands):
        return function(*[
            o if i in loose or spec.memory_space == pltpu.SMEM else pltpu.with_memory_space_constraint(o, pltpu.HBM)
            for i, (o, spec) in enumerate(zip(operands, in_specs))
        ])

    return run


def cost(flops, data):
    return pl.CostEstimate(flops=int(flops), bytes_accessed=int(data), transcendentals=0)


def fixed(shape):
    zeros = (0,) * len(shape)
    return pl.BlockSpec(shape, lambda *_: zeros, pipeline_mode=pl.Buffered(1))


def shaped(shape, dtype):
    return jax.ShapeDtypeStruct(shape, dtype)


def triangle(lower):
    r = lax.broadcasted_iota(jnp.int32, (CHUNK, CHUNK), 0)
    c = lax.broadcasted_iota(jnp.int32, (CHUNK, CHUNK), 1)
    return r >= c if lower else r <= c


def gates(z):
    la = -RATE * lax.logistic(-z)
    y = -la
    taken = jnp.ones_like(y)
    for n in range(9, 1, -1):
        taken = 1.0 - y * (1.0 / n) * taken
    taken = y * taken
    cum = exact(triangle(True).astype(f32), la, ((1,), (0,)))
    return cum, jnp.exp(-cum) * taken


def turned_last(cum):
    return jnp.broadcast_to(cum[CHUNK - 1 :, :], cum.shape).T


def halves_sum(ones, values):
    high, low = halves(values)
    both = nn(ones.astype(bf16), jnp.concatenate([high, low], 1))
    width = values.shape[1]
    return both[:, :width] + both[:, width:]


def project_kernel(per_part, x_ref, gain_ref, wk_ref, wv_ref, wf_ref, bias_ref,
                   xn_ref, k_ref, v_ref, z_ref, cum_ref, in_ref, s_ref, d_ref, sent_ref, state, decay):
    @pl.when(lax.rem(pl.program_id(0), per_part) == 0)
    def _():
        state[...] = jnp.zeros_like(state)
        decay[...] = jnp.zeros_like(decay)

    x = x_ref[...].astype(f32)
    r1 = lax.rsqrt(jnp.mean(x * x, axis=-1, keepdims=True) + EPS)
    xn = (x * r1 * gain_ref[...]).astype(bf16)
    xn_ref[...] = xn
    k_ref[...] = nn(xn, wk_ref[...]).astype(bf16)
    v_ref[...] = nn(xn, wv_ref[...]).astype(bf16)
    z_ref[...] = nt(xn, wf_ref[...]) + bias_ref[...]
    width = k_ref.shape[1]
    for c in range(x_ref.shape[0] // CHUNK):
        rows = pl.ds(c * CHUNK, CHUNK)
        cum, inflow = gates(z_ref[rows, :])
        cum_ref[rows, :] = cum
        in_ref[rows, :] = inflow
        total = turned_last(cum)
        spread = inflow.astype(bf16)
        keep = jnp.exp(total[:, :1])
        state[:, :width] = keep * (state[:, :width] + tn(spread, k_ref[rows, :]))
        state[:, width:] = keep * (state[:, width:] + tn(spread, v_ref[rows, :]))
        decay[...] += total
    s_ref[0] = state[...]
    d_ref[0] = jnp.exp(decay[...])
    pack(sent_ref, 0, jnp.exp(decay[...]), state[...])


def query_kernel(xn_ref, wq_ref, q_ref):
    q_ref[...] = nn(xn_ref[...], wq_ref[...]).astype(bf16)


def read_kernel(q_ref, k_ref, v_ref, cum_ref, in_ref, e0_ref, wo_ref, o_ref, p_ref, sc_ref, e_ref, left_ref, att_ref, state):
    @pl.when(pl.program_id(0) == 0)
    def _():
        state[...] = e0_ref[...]

    width = q_ref.shape[1]
    lower = triangle(True)
    q, k, v = q_ref[...], k_ref[...], v_ref[...]
    cum, inflow = cum_ref[...], in_ref[...]
    total = turned_last(cum)
    growth = jnp.exp(cum)
    e_ref[0] = state[...]
    i_hi, i_lo = halves(inflow)
    a_hi, a_lo = halves(jnp.where(lower, nt(q, k), 0.0))
    e_hi, e_lo = halves(state[:, :width])
    scores = growth * (nt(q, e_hi) + nt(q, e_lo) + nn(a_hi, i_hi) + (nn(a_hi, i_lo) + nn(a_lo, i_hi)))
    top = jnp.exp(scores - jnp.max(scores, axis=-1, keepdims=True))
    p = top / jnp.sum(top, axis=-1, keepdims=True)
    w = (p * growth).astype(bf16)
    mixing = jnp.where(lower, nt(w, i_hi), 0.0).astype(bf16)
    o = (nn(w, state[:, width:].astype(bf16)) + nn(mixing, v)).astype(bf16)
    o_ref[...] = o
    att_ref[...] = nn(o, wo_ref[...]).astype(bf16)
    p_ref[...] = p
    sc_ref[...] = scores
    keep = jnp.exp(total[:, :1])
    state[:, :width] = keep * (state[:, :width] + tn(i_hi, k))
    state[:, width:] = keep * (state[:, width:] + tn(i_hi, v))
    left_ref[...] = state[...]


def back_kernel(dhn_ref, hid_ref, cot_ref, gain_ref, wo_ref, q_ref, k_ref, v_ref, cum_ref, in_ref, p_ref, sc_ref,
                e_ref, datt_ref, dq_ref, dkl_ref, dvl_ref, h_ref, x1_ref, g_ref, s_ref, d_ref, gg_ref, state, decay):
    step = pl.program_id(0)

    @pl.when(step == 0)
    def _():
        state[...] = jnp.zeros_like(state)
        decay[...] = jnp.zeros_like(decay)
        gg_ref[...] = jnp.zeros_like(gg_ref)

    hidden = hid_ref[...].astype(f32)
    dhn = dhn_ref[...].astype(f32)
    r2 = lax.rsqrt(jnp.mean(hidden * hidden, axis=-1, keepdims=True) + EPS)
    gg_ref[...] += jnp.sum((dhn * hidden * r2).reshape(-1, 8, hidden.shape[1]), axis=0)
    u2 = gain_ref[...] * dhn
    dhid = (
        cot_ref[...].astype(f32)
        + r2 * u2
        - hidden * (r2 * r2 * r2) * jnp.mean(u2 * hidden, axis=-1, keepdims=True)
    )
    datt = dhid.astype(bf16)
    datt_ref[...] = datt
    width = q_ref.shape[1]
    do = nt(datt, wo_ref[...]).astype(bf16)
    lower, upper = triangle(True), triangle(False)
    q, k, v = q_ref[...], k_ref[...], v_ref[...]
    cum, inflow = cum_ref[...], in_ref[...]
    total = turned_last(cum)
    growth = jnp.exp(cum)
    p = p_ref[...]
    i_hi, i_lo = halves(inflow)
    b_hi, b_lo = halves(jnp.where(lower, nt(do, v), 0.0))
    ev_hi, ev_lo = halves(e_ref[0, :, width:])
    dp = growth * (nt(do, ev_hi) + nt(do, ev_lo) + nn(b_hi, i_hi) + (nn(b_hi, i_lo) + nn(b_lo, i_hi)))
    ds = p * (dp - jnp.sum(p * dp, axis=-1, keepdims=True))
    w = (p * growth).astype(bf16)
    gds = (growth * ds).astype(bf16)
    n = jnp.where(lower, nt(gds, i_hi), 0.0).astype(bf16)
    dq_ref[...] = (nn(gds, e_ref[0, :, :width].astype(bf16)) + nn(n, k)).astype(bf16)
    n_t = jnp.where(upper, nt(i_hi, gds), 0.0).astype(bf16)
    m_t = jnp.where(upper, nt(i_hi, w), 0.0).astype(bf16)
    dkl_ref[...] = nn(n_t, q)
    dvl_ref[...] = nn(m_t, do)
    h_ref[...] = ds * sc_ref[...] + p * dp
    a_t = jnp.where(upper, nt(k, q), 0.0).astype(bf16)
    b_t = jnp.where(upper, nt(v, do), 0.0).astype(bf16)
    x1_ref[...] = nn(a_t, gds) + nn(b_t, w)
    keep = jnp.exp(total[:, :1])
    g_k, g_v = tn(gds, q), tn(w, do)
    g_ref[0, :, :width] = g_k
    g_ref[0, :, width:] = g_v
    state[:, :width] = g_k + keep * state[:, :width]
    state[:, width:] = g_v + keep * state[:, width:]
    decay[...] += total
    s_ref[...] = state[...]
    d_ref[...] = jnp.exp(decay[...])


def last_kernel(l0_ref, k_ref, v_ref, z_ref, cum_ref, in_ref, e_ref, g_ref, dkl_ref, dvl_ref, h_ref, x1_ref, dq_ref, x_ref,
                wq_ref, wk_ref, wv_ref, wf_ref, dk_ref, dv_ref, dz_ref, dxn_ref, bias_ref, gg_ref,
                state, wq, wk, wv, wf, sems):
    step, steps = pl.program_id(0), pl.num_programs(0)
    loads = [pltpu.make_async_copy(source, target, sems.at[i])
             for i, (source, target) in enumerate(((wq_ref, wq), (wk_ref, wk), (wv_ref, wv), (wf_ref, wf)))]

    @pl.when(step == 0)
    def _():
        for load in loads:
            load.start()
        state[...] = l0_ref[...]
        bias_ref[...] = jnp.zeros_like(bias_ref)

    width = k_ref.shape[1]
    k, v, z = k_ref[...], v_ref[...], z_ref[...]
    cum, inflow = cum_ref[...], in_ref[...]
    total = turned_last(cum)
    i_hi = inflow.astype(bf16)
    keep = jnp.exp(total[:, :1])
    lg = keep * state[...]
    lg_k, lg_v = lg[:, :width].astype(bf16), lg[:, width:].astype(bf16)
    rows = pl.ds(pl.multiple_of((steps - 1 - step) * CHUNK, CHUNK), CHUNK)
    dk_ref[rows, :] = (dkl_ref[...] + nn(i_hi, lg_k)).astype(bf16)
    dv_ref[rows, :] = (dvl_ref[...] + nn(i_hi, lg_v)).astype(bf16)
    x1 = x1_ref[...]
    x2 = nt(k, lg_k) + nt(v, lg_v)
    met = jnp.broadcast_to(jnp.sum(lg * e_ref[0], axis=1, keepdims=True), (lg.shape[0], CHUNK)).T
    h, r1 = h_ref[...], inflow * x1
    dla = (
        halves_sum(triangle(False), h - r1)
        + r1
        + halves_sum(triangle(True), inflow * x2)
        + met
        - jnp.exp(-cum) * (x1 + x2)
    )
    rate = lax.logistic(-z)
    dz = (dla * RATE * rate * (1.0 - rate)).astype(bf16)
    dz_ref[rows, :] = dz
    bias_ref[...] += jnp.sum(dz.astype(f32).reshape(-1, 8, dz.shape[1]), axis=0)
    state[...] = g_ref[0] + lg

    @pl.when(step == steps - 1)
    def _():
        for load in loads:
            load.wait()
        dxn = nt(dq_ref[...], wq[...]) + nt(dk_ref[...], wk[...]) + nt(dv_ref[...], wv[...]) + nn(dz_ref[...], wf[...])
        dxn_ref[...] = dxn.astype(bf16)
        x = x_ref[...].astype(f32)
        r1 = lax.rsqrt(jnp.mean(x * x, axis=-1, keepdims=True) + EPS)
        gg_ref[...] = jnp.sum((dxn * x * r1).reshape(-1, 8, x.shape[1]), axis=0)


def out_kernel(hid_ref, ffn_ref, *refs):
    refs[-1][0] = (hid_ref[...].astype(f32) + ffn_ref[...].astype(f32)).astype(bf16)


def in_grad_kernel(dhid_ref, dxn_ref, x_ref, gain_ref, *refs):
    x = x_ref[...].astype(f32)
    r1 = lax.rsqrt(jnp.mean(x * x, axis=-1, keepdims=True) + EPS)
    u1 = gain_ref[...] * dxn_ref[...].astype(f32)
    refs[-1][0] = dhid_ref[...].astype(f32) + r1 * u1 - x * (r1 * r1 * r1) * jnp.mean(u1 * x, axis=-1, keepdims=True)


def feed_kernel(first_row, x_ref, att_ref, gain_ref, cot_ref, full_ref, hid_ref, hn_ref, act_ref, dg_ref, du_ref,
                ffn_ref, dhn_ref, weights, x, cot, hid, hn, act, dg, du, ffn, in_sems, out_sems, weight_sems):
    rows, width = x.shape
    units = act.shape[1]
    blocks, _, span, _ = weights.shape
    tiles = [(u, min(TILE, units - u)) for u in range(0, units, TILE)]
    here = pl.ds(first_row, rows)
    reads = [pltpu.make_async_copy(source.at[here, :], target, in_sems.at[i])
             for i, (source, target) in enumerate(((x_ref, x), (cot_ref, cot)))]
    loads = [pltpu.make_async_copy(full_ref.at[:, :, :, pl.ds(u, size)], weights.at[:, :, :, pl.ds(u, size)],
                                   weight_sems.at[i]) for i, (u, size) in enumerate(tiles)]
    writes = [pltpu.make_async_copy(source, target, out_sems.at[i])
              for i, (source, target) in enumerate(
                  ((hid, hid_ref), (hn, hn_ref), (act, act_ref), (dg, dg_ref), (du, du_ref), (ffn, ffn_ref)))]
    for copy in reads + loads:
        copy.start()
    for copy in reads:
        copy.wait()
    hidden = x[...].astype(f32) + att_ref[...].astype(f32)
    hid[...] = hidden.astype(bf16)
    r2 = lax.rsqrt(jnp.mean(hidden * hidden, axis=-1, keepdims=True) + EPS)
    hn[...] = (hidden * r2 * gain_ref[...]).astype(bf16)
    writes[0].start()
    writes[1].start()
    for (u, size), load in zip(tiles, loads):
        load.wait()
        gate, up, dact = (
            nn(left[...], weights[:, i, :, u : u + size].reshape(width, size))
            for i, left in enumerate((hn, hn, cot))
        )
        s = lax.logistic(gate)
        silu = gate * s
        act[:, u : u + size] = (silu * up).astype(bf16)
        dg[:, u : u + size] = (dact * up * s * (1.0 + gate * (1.0 - s))).astype(bf16)
        du[:, u : u + size] = (dact * silu).astype(bf16)
    for write in writes[2:5]:
        write.start()
    group = max(1, TILE // span)
    for b in range(0, blocks, group):
        columns = slice(b * span, (b + group) * span)
        w_gate, w_up, w_down = (weights[b : b + group, i].reshape(group * span, units) for i in range(3))
        ffn[:, columns] = nt(act[...], w_down).astype(bf16)
        dhn_ref[:, columns] = (nt(dg[...], w_gate) + nt(du[...], w_up)).astype(bf16)
    writes[5].start()
    for write in writes:
        write.wait()


def summed(pairs):
    total = tn(*pairs[0])
    for pair in pairs[1:]:
        total = total + tn(*pair)
    return total.astype(bf16)


def down_grad_kernel(*refs):
    cot_ref, act, out_ref = refs[0], refs[1:-1], refs[-1]
    rows = act[0].shape[0]
    block = summed([(cot_ref[i * rows : (i + 1) * rows, :], a[...]) for i, a in enumerate(act)])
    out_ref[...] = block.reshape(out_ref.shape)


def wide_grad_kernel(*refs):
    out_ref = refs[-1]
    count = (len(refs) - 1) // 3
    hn, dg, du = refs[:count], refs[count : 2 * count], refs[2 * count : 3 * count]
    blocks, _, width, units = out_ref.shape
    for i, grads in enumerate((dg, du)):
        block = summed([(h[...], g[...]) for h, g in zip(hn, grads)])
        out_ref[:, i] = block.reshape(blocks, width, units)


def query_grad_kernel(count, first_column, *refs):
    xn_ref, out_ref, block, sems = refs[0], refs[-3], refs[-2], refs[-1]
    datt, dq, o = (refs[1 + i * count : 1 + (i + 1) * count] for i in range(3))
    rows, width = dq[0].shape
    _, groups, span, columns = block.shape
    step, steps = pl.program_id(0), pl.num_programs(0)

    def copy(at):
        slot = lax.rem(at, 2)
        return pltpu.make_async_copy(
            block.at[slot], out_ref.at[pl.ds(at * groups, groups), :, pl.ds(first_column, columns)], sems.at[slot]
        )

    @pl.when(step >= 2)
    def _():
        copy(step - 2).wait()

    xn = [xn_ref[i * rows : (i + 1) * rows, :] for i in range(count)]
    slot = lax.rem(step, 2)
    query = summed([(x, g[...]) for x, g in zip(xn, dq)])
    block[slot, :, :, :width] = query.reshape(groups, span, width)
    output = summed([(d[...], r[...]) for d, r in zip(datt, o)])
    block[slot, :, :, width:] = output.reshape(groups, span, width)
    copy(step).start()

    @pl.when(step == steps - 1)
    def _():
        copy(step - 1).wait()
        copy(step).wait()


def state_grad_kernel(count, *refs):
    xn_ref, out_ref = refs[0], refs[-1]
    dk, dv, dz, bias, gain1, gain2 = (refs[1 + i * count : 1 + (i + 1) * count] for i in range(6))
    rows, width = dk[0].shape
    slots = dz[0].shape[1]
    groups, high, _ = out_ref.shape
    span = high - 16
    xn = [xn_ref[i * rows : (i + 1) * rows, :] for i in range(count)]
    for i, grads in enumerate((dk, dv)):
        block = summed([(x, g[...]) for x, g in zip(xn, grads)])
        out_ref[:, :span, i * width : (i + 1) * width] = block.reshape(groups, span, width)
    forget = tn(xn[0], dz[0][...])
    for x, g in zip(xn[1:], dz[1:]):
        forget = forget + tn(x, g[...])
    pad = 128 - slots % 128

    def padded(values):
        return jnp.concatenate([values, jnp.zeros((values.shape[0], pad), f32)], 1)

    def column(parts):
        total = parts[0][...]
        for part in parts[1:]:
            total = total + part[...]
        return jnp.sum(total.T, axis=1, keepdims=True)

    small = padded(forget)
    lane = lax.broadcasted_iota(jnp.int32, small.shape, 1)
    small = jnp.where(lane == slots, column(gain2), jnp.where(lane == slots + 1, column(gain1), small))
    out_ref[:, :span, 2 * width :] = small.astype(bf16).reshape(groups, span, slots + pad)
    total = bias[0][...]
    for part in bias[1:]:
        total = total + part[...]
    total = padded(jnp.broadcast_to(jnp.sum(total, axis=0, keepdims=True), (16, slots)))
    upper = total.astype(bf16).astype(f32)
    row = lax.broadcasted_iota(jnp.int32, total.shape, 0)
    tail = jnp.where(row == 0, upper, jnp.where(row == 1, total - upper, 0.0)).astype(bf16)
    for g in range(groups):
        out_ref[g, span:, : 2 * width] = jnp.zeros((16, 2 * width), bf16)
        out_ref[g, span:, 2 * width :] = tail


def pack(ref, m, decay, state):
    high, low = halves(decay)
    lane = lax.broadcasted_iota(jnp.int32, decay.shape, 1)
    width = state.shape[1]
    ref[m, :, :width] = state.astype(bf16)
    ref[m, :, width:] = jnp.where(lane == 0, high.astype(f32), low.astype(f32)).astype(bf16)


def fold_kernel(parts, pieces, *refs):
    s_refs, d_refs, (s_out, d_out, sent) = refs[: parts * pieces], refs[parts * pieces : -3], refs[-3:]
    for m in range(parts):
        s, d = s_refs[m * pieces + pieces - 1][...], d_refs[m * pieces + pieces - 1][...]
        for t in reversed(range(pieces - 1)):
            here = d_refs[m * pieces + t][...]
            s, d = s_refs[m * pieces + t][...] + here[:, :1] * s, here * d
        s_out[m], d_out[m] = s, d
        pack(sent, m, d, s)


def hop_kernel(bit, after, first, final, parts, pieces, *refs):
    refs = list(refs)
    s_ref, d_ref, got_ref = refs[:3]
    refs = refs[3:]
    if not first:
        part_s_ref, part_d_ref = refs[:2]
        refs = refs[2:]
    early = (lax.axis_index("seq") & bit) == 0
    takes = early if after else jnp.logical_not(early)
    width = s_ref.shape[2]
    found = []
    for m in range(parts):
        tail = got_ref[m, :, width:].astype(f32)
        there_d, there_s = tail[:, :1] + tail[:, 1:2], got_ref[m, :, :width].astype(f32)
        s, d = s_ref[m], d_ref[m]
        there_wide = jnp.broadcast_to(there_d, d.shape)
        new_s = jnp.where(takes, s + d[:, :1] * there_s, there_s + there_d * s)
        if first:
            part_s, part_d = jnp.where(takes, there_s, 0.0), jnp.where(takes, there_wide, 1.0)
        else:
            part_s, part_d = part_s_ref[m], part_d_ref[m]
            part_s = jnp.where(takes, part_s + part_d[:, :1] * there_s, part_s)
            part_d = jnp.where(takes, part_d * there_wide, part_d)
        found.append((new_s, d * there_wide, part_s, part_d))
    if not final:
        s_out, d_out, part_s_out, part_d_out, sent = refs
        for m, (s, d, part_s, part_d) in enumerate(found):
            s_out[m], d_out[m], part_s_out[m], part_d_out[m] = s, d, part_s, part_d
            pack(sent, m, d, s)
        return
    *own, out = refs
    arriving = jnp.zeros_like(found[0][0])
    for m in reversed(range(parts)) if after else range(parts):
        s, d, part_s, part_d = found[m]
        enters = part_s + part_d[:, :1] * arriving
        arriving = s + d[:, :1] * arriving
        for t in reversed(range(pieces)) if after else range(1):
            out[m * pieces + t if after else m] = enters
            if after and t:
                here = m * pieces + t
                enters = own[here][...] + own[parts * pieces + here][:, :1] * enters


def in_vmem(name, kernel, operands, shapes):
    return pl.pallas_call(
        kernel,
        name=name,
        in_specs=[pl.BlockSpec(memory_space=pltpu.VMEM)] * len(operands),
        out_specs=[pl.BlockSpec(memory_space=pltpu.VMEM)] * len(shapes),
        out_shape=shapes,
        compiler_params=pltpu.CompilerParams(vmem_limit_bytes=12 * MIB),
        cost_estimate=cost(0, 6 * MIB),
    )(*operands)


def scan_states(n, state, decay, sent, after, own=(), pieces=1, ties=()):
    parts, slots, width = state.shape
    part, bit, hops = [], 1, 0
    while bit < n:
        got = lax.ppermute(sent, "seq", [(i, i ^ bit) for i in range(n)])
        final = 2 * bit == n
        shapes = [shaped(state.shape, f32), shaped(decay.shape, f32)] * 2 + [shaped(sent.shape, bf16)]
        if final:
            shapes = [shaped((parts * pieces, slots, width), f32)]
        if hops < len(ties) and ties[hops] is not None:
            state = ties[hops](state, got)
        results = in_vmem(
            "hop",
            functools.partial(hop_kernel, bit, after, not part, final, parts, pieces),
            [state, decay, got, *part, *(own if final else ())],
            shapes,
        )
        if final:
            return results[0]
        state, decay, *part, sent = results
        bit, hops = 2 * bit, hops + 1


def behind_of(value, *first):
    return lax.optimization_barrier((value,) + first)[0]


def join_kernel(has, *refs):
    refs = iter(refs)
    piece, outer, pair, middle, total, coming = (next(refs) if h else None for h in has)
    makes = (piece is not None, pair is not None or coming is not None, total is not None)
    new_pair, new_total, done = (next(refs) if m else None for m in makes)
    me = lax.axis_index("head")
    end = (me == 0) | (me == 3)

    def each(work):
        @pl.loop(0, TILE // 32)
        def _(i):
            work(pl.ds(pl.multiple_of(i * 32, 32), 32))

    def both(a, b, rows):
        return a[rows, :] + b[rows, :]

    @pl.when(end)
    def _():
        def work(rows):
            if coming is not None:
                new_total[rows, :] = coming[rows, :]
            if done is not None:
                done[rows, :] = outer[rows, :]

        each(work)

    @pl.when(jnp.logical_not(end))
    def _():
        def work(rows):
            if piece is not None:
                new_pair[rows, :] = both(piece, outer, rows)
            if pair is not None:
                new_total[rows, :] = both(pair, middle, rows)
            if done is not None:
                done[rows, :] = total[rows, :]

        each(work)


class Line:
    INWARD, OUTWARD, MIDDLE = [(0, 1), (3, 2)], [(1, 0), (2, 3)], [(1, 2), (2, 1)]

    def __init__(self):
        self.piece = self.pair = self.payload = None
        self.returns = False

    def load(self, piece):
        self.piece = self.payload = piece

    def step(self, inputs):
        piece, pair, payload, returns = self.piece, self.pair, self.payload, self.returns
        values = [v for v in (payload, pair) if v is not None] + inputs
        values = list(lax.optimization_barrier(tuple(values)))
        outer = middle = None
        if payload is not None:
            payload = values.pop(0)
            way = (self.INWARD if piece is not None else []) + (self.OUTWARD if returns else [])
            outer = lax.ppermute(payload, "head", way)
        if pair is not None:
            pair = values.pop(0)
            middle = lax.ppermute(pair, "head", self.MIDDLE)
        self.waiting = (piece, outer, pair, middle, payload if returns else None)
        return values

    def join(self, coming=None, after=()):
        piece, outer, pair, middle, total = self.waiting
        if after:
            outer = behind_of(outer, *after)
        if piece is None and total is None:
            outer = None
        operands = [piece, outer, pair, middle, total, coming]
        makes = [piece is not None, pair is not None or coming is not None, total is not None]
        arrays = [o for o in operands if o is not None]
        results = in_vmem(
            "join",
            functools.partial(join_kernel, [o is not None for o in operands]),
            arrays,
            [shaped(arrays[0].shape, bf16)] * sum(makes),
        )
        results = iter(results)
        self.pair, self.payload, done = (next(results) if m else None for m in makes)
        self.returns = pair is not None
        self.piece = coming
        return done


def on_device(tokens, gain_attn, w_query, w_key, w_value, w_forget, forget_bias, w_out, gain_ffn, w_gate, w_up, w_down,
              cotangent):
    parts, part_rows, width = tokens.shape
    rows = parts * part_rows
    head = w_query.shape[1]
    slots = w_forget.shape[1]
    units = w_gate.shape[1]
    n_seq, n_head = lax.axis_size("seq"), lax.axis_size("head")
    span = w_gate.shape[0]
    per_part = pieces = part_rows // TILE
    chunks = TILE // CHUNK
    every = [(m, t) for m in range(parts) for t in range(pieces)]

    x = tokens.reshape(rows, width)
    cot = cotangent.reshape(rows, width)
    gain1 = gain_attn.reshape(1, width)
    gain2 = gain_ffn.reshape(1, width)
    state_scratch = pltpu.VMEM((slots, 2 * head), f32)
    decay_scratch = pltpu.VMEM((slots, 128), f32)
    anywhere = pl.BlockSpec(memory_space=pl.ANY)
    in_place = pl.BlockSpec(memory_space=pltpu.VMEM)

    all_rows = lambda c: pl.BlockSpec((TILE, c), lambda i: (i, 0))
    by_part = lambda c: pl.BlockSpec((1, slots, c), lambda i: (i // per_part, 0, 0))
    forget_rows = w_forget.T
    xn, k, v, z, cum, inflow, local, decay, sent = call(
        "project",
        functools.partial(project_kernel, per_part),
        (rows // TILE,),
        [all_rows(width), fixed((1, width))] + [fixed((width, head))] * 2 + [fixed((slots, width)), fixed((1, slots))],
        [all_rows(width), all_rows(head), all_rows(head)] + [all_rows(slots)] * 3
        + [by_part(2 * head), by_part(128), by_part(2 * head + 128)],
        [shaped((rows, width), bf16)] + [shaped((rows, head), bf16)] * 2
        + [shaped((rows, slots), f32)] * 3 + [shaped((parts, slots, 2 * head), f32), shaped((parts, slots, 128), f32),
                                             shaped((parts, slots, 2 * head + 128), bf16)],
        [state_scratch, decay_scratch],
        cost=cost(2 * rows * width * (2 * head + slots), 2 * rows * width * 3 + 2 * width * 2 * head),
        loose_out=(6, 7, 8),
    )(x, gain1, w_key, w_value, forget_rows, forget_bias.reshape(1, slots))
    q = call(
        "query",
        query_kernel,
        (rows // TILE,),
        [all_rows(width), fixed((width, head))],
        all_rows(head),
        shaped((rows, head), bf16),
        cost=cost(2 * rows * width * head, 2 * rows * (width + head) + 2 * width * head),
    )(xn, w_query)
    stacked = []

    def stack_weights(state, got):
        gate, down, _ = lax.optimization_barrier((w_gate, w_down, got))
        stacked.append(jnp.stack([gate, w_up, down.T]))
        return state

    entering = scan_states(n_seq, local, decay, sent, False, ties=[stack_weights])
    full = lax.all_gather(stacked[0], "seq")

    def chunk_rows(m, t, columns, back):
        start = (m * pieces + t) * chunks
        return pl.BlockSpec((CHUNK, columns), lambda i: (start + (chunks - 1 - i if back else i), 0))

    def own_rows(columns, back):
        return pl.BlockSpec((CHUNK, columns), lambda i: (chunks - 1 - i if back else i, 0))

    def chunk_state(back):
        return pl.BlockSpec((1, slots, 2 * head), lambda i: (chunks - 1 - i if back else i, 0, 0))

    def whole(shape):
        return pl.BlockSpec(shape, lambda i: (0,) * len(shape))

    def state_of(m):
        return pl.BlockSpec((None, slots, 2 * head), lambda i: (m, 0, 0))

    states_shape = shaped((chunks, slots, 2 * head), f32)

    def read(m, t, entering, which):
        return call(
            "read",
            read_kernel,
            (chunks,),
            [chunk_rows(m, t, head, False)] * 3 + [chunk_rows(m, t, slots, False)] * 2
            + [state_of(which), fixed((head, width))],
            [own_rows(head, False), own_rows(slots, False), own_rows(slots, False), chunk_state(False),
             pl.BlockSpec((None, slots, 2 * head), lambda i: (0, 0, 0)), own_rows(width, False)],
            [shaped((TILE, head), bf16), shaped((TILE, slots), f32), shaped((TILE, slots), f32), states_shape,
             shaped((1, slots, 2 * head), f32), shaped((TILE, width), bf16)],
            [state_scratch],
            cost=cost(2 * TILE * head * (600 + width), 2 * TILE * (head * 4 + width) + 2 * head * width),
            loose=(5,),
            loose_out=(4, 5),
        )(q, k, v, cum, inflow, entering, w_out)

    def feed(m, t, attended):
        tile_count = pl.cdiv(units, TILE)
        vmem = pltpu.VMEM
        return call(
            "feed",
            functools.partial(feed_kernel, (m * pieces + t) * TILE),
            (),
            [anywhere, in_place, in_place, anywhere, anywhere],
            [anywhere] * 6 + [in_place],
            [shaped((TILE, width), bf16)] * 2 + [shaped((TILE, units), bf16)] * 3
            + [shaped((TILE, width), bf16)] * 2,
            [vmem((n_seq, 3, span, units), bf16), vmem((TILE, width), bf16), vmem((TILE, width), bf16),
             vmem((TILE, width), bf16), vmem((TILE, width), bf16)] + [vmem((TILE, units), bf16)] * 3
            + [vmem((TILE, width), bf16), pltpu.SemaphoreType.DMA((2,)), pltpu.SemaphoreType.DMA((6,)),
               pltpu.SemaphoreType.DMA((tile_count,))],
            cost=cost(12 * TILE * width * units, 6 * width * units + TILE * width * 14),
            vmem=44,
            loose=(1, 2),
            loose_out=(6,),
        )(x, attended, gain2, cot, full)

    group = max(1, TILE // span)
    columns = group * span
    def down_grads(acts):
        return call(
            "down_grads",
            down_grad_kernel,
            (width // columns // 2,),
            [pl.BlockSpec((rows, 2 * columns), lambda j: (0, j))] + [fixed((TILE, units))] * len(acts),
            pl.BlockSpec((2 * group, span, units), lambda j: (j, 0, 0)),
            shaped((n_seq, span, units + 2 * head), bf16),
            cost=cost(2 * rows * width * units, 2 * (rows * width + rows * units + width * units)),
        )(cot, *acts)

    def wide_grads(normed, gates, ups):
        count = len(normed)
        return call(
            "wide_grads",
            wide_grad_kernel,
            (width // columns,),
            [pl.BlockSpec((TILE, columns), lambda j: (0, j))] * count
            + [fixed((TILE, units))] * (2 * count),
            pl.BlockSpec((group, 2, span, units), lambda j: (j, 0, 0, 0)),
            shaped((n_seq, 2, span, units), bf16),
            cost=cost(4 * rows * width * units, 2 * (rows * width + 2 * rows * units + 2 * width * units)),
        )(*normed, *gates, *ups)

    def back(m, t, dhn, hidden):
        o, p, scores, e_chunks = reads[m, t][:4]
        return call(
            "back",
            back_kernel,
            (chunks,),
            [own_rows(width, True), own_rows(width, True), chunk_rows(m, t, width, True), fixed((1, width)),
             fixed((head, width))]
            + [chunk_rows(m, t, head, True)] * 3 + [chunk_rows(m, t, slots, True)] * 2 + [own_rows(slots, True)] * 2
            + [chunk_state(True)],
            [own_rows(width, True)] + [own_rows(head, True)] * 3 + [own_rows(slots, True)] * 2
            + [chunk_state(True), whole((slots, 2 * head)), whole((slots, 128)), whole((8, width))],
            [shaped((TILE, width), bf16), shaped((TILE, head), bf16),
             shaped((TILE, head), f32), shaped((TILE, head), f32), shaped((TILE, slots), f32),
             shaped((TILE, slots), f32), states_shape, shaped((slots, 2 * head), f32), shaped((slots, 128), f32),
             shaped((8, width), f32)],
            [state_scratch, decay_scratch],
            cost=cost(2 * TILE * width * head + 2 * TILE * head * 1500, TILE * width * 14 + TILE * head * 20),
            loose=(0,),
            loose_out=(7, 8),
        )(dhn, hidden, cot, gain2, w_out, q, k, v, cum, inflow, p, scores, e_chunks)

    def last(m, t, leaving, saved):
        dq, dk_local, dv_local, h_sum, x_local, g_chunks = saved
        here = m * pieces + t
        return call(
            "last",
            last_kernel,
            (chunks,),
            [state_of(here), chunk_rows(m, t, head, True), chunk_rows(m, t, head, True),
             *[chunk_rows(m, t, slots, True)] * 3, chunk_state(True), chunk_state(True), own_rows(head, True),
             own_rows(head, True), own_rows(slots, True), own_rows(slots, True), whole((TILE, head)),
             pl.BlockSpec((TILE, width), lambda i: (here, 0))] + [anywhere] * 4,
            [whole((TILE, head)), whole((TILE, head)), whole((TILE, slots)), whole((TILE, width)), whole((8, slots)),
             whole((8, width))],
            [shaped((TILE, head), bf16), shaped((TILE, head), bf16), shaped((TILE, slots), bf16),
             shaped((TILE, width), bf16), shaped((8, slots), f32), shaped((8, width), f32)],
            [state_scratch] + [pltpu.VMEM((width, head), bf16)] * 3
            + [pltpu.VMEM((slots, width), bf16), pltpu.SemaphoreType.DMA((4,))],
            cost=cost(2 * TILE * width * (3 * head + slots), TILE * width * 8 + TILE * head * 20 + width * head * 6),
            loose=(0,),
            loose_out=(3,),
        )(leaving, k, v, z, cum, inflow, reads[m, t][3], g_chunks, dk_local, dv_local, h_sum, x_local, dq, x,
          w_query, w_key, w_value, forget_rows)

    line = Line()
    live = {}

    def start():
        names = list(live)
        live.update(zip(names, line.step([live[n] for n in names])))

    def end(coming=None, done=None, after=()):
        total = line.join(coming, after)
        if done is not None:
            live[done] = total

    reads, backs, lasts = {}, {}, {}
    outs, in_grads = [None], [None]
    eighth = TILE // 2

    def into(name, kernel, m, t, kept, dtype, inputs, specs):
        spec = pl.BlockSpec((1, eighth, width), lambda i: (m, 2 * t + i, 0))
        old = [] if kept[0] is None else [kept[0]]
        kept[0] = call(
            name,
            kernel,
            (2,),
            specs + [anywhere] * len(old),
            spec,
            shaped(tokens.shape, dtype),
            cost=cost(0, TILE * width * 10),
            loose=(1,),
            aliases={len(specs): 0} if old else None,
        )(*inputs, *old)

    piece_spec = pl.BlockSpec((eighth, width), lambda i: (i, 0))

    def finish_out(m, t):
        into("out", out_kernel, m, t, outs, bf16, [live.pop(("hidden", m, t)), live.pop(("ffn", m, t))],
             [piece_spec, piece_spec])

    def finish_grad(m, t):
        x_rows = pl.BlockSpec((eighth, width), lambda i: (2 * (m * pieces + t) + i, 0))
        into("in_grad", in_grad_kernel, m, t, in_grads, f32, [backs[m, t][0], live.pop(("dxn", m, t)), x, gain1],
             [piece_spec, piece_spec, x_rows, pl.BlockSpec((1, width), lambda i: (0, 0))])

    def go_read(m, t):
        before = live["entering"] if t == 0 else live.pop("left")
        reads[m, t] = read(m, t, before, m if t == 0 else 0)
        if t + 1 < pieces:
            live["left"] = reads[m, t][4]
        return reads[m, t][5]

    def go_feed(m, t):
        made = feed(m, t, live.pop(("att", m, t)))
        for name, value in zip(("hidden", "hn", "act", "dgate", "dup", "ffn_part"), made):
            live[name, m, t] = value
        return made[6]

    def go_back(m, t):
        backs[m, t] = back(m, t, live.pop(("dhn", m, t)), live["hidden", m, t])
        live["back", m, t] = backs[m, t][7]

    def go_last(m, t):
        lasts[m, t] = last(m, t, live["leaving"], backs[m, t][1:7])
        live["dxn_part", m, t] = lasts[m, t][3]

    def taken(name):
        return [live.pop((name, *key)) for key in every]

    live["entering"] = entering
    line.load(go_read(0, 0))
    start()
    end(go_read(0, 1))
    start()
    end(go_read(1, 0))
    start()
    end(go_read(1, 1), ("att", 0, 0))
    live.pop("entering")
    start()
    end(go_feed(0, 0), ("att", 0, 1))
    start()
    end(go_feed(0, 1), ("att", 1, 0))
    start()
    end(go_feed(1, 0), ("att", 1, 1))
    start()
    end(go_feed(1, 1), ("dhn", 0, 0))
    start()
    live["wide_grads"] = wide_grads(taken("hn"), taken("dgate"), taken("dup"))
    end(live.pop(("ffn_part", 0, 0)), ("dhn", 0, 1))
    start()
    wide_shares = lax.psum_scatter(live.pop("wide_grads"), "seq", scatter_dimension=0)
    go_back(0, 0)
    go_back(0, 1)
    end(live.pop(("ffn_part", 0, 1)), ("dhn", 1, 0))
    start()
    go_back(1, 0)
    live["down"] = down_grads(taken("act"))
    end(live.pop(("ffn_part", 1, 0)), ("dhn", 1, 1))
    start()
    go_back(1, 1)
    taken("back")
    own = [backs[key][7] for key in every] + [backs[key][8] for key in every]
    folded = in_vmem(
        "fold",
        functools.partial(fold_kernel, parts, pieces),
        own,
        [shaped(local.shape, f32), shaped(decay.shape, f32), shaped(sent.shape, bf16)],
    )

    xn_columns = [pl.BlockSpec((rows, TILE), lambda j: (0, j))]
    piece_columns = [pl.BlockSpec((TILE, TILE), lambda j: (0, j))] * len(every)
    piece_whole = [fixed((TILE, head))] * len(every)
    made = []

    def beside_first(state, got):
        live["xn"] = xn
        end(behind_of(live.pop(("ffn_part", 1, 1)), got), ("ffn", 0, 0))
        start()
        made.extend((live.pop("xn"), live.pop("down")))
        return state

    def beside_second(state, got):
        grads = call(
            "query_grads",
            functools.partial(query_grad_kernel, len(every), units),
            (width // columns // 2,),
            [pl.BlockSpec((rows, 2 * columns), lambda j: (0, j))]
            + [pl.BlockSpec((TILE, 2 * columns), lambda j: (0, j))] * len(every) + piece_whole * 2 + [anywhere],
            anywhere,
            shaped((n_seq, span, units + 2 * head), bf16),
            [pltpu.VMEM((2, 2 * group, span, 2 * head), bf16), pltpu.SemaphoreType.DMA((2,))],
            cost=cost(12 * rows * width * head, 3 * (4 * rows * width + 4 * rows * head + 4 * width * head)),
            aliases={1 + 3 * len(every): 0},
        )(behind_of(made[0], state), *[backs[key][0] for key in every], *[backs[key][1] for key in every],
          *[reads[key][0] for key in every], made[1])
        made.append(grads)
        return behind_of(state, grads)

    ties = [beside_first, beside_second]
    live["leaving"] = scan_states(n_seq, *folded, True, own, pieces, ties)
    live["query_grads"], live["wide"] = made[2], wide_shares
    go_last(0, 0)
    end(live.pop(("dxn_part", 0, 0)), ("ffn", 0, 1))
    start()
    wide_shares = live.pop("wide")
    down_shares = lax.psum_scatter(live.pop("query_grads"), "seq", scatter_dimension=0)
    go_last(0, 1)
    go_last(1, 0)
    live["xn"] = xn
    end(live.pop(("dxn_part", 0, 1)), ("ffn", 1, 0))
    start()
    go_last(1, 1)
    live.pop("leaving")
    few = [pl.BlockSpec((8, TILE), lambda j: (0, j))] * len(every)
    live["state_grads"] = call(
        "state_grads",
        functools.partial(state_grad_kernel, len(every)),
        (width // TILE,),
        xn_columns + piece_whole * 2 + [fixed((TILE, slots))] * len(every) + [fixed((8, slots))] * len(every) + few * 2,
        pl.BlockSpec((group, span + 16, 2 * head + 128), lambda j: (j, 0, 0)),
        shaped((n_seq, span + 16, 2 * head + 128), bf16),
        cost=cost(4 * rows * width * head, 2 * rows * width + 4 * rows * head + 4 * width * head),
    )(live.pop("xn"), *[lasts[key][i] for i in (0, 1, 2, 4, 5) for key in every], *[backs[key][9] for key in every])
    end(live.pop(("dxn_part", 1, 0)), ("ffn", 1, 1))
    start()
    attn_shares = lax.psum_scatter(live.pop("state_grads"), "seq", scatter_dimension=0)
    finish_out(0, 0)
    finish_out(0, 1)
    live["out"], live["down"] = outs[0], down_shares
    end(live.pop(("dxn_part", 1, 1)), ("dxn", 0, 0))
    start()
    outs[0], down_shares = live.pop("out"), live.pop("down")
    finish_out(1, 0)
    finish_out(1, 1)
    finish_grad(0, 0)
    live["out"], live["in_grad"] = outs[0], in_grads[0]
    end(None, ("dxn", 0, 1))
    start()
    in_grads[0] = live.pop("in_grad")
    finish_grad(0, 1)
    live["in_grad"] = in_grads[0]
    end(None, ("dxn", 1, 0))
    start()
    in_grads[0] = live.pop("in_grad")
    late = behind_of(attn_shares, in_grads[0]).astype(f32)
    gain1_total = late[:span, 2 * head + slots + 1]
    others = [lax.ppermute(gain1_total, "head", [(i, i ^ d) for i in range(n_head)]) for d in (1, 2, 3)]
    gain1_total = (gain1_total + others[0]) + (others[1] + others[2])
    finish_grad(1, 0)
    end(None, ("dxn", 1, 1), (gain1_total, in_grads[0]))
    finish_grad(1, 1)
    small_shares = late[:, 2 * head :]
    query_shares = down_shares[:, units:].astype(f32)

    return (
        live["out"],
        in_grads[0],
        gain1_total,
        query_shares[:, :head],
        late[:span, :head],
        late[:span, head : 2 * head],
        small_shares[:span, :slots],
        small_shares[span, :slots] + small_shares[span + 1, :slots],
        query_shares[:, head:].T,
        small_shares[:span, slots],
        wide_shares[0].astype(f32),
        wide_shares[1].astype(f32),
        down_shares[:, :units].astype(f32).T,
    )


def solution(mesh):
    rows, both = P(None, "seq", None), P("seq", "head")
    by_head, down = P(None, "head"), P("head", "seq")
    return jax.shard_map(
        on_device,
        mesh=mesh,
        in_specs=(rows, P(), by_head, by_head, by_head, by_head, P("head"), P("head", None), P(), both, both, down, rows),
        out_specs=(rows, rows, P("seq"), both, both, both, both, P("head"), down, P("seq"), both, both, down),
        check_vma=False,
    )
```
